32 devices in a mesh: depth: 2 (over y), row: 4 (over x, core), col: 4 (over z).
Axes of the slice: x: 2, y: 2, z: 4, core: 2. Of those that a mesh axis runs over, the one named last changes fastest.
Arguments:
- volume: bfloat16 [64, 64, 4096], P('depth', 'row', 'col'), may hold values from -6 to 6
- first_weight: bfloat16 [64, 864], replicated, may hold values from -0.21875 to 0.21875
- second_weight: bfloat16 [128, 1728], replicated, may hold values from -0.15625 to 0.15625
- cotangent: bfloat16 [16, 16, 4096], P('depth', 'row', 'col'), may hold values from -0.011962891 to 0.011962891
Outputs:
- first_grad: float32 [64, 864], replicated
- second_grad: float32 [128, 1728], replicated
The draws below stay inside these ranges and needn't reach their ends.
All inputs are finite; a program needn't handle non-finite values.
Results may differ from the reference program's by a relative error of at most 0.0047.
Values may be sent and summed in bfloat16 or wider, within the bound.
No kernel may reach another device: no remote copies, remote signals or barrier semaphores. Data moves between devices by JAX's collectives and lax.ppermute only.
A program may use at most 128 MiB of HBM per device.

```python
import jax
import jax.numpy as jnp
from jax import lax

C0 = 32
C1 = 64
C2 = 128
ND = 64
NR = 64
NC = 128


def block_levels(key, dims, pieces, smallest, high):
    gain, own = 1.0, jax.random.fold_in(key, 6)
    for dim, shards_of in pieces:
        steps = jnp.exp(jax.random.uniform(jax.random.fold_in(own, dim), (shards_of,), jnp.float32, smallest / len(pieces), high / len(pieces)))
        gain = gain * jnp.repeat(steps, dims[dim] // shards_of).reshape([-1 if axis == dim else 1 for axis in range(len(dims))])
    return gain


def noise(own_key, dims, deviation, limit, pieces=(), held_as=jnp.bfloat16):
    loudness = block_levels(own_key, dims, pieces, -0.22, 0.18) if pieces else 1.0
    drawn = jax.random.normal(own_key, dims, jnp.float32) * deviation * loudness
    return jnp.minimum(jnp.maximum(drawn, -limit), limit).astype(held_as)


def setup_inputs(seed: int = 0) -> dict:
    seeds = jax.random.split(jax.random.key(seed), 5)
    volume = noise(seeds[0], (ND, NR, NC * C0), 1.0, 6.0, ((0, 2), (1, 4), (2, 4)))
    first_weight = noise(seeds[1], (C1, 27 * C0), (27 * C0) ** -0.5, 0.21875)
    second_weight = noise(seeds[2], (C2, 27 * C1), (27 * C1) ** -0.5, 0.15625)
    cotangent = noise(seeds[3], (ND // 4, NR // 4, NC // 4 * C2), 0.002, 0.011962891, ((0, 2), (1, 4), (2, 4)))
    return {"volume": volume, "first_weight": first_weight, "second_weight": second_weight, "cotangent": cotangent}


def leaky(values):
    return 0.6 * values + 0.4 * (jnp.sqrt(values * values + 1.0) - 1.0)

def leaky_slope(values):
    return 0.6 + 0.4 * values / jnp.sqrt(values * values + 1.0)

def conv_plain(field, weight_mat, in_chan):
    kernel = weight_mat.reshape(weight_mat.shape[0], 3, 3, 3, in_chan).transpose(0, 4, 1, 2, 3)
    result = lax.conv_general_dilated(field[None], kernel, (2, 2, 2), ((1, 0), (1, 0), (1, 0)), dimension_numbers=('NCDHW', 'OIDHW', 'NCDHW'), precision=lax.Precision.HIGHEST)
    return result[0]

def reference(volume, first_weight, second_weight, cotangent):
    volume_f = volume.astype(jnp.float32).reshape(ND, NR, NC, C0).transpose(3, 0, 1, 2)
    upstream = cotangent.astype(jnp.float32).reshape(ND // 4, NR // 4, NC // 4, C2).transpose(3, 0, 1, 2)
    first_f = first_weight.astype(jnp.float32)
    second_f = second_weight.astype(jnp.float32)
    pre_one = conv_plain(volume_f, first_f, C0)
    hidden = lax.optimization_barrier(leaky(pre_one).astype(jnp.bfloat16))
    hidden_f = hidden.astype(jnp.float32)

    def second_section(hidden_in, weight_mat):
        return conv_plain(hidden_in, weight_mat, C1)
    pre_two, pullback_two = jax.vjp(second_section, hidden_f, second_f)
    delta_two = lax.optimization_barrier((upstream * leaky_slope(pre_two)).astype(jnp.bfloat16))
    back_one, second_grad = pullback_two(delta_two.astype(jnp.float32))
    delta_one = lax.optimization_barrier((back_one * leaky_slope(pre_one)).astype(jnp.bfloat16))

    def first_section(weight_mat):
        return conv_plain(volume_f, weight_mat, C0)
    unused_out, pullback_one = jax.vjp(first_section, first_f)
    first_grad = pullback_one(delta_one.astype(jnp.float32))[0]
    return (first_grad, second_grad)
```

```python
import jax
import jax.numpy as jnp
from jax import lax
from jax.experimental import pallas as pl
from jax.experimental.pallas import tpu as pltpu
from jax.sharding import PartitionSpec as P

LANES = 128
SECOND_ROWS = 27 * 64
F32 = jnp.float32
BF16 = jnp.bfloat16


def pairs_on_line(count, kind):
    firsts = range(kind, count - 1, 2)
    swapped = [(i, i + 1) for i in firsts] + [(i + 1, i) for i in firsts]
    met = {i for i, j in swapped}
    return swapped + [(i, i) for i in range(count) if i not in met]


def add_up(*terms):
    terms = [term.astype(F32) for term in terms]
    while len(terms) > 1:
        terms = [terms[n] + terms[n + 1] for n in range(0, len(terms), 2)]
    return terms[0].astype(BF16)


def matmul(left, right):
    return lax.dot_general(left, right, (((1,), (0,)), ((), ())), preferred_element_type=F32)


def pack(flag_ref, vol_ref, cot_ref, dep_ref, row_a_ref, row_b_ref, edge_a_ref, edge_b_ref, col_a_ref, col_b_ref):
    first_plane, row_even, col_even = flag_ref[0] == 0, flag_ref[1] == 0, flag_ref[2] == 0
    row_inner, col_inner = flag_ref[3] != 0, flag_ref[4] != 0
    planes, high, width = vol_ref.shape
    cots = cot_ref.shape[0]

    def rows(block, a_ref, b_ref, n):
        low, top = block[:4], block[high - 4 :]
        a_ref[n] = jnp.where(row_even, top, low).astype(BF16)
        b_ref[n] = jnp.where(row_inner, jnp.where(row_even, low, top), 0.0).astype(BF16)

    def plane(d, carry):
        block = vol_ref[d].astype(F32)
        rows(block, row_a_ref, row_b_ref, d)
        left, right = block[:, :LANES], block[:, width - LANES :]
        col_a_ref[d] = jnp.where(col_even, right, left).astype(BF16)
        col_b_ref[d] = jnp.where(col_inner, jnp.where(col_even, left, right), 0.0).astype(BF16)
        return carry

    lax.fori_loop(0, planes, plane, 0)
    for q in range(4):
        block = jnp.where(first_plane, vol_ref[planes - 4 + q].astype(F32), vol_ref[q].astype(F32))
        dep_ref[q] = block.astype(BF16)
        rows(block, edge_a_ref, edge_b_ref, q)
    cot = cot_ref[...].astype(F32)
    dep_ref[4] = jnp.concatenate([cot[0]] * 4, axis=0).astype(BF16)
    edge_a_ref[4] = cot[0].astype(BF16)
    edge_b_ref[4] = jnp.where(row_inner, cot[0], 0.0).astype(BF16)
    for g in range(cots // 4):
        tops = jnp.concatenate([cot[4 * g + n, :1] for n in range(4)], axis=0)
        row_a_ref[planes + g] = tops.astype(BF16)
        row_b_ref[planes + g] = jnp.where(row_inner, tops, 0.0).astype(BF16)
        side = jnp.concatenate([cot[4 * g + n, :, :LANES] for n in range(4)], axis=0)
        col_a_ref[planes + g] = side.astype(BF16)
        col_b_ref[planes + g] = jnp.where(col_inner, side, 0.0).astype(BF16)


def pack_corners(flag_ref, dep_ref, row_a_ref, row_b_ref, edge_a_ref, edge_b_ref, col_a_ref, col_b_ref):
    row_even, col_even, col_inner = flag_ref[1] == 0, flag_ref[2] == 0, flag_ref[4] != 0
    width = dep_ref.shape[2]
    groups = row_a_ref.shape[0]
    planes = (groups * 16) // 17
    faces = (slice(0, LANES), slice(width - LANES, width))

    def store(n, left, right):
        col_a_ref[n] = jnp.where(col_even, right, left).astype(BF16)
        col_b_ref[n] = jnp.where(col_inner, jnp.where(col_even, left, right), 0.0).astype(BF16)

    def lower_upper(a_ref, b_ref, source, target):
        values = []
        for lanes in faces:
            a, b = a_ref[source, :, lanes].astype(F32), b_ref[source, :, lanes].astype(F32)
            values.append(jnp.concatenate([jnp.where(row_even, b, a), jnp.where(row_even, a, b)], axis=0))
        store(target, *values)

    def plane(d, carry):
        lower_upper(row_a_ref, row_b_ref, d, d)
        return carry

    lax.fori_loop(0, planes, plane, 0)
    for q in range(4):
        lower_upper(edge_a_ref, edge_b_ref, q, planes + q)
        left, right = [dep_ref[q, :, lanes].astype(F32) for lanes in faces]
        for n in range(2):
            store(planes + 4 + 2 * q + n, left[8 * n : 8 * n + 8], right[8 * n : 8 * n + 8])
    lanes = faces[0]
    tops = [
        jnp.where(row_even, row_a_ref[g, :, lanes].astype(F32), row_b_ref[g, :, lanes].astype(F32))
        for g in range(planes, groups)
    ]
    corner = jnp.where(row_even, edge_a_ref[4, :, lanes].astype(F32), edge_b_ref[4, :, lanes].astype(F32))
    own = dep_ref[4, :, lanes].astype(F32)[:4]
    for n, values in enumerate((jnp.concatenate(tops, axis=0), jnp.concatenate([own, corner], axis=0))):
        col_a_ref[planes + 12 + n] = values.astype(BF16)
        col_b_ref[planes + 12 + n] = jnp.where(col_inner, values, 0.0).astype(BF16)


def bands(first_ref, second_ref, w1_ref, w2_ref, w2b_ref):
    out_chan = first_ref.shape[0]
    first = first_ref[...].astype(F32)
    blank = jnp.zeros((out_chan, LANES), F32)
    for tap in range(9):
        rows = slice(tap * LANES, (tap + 1) * LANES)
        taps = first[:, tap * 96 : (tap + 1) * 96]
        main_even = jnp.concatenate([taps[:, 32:], blank[:, :64]], axis=1)
        main_odd = jnp.concatenate([blank[:, :32], taps], axis=1)
        prev_even = jnp.concatenate([blank[:, :96], taps[:, :32]], axis=1)
        w1_ref[rows] = jnp.concatenate([main_even, main_odd, prev_even, blank], axis=0).T.astype(BF16)
        main = second_ref[tap * 192 + 64 : (tap + 1) * 192, :]
        prev = jnp.concatenate([jnp.zeros((64, LANES), BF16), second_ref[tap * 192 : tap * 192 + 64, :]], axis=0)
        both = jnp.concatenate([main, prev], axis=1)
        w2_ref[rows] = both
        w2b_ref[tap] = both.astype(F32).T.astype(BF16)


def split_rows(stage, tiles, index, blocks):
    for m in blocks:
        rows = [stage[m, pl.ds(4 + s, 8, stride=4), :] for s in range(-1, 4)]
        for b in range(3):
            tiles[b, index, m] = jnp.concatenate([rows[b], rows[b + 2]], axis=0).astype(BF16)


def clear_stage(stage):
    stage[:, :, 0:8, :] = jnp.zeros(stage.shape[:2] + (8, LANES), F32)
    stage[:, :, 24:40, :] = jnp.zeros(stage.shape[:2] + (16, LANES), F32)


def ahead(even, a, b):
    return jnp.where(even, a.astype(F32), b.astype(F32))


def behind(even, a, b):
    return jnp.where(even, b.astype(F32), a.astype(F32))


def own_blocks(
    flag_ref, vol_ref, dep_ref, row_a_ref, row_b_ref, edge_a_ref, edge_b_ref, w1_ref, tiles, parts, stage
):
    first_plane, row_even = flag_ref[0] == 0, flag_ref[1] == 0
    planes = vol_ref.shape[0]
    blocks = vol_ref.shape[2] // LANES
    clear_stage(stage)

    def place(n, target, own, a, b, keep):
        def kept(values):
            return values if keep is None else jnp.where(keep, values, 0.0)

        for m in range(blocks):
            lanes = slice(m * LANES, (m + 1) * LANES)
            stage[n, m, 8:24, :] = kept(own(lanes).astype(F32))
            stage[n, m, 4:8, :] = kept(behind(row_even, a(lanes), b(lanes)))
            stage[n, m, 24:28, :] = kept(ahead(row_even, a(lanes), b(lanes)))
        split_rows(stage.at[n], tiles, target, range(blocks))

    def place_own(pair, carry):
        for n in range(2):
            d = 2 * pair + n
            place(
                n, d + 3, lambda lanes: vol_ref[d, :, lanes],
                lambda lanes: row_a_ref[d, :, lanes], lambda lanes: row_b_ref[d, :, lanes], None,
            )
        return carry

    def place_halo(target, q, keep):
        place(
            target % 2, target, lambda lanes: dep_ref[q, :, lanes],
            lambda lanes: edge_a_ref[q, :, lanes], lambda lanes: edge_b_ref[q, :, lanes], keep,
        )

    lax.fori_loop(0, planes // 2, place_own, 0)
    for q in range(3):
        place_halo(q, q + 1, jnp.logical_not(first_plane))
    for q in range(4):
        place_halo(planes + 3 + q, q, first_plane)
    tiles[:, planes + 7 :] = jnp.zeros((3, 2, blocks, 16, LANES), BF16)

    def product(pair, carry):
        taps = []
        for a in range(3):
            for b in range(3):
                both = [tiles[b, 4 * pair + 2 * n + a].reshape(blocks * 16, LANES) for n in range(2)]
                taps.append(jnp.concatenate(both, axis=0))
        found = matmul(jnp.concatenate(taps, axis=1), w1_ref[...])
        parts[pl.ds(2 * pair, 2)] = found.reshape(2, blocks, 16, 2 * LANES)
        return carry

    lax.fori_loop(0, planes // 4 + 2, product, 0)


def body(
    flag_ref, place_ref, tiles, parts, dep_ref, row_a_ref, row_b_ref, edge_a_ref, edge_b_ref,
    side_a_ref, side_b_ref, col_a_ref, col_b_ref, cot_ref, w1_ref, w2_ref, w2b_ref, keep_ref, give_ref,
    out_ref, stage, rim_tiles, rim_parts, slopes, hid, pairs, ups, deltas, shifted,
):
    first_plane, row_even, col_even = flag_ref[0] == 0, flag_ref[1] == 0, flag_ref[2] == 0
    planes = tiles.shape[1] - 9
    blocks = tiles.shape[2]
    half_planes = planes // 4
    hidden_planes = planes // 2 + 3

    clear_stage(stage)

    def place(n, target, source, side_a, side_b, keep):
        for m, choose in ((0, behind), (1, ahead)):
            corners = choose(col_even, col_a_ref[source], col_b_ref[source])
            own = choose(col_even, side_a, side_b)
            if keep is not None:
                corners, own = jnp.where(keep, corners, 0.0), jnp.where(keep, own, 0.0)
            stage[n, m, 4:8, :] = corners[:4]
            stage[n, m, 8:24, :] = own
            stage[n, m, 24:28, :] = corners[4:]
        split_rows(stage.at[n], rim_tiles, target, range(2))

    def place_own(group, carry):
        for n in range(4):
            d = 4 * group + n
            place(n, d + 3, d, side_a_ref[d], side_b_ref[d], None)
        return carry

    def place_halo(target, q, keep):
        start = planes + 4 + 2 * q
        side_a = jnp.concatenate([col_a_ref[start].astype(F32), col_a_ref[start + 1].astype(F32)], axis=0)
        side_b = jnp.concatenate([col_b_ref[start].astype(F32), col_b_ref[start + 1].astype(F32)], axis=0)
        place(target % 4, target, planes + q, side_a, side_b, keep)

    lax.fori_loop(0, planes // 4, place_own, 0)
    for q in range(3):
        place_halo(q, q + 1, jnp.logical_not(first_plane))
    for q in range(4):
        place_halo(planes + 3 + q, q, first_plane)

    taps = []
    for a in range(3):
        for b in range(3):
            rows = [rim_tiles[b, 2 * i + a].reshape(32, LANES) for i in range(hidden_planes)]
            taps.append(jnp.concatenate(rows, axis=0))
    found = matmul(jnp.concatenate(taps, axis=1), w1_ref[...])
    rim_parts[...] = found.reshape(hidden_planes, 2, 16, 2 * LANES)

    def conv_one(i, carry):
        main, prev = parts[i, :, :, :LANES], parts[i, :, :, LANES:]
        rim, rim_prev = rim_parts[i, :, :, :LANES], rim_parts[i, 0:1, :, LANES:]
        blank = jnp.zeros((1, 16, LANES), F32)
        pre = jnp.concatenate([rim[:1], main, rim[1:]], axis=0) + jnp.concatenate([blank, rim_prev, prev], axis=0)
        root = jnp.sqrt(pre * pre + 1.0)
        slopes[i] = 0.6 + 0.4 * pre / root
        hidden = (0.6 * pre + 0.4 * (root - 1.0)).astype(BF16).astype(F32)
        odd = hidden[:, 8:, :]
        hid[0, i] = pltpu.roll(odd, 1, 1)
        hid[1, i] = hidden[:, :8, :]
        hid[2, i] = odd
        return carry

    lax.fori_loop(0, hidden_planes, conv_one, 0)

    wide = (blocks + 2) * 16

    def pair(i, carry):
        for b in range(3):
            pairs[b, i] = jnp.concatenate([hid[b, i], hid[b, i + half_planes]], axis=1).astype(BF16)
        return carry

    lax.fori_loop(0, half_planes + 3, pair, 0)

    ups[...] = jnp.zeros_like(ups)
    for k in range(blocks):
        lanes = slice(k * LANES, (k + 1) * LANES)
        ups[0:half_planes, k, 1:5, :] = cot_ref[:, :, lanes].astype(F32)
        ups[half_planes, k, 1:5, :] = jnp.where(first_plane, dep_ref[4, 0:4, lanes].astype(F32), 0.0)
        for g in range(half_planes // 4):
            tops = ahead(row_even, row_a_ref[planes + g, :, lanes], row_b_ref[planes + g, :, lanes])
            for n in range(4):
                ups[4 * g + n, k, 5:6, :] = tops[n : n + 1]
        corner = ahead(row_even, edge_a_ref[4, :, lanes], edge_b_ref[4, :, lanes])[:1]
        ups[half_planes, k, 5:6, :] = jnp.where(first_plane, corner, 0.0)
    for g in range(half_planes // 4):
        side = ahead(col_even, side_a_ref[planes + g], side_b_ref[planes + g])
        for n in range(4):
            ups[4 * g + n, blocks, 1:5, :] = side[4 * n : 4 * n + 4]
    tops = ahead(col_even, col_a_ref[planes + 12], col_b_ref[planes + 12])
    for n in range(half_planes):
        ups[n, blocks, 5:6, :] = tops[n : n + 1]
    beyond = jnp.where(first_plane, ahead(col_even, col_a_ref[planes + 13], col_b_ref[planes + 13]), 0.0)
    ups[half_planes, blocks, 1:6, :] = beyond[:5]

    quarter = half_planes // 2

    def conv_two(t, carry):
        taps = [pairs[b, 2 * t + a].reshape(wide, LANES) for a in range(3) for b in range(3)]
        parts = matmul(jnp.concatenate(taps, axis=1), w2_ref[...]).reshape(blocks + 2, 16, 2 * LANES)
        pre = parts[1:, :, :LANES] + parts[:-1, :, LANES:]
        slope = 0.6 + 0.4 * pre / jnp.sqrt(pre * pre + 1.0)
        upstream = jnp.concatenate([ups[t], ups[t + quarter]], axis=1)
        delta = (upstream * slope).astype(BF16).astype(F32)
        moved = jnp.concatenate([pltpu.roll(delta[:, :8], 7, 1), pltpu.roll(delta[:, 8:], 7, 1)], axis=1)
        deltas[t] = delta
        shifted[t] = moved.astype(BF16)
        return carry

    lax.fori_loop(0, quarter + 1, conv_two, 0)

    sublane = lax.broadcasted_iota(jnp.int32, (1, 1, 16, 1), 2) % 8
    own_rows = jnp.logical_and(sublane >= 1, sublane <= 4)

    def with_next(values):
        values = values.T
        edge = jnp.zeros((LANES, values.shape[1] // blocks), values.dtype)
        here = jnp.concatenate([edge, values], axis=1)
        after = jnp.concatenate([values, edge], axis=1)
        return jnp.concatenate([here, after], axis=0)

    own_delta = [jnp.where(own_rows[0], deltas[t, 0:blocks], 0.0) for t in range(quarter)]
    left = with_next(jnp.stack(own_delta, axis=1).reshape(blocks * quarter * 16, LANES)).astype(BF16)

    def second_taps(tap):
        a, b = tap // 3, tap % 3
        found = [pairs[b, 2 * t + a, 0 : blocks + 1] for t in range(quarter)]
        return jnp.stack(found, axis=1).reshape((blocks + 1) * quarter * 16, LANES)

    for tap in range(0, 9, 2):
        right = [second_taps(x) for x in range(tap, min(tap + 2, 9))]
        found = matmul(left, jnp.concatenate(right, axis=1))
        for n in range(len(right)):
            row = (tap + n) * 192
            lanes = slice(n * LANES, (n + 1) * LANES)
            out_ref[row : row + 64, :] = found[LANES:, lanes].T[64:]
            out_ref[row + 64 : row + 192, :] = found[:LANES, lanes].T

    def pack(values):
        both = jnp.concatenate([values[:, :-1], values[:, 1:]], axis=3)
        return both.reshape(quarter * blocks * 16, 2 * LANES)

    plain = deltas[...].astype(BF16)
    moved = shifted[...]
    here, after = pack(plain[:-1]), pack(plain[1:])
    here_up, after_up = pack(moved[:-1]), pack(moved[1:])

    def back(terms):
        joined = jnp.concatenate([values for values, a, b in terms], axis=1)
        weights = jnp.concatenate([w2b_ref[3 * a + b] for values, a, b in terms], axis=0)
        return matmul(joined, weights).reshape(quarter, blocks, 16, LANES)

    rows = [
        [back([(here, 1, 1)]), back([(here_up, 1, 0), (here, 1, 2)])],
        [
            back([(after, 0, 1), (here, 2, 1)]),
            back([(after_up, 0, 0), (after, 0, 2), (here_up, 2, 0), (here, 2, 2)]),
        ],
    ]
    own_list = []
    for i in range(planes // 2):
        t, parity = i // 2, i % 2
        half = slice(0, 8) if t < quarter else slice(8, 16)
        back_one = jnp.concatenate([rows[parity][p][t % quarter, :, half, :] for p in (0, 1)], axis=1)
        delta = back_one * slopes[i + 1, 1 : blocks + 1]
        own_list.append(jnp.where(own_rows[0], delta, 0.0).astype(BF16))
    left_one = with_next(jnp.stack(own_list, axis=1).reshape(blocks * (planes // 2) * 16, LANES))

    def first_taps(tap):
        a, b = tap // 3, tap % 3
        found = []
        for m in range(blocks + 1):
            for i in range(planes // 2):
                index = 2 * (i + 1) + a
                found.append(rim_tiles[b, index, 0] if m == 0 else tiles[b, index, m - 1])
        return jnp.concatenate(found, axis=0)

    for tap in range(0, 9, 2):
        right = [first_taps(x) for x in range(tap, min(tap + 2, 9))]
        found = matmul(left_one, jnp.concatenate(right, axis=1))
        for n in range(len(right)):
            main = found[:LANES, n * LANES : (n + 1) * LANES]
            prev = found[LANES : LANES + 64, n * LANES : (n + 1) * LANES]
            even = jnp.concatenate([prev[:, 96:], main[:64, :64]], axis=1)
            grad = jnp.concatenate([even + main[64:, 32:], jnp.zeros((64, 32), F32)], axis=1)
            row = SECOND_ROWS + (tap + n) * 64
            out_ref[row : row + 64, :] = grad

    core, square = place_ref[0], place_ref[1]
    squares, size = keep_ref.shape[0], keep_ref.shape[1]
    for n in range(squares):
        for ref, half in ((keep_ref, core), (give_ref, 1 - core)):
            start = pl.multiple_of((half * squares + (square ^ n)) * size, 8)
            ref[n] = out_ref[pl.ds(start, size), :].astype(BF16)


def unpack(place_ref, keep_ref, got_ref, g1_ref, g2_ref, sums):
    core, square = place_ref[0], place_ref[1]
    squares, size = keep_ref.shape[0], keep_ref.shape[1]
    for n in range(squares):
        for ref, half in ((keep_ref, core), (got_ref, 1 - core)):
            start = pl.multiple_of((half * squares + (square ^ n)) * size, 8)
            sums[pl.ds(start, size), :] = ref[n].astype(F32)
    first = sums[SECOND_ROWS:, :]
    g1_ref[...] = jnp.concatenate([first[tap * 64 : (tap + 1) * 64, :96] for tap in range(9)], axis=1)
    g2_ref[...] = sums[:SECOND_ROWS, :]


def local_grads(flags, place, squares, volume, faces, corners, cotangent, weights):
    planes = volume.shape[0]
    blocks = volume.shape[2] // LANES
    hidden_planes = planes // 2 + 3
    out_planes = planes // 4
    rows = SECOND_ROWS + 9 * 64
    whole = pl.BlockSpec(memory_space=pltpu.VMEM)
    smem = pl.BlockSpec(memory_space=pltpu.SMEM)
    dep, row_a, row_b, edge_a, edge_b = faces
    tiles, parts = pl.pallas_call(
        own_blocks,
        out_shape=[
            jax.ShapeDtypeStruct((3, planes + 9, blocks, 16, LANES), BF16),
            jax.ShapeDtypeStruct((hidden_planes + 1, blocks, 16, 2 * LANES), F32),
        ],
        in_specs=[smem] + [whole] * 7,
        out_specs=[whole] * 2,
        scratch_shapes=[pltpu.VMEM((2, blocks, 40, LANES), F32)],
        compiler_params=pltpu.CompilerParams(vmem_limit_bytes=16 * 1024 * 1024),
        cost_estimate=pl.CostEstimate(flops=2 * 10**9, bytes_accessed=10**7, transcendentals=0),
    )(flags, volume, *faces, weights[0])
    scratch = [
        pltpu.VMEM((rows, LANES), F32),
        pltpu.VMEM((4, 2, 40, LANES), F32),
        pltpu.VMEM((3, planes + 7, 2, 16, LANES), BF16),
        pltpu.VMEM((hidden_planes, 2, 16, 2 * LANES), F32),
        pltpu.VMEM((hidden_planes, blocks + 2, 16, LANES), F32),
        pltpu.VMEM((3, hidden_planes, blocks + 2, 8, LANES), F32),
        pltpu.VMEM((3, out_planes + 3, blocks + 2, 16, LANES), BF16),
        pltpu.VMEM((out_planes + 1, blocks + 1, 8, LANES), F32),
        pltpu.VMEM((out_planes // 2 + 1, blocks + 1, 16, LANES), F32),
        pltpu.VMEM((out_planes // 2 + 1, blocks + 1, 16, LANES), BF16),
    ]
    operands = (tiles, parts, *faces, *corners, cotangent, *weights)
    return pl.pallas_call(
        body,
        out_shape=[jax.ShapeDtypeStruct((squares, rows // (2 * squares), LANES), BF16)] * 2,
        in_specs=[smem] * 2 + [whole] * len(operands),
        out_specs=[whole] * 2,
        scratch_shapes=scratch,
        compiler_params=pltpu.CompilerParams(vmem_limit_bytes=28 * 1024 * 1024),
        cost_estimate=pl.CostEstimate(flops=4 * 10**9, bytes_accessed=10**7, transcendentals=0),
    )(flags, place, *operands)


def shards(volume, first_weight, second_weight, cotangent):
    half = lax.axis_index("depth")
    row, col = lax.axis_index("row"), lax.axis_index("col")
    rows, cols = lax.axis_size("row"), lax.axis_size("col")
    inner = [jnp.logical_and(i > 0, i < n - 1).astype(jnp.int32) for i, n in ((row, rows), (col, cols))]
    flags = jnp.stack([half, row % 2, col % 2, *inner])
    whole = pl.BlockSpec(memory_space=pltpu.VMEM)
    smem = pl.BlockSpec(memory_space=pltpu.SMEM)
    small = pltpu.CompilerParams(vmem_limit_bytes=12 * 1024 * 1024)
    planes, high, width = volume.shape
    groups = planes + cotangent.shape[0] // 4
    faces = [(5, high, width)] + [(groups, 4, width)] * 2 + [(5, 4, width)] * 2 + [(groups, high, LANES)] * 2
    dep, row_a, row_b, edge_a, edge_b, side_a, side_b = pl.pallas_call(
        pack,
        out_shape=[jax.ShapeDtypeStruct(shape, BF16) for shape in faces],
        in_specs=[smem] + [whole] * 2,
        out_specs=[whole] * 7,
        compiler_params=small,
    )(flags, volume, cotangent)

    def to_edge(block, kind):
        line = pairs_on_line(rows, kind)
        route = [(d * rows + i, (1 - d) * rows + j) for d in (0, 1) for i, j in line]
        return lax.ppermute(block, ("depth", "row"), route)

    def to_col(block, kind):
        return lax.ppermute(block, "col", pairs_on_line(cols, kind))

    edge_a, edge_b = to_edge(edge_a, 0), to_edge(edge_b, 1)
    row_a = lax.ppermute(row_a, "row", pairs_on_line(rows, 0))
    side_a, side_b = to_col(side_a, 0), to_col(side_b, 1)
    dep = lax.ppermute(dep, "depth", [(0, 1), (1, 0)])
    row_b = lax.ppermute(row_b, "row", pairs_on_line(rows, 1))
    col_a, col_b = pl.pallas_call(
        pack_corners,
        out_shape=[jax.ShapeDtypeStruct((planes + 14, 8, LANES), BF16)] * 2,
        in_specs=[smem] + [whole] * 5,
        out_specs=[whole] * 2,
        compiler_params=small,
    )(flags, dep, row_a, row_b, edge_a, edge_b)
    col_a, col_b, first_taps, second_taps = lax.optimization_barrier((col_a, col_b, first_weight, second_weight.T))
    col_a, col_b = to_col(col_a, 0), to_col(col_b, 1)

    weights = pl.pallas_call(
        bands,
        out_shape=[jax.ShapeDtypeStruct(shape, BF16) for shape in ((1152, 256), (1152, 256), (9, 256, 128))],
        in_specs=[whole] * 2,
        out_specs=[whole] * 3,
        compiler_params=small,
    )(first_taps, second_taps)
    spot = lax.axis_index(("depth", "row"))
    squares = lax.axis_size(("depth", "row")) // 2
    where = jnp.stack([spot % 2, spot // 2])
    faces, corners = (dep, row_a, row_b, edge_a, edge_b), (side_a, side_b, col_a, col_b)
    keep, give = local_grads(flags, where, squares, volume, faces, corners, cotangent, weights)

    def to_square(block, n):
        route = [(2 * i + c, 2 * (i ^ n) + c) for i in range(squares) for c in (0, 1)]
        return lax.ppermute(block, ("depth", "row"), route)

    def to_core(block):
        return lax.ppermute(block, ("depth", "row"), [(i, i ^ 1) for i in range(2 * squares)])

    def along_col(block, n):
        return lax.ppermute(block, "col", [(i, i ^ n) for i in range(cols)])

    both = add_up(keep, to_core(give))
    share = add_up(both[0], *[to_square(both[n], n) for n in range(1, squares)])
    share = add_up(share, *[along_col(share, n) for n in range(1, cols)])
    mine = jnp.stack([share] + [to_square(share, n) for n in range(1, squares)])
    other = to_core(mine)
    grads = [jax.ShapeDtypeStruct(shape, F32) for shape in (first_weight.shape, second_weight.shape[::-1])]
    first_grad, second_grad = pl.pallas_call(
        unpack,
        out_shape=grads,
        in_specs=[smem] + [whole] * 2,
        out_specs=[whole] * 2,
        scratch_shapes=[pltpu.VMEM((mine.shape[0] * mine.shape[1] * 2, LANES), F32)],
        compiler_params=small,
    )(where, mine, other)
    return first_grad, second_grad.T


def solution(mesh):
    placed = (P("depth", "row", "col"), P(), P(), P("depth", "row", "col"))
    return jax.shard_map(shards, mesh=mesh, in_specs=placed, out_specs=(P(), P()), check_vma=False)
```

```python
import jax
import jax.numpy as jnp
from jax import lax
from jax.experimental import pallas as pl
from jax.experimental.pallas import tpu as pltpu
from jax.sharding import PartitionSpec as P

LANES = 128
SECOND_ROWS = 27 * 64
FIRST_BLOCKS = 7
F32 = jnp.float32
BF16 = jnp.bfloat16


def pairs_on_line(count, kind):
    firsts = range(kind, count - 1, 2)
    swapped = [(i, i + 1) for i in firsts] + [(i + 1, i) for i in firsts]
    met = {i for i, j in swapped}
    return swapped + [(i, i) for i in range(count) if i not in met]


def pairs_of_lines(lines, count, kind):
    route = []
    for line in range(lines):
        for i, j in pairs_on_line(count, kind):
            route.append((line * count + i, (line ^ 1 if i == j else line) * count + j))
    return route


def add_up(*terms):
    terms = [term.astype(F32) for term in terms]
    while len(terms) > 1:
        terms = [terms[n] + terms[n + 1] for n in range(0, len(terms), 2)]
    return terms[0].astype(BF16)


def matmul(left, right):
    return lax.dot_general(left, right, (((1,), (0,)), ((), ())), preferred_element_type=F32)


def bring(flag_ref, vol_hbm, cot_hbm, vol_ref, cot_ref, dep_ref, arrived):
    first_plane = flag_ref[0] == 0
    planes = vol_ref.shape[0]
    inner = pl.ds(4, planes - 8)
    copies = [pltpu.make_async_copy(cot_hbm, cot_ref, arrived.at[0])]
    for n, part in enumerate((pl.ds(0, 4), pl.ds(planes - 4, 4), inner)):
        copies.append(pltpu.make_async_copy(vol_hbm.at[part], vol_ref.at[part], arrived.at[1 + n]))
    for copy in copies:
        copy.start()
    for copy in copies[:3]:
        copy.wait()
    dep_ref[16] = cot_ref[0]
    for q in range(4):
        block = jnp.where(first_plane, vol_ref[planes - 4 + q].astype(F32), vol_ref[q].astype(F32))
        for g in range(4):
            dep_ref[4 * q + g] = block[4 * g : 4 * g + 4].astype(BF16)
    copies[3].wait()


def pack(
    flag_ref, vol_ref, cot_ref, first_hbm, second_hbm, row_a_ref, row_b_ref, col_a_ref, col_b_ref,
    first_ref, second_ref, arrived,
):
    row_even, col_even = flag_ref[1] == 0, flag_ref[2] == 0
    row_inner, col_inner = flag_ref[3] != 0, flag_ref[4] != 0
    planes, high, width = vol_ref.shape
    cots = cot_ref.shape[0]
    copies = [
        pltpu.make_async_copy(first_hbm, first_ref, arrived.at[0]),
        pltpu.make_async_copy(second_hbm, second_ref, arrived.at[1]),
    ]
    for copy in copies:
        copy.start()

    cot = cot_ref[...].astype(F32)
    for g in range(cots // 4):
        tops = jnp.concatenate([cot[4 * g + n, :1] for n in range(4)], axis=0)
        row_a_ref[planes + g] = tops.astype(BF16)
        row_b_ref[planes + g] = jnp.where(row_inner, tops, 0.0).astype(BF16)
        side = jnp.concatenate([cot[4 * g + n, :, :LANES] for n in range(4)], axis=0)
        col_a_ref[planes + g] = side.astype(BF16)
        col_b_ref[planes + g] = jnp.where(col_inner, side, 0.0).astype(BF16)

    def plane(d, carry):
        block = vol_ref[d].astype(F32)
        low, top = block[:4], block[high - 4 :]
        row_a_ref[d] = jnp.where(row_even, top, low).astype(BF16)
        row_b_ref[d] = jnp.where(row_inner, jnp.where(row_even, low, top), 0.0).astype(BF16)
        left, right = block[:, :LANES], block[:, width - LANES :]
        col_a_ref[d] = jnp.where(col_even, right, left).astype(BF16)
        col_b_ref[d] = jnp.where(col_inner, jnp.where(col_even, left, right), 0.0).astype(BF16)
        return carry

    lax.fori_loop(0, planes, plane, 0, unroll=2)
    for copy in copies:
        copy.wait()


def pack_corners(flag_ref, dep_ref, row_a_ref, row_b_ref, edge_a_ref, edge_b_ref, col_a_ref, col_b_ref):
    row_even, col_even, col_inner = flag_ref[1] == 0, flag_ref[2] == 0, flag_ref[4] != 0
    width = dep_ref.shape[2]
    groups = row_a_ref.shape[0]
    planes = (groups * 16) // 17
    faces = (slice(0, LANES), slice(width - LANES, width))

    def store(n, left, right):
        col_a_ref[n] = jnp.where(col_even, right, left).astype(BF16)
        col_b_ref[n] = jnp.where(col_inner, jnp.where(col_even, left, right), 0.0).astype(BF16)

    def lower_upper(a_ref, b_ref, source, target):
        values = []
        for lanes in faces:
            a, b = a_ref[source, :, lanes].astype(F32), b_ref[source, :, lanes].astype(F32)
            values.append(jnp.concatenate([jnp.where(row_even, b, a), jnp.where(row_even, a, b)], axis=0))
        store(target, *values)

    def plane(d, carry):
        lower_upper(row_a_ref, row_b_ref, d, d)
        return carry

    lax.fori_loop(0, planes, plane, 0)
    for q in range(4):
        lower_upper(edge_a_ref, edge_b_ref, q, planes + q)
        for n in range(2):
            units = range(4 * q + 2 * n, 4 * q + 2 * n + 2)
            store(
                planes + 4 + 2 * q + n,
                *[jnp.concatenate([dep_ref[u, :, lanes].astype(F32) for u in units], axis=0) for lanes in faces],
            )
    lanes = faces[0]
    tops = [
        jnp.where(row_even, row_a_ref[g, :, lanes].astype(F32), row_b_ref[g, :, lanes].astype(F32))
        for g in range(planes, groups)
    ]
    corner = jnp.where(row_even, edge_a_ref[4, :, lanes].astype(F32), edge_b_ref[4, :, lanes].astype(F32))
    own = dep_ref[16, :, lanes].astype(F32)
    for n, values in enumerate((jnp.concatenate(tops, axis=0), jnp.concatenate([own, corner], axis=0))):
        col_a_ref[planes + 12 + n] = values.astype(BF16)
        col_b_ref[planes + 12 + n] = jnp.where(col_inner, values, 0.0).astype(BF16)


def bands(first_ref, second_ref, w1_ref, w2_ref, w2b_ref):
    out_chan = first_ref.shape[0]
    first = first_ref[...].astype(F32)
    blank = jnp.zeros((out_chan, LANES), F32)
    for tap in range(9):
        rows = slice(tap * LANES, (tap + 1) * LANES)
        taps = first[:, tap * 96 : (tap + 1) * 96]
        main_even = jnp.concatenate([taps[:, 32:], blank[:, :64]], axis=1)
        main_odd = jnp.concatenate([blank[:, :32], taps], axis=1)
        prev_even = jnp.concatenate([blank[:, :96], taps[:, :32]], axis=1)
        w1_ref[rows] = jnp.concatenate([main_even, main_odd, prev_even, blank], axis=0).T.astype(BF16)
        main = second_ref[tap * 192 + 64 : (tap + 1) * 192, :]
        prev = jnp.concatenate([jnp.zeros((64, LANES), BF16), second_ref[tap * 192 : tap * 192 + 64, :]], axis=0)
        both = jnp.concatenate([main, prev], axis=1)
        w2_ref[rows] = both
        w2b_ref[tap] = both.astype(F32).T.astype(BF16)


def split_rows(stage, tiles, index, blocks):
    for m in blocks:
        rows = [stage[m, pl.ds(4 + s, 8, stride=4), :] for s in range(-1, 4)]
        for b in range(3):
            tiles[b, index, m] = jnp.concatenate([rows[b], rows[b + 2]], axis=0).astype(BF16)


def clear_stage(stage):
    stage[:, :, 0:8, :] = jnp.zeros(stage.shape[:2] + (8, LANES), F32)
    stage[:, :, 24:40, :] = jnp.zeros(stage.shape[:2] + (16, LANES), F32)


def ahead(even, a, b):
    return jnp.where(even, a.astype(F32), b.astype(F32))


def behind(even, a, b):
    return jnp.where(even, b.astype(F32), a.astype(F32))


def own_blocks(
    flag_ref, vol_ref, dep_ref, row_a_ref, row_b_ref, edge_a_ref, edge_b_ref, w1_ref, tiles, parts, stage
):
    first_plane, row_even = flag_ref[0] == 0, flag_ref[1] == 0
    planes = vol_ref.shape[0]
    blocks = vol_ref.shape[2] // LANES
    clear_stage(stage)

    def place(n, target, own, a, b, keep):
        def kept(values):
            return values if keep is None else jnp.where(keep, values, 0.0)

        for m in range(blocks):
            lanes = slice(m * LANES, (m + 1) * LANES)
            stage[n, m, 8:24, :] = kept(own(lanes).astype(F32))
            stage[n, m, 4:8, :] = kept(behind(row_even, a(lanes), b(lanes)))
            stage[n, m, 24:28, :] = kept(ahead(row_even, a(lanes), b(lanes)))
        split_rows(stage.at[n], tiles, target, range(blocks))

    def place_own(pair, carry):
        for n in range(2):
            d = 2 * pair + n
            place(
                n, d + 3, lambda lanes: vol_ref[d, :, lanes],
                lambda lanes: row_a_ref[d, :, lanes], lambda lanes: row_b_ref[d, :, lanes], None,
            )
        return carry

    def place_halo(target, q, keep):
        place(
            target % 2, target,
            lambda lanes: jnp.concatenate([dep_ref[4 * q + g, :, lanes].astype(F32) for g in range(4)], axis=0),
            lambda lanes: edge_a_ref[q, :, lanes], lambda lanes: edge_b_ref[q, :, lanes], keep,
        )

    lax.fori_loop(0, planes // 2, place_own, 0)
    for q in range(3):
        place_halo(q, q + 1, jnp.logical_not(first_plane))
    for q in range(4):
        place_halo(planes + 3 + q, q, first_plane)
    tiles[:, planes + 7 :] = jnp.zeros((3, 2, blocks, 16, LANES), BF16)

    def product(pair, carry):
        taps = []
        for a in range(3):
            for b in range(3):
                both = [tiles[b, 4 * pair + 2 * n + a].reshape(blocks * 16, LANES) for n in range(2)]
                taps.append(jnp.concatenate(both, axis=0))
        found = matmul(jnp.concatenate(taps, axis=1), w1_ref[...])
        parts[pl.ds(2 * pair, 2)] = found.reshape(2, blocks, 16, 2 * LANES)
        return carry

    lax.fori_loop(0, planes // 4 + 2, product, 0)


def body(
    flag_ref, place_ref, tiles, parts, dep_ref, row_a_ref, row_b_ref, edge_a_ref, edge_b_ref,
    side_a_ref, side_b_ref, col_a_ref, col_b_ref, cot_ref, w1_ref, w2_ref, w2b_ref, keep_ref, give_ref,
    out_ref, stage, rim_tiles, rim_parts, slopes, hid, pairs, ups, deltas, shifted,
):
    first_plane, row_even, col_even = flag_ref[0] == 0, flag_ref[1] == 0, flag_ref[2] == 0
    planes = tiles.shape[1] - 9
    blocks = tiles.shape[2]
    half_planes = planes // 4
    hidden_planes = planes // 2 + 3

    clear_stage(stage)

    def place(n, target, source, side_a, side_b, keep):
        for m, choose in ((0, behind), (1, ahead)):
            corners = choose(col_even, col_a_ref[source], col_b_ref[source])
            own = choose(col_even, side_a, side_b)
            if keep is not None:
                corners, own = jnp.where(keep, corners, 0.0), jnp.where(keep, own, 0.0)
            stage[n, m, 4:8, :] = corners[:4]
            stage[n, m, 8:24, :] = own
            stage[n, m, 24:28, :] = corners[4:]
        split_rows(stage.at[n], rim_tiles, target, range(2))

    def place_own(group, carry):
        for n in range(4):
            d = 4 * group + n
            place(n, d + 3, d, side_a_ref[d], side_b_ref[d], None)
        return carry

    def place_halo(target, q, keep):
        start = planes + 4 + 2 * q
        side_a = jnp.concatenate([col_a_ref[start].astype(F32), col_a_ref[start + 1].astype(F32)], axis=0)
        side_b = jnp.concatenate([col_b_ref[start].astype(F32), col_b_ref[start + 1].astype(F32)], axis=0)
        place(target % 4, target, planes + q, side_a, side_b, keep)

    lax.fori_loop(0, planes // 4, place_own, 0)
    for q in range(3):
        place_halo(q, q + 1, jnp.logical_not(first_plane))
    for q in range(4):
        place_halo(planes + 3 + q, q, first_plane)

    taps = []
    for a in range(3):
        for b in range(3):
            rows = [rim_tiles[b, 2 * i + a].reshape(32, LANES) for i in range(hidden_planes)]
            taps.append(jnp.concatenate(rows, axis=0))
    found = matmul(jnp.concatenate(taps, axis=1), w1_ref[...])
    rim_parts[...] = found.reshape(hidden_planes, 2, 16, 2 * LANES)

    def conv_one(i, carry):
        main, prev = parts[i, :, :, :LANES], parts[i, :, :, LANES:]
        rim, rim_prev = rim_parts[i, :, :, :LANES], rim_parts[i, 0:1, :, LANES:]
        blank = jnp.zeros((1, 16, LANES), F32)
        pre = jnp.concatenate([rim[:1], main, rim[1:]], axis=0) + jnp.concatenate([blank, rim_prev, prev], axis=0)
        root = jnp.sqrt(pre * pre + 1.0)
        slopes[i] = 0.6 + 0.4 * pre / root
        hidden = (0.6 * pre + 0.4 * (root - 1.0)).astype(BF16).astype(F32)
        odd = hidden[:, 8:, :]
        hid[0, i] = pltpu.roll(odd, 1, 1)
        hid[1, i] = hidden[:, :8, :]
        hid[2, i] = odd
        return carry

    lax.fori_loop(0, hidden_planes, conv_one, 0)

    wide = (blocks + 2) * 16

    def pair(i, carry):
        for b in range(3):
            pairs[b, i] = jnp.concatenate([hid[b, i], hid[b, i + half_planes]], axis=1).astype(BF16)
        return carry

    lax.fori_loop(0, half_planes + 3, pair, 0)

    ups[...] = jnp.zeros_like(ups)
    for k in range(blocks):
        lanes = slice(k * LANES, (k + 1) * LANES)
        ups[0:half_planes, k, 1:5, :] = cot_ref[:, :, lanes].astype(F32)
        ups[half_planes, k, 1:5, :] = jnp.where(first_plane, dep_ref[16, :, lanes].astype(F32), 0.0)
        for g in range(half_planes // 4):
            tops = ahead(row_even, row_a_ref[planes + g, :, lanes], row_b_ref[planes + g, :, lanes])
            for n in range(4):
                ups[4 * g + n, k, 5:6, :] = tops[n : n + 1]
        corner = ahead(row_even, edge_a_ref[4, :, lanes], edge_b_ref[4, :, lanes])[:1]
        ups[half_planes, k, 5:6, :] = jnp.where(first_plane, corner, 0.0)
    for g in range(half_planes // 4):
        side = ahead(col_even, side_a_ref[planes + g], side_b_ref[planes + g])
        for n in range(4):
            ups[4 * g + n, blocks, 1:5, :] = side[4 * n : 4 * n + 4]
    tops = ahead(col_even, col_a_ref[planes + 12], col_b_ref[planes + 12])
    for n in range(half_planes):
        ups[n, blocks, 5:6, :] = tops[n : n + 1]
    beyond = jnp.where(first_plane, ahead(col_even, col_a_ref[planes + 13], col_b_ref[planes + 13]), 0.0)
    ups[half_planes, blocks, 1:6, :] = beyond[:5]

    quarter = half_planes // 2

    def conv_two(t, carry):
        taps = [pairs[b, 2 * t + a].reshape(wide, LANES) for a in range(3) for b in range(3)]
        parts = matmul(jnp.concatenate(taps, axis=1), w2_ref[...]).reshape(blocks + 2, 16, 2 * LANES)
        pre = parts[1:, :, :LANES] + parts[:-1, :, LANES:]
        slope = 0.6 + 0.4 * pre / jnp.sqrt(pre * pre + 1.0)
        upstream = jnp.concatenate([ups[t], ups[t + quarter]], axis=1)
        delta = (upstream * slope).astype(BF16).astype(F32)
        moved = jnp.concatenate([pltpu.roll(delta[:, :8], 7, 1), pltpu.roll(delta[:, 8:], 7, 1)], axis=1)
        deltas[t] = delta
        shifted[t] = moved.astype(BF16)
        return carry

    lax.fori_loop(0, quarter + 1, conv_two, 0)

    sublane = lax.broadcasted_iota(jnp.int32, (1, 1, 16, 1), 2) % 8
    own_rows = jnp.logical_and(sublane >= 1, sublane <= 4)

    def with_next(values):
        values = values.T
        edge = jnp.zeros((LANES, values.shape[1] // blocks), values.dtype)
        here = jnp.concatenate([edge, values], axis=1)
        after = jnp.concatenate([values, edge], axis=1)
        return jnp.concatenate([here, after], axis=0)

    own_delta = [jnp.where(own_rows[0], deltas[t, 0:blocks], 0.0) for t in range(quarter)]
    left = with_next(jnp.stack(own_delta, axis=1).reshape(blocks * quarter * 16, LANES)).astype(BF16)

    def second_taps(tap):
        a, b = tap // 3, tap % 3
        found = [pairs[b, 2 * t + a, 0 : blocks + 1] for t in range(quarter)]
        return jnp.stack(found, axis=1).reshape((blocks + 1) * quarter * 16, LANES)

    for tap in range(0, 9, 2):
        right = [second_taps(x) for x in range(tap, min(tap + 2, 9))]
        found = matmul(left, jnp.concatenate(right, axis=1))
        for n in range(len(right)):
            row = (tap + n) * 192
            lanes = slice(n * LANES, (n + 1) * LANES)
            out_ref[row : row + 64, :] = found[LANES:, lanes].T[64:]
            out_ref[row + 64 : row + 192, :] = found[:LANES, lanes].T

    def pack(values):
        both = jnp.concatenate([values[:, :-1], values[:, 1:]], axis=3)
        return both.reshape(quarter * blocks * 16, 2 * LANES)

    plain = deltas[...].astype(BF16)
    moved = shifted[...]
    here, after = pack(plain[:-1]), pack(plain[1:])
    here_up, after_up = pack(moved[:-1]), pack(moved[1:])

    def back(terms):
        joined = jnp.concatenate([values for values, a, b in terms], axis=1)
        weights = jnp.concatenate([w2b_ref[3 * a + b] for values, a, b in terms], axis=0)
        return matmul(joined, weights).reshape(quarter, blocks, 16, LANES)

    rows = [
        [back([(here, 1, 1)]), back([(here_up, 1, 0), (here, 1, 2)])],
        [
            back([(after, 0, 1), (here, 2, 1)]),
            back([(after_up, 0, 0), (after, 0, 2), (here_up, 2, 0), (here, 2, 2)]),
        ],
    ]
    own_list = []
    for i in range(planes // 2):
        t, parity = i // 2, i % 2
        half = slice(0, 8) if t < quarter else slice(8, 16)
        back_one = jnp.concatenate([rows[parity][p][t % quarter, :, half, :] for p in (0, 1)], axis=1)
        delta = back_one * slopes[i + 1, 1 : blocks + 1]
        own_list.append(jnp.where(own_rows[0], delta, 0.0).astype(BF16))
    left_one = with_next(jnp.stack(own_list, axis=1).reshape(blocks * (planes // 2) * 16, LANES))

    def first_taps(tap):
        a, b = tap // 3, tap % 3
        found = []
        for m in range(blocks + 1):
            for i in range(planes // 2):
                index = 2 * (i + 1) + a
                found.append(rim_tiles[b, index, 0] if m == 0 else tiles[b, index, m - 1])
        return jnp.concatenate(found, axis=0)

    grads = []
    for tap in range(0, 9, 2):
        right = [first_taps(x) for x in range(tap, min(tap + 2, 9))]
        found = matmul(left_one, jnp.concatenate(right, axis=1))
        for n in range(len(right)):
            main = found[:LANES, n * LANES : (n + 1) * LANES]
            prev = found[LANES : LANES + 64, n * LANES : (n + 1) * LANES]
            even = jnp.concatenate([prev[:, 96:], main[:64, :64]], axis=1)
            grads.append(even + main[64:, 32:])
    grads.append(jnp.zeros((64, FIRST_BLOCKS * LANES - 9 * 96), F32))
    first = jnp.concatenate(grads, axis=1)
    for n in range(FIRST_BLOCKS):
        row = SECOND_ROWS + 64 * n
        out_ref[row : row + 64, :] = first[:, n * LANES : (n + 1) * LANES]
    used = SECOND_ROWS + 64 * FIRST_BLOCKS
    if out_ref.shape[0] > used:
        out_ref[used:, :] = jnp.zeros((out_ref.shape[0] - used, LANES), F32)

    core, square = place_ref[0], place_ref[1]
    squares, size = keep_ref.shape[0], keep_ref.shape[1]
    for n in range(squares):
        for ref, half in ((keep_ref, core), (give_ref, 1 - core)):
            start = pl.multiple_of((half * squares + (square ^ n)) * size, 8)
            ref[n] = out_ref[pl.ds(start, size), :].astype(BF16)


def unpack(place_ref, keep_ref, got_ref, g1_ref, g2_ref, sums):
    core, square = place_ref[0], place_ref[1]
    squares, size = keep_ref.shape[0], keep_ref.shape[1]
    for n in range(squares):
        for ref, half in ((keep_ref, core), (got_ref, 1 - core)):
            start = pl.multiple_of((half * squares + (square ^ n)) * size, 8)
            sums[pl.ds(start, size), :] = ref[n].astype(F32)
    first = [sums[SECOND_ROWS + 64 * n : SECOND_ROWS + 64 * (n + 1), :] for n in range(FIRST_BLOCKS)]
    g1_ref[...] = jnp.concatenate(first, axis=1)[:, : g1_ref.shape[1]]
    g2_ref[...] = sums[:SECOND_ROWS, :]


def local_grads(flags, place, squares, volume, faces, corners, cotangent, weights):
    planes = volume.shape[0]
    blocks = volume.shape[2] // LANES
    hidden_planes = planes // 2 + 3
    out_planes = planes // 4
    unit = 2 * squares * 16
    rows = -(-(SECOND_ROWS + 64 * FIRST_BLOCKS) // unit) * unit
    whole = pl.BlockSpec(memory_space=pltpu.VMEM)
    smem = pl.BlockSpec(memory_space=pltpu.SMEM)
    dep, row_a, row_b, edge_a, edge_b = faces
    tiles, parts = pl.pallas_call(
        own_blocks,
        out_shape=[
            jax.ShapeDtypeStruct((3, planes + 9, blocks, 16, LANES), BF16),
            jax.ShapeDtypeStruct((hidden_planes + 1, blocks, 16, 2 * LANES), F32),
        ],
        in_specs=[smem] + [whole] * 7,
        out_specs=[whole] * 2,
        scratch_shapes=[pltpu.VMEM((2, blocks, 40, LANES), F32)],
        compiler_params=pltpu.CompilerParams(vmem_limit_bytes=16 * 1024 * 1024),
        cost_estimate=pl.CostEstimate(flops=2 * 10**9, bytes_accessed=10**7, transcendentals=0),
    )(flags, volume, *faces, weights[0])
    scratch = [
        pltpu.VMEM((rows, LANES), F32),
        pltpu.VMEM((4, 2, 40, LANES), F32),
        pltpu.VMEM((3, planes + 7, 2, 16, LANES), BF16),
        pltpu.VMEM((hidden_planes, 2, 16, 2 * LANES), F32),
        pltpu.VMEM((hidden_planes, blocks + 2, 16, LANES), F32),
        pltpu.VMEM((3, hidden_planes, blocks + 2, 8, LANES), F32),
        pltpu.VMEM((3, out_planes + 3, blocks + 2, 16, LANES), BF16),
        pltpu.VMEM((out_planes + 1, blocks + 1, 8, LANES), F32),
        pltpu.VMEM((out_planes // 2 + 1, blocks + 1, 16, LANES), F32),
        pltpu.VMEM((out_planes // 2 + 1, blocks + 1, 16, LANES), BF16),
    ]
    operands = (tiles, parts, *faces, *corners, cotangent, *weights)
    return pl.pallas_call(
        body,
        out_shape=[jax.ShapeDtypeStruct((squares, rows // (2 * squares), LANES), BF16)] * 2,
        in_specs=[smem] * 2 + [whole] * len(operands),
        out_specs=[whole] * 2,
        scratch_shapes=scratch,
        compiler_params=pltpu.CompilerParams(vmem_limit_bytes=28 * 1024 * 1024),
        cost_estimate=pl.CostEstimate(flops=4 * 10**9, bytes_accessed=10**7, transcendentals=0),
    )(flags, place, *operands)


def shards(volume, first_weight, second_weight, cotangent):
    half = lax.axis_index("depth")
    row, col = lax.axis_index("row"), lax.axis_index("col")
    rows, cols = lax.axis_size("row"), lax.axis_size("col")
    inner = [jnp.logical_and(i > 0, i < n - 1).astype(jnp.int32) for i, n in ((row, rows), (col, cols))]
    flags = jnp.stack([half, row % 2, col % 2, *inner])
    whole = pl.BlockSpec(memory_space=pltpu.VMEM)
    smem = pl.BlockSpec(memory_space=pltpu.SMEM)
    small = pltpu.CompilerParams(vmem_limit_bytes=12 * 1024 * 1024)
    planes, high, width = volume.shape
    groups = planes + cotangent.shape[0] // 4
    in_hbm = pl.BlockSpec(memory_space=pltpu.HBM)

    def stay(argument):
        return pltpu.with_memory_space_constraint(argument, pltpu.HBM)

    volume, cotangent, dep = pl.pallas_call(
        bring,
        out_shape=[jax.ShapeDtypeStruct(shape, BF16) for shape in (volume.shape, cotangent.shape, (17, 4, width))],
        in_specs=[smem] + [in_hbm] * 2,
        out_specs=[whole] * 3,
        scratch_shapes=[pltpu.SemaphoreType.DMA((4,))],
        compiler_params=small,
    )(flags, stay(volume), stay(cotangent))
    weights = (first_weight, second_weight.T)
    shapes = [(groups, 4, width)] * 2 + [(groups, high, LANES)] * 2
    shapes += [weight.shape for weight in weights]
    row_a, row_b, side_a, side_b, first_taps, second_taps = pl.pallas_call(
        pack,
        out_shape=[jax.ShapeDtypeStruct(shape, BF16) for shape in shapes],
        in_specs=[smem] + [whole] * 2 + [in_hbm] * 2,
        out_specs=[whole] * len(shapes),
        scratch_shapes=[pltpu.SemaphoreType.DMA((2,))],
        compiler_params=small,
    )(flags, volume, cotangent, *[stay(weight) for weight in weights])

    def to_col(block, kind):
        return lax.ppermute(block, ("row", "col"), pairs_of_lines(rows, cols, kind))

    dep = lax.ppermute(dep, "depth", [(0, 1), (1, 0)])
    row_a = lax.ppermute(row_a, "row", pairs_on_line(rows, 0))
    row_b = lax.ppermute(row_b, "row", pairs_on_line(rows, 1))
    row_a, side_a, side_b = lax.optimization_barrier((row_a, side_a, side_b))
    side_a, side_b = to_col(side_a, 0), to_col(side_b, 1)

    low, top = [jnp.concatenate([dep[n : n + 1] for n in (*range(k, 16, 4), 16)], axis=0) for k in (0, 3)]
    even, ends = row % 2 == 0, jnp.logical_or(row == 0, row == rows - 1)
    edge_a = jnp.where(even, top, low)
    edge_b = jnp.where(ends, 0, jnp.where(even, low, top))
    edge_a = lax.ppermute(edge_a, "row", pairs_on_line(rows, 0))
    edge_b = lax.ppermute(edge_b, ("depth", "row"), pairs_of_lines(2, rows, 1))
    weights = pl.pallas_call(
        bands,
        out_shape=[jax.ShapeDtypeStruct(shape, BF16) for shape in ((1152, 256), (1152, 256), (9, 256, 128))],
        in_specs=[whole] * 2,
        out_specs=[whole] * 3,
        compiler_params=small,
    )(first_taps, second_taps)
    col_a, col_b = pl.pallas_call(
        pack_corners,
        out_shape=[jax.ShapeDtypeStruct((planes + 14, 8, LANES), BF16)] * 2,
        in_specs=[smem] + [whole] * 5,
        out_specs=[whole] * 2,
        compiler_params=small,
    )(flags, dep, row_a, row_b, edge_a, edge_b)
    col_a, col_b, volume = lax.optimization_barrier((col_a, col_b, volume))
    col_a, col_b = to_col(col_a, 0), to_col(col_b, 1)

    spot = lax.axis_index(("depth", "row"))
    squares = lax.axis_size(("depth", "row")) // 2
    where = jnp.stack([spot % 2, spot // 2])
    faces, corners = (dep, row_a, row_b, edge_a, edge_b), (side_a, side_b, col_a, col_b)
    keep, give = local_grads(flags, where, squares, volume, faces, corners, cotangent, weights)

    def to_square(block, n):
        route = [(2 * i + c, 2 * (i ^ n) + c) for i in range(squares) for c in (0, 1)]
        return lax.ppermute(block, ("depth", "row"), route)

    def to_core(block):
        return lax.ppermute(block, ("depth", "row"), [(i, i ^ 1) for i in range(2 * squares)])

    def along_col(block, n):
        return lax.ppermute(block, "col", [(i, i ^ n) for i in range(cols)])

    both = add_up(keep, to_core(give))
    share = add_up(both[0], *[to_square(both[n], n) for n in range(1, squares)])
    share = add_up(share, *[along_col(share, n) for n in range(1, cols)])
    mine = jnp.stack([share] + [to_square(share, n) for n in range(1, squares)])
    other = to_core(mine)
    grads = [jax.ShapeDtypeStruct(shape, F32) for shape in (first_weight.shape, second_weight.shape[::-1])]
    first_grad, second_grad = pl.pallas_call(
        unpack,
        out_shape=grads,
        in_specs=[smem] + [whole] * 2,
        out_specs=[whole] * 2,
        scratch_shapes=[pltpu.VMEM((mine.shape[0] * mine.shape[1] * 2, LANES), F32)],
        compiler_params=small,
    )(where, mine, other)
    return first_grad, second_grad.T


def solution(mesh):
    placed = (P("depth", "row", "col"), P(), P(), P("depth", "row", "col"))
    return jax.shard_map(shards, mesh=mesh, in_specs=placed, out_specs=(P(), P()), check_vma=False)
```

```python
import jax
import jax.numpy as jnp
from jax import lax
from jax.experimental import pallas as pl
from jax.experimental.pallas import tpu as pltpu
from jax.sharding import PartitionSpec as P

LANES = 128
SECOND_ROWS = 27 * 64
FIRST_BLOCKS = 7
F32 = jnp.float32
BF16 = jnp.bfloat16


def pairs_on_line(count, kind):
    firsts = range(kind, count - 1, 2)
    swapped = [(i, i + 1) for i in firsts] + [(i + 1, i) for i in firsts]
    met = {i for i, j in swapped}
    return swapped + [(i, i) for i in range(count) if i not in met]


def pairs_of_lines(lines, count, kind):
    route = []
    for line in range(lines):
        for i, j in pairs_on_line(count, kind):
            route.append((line * count + i, (line ^ 1 if i == j else line) * count + j))
    return route


def add_up(*terms):
    terms = [term.astype(F32) for term in terms]
    while len(terms) > 1:
        terms = [terms[n] + terms[n + 1] for n in range(0, len(terms), 2)]
    return terms[0].astype(BF16)


def matmul(left, right):
    return lax.dot_general(left, right, (((1,), (0,)), ((), ())), preferred_element_type=F32)


def bring(flag_ref, vol_hbm, cot_hbm, vol_ref, cot_ref, dep_ref, arrived):
    first_plane = flag_ref[0] == 0
    planes = vol_ref.shape[0]
    inner = pl.ds(4, planes - 8)
    copies = [pltpu.make_async_copy(cot_hbm, cot_ref, arrived.at[0])]
    for n, part in enumerate((pl.ds(0, 4), pl.ds(planes - 4, 4), inner)):
        copies.append(pltpu.make_async_copy(vol_hbm.at[part], vol_ref.at[part], arrived.at[1 + n]))
    for copy in copies:
        copy.start()
    for copy in copies[:3]:
        copy.wait()
    dep_ref[16] = cot_ref[0]
    for q in range(4):
        block = jnp.where(first_plane, vol_ref[planes - 4 + q].astype(F32), vol_ref[q].astype(F32))
        for g in range(4):
            dep_ref[4 * q + g] = block[4 * g : 4 * g + 4].astype(BF16)
    copies[3].wait()


def pack(
    flag_ref, vol_ref, cot_ref, first_hbm, second_hbm, row_b_ref, row_a_ref, col_a_ref, col_b_ref,
    first_ref, second_ref, arrived,
):
    row_even, col_even = flag_ref[1] == 0, flag_ref[2] == 0
    row_inner, col_inner = flag_ref[3] != 0, flag_ref[4] != 0
    planes, high, width = vol_ref.shape
    cots = cot_ref.shape[0]
    copies = [
        pltpu.make_async_copy(first_hbm, first_ref, arrived.at[0]),
        pltpu.make_async_copy(second_hbm, second_ref, arrived.at[1]),
    ]
    for copy in copies:
        copy.start()

    cot = cot_ref[...].astype(F32)
    for g in range(cots // 4):
        tops = jnp.concatenate([cot[4 * g + n, :1] for n in range(4)], axis=0)
        row_a_ref[planes + g] = tops.astype(BF16)
        row_b_ref[planes + g] = jnp.where(row_inner, tops, 0.0).astype(BF16)
        side = jnp.concatenate([cot[4 * g + n, :, :LANES] for n in range(4)], axis=0)
        col_a_ref[planes + g] = side.astype(BF16)
        col_b_ref[planes + g] = jnp.where(col_inner, side, 0.0).astype(BF16)

    def plane(d, carry):
        block = vol_ref[d].astype(F32)
        low, top = block[:4], block[high - 4 :]
        row_a_ref[d] = jnp.where(row_even, top, low).astype(BF16)
        row_b_ref[d] = jnp.where(row_inner, jnp.where(row_even, low, top), 0.0).astype(BF16)
        left, right = block[:, :LANES], block[:, width - LANES :]
        col_a_ref[d] = jnp.where(col_even, right, left).astype(BF16)
        col_b_ref[d] = jnp.where(col_inner, jnp.where(col_even, left, right), 0.0).astype(BF16)
        return carry

    lax.fori_loop(0, planes, plane, 0, unroll=2)
    for copy in copies:
        copy.wait()


def pack_corners(flag_ref, dep_ref, row_a_ref, row_b_ref, edge_a_ref, edge_b_ref, col_a_ref, col_b_ref):
    row_even, col_even, col_inner = flag_ref[1] == 0, flag_ref[2] == 0, flag_ref[4] != 0
    width = dep_ref.shape[2]
    groups = row_a_ref.shape[0]
    planes = (groups * 16) // 17
    faces = (slice(0, LANES), slice(width - LANES, width))

    def store(n, left, right):
        col_a_ref[n] = jnp.where(col_even, right, left).astype(BF16)
        col_b_ref[n] = jnp.where(col_inner, jnp.where(col_even, left, right), 0.0).astype(BF16)

    def lower_upper(a_ref, b_ref, source, target):
        values = []
        for lanes in faces:
            a, b = a_ref[source, :, lanes].astype(F32), b_ref[source, :, lanes].astype(F32)
            values.append(jnp.concatenate([jnp.where(row_even, b, a), jnp.where(row_even, a, b)], axis=0))
        store(target, *values)

    def plane(d, carry):
        lower_upper(row_a_ref, row_b_ref, d, d)
        return carry

    lax.fori_loop(0, planes, plane, 0)
    for q in range(4):
        lower_upper(edge_a_ref, edge_b_ref, q, planes + q)
        for n in range(2):
            units = range(4 * q + 2 * n, 4 * q + 2 * n + 2)
            store(
                planes + 4 + 2 * q + n,
                *[jnp.concatenate([dep_ref[u, :, lanes].astype(F32) for u in units], axis=0) for lanes in faces],
            )
    lanes = faces[0]
    tops = [
        jnp.where(row_even, row_a_ref[g, :, lanes].astype(F32), row_b_ref[g, :, lanes].astype(F32))
        for g in range(planes, groups)
    ]
    corner = jnp.where(row_even, edge_a_ref[4, :, lanes].astype(F32), edge_b_ref[4, :, lanes].astype(F32))
    own = dep_ref[16, :, lanes].astype(F32)
    for n, values in enumerate((jnp.concatenate(tops, axis=0), jnp.concatenate([own, corner], axis=0))):
        col_a_ref[planes + 12 + n] = values.astype(BF16)
        col_b_ref[planes + 12 + n] = jnp.where(col_inner, values, 0.0).astype(BF16)


def bands(first_ref, second_ref, w1_ref, w2_ref, w2b_ref):
    out_chan = first_ref.shape[0]
    first = first_ref[...].astype(F32)
    blank = jnp.zeros((out_chan, LANES), F32)
    for tap in range(9):
        rows = slice(tap * LANES, (tap + 1) * LANES)
        taps = first[:, tap * 96 : (tap + 1) * 96]
        main_even = jnp.concatenate([taps[:, 32:], blank[:, :64]], axis=1)
        main_odd = jnp.concatenate([blank[:, :32], taps], axis=1)
        prev_even = jnp.concatenate([blank[:, :96], taps[:, :32]], axis=1)
        w1_ref[rows] = jnp.concatenate([main_even, main_odd, prev_even, blank], axis=0).T.astype(BF16)
        main = second_ref[tap * 192 + 64 : (tap + 1) * 192, :]
        prev = jnp.concatenate([jnp.zeros((64, LANES), BF16), second_ref[tap * 192 : tap * 192 + 64, :]], axis=0)
        both = jnp.concatenate([main, prev], axis=1)
        w2_ref[rows] = both
        w2b_ref[tap] = both.astype(F32).T.astype(BF16)


def split_rows(stage, tiles, index, blocks):
    for m in blocks:
        rows = [stage[m, pl.ds(4 + s, 8, stride=4), :] for s in range(-1, 4)]
        for b in range(3):
            tiles[b, index, m] = jnp.concatenate([rows[b], rows[b + 2]], axis=0).astype(BF16)


def clear_stage(stage):
    stage[:, :, 0:8, :] = jnp.zeros(stage.shape[:2] + (8, LANES), F32)
    stage[:, :, 24:40, :] = jnp.zeros(stage.shape[:2] + (16, LANES), F32)


def ahead(even, a, b):
    return jnp.where(even, a.astype(F32), b.astype(F32))


def behind(even, a, b):
    return jnp.where(even, b.astype(F32), a.astype(F32))


def own_blocks(
    flag_ref, vol_ref, dep_ref, row_a_ref, row_b_ref, edge_a_ref, edge_b_ref, w1_ref, tiles, parts, stage
):
    first_plane, row_even = flag_ref[0] == 0, flag_ref[1] == 0
    planes = vol_ref.shape[0]
    blocks = vol_ref.shape[2] // LANES
    clear_stage(stage)

    def place(n, target, own, a, b, keep):
        def kept(values):
            return values if keep is None else jnp.where(keep, values, 0.0)

        for m in range(blocks):
            lanes = slice(m * LANES, (m + 1) * LANES)
            stage[n, m, 8:24, :] = kept(own(lanes).astype(F32))
            stage[n, m, 4:8, :] = kept(behind(row_even, a(lanes), b(lanes)))
            stage[n, m, 24:28, :] = kept(ahead(row_even, a(lanes), b(lanes)))
        split_rows(stage.at[n], tiles, target, range(blocks))

    def place_own(pair, carry):
        for n in range(2):
            d = 2 * pair + n
            place(
                n, d + 3, lambda lanes: vol_ref[d, :, lanes],
                lambda lanes: row_a_ref[d, :, lanes], lambda lanes: row_b_ref[d, :, lanes], None,
            )
        return carry

    def place_halo(target, q, keep):
        place(
            target % 2, target,
            lambda lanes: jnp.concatenate([dep_ref[4 * q + g, :, lanes].astype(F32) for g in range(4)], axis=0),
            lambda lanes: edge_a_ref[q, :, lanes], lambda lanes: edge_b_ref[q, :, lanes], keep,
        )

    lax.fori_loop(0, planes // 2, place_own, 0)
    for q in range(3):
        place_halo(q, q + 1, jnp.logical_not(first_plane))
    for q in range(4):
        place_halo(planes + 3 + q, q, first_plane)
    tiles[:, planes + 7 :] = jnp.zeros((3, 2, blocks, 16, LANES), BF16)

    group = 5

    def product(step, carry):
        taps = []
        for a in range(3):
            for b in range(3):
                start = 2 * group * step + a
                found = [tiles[b, start + 2 * n].reshape(blocks * 16, LANES) for n in range(group)]
                taps.append(jnp.concatenate(found, axis=0))
        found = matmul(jnp.concatenate(taps, axis=1), w1_ref[...])
        parts[pl.ds(group * step, group)] = found.reshape(group, blocks, 16, 2 * LANES)
        return carry

    lax.fori_loop(0, parts.shape[0] // group, product, 0)


def body(
    flag_ref, place_ref, tiles, parts, dep_ref, row_a_ref, row_b_ref, edge_a_ref, edge_b_ref,
    side_a_ref, side_b_ref, col_a_ref, col_b_ref, cot_ref, w1_ref, w2_ref, w2b_ref, keep_ref, give_ref,
    out_ref, stage, rim_tiles, rim_parts, slopes, hid, pairs, ups, deltas, shifted,
):
    first_plane, row_even, col_even = flag_ref[0] == 0, flag_ref[1] == 0, flag_ref[2] == 0
    planes = tiles.shape[1] - 9
    blocks = tiles.shape[2]
    half_planes = planes // 4
    hidden_planes = planes // 2 + 3

    clear_stage(stage)

    def place(n, target, source, side_a, side_b, keep):
        for m, choose in ((0, behind), (1, ahead)):
            corners = choose(col_even, col_a_ref[source], col_b_ref[source])
            own = choose(col_even, side_a, side_b)
            if keep is not None:
                corners, own = jnp.where(keep, corners, 0.0), jnp.where(keep, own, 0.0)
            stage[n, m, 4:8, :] = corners[:4]
            stage[n, m, 8:24, :] = own
            stage[n, m, 24:28, :] = corners[4:]
        split_rows(stage.at[n], rim_tiles, target, range(2))

    def place_own(group, carry):
        for n in range(4):
            d = 4 * group + n
            place(n, d + 3, d, side_a_ref[d], side_b_ref[d], None)
        return carry

    def place_halo(target, q, keep):
        start = planes + 4 + 2 * q
        side_a = jnp.concatenate([col_a_ref[start].astype(F32), col_a_ref[start + 1].astype(F32)], axis=0)
        side_b = jnp.concatenate([col_b_ref[start].astype(F32), col_b_ref[start + 1].astype(F32)], axis=0)
        place(target % 4, target, planes + q, side_a, side_b, keep)

    lax.fori_loop(0, planes // 4, place_own, 0)
    for q in range(3):
        place_halo(q, q + 1, jnp.logical_not(first_plane))
    for q in range(4):
        place_halo(planes + 3 + q, q, first_plane)

    taps = []
    for a in range(3):
        for b in range(3):
            rows = [rim_tiles[b, 2 * i + a].reshape(32, LANES) for i in range(hidden_planes)]
            taps.append(jnp.concatenate(rows, axis=0))
    found = matmul(jnp.concatenate(taps, axis=1), w1_ref[...])
    rim_parts[...] = found.reshape(hidden_planes, 2, 16, 2 * LANES)

    def conv_one(i, carry):
        main, prev = parts[i, :, :, :LANES], parts[i, :, :, LANES:]
        rim, rim_prev = rim_parts[i, :, :, :LANES], rim_parts[i, 0:1, :, LANES:]
        blank = jnp.zeros((1, 16, LANES), F32)
        pre = jnp.concatenate([rim[:1], main, rim[1:]], axis=0) + jnp.concatenate([blank, rim_prev, prev], axis=0)
        square = pre * pre + 1.0
        inverse = lax.rsqrt(square)
        slopes[i] = 0.6 + 0.4 * (pre * inverse)
        hidden = (0.6 * pre + 0.4 * (square * inverse - 1.0)).astype(BF16).astype(F32)
        odd = hidden[:, 8:, :]
        hid[0, i] = pltpu.roll(odd, 1, 1)
        hid[1, i] = hidden[:, :8, :]
        hid[2, i] = odd
        return carry

    lax.fori_loop(0, hidden_planes, conv_one, 0)

    wide = (blocks + 2) * 16

    def pair(i, carry):
        for b in range(3):
            pairs[b, i] = jnp.concatenate([hid[b, i], hid[b, i + half_planes]], axis=1).astype(BF16)
        return carry

    lax.fori_loop(0, half_planes + 3, pair, 0)

    ups[...] = jnp.zeros_like(ups)
    for k in range(blocks):
        lanes = slice(k * LANES, (k + 1) * LANES)
        ups[0:half_planes, k, 1:5, :] = cot_ref[:, :, lanes].astype(F32)
        ups[half_planes, k, 1:5, :] = jnp.where(first_plane, dep_ref[16, :, lanes].astype(F32), 0.0)
        for g in range(half_planes // 4):
            tops = ahead(row_even, row_a_ref[planes + g, :, lanes], row_b_ref[planes + g, :, lanes])
            for n in range(4):
                ups[4 * g + n, k, 5:6, :] = tops[n : n + 1]
        corner = ahead(row_even, edge_a_ref[4, :, lanes], edge_b_ref[4, :, lanes])[:1]
        ups[half_planes, k, 5:6, :] = jnp.where(first_plane, corner, 0.0)
    for g in range(half_planes // 4):
        side = ahead(col_even, side_a_ref[planes + g], side_b_ref[planes + g])
        for n in range(4):
            ups[4 * g + n, blocks, 1:5, :] = side[4 * n : 4 * n + 4]
    tops = ahead(col_even, col_a_ref[planes + 12], col_b_ref[planes + 12])
    for n in range(half_planes):
        ups[n, blocks, 5:6, :] = tops[n : n + 1]
    beyond = jnp.where(first_plane, ahead(col_even, col_a_ref[planes + 13], col_b_ref[planes + 13]), 0.0)
    ups[half_planes, blocks, 1:6, :] = beyond[:5]

    quarter = half_planes // 2

    taps = []
    for a in range(3):
        for b in range(3):
            rows = [pairs[b, 2 * t + a].reshape(wide, LANES) for t in range(quarter + 1)]
            taps.append(jnp.concatenate(rows, axis=0))
    found = matmul(jnp.concatenate(taps, axis=1), w2_ref[...]).reshape(quarter + 1, blocks + 2, 16, 2 * LANES)
    for t in range(quarter + 1):
        pre = found[t, 1:, :, :LANES] + found[t, :-1, :, LANES:]
        slope = 0.6 + 0.4 * (pre * lax.rsqrt(pre * pre + 1.0))
        upstream = jnp.concatenate([ups[t], ups[t + quarter]], axis=1)
        delta = (upstream * slope).astype(BF16).astype(F32)
        moved = jnp.concatenate([pltpu.roll(delta[:, :8], 7, 1), pltpu.roll(delta[:, 8:], 7, 1)], axis=1)
        deltas[t] = delta
        shifted[t] = moved.astype(BF16)

    sublane = lax.broadcasted_iota(jnp.int32, (1, 1, 16, 1), 2) % 8
    own_rows = jnp.logical_and(sublane >= 1, sublane <= 4)

    def with_next(values, needed):
        values = values.T
        edge = jnp.zeros((LANES, values.shape[1] // blocks), values.dtype)
        here = jnp.concatenate([edge, values], axis=1)
        after = jnp.concatenate([values, edge], axis=1)[:needed]
        return jnp.concatenate([here, after], axis=0)

    own_delta = [jnp.where(own_rows[0], deltas[t, 0:blocks], 0.0) for t in range(quarter)]
    left = with_next(jnp.stack(own_delta, axis=1).reshape(blocks * quarter * 16, LANES), LANES).astype(BF16)

    def second_taps(tap):
        a, b = tap // 3, tap % 3
        found = [pairs[b, 2 * t + a, 0 : blocks + 1] for t in range(quarter)]
        return jnp.stack(found, axis=1).reshape((blocks + 1) * quarter * 16, LANES)

    for tap in range(0, 9, 2):
        right = [second_taps(x) for x in range(tap, min(tap + 2, 9))]
        found = matmul(left, jnp.concatenate(right, axis=1))
        for n in range(len(right)):
            row = (tap + n) * 192
            lanes = slice(n * LANES, (n + 1) * LANES)
            out_ref[row : row + 64, :] = found[LANES:, lanes].T[64:]
            out_ref[row + 64 : row + 192, :] = found[:LANES, lanes].T

    def pack(values):
        both = jnp.concatenate([values[:, :-1], values[:, 1:]], axis=3)
        return both.reshape(quarter * blocks * 16, 2 * LANES)

    plain = deltas[...].astype(BF16)
    moved = shifted[...]
    here, after = pack(plain[:-1]), pack(plain[1:])
    here_up, after_up = pack(moved[:-1]), pack(moved[1:])

    def back(terms):
        joined = jnp.concatenate([values for values, a, b in terms], axis=1)
        weights = jnp.concatenate([w2b_ref[3 * a + b] for values, a, b in terms], axis=0)
        return matmul(joined, weights).reshape(quarter, blocks, 16, LANES)

    rows = [
        [back([(here, 1, 1)]), back([(here_up, 1, 0), (here, 1, 2)])],
        [
            back([(after, 0, 1), (here, 2, 1)]),
            back([(after_up, 0, 0), (after, 0, 2), (here_up, 2, 0), (here, 2, 2)]),
        ],
    ]
    own_list = []
    for i in range(planes // 2):
        t, parity = i // 2, i % 2
        half = slice(0, 8) if t < quarter else slice(8, 16)
        back_one = jnp.concatenate([rows[parity][p][t % quarter, :, half, :] for p in (0, 1)], axis=1)
        delta = back_one * slopes[i + 1, 1 : blocks + 1]
        own_list.append(jnp.where(own_rows[0], delta, 0.0).astype(BF16))
    left_one = with_next(jnp.stack(own_list, axis=1).reshape(blocks * (planes // 2) * 16, LANES), 64)

    def first_taps(tap):
        a, b = tap // 3, tap % 3
        found = []
        for m in range(blocks + 1):
            for i in range(planes // 2):
                index = 2 * (i + 1) + a
                found.append(rim_tiles[b, index, 0] if m == 0 else tiles[b, index, m - 1])
        return jnp.concatenate(found, axis=0)

    grads = []
    for tap in range(0, 9, 2):
        right = [first_taps(x) for x in range(tap, min(tap + 2, 9))]
        found = matmul(left_one, jnp.concatenate(right, axis=1))
        for n in range(len(right)):
            main = found[:LANES, n * LANES : (n + 1) * LANES]
            prev = found[LANES:, n * LANES : (n + 1) * LANES]
            even = jnp.concatenate([prev[:, 96:], main[:64, :64]], axis=1)
            grads.append(even + main[64:, 32:])
    grads.append(jnp.zeros((64, FIRST_BLOCKS * LANES - 9 * 96), F32))
    first = jnp.concatenate(grads, axis=1)
    for n in range(FIRST_BLOCKS):
        row = SECOND_ROWS + 64 * n
        out_ref[row : row + 64, :] = first[:, n * LANES : (n + 1) * LANES]
    used = SECOND_ROWS + 64 * FIRST_BLOCKS
    if out_ref.shape[0] > used:
        out_ref[used:, :] = jnp.zeros((out_ref.shape[0] - used, LANES), F32)

    core, square = place_ref[0], place_ref[1]
    squares, size = keep_ref.shape[0], keep_ref.shape[1]
    for n in range(squares):
        for ref, half in ((keep_ref, core), (give_ref, 1 - core)):
            start = pl.multiple_of((half * squares + (square ^ n)) * size, 8)
            ref[n] = out_ref[pl.ds(start, size), :].astype(BF16)


def unpack(place_ref, keep_ref, got_ref, g1_ref, g2_ref, sums):
    core, square = place_ref[0], place_ref[1]
    squares, size = keep_ref.shape[0], keep_ref.shape[1]
    for n in range(squares):
        for ref, half in ((keep_ref, core), (got_ref, 1 - core)):
            start = pl.multiple_of((half * squares + (square ^ n)) * size, 8)
            sums[pl.ds(start, size), :] = ref[n].astype(F32)
    first = [sums[SECOND_ROWS + 64 * n : SECOND_ROWS + 64 * (n + 1), :] for n in range(FIRST_BLOCKS)]
    g1_ref[...] = jnp.concatenate(first, axis=1)[:, : g1_ref.shape[1]]
    g2_ref[...] = sums[:SECOND_ROWS, :]


def local_grads(flags, place, squares, volume, faces, corners, cotangent, weights):
    planes = volume.shape[0]
    blocks = volume.shape[2] // LANES
    hidden_planes = planes // 2 + 3
    out_planes = planes // 4
    unit = 2 * squares * 16
    rows = -(-(SECOND_ROWS + 64 * FIRST_BLOCKS) // unit) * unit
    whole = pl.BlockSpec(memory_space=pltpu.VMEM)
    smem = pl.BlockSpec(memory_space=pltpu.SMEM)
    dep, row_a, row_b, edge_a, edge_b = faces
    tiles, parts = pl.pallas_call(
        own_blocks,
        out_shape=[
            jax.ShapeDtypeStruct((3, planes + 9, blocks, 16, LANES), BF16),
            jax.ShapeDtypeStruct((hidden_planes + 1, blocks, 16, 2 * LANES), F32),
        ],
        in_specs=[smem] + [whole] * 7,
        out_specs=[whole] * 2,
        scratch_shapes=[pltpu.VMEM((2, blocks, 40, LANES), F32)],
        compiler_params=pltpu.CompilerParams(vmem_limit_bytes=16 * 1024 * 1024),
        cost_estimate=pl.CostEstimate(flops=2 * 10**9, bytes_accessed=10**7, transcendentals=0),
    )(flags, volume, *faces, weights[0])
    scratch = [
        pltpu.VMEM((rows, LANES), F32),
        pltpu.VMEM((4, 2, 40, LANES), F32),
        pltpu.VMEM((3, planes + 7, 2, 16, LANES), BF16),
        pltpu.VMEM((hidden_planes, 2, 16, 2 * LANES), F32),
        pltpu.VMEM((hidden_planes, blocks + 2, 16, LANES), F32),
        pltpu.VMEM((3, hidden_planes, blocks + 2, 8, LANES), F32),
        pltpu.VMEM((3, out_planes + 3, blocks + 2, 16, LANES), BF16),
        pltpu.VMEM((out_planes + 1, blocks + 1, 8, LANES), F32),
        pltpu.VMEM((out_planes // 2 + 1, blocks + 1, 16, LANES), F32),
        pltpu.VMEM((out_planes // 2 + 1, blocks + 1, 16, LANES), BF16),
    ]
    operands = (tiles, parts, *faces, *corners, cotangent, *weights)
    return pl.pallas_call(
        body,
        out_shape=[jax.ShapeDtypeStruct((squares, rows // (2 * squares), LANES), BF16)] * 2,
        in_specs=[smem] * 2 + [whole] * len(operands),
        out_specs=[whole] * 2,
        scratch_shapes=scratch,
        compiler_params=pltpu.CompilerParams(vmem_limit_bytes=28 * 1024 * 1024),
        cost_estimate=pl.CostEstimate(flops=4 * 10**9, bytes_accessed=10**7, transcendentals=0),
    )(flags, place, *operands)


def shards(volume, first_weight, second_weight, cotangent):
    half = lax.axis_index("depth")
    row, col = lax.axis_index("row"), lax.axis_index("col")
    rows, cols = lax.axis_size("row"), lax.axis_size("col")
    inner = [jnp.logical_and(i > 0, i < n - 1).astype(jnp.int32) for i, n in ((row, rows), (col, cols))]
    flags = jnp.stack([half, row % 2, col % 2, *inner])
    whole = pl.BlockSpec(memory_space=pltpu.VMEM)
    smem = pl.BlockSpec(memory_space=pltpu.SMEM)
    small = pltpu.CompilerParams(vmem_limit_bytes=12 * 1024 * 1024)
    planes, high, width = volume.shape
    groups = planes + cotangent.shape[0] // 4
    in_hbm = pl.BlockSpec(memory_space=pltpu.HBM)

    def stay(argument):
        return pltpu.with_memory_space_constraint(argument, pltpu.HBM)

    volume, cotangent, dep = pl.pallas_call(
        bring,
        out_shape=[jax.ShapeDtypeStruct(shape, BF16) for shape in (volume.shape, cotangent.shape, (17, 4, width))],
        in_specs=[smem] + [in_hbm] * 2,
        out_specs=[whole] * 3,
        scratch_shapes=[pltpu.SemaphoreType.DMA((4,))],
        compiler_params=small,
    )(flags, stay(volume), stay(cotangent))
    weights = (first_weight, second_weight.T)
    shapes = [(groups, 4, width)] * 2 + [(groups, high, LANES)] * 2
    shapes += [weight.shape for weight in weights]
    row_b, row_a, side_a, side_b, first_taps, second_taps = pl.pallas_call(
        pack,
        out_shape=[jax.ShapeDtypeStruct(shape, BF16) for shape in shapes],
        in_specs=[smem] + [whole] * 2 + [in_hbm] * 2,
        out_specs=[whole] * len(shapes),
        scratch_shapes=[pltpu.SemaphoreType.DMA((2,))],
        compiler_params=small,
    )(flags, volume, cotangent, *[stay(weight) for weight in weights])

    def to_col(block, kind):
        return lax.ppermute(block, ("row", "col"), pairs_of_lines(rows, cols, kind))

    dep = lax.ppermute(dep, "depth", [(0, 1), (1, 0)])
    row_a = lax.ppermute(row_a, "row", pairs_on_line(rows, 0))
    row_b = lax.ppermute(row_b, ("depth", "row"), pairs_of_lines(2, rows, 1))
    row_a, side_a, side_b = lax.optimization_barrier((row_a, side_a, side_b))
    side_a, side_b = to_col(side_a, 0), to_col(side_b, 1)

    low, top = [jnp.concatenate([dep[n : n + 1] for n in (*range(k, 16, 4), 16)], axis=0) for k in (0, 3)]
    even, ends = row % 2 == 0, jnp.logical_or(row == 0, row == rows - 1)
    edge_a = jnp.where(even, top, low)
    edge_b = jnp.where(ends, 0, jnp.where(even, low, top))
    edge_a = lax.ppermute(edge_a, "row", pairs_on_line(rows, 0))
    edge_b = lax.ppermute(edge_b, ("depth", "row"), pairs_of_lines(2, rows, 1))
    weights = pl.pallas_call(
        bands,
        out_shape=[jax.ShapeDtypeStruct(shape, BF16) for shape in ((1152, 256), (1152, 256), (9, 256, 128))],
        in_specs=[whole] * 2,
        out_specs=[whole] * 3,
        compiler_params=small,
    )(first_taps, second_taps)
    col_a, col_b = pl.pallas_call(
        pack_corners,
        out_shape=[jax.ShapeDtypeStruct((planes + 14, 8, LANES), BF16)] * 2,
        in_specs=[smem] + [whole] * 5,
        out_specs=[whole] * 2,
        compiler_params=small,
    )(flags, dep, row_a, row_b, edge_a, edge_b)
    col_a, col_b, volume = lax.optimization_barrier((col_a, col_b, volume))
    col_a, col_b = to_col(col_a, 0), to_col(col_b, 1)

    spot = lax.axis_index(("depth", "row"))
    squares = lax.axis_size(("depth", "row")) // 2
    where = jnp.stack([spot % 2, spot // 2])
    faces, corners = (dep, row_a, row_b, edge_a, edge_b), (side_a, side_b, col_a, col_b)
    keep, give = local_grads(flags, where, squares, volume, faces, corners, cotangent, weights)

    def to_square(block, n):
        route = [(2 * i + c, 2 * (i ^ n) + c) for i in range(squares) for c in (0, 1)]
        return lax.ppermute(block, ("depth", "row"), route)

    def to_core(block):
        return lax.ppermute(block, ("depth", "row"), [(i, i ^ 1) for i in range(2 * squares)])

    def along_col(block, n):
        return lax.ppermute(block, "col", [(i, i ^ n) for i in range(cols)])

    both = add_up(keep, to_core(give))
    share = add_up(both[0], *[to_square(both[n], n) for n in range(1, squares)])
    share = add_up(share, *[along_col(share, n) for n in range(1, cols)])
    mine = jnp.stack([share] + [to_square(share, n) for n in range(1, squares)])
    other = to_core(mine)
    grads = [jax.ShapeDtypeStruct(shape, F32) for shape in (first_weight.shape, second_weight.shape[::-1])]
    first_grad, second_grad = pl.pallas_call(
        unpack,
        out_shape=grads,
        in_specs=[smem] + [whole] * 2,
        out_specs=[whole] * 2,
        scratch_shapes=[pltpu.VMEM((mine.shape[0] * mine.shape[1] * 2, LANES), F32)],
        compiler_params=small,
    )(where, mine, other)
    return first_grad, second_grad.T


def solution(mesh):
    placed = (P("depth", "row", "col"), P(), P(), P("depth", "row", "col"))
    return jax.shard_map(shards, mesh=mesh, in_specs=placed, out_specs=(P(), P()), check_vma=False)
```

```python
import functools

import jax
import jax.numpy as jnp
from jax import lax
from jax.experimental import pallas as pl
from jax.experimental.pallas import tpu as pltpu
from jax.sharding import PartitionSpec as P

LANES = 128
SECOND_ROWS = 27 * 64
FIRST_BLOCKS = 7
F32 = jnp.float32
BF16 = jnp.bfloat16


def pairs_on_line(count, kind):
    firsts = range(kind, count - 1, 2)
    swapped = [(i, i + 1) for i in firsts] + [(i + 1, i) for i in firsts]
    met = {i for i, j in swapped}
    return swapped + [(i, i) for i in range(count) if i not in met]


def pairs_of_lines(lines, count, kind):
    route = []
    for line in range(lines):
        for i, j in pairs_on_line(count, kind):
            route.append((line * count + i, (line ^ 1 if i == j else line) * count + j))
    return route


def add_up(*terms):
    terms = [term.astype(F32) for term in terms]
    while len(terms) > 1:
        terms = [terms[n] + terms[n + 1] for n in range(0, len(terms), 2)]
    return terms[0].astype(BF16)


def matmul(left, right):
    return lax.dot_general(left, right, (((1,), (0,)), ((), ())), preferred_element_type=F32)


def bring(flag_ref, vol_hbm, cot_hbm, vol_ref, cot_ref, dep_ref, arrived):
    first_plane = flag_ref[0] == 0
    planes = vol_ref.shape[0]
    inner = pl.ds(4, planes - 8)
    copies = [pltpu.make_async_copy(cot_hbm, cot_ref, arrived.at[0])]
    for n, part in enumerate((pl.ds(0, 4), pl.ds(planes - 4, 4), inner)):
        copies.append(pltpu.make_async_copy(vol_hbm.at[part], vol_ref.at[part], arrived.at[1 + n]))
    for copy in copies:
        copy.start()
    for copy in copies[:3]:
        copy.wait()
    dep_ref[16] = cot_ref[0]
    for q in range(4):
        block = jnp.where(first_plane, vol_ref[planes - 4 + q].astype(F32), vol_ref[q].astype(F32))
        for g in range(4):
            dep_ref[4 * q + g] = block[4 * g : 4 * g + 4].astype(BF16)
    copies[3].wait()


def pack(
    flag_ref, vol_ref, cot_ref, first_hbm, second_hbm, row_b_ref, row_a_ref, col_a_ref, col_b_ref,
    first_ref, second_ref, arrived,
):
    row_even, col_even = flag_ref[1] == 0, flag_ref[2] == 0
    row_inner, col_inner = flag_ref[3] != 0, flag_ref[4] != 0
    planes, high, width = vol_ref.shape
    cots = cot_ref.shape[0]
    copies = [
        pltpu.make_async_copy(first_hbm, first_ref, arrived.at[0]),
        pltpu.make_async_copy(second_hbm, second_ref, arrived.at[1]),
    ]
    for copy in copies:
        copy.start()

    cot = cot_ref[...].astype(F32)
    for g in range(cots // 4):
        tops = jnp.concatenate([cot[4 * g + n, :1] for n in range(4)], axis=0)
        row_a_ref[planes + g] = tops.astype(BF16)
        row_b_ref[planes + g] = jnp.where(row_inner, tops, 0.0).astype(BF16)
        side = jnp.concatenate([cot[4 * g + n, :, :LANES] for n in range(4)], axis=0)
        col_a_ref[planes + g] = side.astype(BF16)
        col_b_ref[planes + g] = jnp.where(col_inner, side, 0.0).astype(BF16)

    def plane(d, carry):
        block = vol_ref[d].astype(F32)
        low, top = block[:4], block[high - 4 :]
        row_a_ref[d] = jnp.where(row_even, top, low).astype(BF16)
        row_b_ref[d] = jnp.where(row_inner, jnp.where(row_even, low, top), 0.0).astype(BF16)
        left, right = block[:, :LANES], block[:, width - LANES :]
        col_a_ref[d] = jnp.where(col_even, right, left).astype(BF16)
        col_b_ref[d] = jnp.where(col_inner, jnp.where(col_even, left, right), 0.0).astype(BF16)
        return carry

    lax.fori_loop(0, planes, plane, 0, unroll=2)
    for copy in copies:
        copy.wait()


def pack_corners(flag_ref, dep_ref, row_a_ref, row_b_ref, edge_a_ref, edge_b_ref, col_a_ref, col_b_ref):
    row_even, col_even, col_inner = flag_ref[1] == 0, flag_ref[2] == 0, flag_ref[4] != 0
    width = dep_ref.shape[2]
    groups = row_a_ref.shape[0]
    planes = (groups * 16) // 17
    faces = (slice(0, LANES), slice(width - LANES, width))

    def store(n, left, right):
        col_a_ref[n] = jnp.where(col_even, right, left).astype(BF16)
        col_b_ref[n] = jnp.where(col_inner, jnp.where(col_even, left, right), 0.0).astype(BF16)

    def lower_upper(a_ref, b_ref, source, target):
        values = []
        for lanes in faces:
            a, b = a_ref[source, :, lanes].astype(F32), b_ref[source, :, lanes].astype(F32)
            values.append(jnp.concatenate([jnp.where(row_even, b, a), jnp.where(row_even, a, b)], axis=0))
        store(target, *values)

    def plane(d, carry):
        lower_upper(row_a_ref, row_b_ref, d, d)
        return carry

    lax.fori_loop(0, planes, plane, 0)
    for q in range(4):
        lower_upper(edge_a_ref, edge_b_ref, q, planes + q)
        for n in range(2):
            units = range(4 * q + 2 * n, 4 * q + 2 * n + 2)
            store(
                planes + 4 + 2 * q + n,
                *[jnp.concatenate([dep_ref[u, :, lanes].astype(F32) for u in units], axis=0) for lanes in faces],
            )
    lanes = faces[0]
    tops = [
        jnp.where(row_even, row_a_ref[g, :, lanes].astype(F32), row_b_ref[g, :, lanes].astype(F32))
        for g in range(planes, groups)
    ]
    corner = jnp.where(row_even, edge_a_ref[4, :, lanes].astype(F32), edge_b_ref[4, :, lanes].astype(F32))
    own = dep_ref[16, :, lanes].astype(F32)
    for n, values in enumerate((jnp.concatenate(tops, axis=0), jnp.concatenate([own, corner], axis=0))):
        col_a_ref[planes + 12 + n] = values.astype(BF16)
        col_b_ref[planes + 12 + n] = jnp.where(col_inner, values, 0.0).astype(BF16)


def bands(first_ref, second_ref, w1_ref, w2_ref, w2b_ref):
    out_chan = first_ref.shape[0]
    first = first_ref[...].astype(F32)
    blank = jnp.zeros((out_chan, LANES), F32)
    for tap in range(9):
        rows = slice(tap * LANES, (tap + 1) * LANES)
        taps = first[:, tap * 96 : (tap + 1) * 96]
        main_even = jnp.concatenate([taps[:, 32:], blank[:, :64]], axis=1)
        main_odd = jnp.concatenate([blank[:, :32], taps], axis=1)
        prev_even = jnp.concatenate([blank[:, :96], taps[:, :32]], axis=1)
        w1_ref[rows] = jnp.concatenate([main_even, main_odd, prev_even, blank], axis=0).T.astype(BF16)
        main = second_ref[tap * 192 + 64 : (tap + 1) * 192, :]
        prev = jnp.concatenate([jnp.zeros((64, LANES), BF16), second_ref[tap * 192 : tap * 192 + 64, :]], axis=0)
        both = jnp.concatenate([main, prev], axis=1)
        w2_ref[rows] = both
        w2b_ref[tap] = both.astype(F32).T.astype(BF16)


def split_rows(stage, tiles, index, blocks):
    for m in blocks:
        rows = [stage[m, pl.ds(4 + s, 8, stride=4), :] for s in range(-1, 4)]
        for b in range(3):
            tiles[b, index, m] = jnp.concatenate([rows[b], rows[b + 2]], axis=0).astype(BF16)


def clear_stage(stage):
    stage[:, :, 0:8, :] = jnp.zeros(stage.shape[:2] + (8, LANES), F32)
    stage[:, :, 24:40, :] = jnp.zeros(stage.shape[:2] + (16, LANES), F32)


def ahead(even, a, b):
    return jnp.where(even, a.astype(F32), b.astype(F32))


def behind(even, a, b):
    return jnp.where(even, b.astype(F32), a.astype(F32))


def own_blocks(
    flag_ref, vol_ref, dep_ref, row_a_ref, row_b_ref, edge_a_ref, edge_b_ref, w1_ref, tiles, parts, stage
):
    first_plane, row_even = flag_ref[0] == 0, flag_ref[1] == 0
    planes = vol_ref.shape[0]
    blocks = vol_ref.shape[2] // LANES
    clear_stage(stage)

    def place(n, target, own, a, b, keep):
        def kept(values):
            return values if keep is None else jnp.where(keep, values, 0.0)

        for m in range(blocks):
            lanes = slice(m * LANES, (m + 1) * LANES)
            stage[n, m, 8:24, :] = kept(own(lanes).astype(F32))
            stage[n, m, 4:8, :] = kept(behind(row_even, a(lanes), b(lanes)))
            stage[n, m, 24:28, :] = kept(ahead(row_even, a(lanes), b(lanes)))
        split_rows(stage.at[n], tiles, target, range(blocks))

    def place_own(pair, carry):
        for n in range(2):
            d = 2 * pair + n
            place(
                n, d + 3, lambda lanes: vol_ref[d, :, lanes],
                lambda lanes: row_a_ref[d, :, lanes], lambda lanes: row_b_ref[d, :, lanes], None,
            )
        return carry

    def place_halo(target, q, keep):
        place(
            target % 2, target,
            lambda lanes: jnp.concatenate([dep_ref[4 * q + g, :, lanes].astype(F32) for g in range(4)], axis=0),
            lambda lanes: edge_a_ref[q, :, lanes], lambda lanes: edge_b_ref[q, :, lanes], keep,
        )

    lax.fori_loop(0, planes // 2, place_own, 0)
    for q in range(3):
        place_halo(q, q + 1, jnp.logical_not(first_plane))
    for q in range(4):
        place_halo(planes + 3 + q, q, first_plane)
    tiles[:, planes + 7 :] = jnp.zeros((3, 2, blocks, 16, LANES), BF16)

    group = 5

    def product(step, carry):
        taps = []
        for a in range(3):
            for b in range(3):
                start = 2 * group * step + a
                found = [tiles[b, start + 2 * n].reshape(blocks * 16, LANES) for n in range(group)]
                taps.append(jnp.concatenate(found, axis=0))
        found = matmul(jnp.concatenate(taps, axis=1), w1_ref[...])
        parts[pl.ds(group * step, group)] = found.reshape(group, blocks, 16, 2 * LANES)
        return carry

    lax.fori_loop(0, parts.shape[0] // group, product, 0)


def own_rows():
    sublane = lax.broadcasted_iota(jnp.int32, (1, 16, 1), 1) % 8
    return jnp.logical_and(sublane >= 1, sublane <= 4)


def with_next(blocks, values, needed):
    values = values.T
    edge = jnp.zeros((LANES, values.shape[1] // blocks), values.dtype)
    here = jnp.concatenate([edge, values], axis=1)
    after = jnp.concatenate([values, edge], axis=1)[:needed]
    return jnp.concatenate([here, after], axis=0)


def hand_out(place_ref, out_ref, keep_ref, give_ref):
    core, square = place_ref[0], place_ref[1]
    squares, size = keep_ref.shape[0], keep_ref.shape[1]
    for n in range(squares):
        for ref, half in ((keep_ref, core), (give_ref, 1 - core)):
            start = pl.multiple_of((half * squares + (square ^ n)) * size, 8)
            ref[n] = out_ref[pl.ds(start, size), :].astype(BF16)


def body(
    flag_ref, place_ref, tiles, parts, dep_ref, row_a_ref, row_b_ref, edge_a_ref, edge_b_ref,
    side_a_ref, side_b_ref, col_a_ref, col_b_ref, cot_ref, w1_ref, w2_ref,
    keep_ref, give_ref, tail_ref, rim_tiles, slopes, deltas, shifted,
    out_ref, stage, rim_parts, hid, pairs, ups,
):
    first_plane, row_even, col_even = flag_ref[0] == 0, flag_ref[1] == 0, flag_ref[2] == 0
    planes = tiles.shape[1] - 9
    blocks = tiles.shape[2]
    half_planes = planes // 4
    hidden_planes = planes // 2 + 3

    clear_stage(stage)

    def place(n, target, source, side_a, side_b, keep):
        for m, choose in ((0, behind), (1, ahead)):
            corners = choose(col_even, col_a_ref[source], col_b_ref[source])
            own = choose(col_even, side_a, side_b)
            if keep is not None:
                corners, own = jnp.where(keep, corners, 0.0), jnp.where(keep, own, 0.0)
            stage[n, m, 4:8, :] = corners[:4]
            stage[n, m, 8:24, :] = own
            stage[n, m, 24:28, :] = corners[4:]
        split_rows(stage.at[n], rim_tiles, target, range(2))

    def place_own(group, carry):
        for n in range(4):
            d = 4 * group + n
            place(n, d + 3, d, side_a_ref[d], side_b_ref[d], None)
        return carry

    def place_halo(target, q, keep):
        start = planes + 4 + 2 * q
        side_a = jnp.concatenate([col_a_ref[start].astype(F32), col_a_ref[start + 1].astype(F32)], axis=0)
        side_b = jnp.concatenate([col_b_ref[start].astype(F32), col_b_ref[start + 1].astype(F32)], axis=0)
        place(target % 4, target, planes + q, side_a, side_b, keep)

    lax.fori_loop(0, planes // 4, place_own, 0)
    for q in range(3):
        place_halo(q, q + 1, jnp.logical_not(first_plane))
    for q in range(4):
        place_halo(planes + 3 + q, q, first_plane)

    taps = []
    for a in range(3):
        for b in range(3):
            rows = [rim_tiles[b, 2 * i + a].reshape(32, LANES) for i in range(hidden_planes)]
            taps.append(jnp.concatenate(rows, axis=0))
    found = matmul(jnp.concatenate(taps, axis=1), w1_ref[...])
    rim_parts[...] = found.reshape(hidden_planes, 2, 16, 2 * LANES)

    def conv_one(i, carry):
        main, prev = parts[i, :, :, :LANES], parts[i, :, :, LANES:]
        rim, rim_prev = rim_parts[i, :, :, :LANES], rim_parts[i, 0:1, :, LANES:]
        blank = jnp.zeros((1, 16, LANES), F32)
        pre = jnp.concatenate([rim[:1], main, rim[1:]], axis=0) + jnp.concatenate([blank, rim_prev, prev], axis=0)
        square = pre * pre + 1.0
        inverse = lax.rsqrt(square)
        slopes[i] = 0.6 + 0.4 * (pre * inverse)
        hidden = (0.6 * pre + 0.4 * (square * inverse - 1.0)).astype(BF16).astype(F32)
        odd = hidden[:, 8:, :]
        hid[0, i] = pltpu.roll(odd, 1, 1)
        hid[1, i] = hidden[:, :8, :]
        hid[2, i] = odd
        return carry

    lax.fori_loop(0, hidden_planes, conv_one, 0)

    wide = (blocks + 2) * 16

    def pair(i, carry):
        for b in range(3):
            pairs[b, i] = jnp.concatenate([hid[b, i], hid[b, i + half_planes]], axis=1).astype(BF16)
        return carry

    lax.fori_loop(0, half_planes + 3, pair, 0)

    ups[...] = jnp.zeros_like(ups)
    for k in range(blocks):
        lanes = slice(k * LANES, (k + 1) * LANES)
        ups[0:half_planes, k, 1:5, :] = cot_ref[:, :, lanes].astype(F32)
        ups[half_planes, k, 1:5, :] = jnp.where(first_plane, dep_ref[16, :, lanes].astype(F32), 0.0)
        for g in range(half_planes // 4):
            tops = ahead(row_even, row_a_ref[planes + g, :, lanes], row_b_ref[planes + g, :, lanes])
            for n in range(4):
                ups[4 * g + n, k, 5:6, :] = tops[n : n + 1]
        corner = ahead(row_even, edge_a_ref[4, :, lanes], edge_b_ref[4, :, lanes])[:1]
        ups[half_planes, k, 5:6, :] = jnp.where(first_plane, corner, 0.0)
    for g in range(half_planes // 4):
        side = ahead(col_even, side_a_ref[planes + g], side_b_ref[planes + g])
        for n in range(4):
            ups[4 * g + n, blocks, 1:5, :] = side[4 * n : 4 * n + 4]
    tops = ahead(col_even, col_a_ref[planes + 12], col_b_ref[planes + 12])
    for n in range(half_planes):
        ups[n, blocks, 5:6, :] = tops[n : n + 1]
    beyond = jnp.where(first_plane, ahead(col_even, col_a_ref[planes + 13], col_b_ref[planes + 13]), 0.0)
    ups[half_planes, blocks, 1:6, :] = beyond[:5]

    quarter = half_planes // 2

    taps = []
    for a in range(3):
        for b in range(3):
            rows = [pairs[b, 2 * t + a].reshape(wide, LANES) for t in range(quarter + 1)]
            taps.append(jnp.concatenate(rows, axis=0))
    found = matmul(jnp.concatenate(taps, axis=1), w2_ref[...]).reshape(quarter + 1, blocks + 2, 16, 2 * LANES)
    for t in range(quarter + 1):
        pre = found[t, 1:, :, :LANES] + found[t, :-1, :, LANES:]
        slope = 0.6 + 0.4 * (pre * lax.rsqrt(pre * pre + 1.0))
        upstream = jnp.concatenate([ups[t], ups[t + quarter]], axis=1)
        delta = (upstream * slope).astype(BF16).astype(F32)
        moved = jnp.concatenate([pltpu.roll(delta[:, :8], 7, 1), pltpu.roll(delta[:, 8:], 7, 1)], axis=1)
        deltas[t] = delta
        shifted[t] = moved.astype(BF16)

    own_delta = [jnp.where(own_rows(), deltas[t, 0:blocks], 0.0) for t in range(quarter)]
    left = with_next(blocks, jnp.stack(own_delta, axis=1).reshape(blocks * quarter * 16, LANES), LANES).astype(BF16)

    def second_taps(tap):
        a, b = tap // 3, tap % 3
        found = [pairs[b, 2 * t + a, 0 : blocks + 1] for t in range(quarter)]
        return jnp.stack(found, axis=1).reshape((blocks + 1) * quarter * 16, LANES)

    for tap in range(0, 9, 2):
        right = [second_taps(x) for x in range(tap, min(tap + 2, 9))]
        found = matmul(left, jnp.concatenate(right, axis=1))
        for n in range(len(right)):
            row = (tap + n) * 192
            lanes = slice(n * LANES, (n + 1) * LANES)
            out_ref[row : row + 64, :] = found[LANES:, lanes].T[64:]
            out_ref[row + 64 : row + 192, :] = found[:LANES, lanes].T

    cut = tail_ref.shape[0]
    tail_ref[...] = out_ref[out_ref.shape[0] - cut :, :]
    hand_out(place_ref, out_ref, keep_ref, give_ref)


def transposed(
    place_ref, tiles, rim_tiles, slopes, deltas, shifted, w2b_ref, tail_ref, keep_ref, give_ref, out_ref
):
    planes, blocks = tiles.shape[1] - 9, tiles.shape[2]
    quarter = planes // 8

    def pack(values):
        both = jnp.concatenate([values[:, :-1], values[:, 1:]], axis=3)
        return both.reshape(quarter * blocks * 16, 2 * LANES)

    plain = deltas[...].astype(BF16)
    moved = shifted[...]
    here, after = pack(plain[:-1]), pack(plain[1:])
    here_up, after_up = pack(moved[:-1]), pack(moved[1:])

    def back(terms):
        joined = jnp.concatenate([values for values, a, b in terms], axis=1)
        weights = jnp.concatenate([w2b_ref[3 * a + b] for values, a, b in terms], axis=0)
        return matmul(joined, weights).reshape(quarter, blocks, 16, LANES)

    rows = [
        [back([(here, 1, 1)]), back([(here_up, 1, 0), (here, 1, 2)])],
        [
            back([(after, 0, 1), (here, 2, 1)]),
            back([(after_up, 0, 0), (after, 0, 2), (here_up, 2, 0), (here, 2, 2)]),
        ],
    ]
    own_list = []
    for i in range(planes // 2):
        t, parity = i // 2, i % 2
        half = slice(0, 8) if t < quarter else slice(8, 16)
        back_one = jnp.concatenate([rows[parity][p][t % quarter, :, half, :] for p in (0, 1)], axis=1)
        delta = back_one * slopes[i + 1, 1 : blocks + 1]
        own_list.append(jnp.where(own_rows(), delta, 0.0).astype(BF16))
    left_one = with_next(blocks, jnp.stack(own_list, axis=1).reshape(blocks * (planes // 2) * 16, LANES), 64)

    def first_taps(tap):
        a, b = tap // 3, tap % 3
        found = []
        for m in range(blocks + 1):
            for i in range(planes // 2):
                index = 2 * (i + 1) + a
                found.append(rim_tiles[b, index, 0] if m == 0 else tiles[b, index, m - 1])
        return jnp.concatenate(found, axis=0)

    grads = []
    for tap in range(0, 9, 2):
        right = [first_taps(x) for x in range(tap, min(tap + 2, 9))]
        found = matmul(left_one, jnp.concatenate(right, axis=1))
        for n in range(len(right)):
            main = found[:LANES, n * LANES : (n + 1) * LANES]
            prev = found[LANES:, n * LANES : (n + 1) * LANES]
            even = jnp.concatenate([prev[:, 96:], main[:64, :64]], axis=1)
            grads.append(even + main[64:, 32:])
    grads.append(jnp.zeros((64, FIRST_BLOCKS * LANES - 9 * 96), F32))
    first = jnp.concatenate(grads, axis=1)
    start = tail_ref.shape[0]
    out_ref[:start, :] = tail_ref[...]
    for n in range(FIRST_BLOCKS):
        out_ref[start + 64 * n : start + 64 * (n + 1), :] = first[:, n * LANES : (n + 1) * LANES]
    used = start + 64 * FIRST_BLOCKS
    if out_ref.shape[0] > used:
        out_ref[used:, :] = jnp.zeros((out_ref.shape[0] - used, LANES), F32)
    hand_out(place_ref, out_ref, keep_ref, give_ref)


def unpack(place_ref, keep_ref, got_ref, g1_ref, g2_ref, sums, share):
    core, square = place_ref[0], place_ref[1]
    squares, size = keep_ref.shape[0], keep_ref.shape[1]
    for n in range(squares):
        for ref, half in ((keep_ref, core), (got_ref, 1 - core)):
            number = half * squares + (square ^ n)
            values = ref[n].astype(F32)
            sums[pl.ds(pl.multiple_of(number * share, 8), share), :] = values[:share]
            start = pl.multiple_of(2 * squares * share + number * (size - share), 8)
            sums[pl.ds(start, size - share), :] = values[share:]
    first = [sums[SECOND_ROWS + 64 * n : SECOND_ROWS + 64 * (n + 1), :] for n in range(FIRST_BLOCKS)]
    g1_ref[...] = jnp.concatenate(first, axis=1)[:, : g1_ref.shape[1]]
    g2_ref[...] = sums[:SECOND_ROWS, :]


def local_grads(flags, place, squares, volume, faces, corners, cotangent, weights):
    planes = volume.shape[0]
    blocks = volume.shape[2] // LANES
    hidden_planes = planes // 2 + 3
    out_planes = planes // 4
    whole = pl.BlockSpec(memory_space=pltpu.VMEM)
    smem = pl.BlockSpec(memory_space=pltpu.SMEM)
    dep, row_a, row_b, edge_a, edge_b = faces
    tiles, parts = pl.pallas_call(
        own_blocks,
        out_shape=[
            jax.ShapeDtypeStruct((3, planes + 9, blocks, 16, LANES), BF16),
            jax.ShapeDtypeStruct((hidden_planes + 1, blocks, 16, 2 * LANES), F32),
        ],
        in_specs=[smem] + [whole] * 7,
        out_specs=[whole] * 2,
        scratch_shapes=[pltpu.VMEM((2, blocks, 40, LANES), F32)],
        compiler_params=pltpu.CompilerParams(vmem_limit_bytes=16 * 1024 * 1024),
        cost_estimate=pl.CostEstimate(flops=2 * 10**9, bytes_accessed=10**7, transcendentals=0),
    )(flags, volume, *faces, weights[0])
    unit = 2 * squares * 16
    early = SECOND_ROWS // unit * unit
    late = -(-(SECOND_ROWS - early + 64 * FIRST_BLOCKS) // unit) * unit

    def shares(rows):
        return [jax.ShapeDtypeStruct((squares, rows // (2 * squares), LANES), BF16)] * 2

    operands = (tiles, parts, *faces, *corners, cotangent, *weights[:2])
    keep, give, tail, rim_tiles, slopes, deltas, shifted = pl.pallas_call(
        body,
        out_shape=shares(early)
        + [
            jax.ShapeDtypeStruct((SECOND_ROWS - early, LANES), F32),
            jax.ShapeDtypeStruct((3, planes + 7, 2, 16, LANES), BF16),
            jax.ShapeDtypeStruct((hidden_planes, blocks + 2, 16, LANES), F32),
            jax.ShapeDtypeStruct((out_planes // 2 + 1, blocks + 1, 16, LANES), F32),
            jax.ShapeDtypeStruct((out_planes // 2 + 1, blocks + 1, 16, LANES), BF16),
        ],
        in_specs=[smem] * 2 + [whole] * len(operands),
        out_specs=[whole] * 7,
        scratch_shapes=[
            pltpu.VMEM((SECOND_ROWS, LANES), F32),
            pltpu.VMEM((4, 2, 40, LANES), F32),
            pltpu.VMEM((hidden_planes, 2, 16, 2 * LANES), F32),
            pltpu.VMEM((3, hidden_planes, blocks + 2, 8, LANES), F32),
            pltpu.VMEM((3, out_planes + 3, blocks + 2, 16, LANES), BF16),
            pltpu.VMEM((out_planes + 1, blocks + 1, 8, LANES), F32),
        ],
        compiler_params=pltpu.CompilerParams(vmem_limit_bytes=24 * 1024 * 1024),
        cost_estimate=pl.CostEstimate(flops=4 * 10**9, bytes_accessed=10**7, transcendentals=0),
    )(flags, place, *operands)
    rest = (tiles, rim_tiles, slopes, deltas, shifted, weights[2], tail)
    return keep, give, rest, shares(late)


def late_grads(place, rest, out_shape):
    whole = pl.BlockSpec(memory_space=pltpu.VMEM)
    squares, size = out_shape[0].shape[0], out_shape[0].shape[1]
    return pl.pallas_call(
        transposed,
        out_shape=out_shape,
        in_specs=[pl.BlockSpec(memory_space=pltpu.SMEM)] + [whole] * len(rest),
        out_specs=[whole] * 2,
        scratch_shapes=[pltpu.VMEM((2 * squares * size, LANES), F32)],
        compiler_params=pltpu.CompilerParams(vmem_limit_bytes=24 * 1024 * 1024),
        cost_estimate=pl.CostEstimate(flops=2 * 10**9, bytes_accessed=10**7, transcendentals=0),
    )(place, *rest)


def shards(volume, first_weight, second_weight, cotangent):
    half = lax.axis_index("depth")
    row, col = lax.axis_index("row"), lax.axis_index("col")
    rows, cols = lax.axis_size("row"), lax.axis_size("col")
    inner = [jnp.logical_and(i > 0, i < n - 1).astype(jnp.int32) for i, n in ((row, rows), (col, cols))]
    flags = jnp.stack([half, row % 2, col % 2, *inner])
    whole = pl.BlockSpec(memory_space=pltpu.VMEM)
    smem = pl.BlockSpec(memory_space=pltpu.SMEM)
    small = pltpu.CompilerParams(vmem_limit_bytes=12 * 1024 * 1024)
    planes, high, width = volume.shape
    groups = planes + cotangent.shape[0] // 4
    in_hbm = pl.BlockSpec(memory_space=pltpu.HBM)

    def stay(argument):
        return pltpu.with_memory_space_constraint(argument, pltpu.HBM)

    volume, cotangent, dep = pl.pallas_call(
        bring,
        out_shape=[jax.ShapeDtypeStruct(shape, BF16) for shape in (volume.shape, cotangent.shape, (17, 4, width))],
        in_specs=[smem] + [in_hbm] * 2,
        out_specs=[whole] * 3,
        scratch_shapes=[pltpu.SemaphoreType.DMA((4,))],
        compiler_params=small,
    )(flags, stay(volume), stay(cotangent))
    weights = (first_weight, second_weight.T)
    shapes = [(groups, 4, width)] * 2 + [(groups, high, LANES)] * 2
    shapes += [weight.shape for weight in weights]
    row_b, row_a, side_a, side_b, first_taps, second_taps = pl.pallas_call(
        pack,
        out_shape=[jax.ShapeDtypeStruct(shape, BF16) for shape in shapes],
        in_specs=[smem] + [whole] * 2 + [in_hbm] * 2,
        out_specs=[whole] * len(shapes),
        scratch_shapes=[pltpu.SemaphoreType.DMA((2,))],
        compiler_params=small,
    )(flags, volume, cotangent, *[stay(weight) for weight in weights])

    def to_col(block, kind):
        return lax.ppermute(block, ("row", "col"), pairs_of_lines(rows, cols, kind))

    dep = lax.ppermute(dep, "depth", [(0, 1), (1, 0)])
    row_a = lax.ppermute(row_a, "row", pairs_on_line(rows, 0))
    row_b = lax.ppermute(row_b, ("depth", "row"), pairs_of_lines(2, rows, 1))
    row_a, side_a, side_b = lax.optimization_barrier((row_a, side_a, side_b))
    side_a, side_b = to_col(side_a, 0), to_col(side_b, 1)

    low, top = [jnp.concatenate([dep[n : n + 1] for n in (*range(k, 16, 4), 16)], axis=0) for k in (0, 3)]
    even, ends = row % 2 == 0, jnp.logical_or(row == 0, row == rows - 1)
    edge_a = jnp.where(even, top, low)
    edge_b = jnp.where(ends, 0, jnp.where(even, low, top))
    edge_a = lax.ppermute(edge_a, "row", pairs_on_line(rows, 0))
    edge_b = lax.ppermute(edge_b, ("depth", "row"), pairs_of_lines(2, rows, 1))
    weights = pl.pallas_call(
        bands,
        out_shape=[jax.ShapeDtypeStruct(shape, BF16) for shape in ((1152, 256), (1152, 256), (9, 256, 128))],
        in_specs=[whole] * 2,
        out_specs=[whole] * 3,
        compiler_params=small,
    )(first_taps, second_taps)
    col_a, col_b = pl.pallas_call(
        pack_corners,
        out_shape=[jax.ShapeDtypeStruct((planes + 14, 8, LANES), BF16)] * 2,
        in_specs=[smem] + [whole] * 5,
        out_specs=[whole] * 2,
        compiler_params=small,
    )(flags, dep, row_a, row_b, edge_a, edge_b)
    col_a, col_b, volume = lax.optimization_barrier((col_a, col_b, volume))
    col_a, col_b = to_col(col_a, 0), to_col(col_b, 1)

    spot = lax.axis_index(("depth", "row"))
    squares = lax.axis_size(("depth", "row")) // 2
    where = jnp.stack([spot % 2, spot // 2])
    def to_square(block, n):
        route = [(2 * i + c, 2 * (i ^ n) + c) for i in range(squares) for c in (0, 1)]
        return lax.ppermute(block, ("depth", "row"), route)

    def to_core(block):
        return lax.ppermute(block, ("depth", "row"), [(i, i ^ 1) for i in range(2 * squares)])

    def along_col(block, n):
        return lax.ppermute(block, "col", [(i, i ^ n) for i in range(cols)])

    faces, corners = (dep, row_a, row_b, edge_a, edge_b), (side_a, side_b, col_a, col_b)
    keep, give, rest, late_shape = local_grads(flags, where, squares, volume, faces, corners, cotangent, weights)
    got, rest = lax.optimization_barrier((to_core(give), rest))
    both = add_up(keep, got)
    near = [to_square(both[n], n) for n in range(1, squares)]
    keep, give = late_grads(where, rest, late_shape)
    near, give = lax.optimization_barrier((near, give))
    share = add_up(both[0], *near)
    far = [along_col(share, n) for n in range(1, cols)]
    both = add_up(keep, to_core(give))
    late = add_up(both[0], *[to_square(both[n], n) for n in range(1, squares)])
    far, late = lax.optimization_barrier((far, late))
    found = [add_up(share, *far), add_up(late, *[along_col(late, n) for n in range(1, cols)])]
    share = jnp.concatenate(found, axis=0)
    mine = jnp.stack([share] + [to_square(share, n) for n in range(1, squares)])
    other = to_core(mine)
    grads = [jax.ShapeDtypeStruct(shape, F32) for shape in (first_weight.shape, second_weight.shape[::-1])]
    first_grad, second_grad = pl.pallas_call(
        functools.partial(unpack, share=found[0].shape[0]),
        out_shape=grads,
        in_specs=[smem] + [whole] * 2,
        out_specs=[whole] * 2,
        scratch_shapes=[pltpu.VMEM((mine.shape[0] * mine.shape[1] * 2, LANES), F32)],
        compiler_params=small,
    )(where, mine, other)
    return first_grad, second_grad.T


def solution(mesh):
    placed = (P("depth", "row", "col"), P(), P(), P("depth", "row", "col"))
    return jax.shard_map(shards, mesh=mesh, in_specs=placed, out_specs=(P(), P()), check_vma=False)
```

```python
import jax
import jax.numpy as jnp
from jax import lax
from jax.experimental import pallas as pl
from jax.experimental.pallas import tpu as pltpu
from jax.sharding import PartitionSpec as P

LANES = 128
SECOND_ROWS = 27 * 64
FIRST_BLOCKS = 7
F32 = jnp.float32
BF16 = jnp.bfloat16


def pairs_on_line(count, kind):
    firsts = range(kind, count - 1, 2)
    swapped = [(i, i + 1) for i in firsts] + [(i + 1, i) for i in firsts]
    met = {i for i, j in swapped}
    return swapped + [(i, i) for i in range(count) if i not in met]


def pairs_of_lines(lines, count, kind):
    route = []
    for line in range(lines):
        for i, j in pairs_on_line(count, kind):
            route.append((line * count + i, (line ^ 1 if i == j else line) * count + j))
    return route


def add_up(*terms):
    terms = [term.astype(F32) for term in terms]
    while len(terms) > 1:
        terms = [terms[n] + terms[n + 1] for n in range(0, len(terms), 2)]
    return terms[0].astype(BF16)


def matmul(left, right):
    return lax.dot_general(left, right, (((1,), (0,)), ((), ())), preferred_element_type=F32)


def bring(flag_ref, vol_hbm, cot_hbm, vol_ref, cot_ref, dep_ref, arrived):
    first_plane = flag_ref[0] == 0
    planes = vol_ref.shape[0]
    inner = pl.ds(4, planes - 8)
    copies = [pltpu.make_async_copy(cot_hbm, cot_ref, arrived.at[0])]
    for n, part in enumerate((pl.ds(0, 4), pl.ds(planes - 4, 4), inner)):
        copies.append(pltpu.make_async_copy(vol_hbm.at[part], vol_ref.at[part], arrived.at[1 + n]))
    for copy in copies:
        copy.start()
    for copy in copies[:3]:
        copy.wait()
    dep_ref[16] = cot_ref[0]
    for q in range(4):
        block = jnp.where(first_plane, vol_ref[planes - 4 + q].astype(F32), vol_ref[q].astype(F32))
        for g in range(4):
            dep_ref[4 * q + g] = block[4 * g : 4 * g + 4].astype(BF16)
    copies[3].wait()


def pack(
    flag_ref, vol_ref, cot_ref, first_hbm, second_hbm, row_b_ref, row_a_ref, col_a_ref, col_b_ref,
    first_ref, second_ref, arrived,
):
    row_even, col_even = flag_ref[1] == 0, flag_ref[2] == 0
    row_inner, col_inner = flag_ref[3] != 0, flag_ref[4] != 0
    planes, high, width = vol_ref.shape
    cots = cot_ref.shape[0]
    copies = [
        pltpu.make_async_copy(first_hbm, first_ref, arrived.at[0]),
        pltpu.make_async_copy(second_hbm, second_ref, arrived.at[1]),
    ]
    for copy in copies:
        copy.start()

    cot = cot_ref[...].astype(F32)
    for g in range(cots // 4):
        tops = jnp.concatenate([cot[4 * g + n, :1] for n in range(4)], axis=0)
        row_a_ref[planes + g] = tops.astype(BF16)
        row_b_ref[planes + g] = jnp.where(row_inner, tops, 0.0).astype(BF16)
        side = jnp.concatenate([cot[4 * g + n, :, :LANES] for n in range(4)], axis=0)
        col_a_ref[planes + g] = side.astype(BF16)
        col_b_ref[planes + g] = jnp.where(col_inner, side, 0.0).astype(BF16)

    def plane(d, carry):
        block = vol_ref[d].astype(F32)
        low, top = block[:4], block[high - 4 :]
        row_a_ref[d] = jnp.where(row_even, top, low).astype(BF16)
        row_b_ref[d] = jnp.where(row_inner, jnp.where(row_even, low, top), 0.0).astype(BF16)
        left, right = block[:, :LANES], block[:, width - LANES :]
        col_a_ref[d] = jnp.where(col_even, right, left).astype(BF16)
        col_b_ref[d] = jnp.where(col_inner, jnp.where(col_even, left, right), 0.0).astype(BF16)
        return carry

    lax.fori_loop(0, planes, plane, 0, unroll=2)
    for copy in copies:
        copy.wait()


def pack_corners(flag_ref, dep_ref, row_a_ref, row_b_ref, edge_a_ref, edge_b_ref, col_a_ref, col_b_ref):
    row_even, col_even, col_inner = flag_ref[1] == 0, flag_ref[2] == 0, flag_ref[4] != 0
    width = dep_ref.shape[2]
    groups = row_a_ref.shape[0]
    planes = (groups * 16) // 17
    faces = (slice(0, LANES), slice(width - LANES, width))

    def store(n, left, right):
        col_a_ref[n] = jnp.where(col_even, right, left).astype(BF16)
        col_b_ref[n] = jnp.where(col_inner, jnp.where(col_even, left, right), 0.0).astype(BF16)

    def lower_upper(a_ref, b_ref, source, target):
        values = []
        for lanes in faces:
            a, b = a_ref[source, :, lanes].astype(F32), b_ref[source, :, lanes].astype(F32)
            values.append(jnp.concatenate([jnp.where(row_even, b, a), jnp.where(row_even, a, b)], axis=0))
        store(target, *values)

    def plane(d, carry):
        lower_upper(row_a_ref, row_b_ref, d, d)
        return carry

    lax.fori_loop(0, planes, plane, 0)
    for q in range(4):
        lower_upper(edge_a_ref, edge_b_ref, q, planes + q)
        for n in range(2):
            units = range(4 * q + 2 * n, 4 * q + 2 * n + 2)
            store(
                planes + 4 + 2 * q + n,
                *[jnp.concatenate([dep_ref[u, :, lanes].astype(F32) for u in units], axis=0) for lanes in faces],
            )
    lanes = faces[0]
    tops = [
        jnp.where(row_even, row_a_ref[g, :, lanes].astype(F32), row_b_ref[g, :, lanes].astype(F32))
        for g in range(planes, groups)
    ]
    corner = jnp.where(row_even, edge_a_ref[4, :, lanes].astype(F32), edge_b_ref[4, :, lanes].astype(F32))
    own = dep_ref[16, :, lanes].astype(F32)
    for n, values in enumerate((jnp.concatenate(tops, axis=0), jnp.concatenate([own, corner], axis=0))):
        col_a_ref[planes + 12 + n] = values.astype(BF16)
        col_b_ref[planes + 12 + n] = jnp.where(col_inner, values, 0.0).astype(BF16)


def bands(first_ref, second_ref, w1_ref, w2_ref, w2b_ref):
    out_chan = first_ref.shape[0]
    first = first_ref[...].astype(F32)
    blank = jnp.zeros((out_chan, LANES), F32)
    for tap in range(9):
        rows = slice(tap * LANES, (tap + 1) * LANES)
        taps = first[:, tap * 96 : (tap + 1) * 96]
        main_even = jnp.concatenate([taps[:, 32:], blank[:, :64]], axis=1)
        main_odd = jnp.concatenate([blank[:, :32], taps], axis=1)
        prev_even = jnp.concatenate([blank[:, :96], taps[:, :32]], axis=1)
        w1_ref[rows] = jnp.concatenate([main_even, main_odd, prev_even, blank], axis=0).T.astype(BF16)
        main = second_ref[tap * 192 + 64 : (tap + 1) * 192, :]
        prev = jnp.concatenate([jnp.zeros((64, LANES), BF16), second_ref[tap * 192 : tap * 192 + 64, :]], axis=0)
        both = jnp.concatenate([main, prev], axis=1)
        w2_ref[rows] = both
        w2b_ref[tap] = both.astype(F32).T.astype(BF16)


def split_rows(stage, tiles, index, blocks):
    for m in blocks:
        rows = [stage[m, pl.ds(4 + s, 8, stride=4), :] for s in range(-1, 4)]
        for b in range(3):
            tiles[b, index, m] = jnp.concatenate([rows[b], rows[b + 2]], axis=0).astype(BF16)


def clear_stage(stage):
    stage[:, :, 0:8, :] = jnp.zeros(stage.shape[:2] + (8, LANES), F32)
    stage[:, :, 24:40, :] = jnp.zeros(stage.shape[:2] + (16, LANES), F32)


def ahead(even, a, b):
    return jnp.where(even, a.astype(F32), b.astype(F32))


def behind(even, a, b):
    return jnp.where(even, b.astype(F32), a.astype(F32))


def own_blocks(
    flag_ref, vol_ref, dep_ref, row_a_ref, row_b_ref, edge_a_ref, edge_b_ref, w1_ref, tiles, parts, stage
):
    first_plane, row_even = flag_ref[0] == 0, flag_ref[1] == 0
    planes = vol_ref.shape[0]
    blocks = vol_ref.shape[2] // LANES
    clear_stage(stage)

    def place(n, target, own, a, b, keep):
        def kept(values):
            return values if keep is None else jnp.where(keep, values, 0.0)

        for m in range(blocks):
            lanes = slice(m * LANES, (m + 1) * LANES)
            stage[n, m, 8:24, :] = kept(own(lanes).astype(F32))
            stage[n, m, 4:8, :] = kept(behind(row_even, a(lanes), b(lanes)))
            stage[n, m, 24:28, :] = kept(ahead(row_even, a(lanes), b(lanes)))
        split_rows(stage.at[n], tiles, target, range(blocks))

    def place_own(pair, carry):
        for n in range(2):
            d = 2 * pair + n
            place(
                n, d + 3, lambda lanes: vol_ref[d, :, lanes],
                lambda lanes: row_a_ref[d, :, lanes], lambda lanes: row_b_ref[d, :, lanes], None,
            )
        return carry

    def place_halo(target, q, keep):
        place(
            target % 2, target,
            lambda lanes: jnp.concatenate([dep_ref[4 * q + g, :, lanes].astype(F32) for g in range(4)], axis=0),
            lambda lanes: edge_a_ref[q, :, lanes], lambda lanes: edge_b_ref[q, :, lanes], keep,
        )

    lax.fori_loop(0, planes // 2, place_own, 0)
    for q in range(3):
        place_halo(q, q + 1, jnp.logical_not(first_plane))
    for q in range(4):
        place_halo(planes + 3 + q, q, first_plane)
    tiles[:, planes + 7 :] = jnp.zeros((3, 2, blocks, 16, LANES), BF16)

    group = 5

    def product(step, carry):
        taps = []
        for a in range(3):
            for b in range(3):
                start = 2 * group * step + a
                found = [tiles[b, start + 2 * n].reshape(blocks * 16, LANES) for n in range(group)]
                taps.append(jnp.concatenate(found, axis=0))
        found = matmul(jnp.concatenate(taps, axis=1), w1_ref[...])
        parts[pl.ds(group * step, group)] = found.reshape(group, blocks, 16, 2 * LANES)
        return carry

    lax.fori_loop(0, parts.shape[0] // group, product, 0)


def mirrored(number, squares):
    bits = squares.bit_length() - 1
    return sum((number >> n & 1) << (bits - 1 - n) for n in range(bits))


def share_number(place_ref, half, squares, n):
    return half * squares + (place_ref[1] ^ jnp.where(half == 0, mirrored(n, squares), n))


def body(
    flag_ref, place_ref, tiles, parts, dep_ref, row_a_ref, row_b_ref, edge_a_ref, edge_b_ref,
    side_a_ref, side_b_ref, col_a_ref, col_b_ref, cot_ref, w1_ref, w2_ref, w2b_ref, keep_ref, give_ref,
    out_ref, stage, rim_tiles, rim_parts, slopes, hid, pairs, ups, deltas, shifted,
):
    first_plane, row_even, col_even = flag_ref[0] == 0, flag_ref[1] == 0, flag_ref[2] == 0
    planes = tiles.shape[1] - 9
    blocks = tiles.shape[2]
    half_planes = planes // 4
    hidden_planes = planes // 2 + 3

    clear_stage(stage)

    def place(n, target, source, side_a, side_b, keep):
        for m, choose in ((0, behind), (1, ahead)):
            corners = choose(col_even, col_a_ref[source], col_b_ref[source])
            own = choose(col_even, side_a, side_b)
            if keep is not None:
                corners, own = jnp.where(keep, corners, 0.0), jnp.where(keep, own, 0.0)
            stage[n, m, 4:8, :] = corners[:4]
            stage[n, m, 8:24, :] = own
            stage[n, m, 24:28, :] = corners[4:]
        split_rows(stage.at[n], rim_tiles, target, range(2))

    def place_own(group, carry):
        for n in range(4):
            d = 4 * group + n
            place(n, d + 3, d, side_a_ref[d], side_b_ref[d], None)
        return carry

    def place_halo(target, q, keep):
        start = planes + 4 + 2 * q
        side_a = jnp.concatenate([col_a_ref[start].astype(F32), col_a_ref[start + 1].astype(F32)], axis=0)
        side_b = jnp.concatenate([col_b_ref[start].astype(F32), col_b_ref[start + 1].astype(F32)], axis=0)
        place(target % 4, target, planes + q, side_a, side_b, keep)

    lax.fori_loop(0, planes // 4, place_own, 0)
    for q in range(3):
        place_halo(q, q + 1, jnp.logical_not(first_plane))
    for q in range(4):
        place_halo(planes + 3 + q, q, first_plane)

    taps = []
    for a in range(3):
        for b in range(3):
            rows = [rim_tiles[b, 2 * i + a].reshape(32, LANES) for i in range(hidden_planes)]
            taps.append(jnp.concatenate(rows, axis=0))
    found = matmul(jnp.concatenate(taps, axis=1), w1_ref[...])
    rim_parts[...] = found.reshape(hidden_planes, 2, 16, 2 * LANES)

    def conv_one(i, carry):
        main, prev = parts[i, :, :, :LANES], parts[i, :, :, LANES:]
        rim, rim_prev = rim_parts[i, :, :, :LANES], rim_parts[i, 0:1, :, LANES:]
        blank = jnp.zeros((1, 16, LANES), F32)
        pre = jnp.concatenate([rim[:1], main, rim[1:]], axis=0) + jnp.concatenate([blank, rim_prev, prev], axis=0)
        square = pre * pre + 1.0
        inverse = lax.rsqrt(square)
        slopes[i] = 0.6 + 0.4 * (pre * inverse)
        hidden = (0.6 * pre + 0.4 * (square * inverse - 1.0)).astype(BF16).astype(F32)
        odd = hidden[:, 8:, :]
        hid[0, i] = pltpu.roll(odd, 1, 1)
        hid[1, i] = hidden[:, :8, :]
        hid[2, i] = odd
        return carry

    lax.fori_loop(0, hidden_planes, conv_one, 0)

    wide = (blocks + 2) * 16

    def pair(i, carry):
        for b in range(3):
            pairs[b, i] = jnp.concatenate([hid[b, i], hid[b, i + half_planes]], axis=1).astype(BF16)
        return carry

    lax.fori_loop(0, half_planes + 3, pair, 0)

    ups[...] = jnp.zeros_like(ups)
    for k in range(blocks):
        lanes = slice(k * LANES, (k + 1) * LANES)
        ups[0:half_planes, k, 1:5, :] = cot_ref[:, :, lanes].astype(F32)
        ups[half_planes, k, 1:5, :] = jnp.where(first_plane, dep_ref[16, :, lanes].astype(F32), 0.0)
        for g in range(half_planes // 4):
            tops = ahead(row_even, row_a_ref[planes + g, :, lanes], row_b_ref[planes + g, :, lanes])
            for n in range(4):
                ups[4 * g + n, k, 5:6, :] = tops[n : n + 1]
        corner = ahead(row_even, edge_a_ref[4, :, lanes], edge_b_ref[4, :, lanes])[:1]
        ups[half_planes, k, 5:6, :] = jnp.where(first_plane, corner, 0.0)
    for g in range(half_planes // 4):
        side = ahead(col_even, side_a_ref[planes + g], side_b_ref[planes + g])
        for n in range(4):
            ups[4 * g + n, blocks, 1:5, :] = side[4 * n : 4 * n + 4]
    tops = ahead(col_even, col_a_ref[planes + 12], col_b_ref[planes + 12])
    for n in range(half_planes):
        ups[n, blocks, 5:6, :] = tops[n : n + 1]
    beyond = jnp.where(first_plane, ahead(col_even, col_a_ref[planes + 13], col_b_ref[planes + 13]), 0.0)
    ups[half_planes, blocks, 1:6, :] = beyond[:5]

    quarter = half_planes // 2

    taps = []
    for a in range(3):
        for b in range(3):
            rows = [pairs[b, 2 * t + a].reshape(wide, LANES) for t in range(quarter + 1)]
            taps.append(jnp.concatenate(rows, axis=0))
    found = matmul(jnp.concatenate(taps, axis=1), w2_ref[...]).reshape(quarter + 1, blocks + 2, 16, 2 * LANES)
    for t in range(quarter + 1):
        pre = found[t, 1:, :, :LANES] + found[t, :-1, :, LANES:]
        slope = 0.6 + 0.4 * (pre * lax.rsqrt(pre * pre + 1.0))
        upstream = jnp.concatenate([ups[t], ups[t + quarter]], axis=1)
        delta = (upstream * slope).astype(BF16).astype(F32)
        moved = jnp.concatenate([pltpu.roll(delta[:, :8], 7, 1), pltpu.roll(delta[:, 8:], 7, 1)], axis=1)
        deltas[t] = delta
        shifted[t] = moved.astype(BF16)

    sublane = lax.broadcasted_iota(jnp.int32, (1, 1, 16, 1), 2) % 8
    own_rows = jnp.logical_and(sublane >= 1, sublane <= 4)

    def with_next(values, needed):
        values = values.T
        edge = jnp.zeros((LANES, values.shape[1] // blocks), values.dtype)
        here = jnp.concatenate([edge, values], axis=1)
        after = jnp.concatenate([values, edge], axis=1)[:needed]
        return jnp.concatenate([here, after], axis=0)

    own_delta = [jnp.where(own_rows[0], deltas[t, 0:blocks], 0.0) for t in range(quarter)]
    left = with_next(jnp.stack(own_delta, axis=1).reshape(blocks * quarter * 16, LANES), LANES).astype(BF16)

    def second_taps(tap):
        a, b = tap // 3, tap % 3
        found = [pairs[b, 2 * t + a, 0 : blocks + 1] for t in range(quarter)]
        return jnp.stack(found, axis=1).reshape((blocks + 1) * quarter * 16, LANES)

    for tap in range(0, 9, 2):
        right = [second_taps(x) for x in range(tap, min(tap + 2, 9))]
        found = matmul(left, jnp.concatenate(right, axis=1))
        for n in range(len(right)):
            row = (tap + n) * 192
            lanes = slice(n * LANES, (n + 1) * LANES)
            out_ref[row : row + 64, :] = found[LANES:, lanes].T[64:]
            out_ref[row + 64 : row + 192, :] = found[:LANES, lanes].T

    def pack(values):
        both = jnp.concatenate([values[:, :-1], values[:, 1:]], axis=3)
        return both.reshape(quarter * blocks * 16, 2 * LANES)

    plain = deltas[...].astype(BF16)
    moved = shifted[...]
    here, after = pack(plain[:-1]), pack(plain[1:])
    here_up, after_up = pack(moved[:-1]), pack(moved[1:])

    def back(terms):
        joined = jnp.concatenate([values for values, a, b in terms], axis=1)
        weights = jnp.concatenate([w2b_ref[3 * a + b] for values, a, b in terms], axis=0)
        return matmul(joined, weights).reshape(quarter, blocks, 16, LANES)

    rows = [
        [back([(here, 1, 1)]), back([(here_up, 1, 0), (here, 1, 2)])],
        [
            back([(after, 0, 1), (here, 2, 1)]),
            back([(after_up, 0, 0), (after, 0, 2), (here_up, 2, 0), (here, 2, 2)]),
        ],
    ]
    own_list = []
    for i in range(planes // 2):
        t, parity = i // 2, i % 2
        half = slice(0, 8) if t < quarter else slice(8, 16)
        back_one = jnp.concatenate([rows[parity][p][t % quarter, :, half, :] for p in (0, 1)], axis=1)
        delta = back_one * slopes[i + 1, 1 : blocks + 1]
        own_list.append(jnp.where(own_rows[0], delta, 0.0).astype(BF16))
    left_one = with_next(jnp.stack(own_list, axis=1).reshape(blocks * (planes // 2) * 16, LANES), 64)

    def first_taps(tap):
        a, b = tap // 3, tap % 3
        found = []
        for m in range(blocks + 1):
            for i in range(planes // 2):
                index = 2 * (i + 1) + a
                found.append(rim_tiles[b, index, 0] if m == 0 else tiles[b, index, m - 1])
        return jnp.concatenate(found, axis=0)

    grads = []
    for tap in range(0, 9, 2):
        right = [first_taps(x) for x in range(tap, min(tap + 2, 9))]
        found = matmul(left_one, jnp.concatenate(right, axis=1))
        for n in range(len(right)):
            main = found[:LANES, n * LANES : (n + 1) * LANES]
            prev = found[LANES:, n * LANES : (n + 1) * LANES]
            even = jnp.concatenate([prev[:, 96:], main[:64, :64]], axis=1)
            grads.append(even + main[64:, 32:])
    grads.append(jnp.zeros((64, FIRST_BLOCKS * LANES - 9 * 96), F32))
    first = jnp.concatenate(grads, axis=1)
    for n in range(FIRST_BLOCKS):
        row = SECOND_ROWS + 64 * n
        out_ref[row : row + 64, :] = first[:, n * LANES : (n + 1) * LANES]
    used = SECOND_ROWS + 64 * FIRST_BLOCKS
    if out_ref.shape[0] > used:
        out_ref[used:, :] = jnp.zeros((out_ref.shape[0] - used, LANES), F32)

    core, squares, size = place_ref[0], keep_ref.shape[0], keep_ref.shape[1]
    for n in range(squares):
        for ref, half in ((keep_ref, core), (give_ref, 1 - core)):
            start = pl.multiple_of(share_number(place_ref, half, squares, n) * size, 8)
            ref[n] = out_ref[pl.ds(start, size), :].astype(ref.dtype)


def unpack(place_ref, keep_ref, got_ref, g1_ref, g2_ref, sums):
    core, squares, size = place_ref[0], keep_ref.shape[0], keep_ref.shape[1]
    for n in range(squares):
        for ref, half in ((keep_ref, core), (got_ref, 1 - core)):
            start = pl.multiple_of(share_number(place_ref, half, squares, n) * size, 8)
            sums[pl.ds(start, size), :] = ref[n].astype(F32)
    first = [sums[SECOND_ROWS + 64 * n : SECOND_ROWS + 64 * (n + 1), :] for n in range(FIRST_BLOCKS)]
    g1_ref[...] = jnp.concatenate(first, axis=1)[:, : g1_ref.shape[1]]
    g2_ref[...] = sums[:SECOND_ROWS, :]


def local_grads(flags, place, squares, volume, faces, corners, cotangent, weights):
    planes = volume.shape[0]
    blocks = volume.shape[2] // LANES
    hidden_planes = planes // 2 + 3
    out_planes = planes // 4
    unit = 2 * squares * 16
    rows = -(-(SECOND_ROWS + 64 * FIRST_BLOCKS) // unit) * unit
    whole = pl.BlockSpec(memory_space=pltpu.VMEM)
    smem = pl.BlockSpec(memory_space=pltpu.SMEM)
    dep, row_a, row_b, edge_a, edge_b = faces
    tiles, parts = pl.pallas_call(
        own_blocks,
        out_shape=[
            jax.ShapeDtypeStruct((3, planes + 9, blocks, 16, LANES), BF16),
            jax.ShapeDtypeStruct((hidden_planes + 1, blocks, 16, 2 * LANES), F32),
        ],
        in_specs=[smem] + [whole] * 7,
        out_specs=[whole] * 2,
        scratch_shapes=[pltpu.VMEM((2, blocks, 40, LANES), F32)],
        compiler_params=pltpu.CompilerParams(vmem_limit_bytes=16 * 1024 * 1024),
        cost_estimate=pl.CostEstimate(flops=2 * 10**9, bytes_accessed=10**7, transcendentals=0),
    )(flags, volume, *faces, weights[0])
    scratch = [
        pltpu.VMEM((rows, LANES), F32),
        pltpu.VMEM((4, 2, 40, LANES), F32),
        pltpu.VMEM((3, planes + 7, 2, 16, LANES), BF16),
        pltpu.VMEM((hidden_planes, 2, 16, 2 * LANES), F32),
        pltpu.VMEM((hidden_planes, blocks + 2, 16, LANES), F32),
        pltpu.VMEM((3, hidden_planes, blocks + 2, 8, LANES), F32),
        pltpu.VMEM((3, out_planes + 3, blocks + 2, 16, LANES), BF16),
        pltpu.VMEM((out_planes + 1, blocks + 1, 8, LANES), F32),
        pltpu.VMEM((out_planes // 2 + 1, blocks + 1, 16, LANES), F32),
        pltpu.VMEM((out_planes // 2 + 1, blocks + 1, 16, LANES), BF16),
    ]
    operands = (tiles, parts, *faces, *corners, cotangent, *weights)
    return pl.pallas_call(
        body,
        out_shape=[jax.ShapeDtypeStruct((squares, rows // (2 * squares), LANES), dtype) for dtype in (F32, BF16)],
        in_specs=[smem] * 2 + [whole] * len(operands),
        out_specs=[whole] * 2,
        scratch_shapes=scratch,
        compiler_params=pltpu.CompilerParams(vmem_limit_bytes=28 * 1024 * 1024),
        cost_estimate=pl.CostEstimate(flops=4 * 10**9, bytes_accessed=10**7, transcendentals=0),
    )(flags, place, *operands)


def shards(volume, first_weight, second_weight, cotangent):
    half = lax.axis_index("depth")
    row, col = lax.axis_index("row"), lax.axis_index("col")
    rows, cols = lax.axis_size("row"), lax.axis_size("col")
    inner = [jnp.logical_and(i > 0, i < n - 1).astype(jnp.int32) for i, n in ((row, rows), (col, cols))]
    flags = jnp.stack([half, row % 2, col % 2, *inner])
    whole = pl.BlockSpec(memory_space=pltpu.VMEM)
    smem = pl.BlockSpec(memory_space=pltpu.SMEM)
    small = pltpu.CompilerParams(vmem_limit_bytes=12 * 1024 * 1024)
    planes, high, width = volume.shape
    groups = planes + cotangent.shape[0] // 4
    in_hbm = pl.BlockSpec(memory_space=pltpu.HBM)

    def stay(argument):
        return pltpu.with_memory_space_constraint(argument, pltpu.HBM)

    volume, cotangent, dep = pl.pallas_call(
        bring,
        out_shape=[jax.ShapeDtypeStruct(shape, BF16) for shape in (volume.shape, cotangent.shape, (17, 4, width))],
        in_specs=[smem] + [in_hbm] * 2,
        out_specs=[whole] * 3,
        scratch_shapes=[pltpu.SemaphoreType.DMA((4,))],
        compiler_params=small,
    )(flags, stay(volume), stay(cotangent))
    weights = (first_weight, second_weight.T)
    shapes = [(groups, 4, width)] * 2 + [(groups, high, LANES)] * 2
    shapes += [weight.shape for weight in weights]
    row_b, row_a, side_a, side_b, first_taps, second_taps = pl.pallas_call(
        pack,
        out_shape=[jax.ShapeDtypeStruct(shape, BF16) for shape in shapes],
        in_specs=[smem] + [whole] * 2 + [in_hbm] * 2,
        out_specs=[whole] * len(shapes),
        scratch_shapes=[pltpu.SemaphoreType.DMA((2,))],
        compiler_params=small,
    )(flags, volume, cotangent, *[stay(weight) for weight in weights])

    def to_col(block, kind):
        return lax.ppermute(block, ("row", "col"), pairs_of_lines(rows, cols, kind))

    dep = lax.ppermute(dep, "depth", [(0, 1), (1, 0)])
    row_a = lax.ppermute(row_a, "row", pairs_on_line(rows, 0))
    row_b = lax.ppermute(row_b, ("depth", "row"), pairs_of_lines(2, rows, 1))
    row_a, side_a, side_b = lax.optimization_barrier((row_a, side_a, side_b))
    side_a, side_b = to_col(side_a, 0), to_col(side_b, 1)

    low, top = [jnp.concatenate([dep[n : n + 1] for n in (*range(k, 16, 4), 16)], axis=0) for k in (0, 3)]
    even, ends = row % 2 == 0, jnp.logical_or(row == 0, row == rows - 1)
    edge_a = jnp.where(even, top, low)
    edge_b = jnp.where(ends, 0, jnp.where(even, low, top))
    edge_a = lax.ppermute(edge_a, "row", pairs_on_line(rows, 0))
    edge_b = lax.ppermute(edge_b, ("depth", "row"), pairs_of_lines(2, rows, 1))
    weights = pl.pallas_call(
        bands,
        out_shape=[jax.ShapeDtypeStruct(shape, BF16) for shape in ((1152, 256), (1152, 256), (9, 256, 128))],
        in_specs=[whole] * 2,
        out_specs=[whole] * 3,
        compiler_params=small,
    )(first_taps, second_taps)
    col_a, col_b = pl.pallas_call(
        pack_corners,
        out_shape=[jax.ShapeDtypeStruct((planes + 14, 8, LANES), BF16)] * 2,
        in_specs=[smem] + [whole] * 5,
        out_specs=[whole] * 2,
        compiler_params=small,
    )(flags, dep, row_a, row_b, edge_a, edge_b)
    col_a, col_b, volume = lax.optimization_barrier((col_a, col_b, volume))
    col_a, col_b = to_col(col_a, 0), to_col(col_b, 1)

    spot = lax.axis_index(("depth", "row"))
    squares = lax.axis_size(("depth", "row")) // 2
    where = jnp.stack([spot % 2, spot // 2])
    faces, corners = (dep, row_a, row_b, edge_a, edge_b), (side_a, side_b, col_a, col_b)
    keep, give = local_grads(flags, where, squares, volume, faces, corners, cotangent, weights)

    steps = squares.bit_length() - 1

    def to_square(block, step):
        bits = (1 << step, 1 << (steps - 1 - step))
        route = [(2 * i + c, 2 * (i ^ bits[c]) + c) for i in range(squares) for c in (0, 1)]
        return lax.ppermute(block, ("depth", "row"), route)

    def to_core(block):
        return lax.ppermute(block, ("depth", "row"), [(i, i ^ 1) for i in range(2 * squares)])

    def along_col(block, n):
        return lax.ppermute(block, "col", [(i, i ^ n) for i in range(cols)])

    both = keep + to_core(give).astype(F32)
    for step in range(steps):
        half = both.shape[0] // 2
        both = both[:half] + to_square(both[half:].astype(BF16), step).astype(F32)
    mine = both.astype(BF16)
    mine = add_up(mine, *[along_col(mine, n) for n in range(1, cols)])
    for step in reversed(range(steps)):
        mine = jnp.concatenate([mine, to_square(mine, step)], axis=0)
    other = to_core(mine)
    grads = [jax.ShapeDtypeStruct(shape, F32) for shape in (first_weight.shape, second_weight.shape[::-1])]
    first_grad, second_grad = pl.pallas_call(
        unpack,
        out_shape=grads,
        in_specs=[smem] + [whole] * 2,
        out_specs=[whole] * 2,
        scratch_shapes=[pltpu.VMEM((mine.shape[0] * mine.shape[1] * 2, LANES), F32)],
        compiler_params=small,
    )(where, mine, other)
    return first_grad, second_grad.T


def solution(mesh):
    placed = (P("depth", "row", "col"), P(), P(), P("depth", "row", "col"))
    return jax.shard_map(shards, mesh=mesh, in_specs=placed, out_specs=(P(), P()), check_vma=False)
```

```python
import jax
import jax.numpy as jnp
from jax import lax
from jax.experimental import pallas as pl
from jax.experimental.pallas import tpu as pltpu
from jax.sharding import PartitionSpec as P

LANES = 128
SECOND_ROWS = 27 * 64
FIRST_BLOCKS = 7
F32 = jnp.float32
BF16 = jnp.bfloat16


def pairs_on_line(count, kind):
    firsts = range(kind, count - 1, 2)
    swapped = [(i, i + 1) for i in firsts] + [(i + 1, i) for i in firsts]
    met = {i for i, j in swapped}
    return swapped + [(i, i) for i in range(count) if i not in met]


def pairs_of_lines(lines, count, kind):
    route = []
    for line in range(lines):
        for i, j in pairs_on_line(count, kind):
            route.append((line * count + i, (line ^ 1 if i == j else line) * count + j))
    return route


def add_up(*terms):
    terms = [term.astype(F32) for term in terms]
    while len(terms) > 1:
        terms = [terms[n] + terms[n + 1] for n in range(0, len(terms), 2)]
    return terms[0].astype(BF16)


def matmul(left, right):
    return lax.dot_general(left, right, (((1,), (0,)), ((), ())), preferred_element_type=F32)


def bring(flag_ref, vol_hbm, cot_hbm, vol_ref, cot_ref, dep_ref, arrived):
    first_plane = flag_ref[0] == 0
    planes = vol_ref.shape[0]
    inner = pl.ds(4, planes - 8)
    copies = [pltpu.make_async_copy(cot_hbm, cot_ref, arrived.at[0])]
    for n, part in enumerate((pl.ds(0, 4), pl.ds(planes - 4, 4), inner)):
        copies.append(pltpu.make_async_copy(vol_hbm.at[part], vol_ref.at[part], arrived.at[1 + n]))
    for copy in copies:
        copy.start()
    for copy in copies[:3]:
        copy.wait()
    dep_ref[16] = cot_ref[0]
    for q in range(4):
        block = jnp.where(first_plane, vol_ref[planes - 4 + q].astype(F32), vol_ref[q].astype(F32))
        for g in range(4):
            dep_ref[4 * q + g] = block[4 * g : 4 * g + 4].astype(BF16)
    copies[3].wait()


def pack_rows(flag_ref, vol_ref, cot_ref, row_b_ref, row_a_ref):
    row_even, row_inner = flag_ref[1] == 0, flag_ref[3] != 0
    planes, high, width = vol_ref.shape
    cots = cot_ref.shape[0]

    def plane(d, carry):
        for m in range(width // LANES):
            lanes = slice(m * LANES, (m + 1) * LANES)
            block = vol_ref[d, :, lanes].astype(F32)
            low, top = block[:4], block[high - 4 :]
            row_a_ref[d, :, lanes] = jnp.where(row_even, top, low).astype(BF16)
            row_b_ref[d, :, lanes] = jnp.where(row_inner, jnp.where(row_even, low, top), 0.0).astype(BF16)
        return carry

    lax.fori_loop(0, planes, plane, 0, unroll=4)
    for g in range(cots // 4):
        tops = jnp.concatenate([cot_ref[4 * g + n].astype(F32)[:1] for n in range(4)], axis=0)
        row_a_ref[planes + g] = tops.astype(BF16)
        row_b_ref[planes + g] = jnp.where(row_inner, tops, 0.0).astype(BF16)


def pack_sides(
    flag_ref, vol_ref, cot_ref, first_hbm, second_hbm, col_a_ref, col_b_ref, first_ref, second_ref, arrived
):
    col_even, col_inner = flag_ref[2] == 0, flag_ref[4] != 0
    planes, high, width = vol_ref.shape
    cots = cot_ref.shape[0]
    copies = [
        pltpu.make_async_copy(first_hbm, first_ref, arrived.at[0]),
        pltpu.make_async_copy(second_hbm, second_ref, arrived.at[1]),
    ]
    for copy in copies:
        copy.start()
    for g in range(cots // 4):
        side = jnp.concatenate([cot_ref[4 * g + n, :, :LANES].astype(F32) for n in range(4)], axis=0)
        col_a_ref[planes + g] = side.astype(BF16)
        col_b_ref[planes + g] = jnp.where(col_inner, side, 0.0).astype(BF16)

    def plane(d, carry):
        left = vol_ref[d, :, :LANES].astype(F32)
        right = vol_ref[d, :, width - LANES :].astype(F32)
        col_a_ref[d] = jnp.where(col_even, right, left).astype(BF16)
        col_b_ref[d] = jnp.where(col_inner, jnp.where(col_even, left, right), 0.0).astype(BF16)
        return carry

    lax.fori_loop(0, planes, plane, 0, unroll=4)
    for copy in copies:
        copy.wait()


def pack_corners(flag_ref, row_b_ref, row_a_ref, dep_ref, edge_a_ref, edge_b_ref, col_a_ref, col_b_ref):
    row_even, col_even, col_inner = flag_ref[1] == 0, flag_ref[2] == 0, flag_ref[4] != 0
    width = dep_ref.shape[2]
    groups = row_a_ref.shape[0]
    planes = (groups * 16) // 17
    faces = (slice(0, LANES), slice(width - LANES, width))

    def store(n, left, right):
        col_a_ref[n] = jnp.where(col_even, right, left).astype(BF16)
        col_b_ref[n] = jnp.where(col_inner, jnp.where(col_even, left, right), 0.0).astype(BF16)

    def lower_upper(a_ref, b_ref, source, target):
        values = []
        for lanes in faces:
            a, b = a_ref[source, :, lanes].astype(F32), b_ref[source, :, lanes].astype(F32)
            values.append(jnp.concatenate([jnp.where(row_even, b, a), jnp.where(row_even, a, b)], axis=0))
        store(target, *values)

    def plane(d, carry):
        lower_upper(row_a_ref, row_b_ref, d, d)
        return carry

    lax.fori_loop(0, planes, plane, 0, unroll=4)
    for q in range(4):
        lower_upper(edge_a_ref, edge_b_ref, q, planes + q)
        for n in range(2):
            units = range(4 * q + 2 * n, 4 * q + 2 * n + 2)
            store(
                planes + 4 + 2 * q + n,
                *[jnp.concatenate([dep_ref[u, :, lanes].astype(F32) for u in units], axis=0) for lanes in faces],
            )
    lanes = faces[0]
    tops = [
        jnp.where(row_even, row_a_ref[g, :, lanes].astype(F32), row_b_ref[g, :, lanes].astype(F32))
        for g in range(planes, groups)
    ]
    corner = jnp.where(row_even, edge_a_ref[4, :, lanes].astype(F32), edge_b_ref[4, :, lanes].astype(F32))
    own = dep_ref[16, :, lanes].astype(F32)
    for n, values in enumerate((jnp.concatenate(tops, axis=0), jnp.concatenate([own, corner], axis=0))):
        col_a_ref[planes + 12 + n] = values.astype(BF16)
        col_b_ref[planes + 12 + n] = jnp.where(col_inner, values, 0.0).astype(BF16)


def bands(first_ref, second_ref, w1_ref, w2_ref, w2b_ref):
    out_chan = first_ref.shape[0]
    first = first_ref[...].astype(F32)
    blank = jnp.zeros((out_chan, LANES), F32)
    for tap in range(9):
        rows = slice(tap * LANES, (tap + 1) * LANES)
        taps = first[:, tap * 96 : (tap + 1) * 96]
        main_even = jnp.concatenate([taps[:, 32:], blank[:, :64]], axis=1)
        main_odd = jnp.concatenate([blank[:, :32], taps], axis=1)
        prev_even = jnp.concatenate([blank[:, :96], taps[:, :32]], axis=1)
        w1_ref[rows] = jnp.concatenate([main_even, main_odd, prev_even, blank], axis=0).T.astype(BF16)
        main = second_ref[tap * 192 + 64 : (tap + 1) * 192, :]
        prev = jnp.concatenate([jnp.zeros((64, LANES), BF16), second_ref[tap * 192 : tap * 192 + 64, :]], axis=0)
        both = jnp.concatenate([main, prev], axis=1)
        w2_ref[rows] = both
        w2b_ref[tap] = both.astype(F32).T.astype(BF16)


def split_rows(stage, tiles, index, blocks):
    for m in blocks:
        rows = [stage[m, pl.ds(4 + s, 8, stride=4), :] for s in range(-1, 4)]
        for b in range(3):
            tiles[b, index, m] = jnp.concatenate([rows[b], rows[b + 2]], axis=0).astype(BF16)


def clear_stage(stage):
    stage[:, :, 0:8, :] = jnp.zeros(stage.shape[:2] + (8, LANES), F32)
    stage[:, :, 24:40, :] = jnp.zeros(stage.shape[:2] + (16, LANES), F32)


def ahead(even, a, b):
    return jnp.where(even, a.astype(F32), b.astype(F32))


def behind(even, a, b):
    return jnp.where(even, b.astype(F32), a.astype(F32))


def own_blocks(
    flag_ref, vol_ref, dep_ref, row_a_ref, row_b_ref, edge_a_ref, edge_b_ref, w1_ref, tiles, parts, stage
):
    first_plane, row_even = flag_ref[0] == 0, flag_ref[1] == 0
    planes = vol_ref.shape[0]
    blocks = vol_ref.shape[2] // LANES
    clear_stage(stage)

    def place(n, target, own, a, b, keep):
        def kept(values):
            return values if keep is None else jnp.where(keep, values, 0.0)

        for m in range(blocks):
            lanes = slice(m * LANES, (m + 1) * LANES)
            stage[n, m, 8:24, :] = kept(own(lanes).astype(F32))
            stage[n, m, 4:8, :] = kept(behind(row_even, a(lanes), b(lanes)))
            stage[n, m, 24:28, :] = kept(ahead(row_even, a(lanes), b(lanes)))
        split_rows(stage.at[n], tiles, target, range(blocks))

    def place_own(pair, carry):
        for n in range(2):
            d = 2 * pair + n
            place(
                n, d + 3, lambda lanes: vol_ref[d, :, lanes],
                lambda lanes: row_a_ref[d, :, lanes], lambda lanes: row_b_ref[d, :, lanes], None,
            )
        return carry

    def place_halo(target, q, keep):
        place(
            target % 2, target,
            lambda lanes: jnp.concatenate([dep_ref[4 * q + g, :, lanes].astype(F32) for g in range(4)], axis=0),
            lambda lanes: edge_a_ref[q, :, lanes], lambda lanes: edge_b_ref[q, :, lanes], keep,
        )

    lax.fori_loop(0, planes // 2, place_own, 0)
    for q in range(3):
        place_halo(q, q + 1, jnp.logical_not(first_plane))
    for q in range(4):
        place_halo(planes + 3 + q, q, first_plane)
    tiles[:, planes + 7 :] = jnp.zeros((3, 2, blocks, 16, LANES), BF16)

    group = 5

    def product(step, carry):
        taps = []
        for a in range(3):
            for b in range(3):
                start = 2 * group * step + a
                found = [tiles[b, start + 2 * n].reshape(blocks * 16, LANES) for n in range(group)]
                taps.append(jnp.concatenate(found, axis=0))
        found = matmul(jnp.concatenate(taps, axis=1), w1_ref[...])
        parts[pl.ds(group * step, group)] = found.reshape(group, blocks, 16, 2 * LANES)
        return carry

    lax.fori_loop(0, parts.shape[0] // group, product, 0)


def body(
    flag_ref, place_ref, tiles, parts, dep_ref, row_a_ref, row_b_ref, edge_a_ref, edge_b_ref,
    side_a_ref, side_b_ref, col_a_ref, col_b_ref, cot_ref, w1_ref, w2_ref, w2b_ref, keep_ref, give_ref,
    out_ref, stage, rim_tiles, rim_parts, slopes, hid, pairs, ups, deltas, shifted,
):
    first_plane, row_even, col_even = flag_ref[0] == 0, flag_ref[1] == 0, flag_ref[2] == 0
    planes = tiles.shape[1] - 9
    blocks = tiles.shape[2]
    half_planes = planes // 4
    hidden_planes = planes // 2 + 3

    clear_stage(stage)

    def place(n, target, source, side_a, side_b, keep):
        for m, choose in ((0, behind), (1, ahead)):
            corners = choose(col_even, col_a_ref[source], col_b_ref[source])
            own = choose(col_even, side_a, side_b)
            if keep is not None:
                corners, own = jnp.where(keep, corners, 0.0), jnp.where(keep, own, 0.0)
            stage[n, m, 4:8, :] = corners[:4]
            stage[n, m, 8:24, :] = own
            stage[n, m, 24:28, :] = corners[4:]
        split_rows(stage.at[n], rim_tiles, target, range(2))

    def place_own(group, carry):
        for n in range(4):
            d = 4 * group + n
            place(n, d + 3, d, side_a_ref[d], side_b_ref[d], None)
        return carry

    def place_halo(target, q, keep):
        start = planes + 4 + 2 * q
        side_a = jnp.concatenate([col_a_ref[start].astype(F32), col_a_ref[start + 1].astype(F32)], axis=0)
        side_b = jnp.concatenate([col_b_ref[start].astype(F32), col_b_ref[start + 1].astype(F32)], axis=0)
        place(target % 4, target, planes + q, side_a, side_b, keep)

    lax.fori_loop(0, planes // 4, place_own, 0)
    for q in range(3):
        place_halo(q, q + 1, jnp.logical_not(first_plane))
    for q in range(4):
        place_halo(planes + 3 + q, q, first_plane)

    taps = []
    for a in range(3):
        for b in range(3):
            rows = [rim_tiles[b, 2 * i + a].reshape(32, LANES) for i in range(hidden_planes)]
            taps.append(jnp.concatenate(rows, axis=0))
    found = matmul(jnp.concatenate(taps, axis=1), w1_ref[...])
    rim_parts[...] = found.reshape(hidden_planes, 2, 16, 2 * LANES)

    def conv_one(i, carry):
        main, prev = parts[i, :, :, :LANES], parts[i, :, :, LANES:]
        rim, rim_prev = rim_parts[i, :, :, :LANES], rim_parts[i, 0:1, :, LANES:]
        blank = jnp.zeros((1, 16, LANES), F32)
        pre = jnp.concatenate([rim[:1], main, rim[1:]], axis=0) + jnp.concatenate([blank, rim_prev, prev], axis=0)
        square = pre * pre + 1.0
        inverse = lax.rsqrt(square)
        slopes[i] = 0.6 + 0.4 * (pre * inverse)
        hidden = (0.6 * pre + 0.4 * (square * inverse - 1.0)).astype(BF16).astype(F32)
        odd = hidden[:, 8:, :]
        hid[0, i] = pltpu.roll(odd, 1, 1)
        hid[1, i] = hidden[:, :8, :]
        hid[2, i] = odd
        return carry

    lax.fori_loop(0, hidden_planes, conv_one, 0)

    wide = (blocks + 2) * 16

    def pair(i, carry):
        for b in range(3):
            pairs[b, i] = jnp.concatenate([hid[b, i], hid[b, i + half_planes]], axis=1).astype(BF16)
        return carry

    lax.fori_loop(0, half_planes + 3, pair, 0)

    ups[...] = jnp.zeros_like(ups)
    for k in range(blocks):
        lanes = slice(k * LANES, (k + 1) * LANES)
        ups[0:half_planes, k, 1:5, :] = cot_ref[:, :, lanes].astype(F32)
        ups[half_planes, k, 1:5, :] = jnp.where(first_plane, dep_ref[16, :, lanes].astype(F32), 0.0)
        for g in range(half_planes // 4):
            tops = ahead(row_even, row_a_ref[planes + g, :, lanes], row_b_ref[planes + g, :, lanes])
            for n in range(4):
                ups[4 * g + n, k, 5:6, :] = tops[n : n + 1]
        corner = ahead(row_even, edge_a_ref[4, :, lanes], edge_b_ref[4, :, lanes])[:1]
        ups[half_planes, k, 5:6, :] = jnp.where(first_plane, corner, 0.0)
    for g in range(half_planes // 4):
        side = ahead(col_even, side_a_ref[planes + g], side_b_ref[planes + g])
        for n in range(4):
            ups[4 * g + n, blocks, 1:5, :] = side[4 * n : 4 * n + 4]
    tops = ahead(col_even, col_a_ref[planes + 12], col_b_ref[planes + 12])
    for n in range(half_planes):
        ups[n, blocks, 5:6, :] = tops[n : n + 1]
    beyond = jnp.where(first_plane, ahead(col_even, col_a_ref[planes + 13], col_b_ref[planes + 13]), 0.0)
    ups[half_planes, blocks, 1:6, :] = beyond[:5]

    quarter = half_planes // 2

    taps = []
    for a in range(3):
        for b in range(3):
            rows = [pairs[b, 2 * t + a].reshape(wide, LANES) for t in range(quarter + 1)]
            taps.append(jnp.concatenate(rows, axis=0))
    found = matmul(jnp.concatenate(taps, axis=1), w2_ref[...]).reshape(quarter + 1, blocks + 2, 16, 2 * LANES)
    for t in range(quarter + 1):
        pre = found[t, 1:, :, :LANES] + found[t, :-1, :, LANES:]
        slope = 0.6 + 0.4 * (pre * lax.rsqrt(pre * pre + 1.0))
        upstream = jnp.concatenate([ups[t], ups[t + quarter]], axis=1)
        delta = (upstream * slope).astype(BF16).astype(F32)
        moved = jnp.concatenate([pltpu.roll(delta[:, :8], 7, 1), pltpu.roll(delta[:, 8:], 7, 1)], axis=1)
        deltas[t] = delta
        shifted[t] = moved.astype(BF16)

    sublane = lax.broadcasted_iota(jnp.int32, (1, 1, 16, 1), 2) % 8
    own_rows = jnp.logical_and(sublane >= 1, sublane <= 4)

    def with_next(values, needed):
        values = values.T
        edge = jnp.zeros((LANES, values.shape[1] // blocks), values.dtype)
        here = jnp.concatenate([edge, values], axis=1)
        after = jnp.concatenate([values, edge], axis=1)[:needed]
        return jnp.concatenate([here, after], axis=0)

    own_delta = [jnp.where(own_rows[0], deltas[t, 0:blocks], 0.0) for t in range(quarter)]
    left = with_next(jnp.stack(own_delta, axis=1).reshape(blocks * quarter * 16, LANES), LANES).astype(BF16)

    def second_taps(tap):
        a, b = tap // 3, tap % 3
        found = [pairs[b, 2 * t + a, 0 : blocks + 1] for t in range(quarter)]
        return jnp.stack(found, axis=1).reshape((blocks + 1) * quarter * 16, LANES)

    for tap in range(0, 9, 2):
        right = [second_taps(x) for x in range(tap, min(tap + 2, 9))]
        found = matmul(left, jnp.concatenate(right, axis=1))
        for n in range(len(right)):
            row = (tap + n) * 192
            lanes = slice(n * LANES, (n + 1) * LANES)
            out_ref[row : row + 64, :] = found[LANES:, lanes].T[64:]
            out_ref[row + 64 : row + 192, :] = found[:LANES, lanes].T

    def pack(values):
        both = jnp.concatenate([values[:, :-1], values[:, 1:]], axis=3)
        return both.reshape(quarter * blocks * 16, 2 * LANES)

    plain = deltas[...].astype(BF16)
    moved = shifted[...]
    here, after = pack(plain[:-1]), pack(plain[1:])
    here_up, after_up = pack(moved[:-1]), pack(moved[1:])

    def back(terms):
        joined = jnp.concatenate([values for values, a, b in terms], axis=1)
        weights = jnp.concatenate([w2b_ref[3 * a + b] for values, a, b in terms], axis=0)
        return matmul(joined, weights).reshape(quarter, blocks, 16, LANES)

    rows = [
        [back([(here, 1, 1)]), back([(here_up, 1, 0), (here, 1, 2)])],
        [
            back([(after, 0, 1), (here, 2, 1)]),
            back([(after_up, 0, 0), (after, 0, 2), (here_up, 2, 0), (here, 2, 2)]),
        ],
    ]
    own_list = []
    for i in range(planes // 2):
        t, parity = i // 2, i % 2
        half = slice(0, 8) if t < quarter else slice(8, 16)
        back_one = jnp.concatenate([rows[parity][p][t % quarter, :, half, :] for p in (0, 1)], axis=1)
        delta = back_one * slopes[i + 1, 1 : blocks + 1]
        own_list.append(jnp.where(own_rows[0], delta, 0.0).astype(BF16))
    left_one = with_next(jnp.stack(own_list, axis=1).reshape(blocks * (planes // 2) * 16, LANES), 64)

    def first_taps(tap):
        a, b = tap // 3, tap % 3
        found = []
        for m in range(blocks + 1):
            for i in range(planes // 2):
                index = 2 * (i + 1) + a
                found.append(rim_tiles[b, index, 0] if m == 0 else tiles[b, index, m - 1])
        return jnp.concatenate(found, axis=0)

    grads = []
    for tap in range(0, 9, 2):
        right = [first_taps(x) for x in range(tap, min(tap + 2, 9))]
        found = matmul(left_one, jnp.concatenate(right, axis=1))
        for n in range(len(right)):
            main = found[:LANES, n * LANES : (n + 1) * LANES]
            prev = found[LANES:, n * LANES : (n + 1) * LANES]
            even = jnp.concatenate([prev[:, 96:], main[:64, :64]], axis=1)
            grads.append(even + main[64:, 32:])
    grads.append(jnp.zeros((64, FIRST_BLOCKS * LANES - 9 * 96), F32))
    first = jnp.concatenate(grads, axis=1)
    for n in range(FIRST_BLOCKS):
        row = SECOND_ROWS + 64 * n
        out_ref[row : row + 64, :] = first[:, n * LANES : (n + 1) * LANES]
    used = SECOND_ROWS + 64 * FIRST_BLOCKS
    if out_ref.shape[0] > used:
        out_ref[used:, :] = jnp.zeros((out_ref.shape[0] - used, LANES), F32)

    core, square = place_ref[0], place_ref[1]
    squares, size = keep_ref.shape[0], keep_ref.shape[1]
    for n in range(squares):
        for ref, half in ((keep_ref, core), (give_ref, 1 - core)):
            start = pl.multiple_of((half * squares + (square ^ n)) * size, 8)
            ref[n] = out_ref[pl.ds(start, size), :].astype(ref.dtype)


def unpack(place_ref, keep_ref, got_ref, g1_hbm, g2_hbm, sums, first, sent):
    core, square = place_ref[0], place_ref[1]
    squares, size = keep_ref.shape[0], keep_ref.shape[1]
    for n in range(squares):
        for ref, half in ((keep_ref, core), (got_ref, 1 - core)):
            start = pl.multiple_of((half * squares + (square ^ n)) * size, 8)
            sums[pl.ds(start, size), :] = ref[n].astype(F32)
    second = pltpu.make_async_copy(sums.at[pl.ds(0, SECOND_ROWS)], g2_hbm, sent.at[0])
    second.start()
    found = [sums[SECOND_ROWS + 64 * n : SECOND_ROWS + 64 * (n + 1), :] for n in range(FIRST_BLOCKS)]
    first[...] = jnp.concatenate(found, axis=1)[:, : first.shape[1]]
    copy = pltpu.make_async_copy(first, g1_hbm, sent.at[1])
    copy.start()
    copy.wait()
    second.wait()


def local_grads(flags, place, squares, volume, faces, corners, cotangent, weights):
    planes = volume.shape[0]
    blocks = volume.shape[2] // LANES
    hidden_planes = planes // 2 + 3
    out_planes = planes // 4
    unit = 2 * squares * 16
    rows = -(-(SECOND_ROWS + 64 * FIRST_BLOCKS) // unit) * unit
    whole = pl.BlockSpec(memory_space=pltpu.VMEM)
    smem = pl.BlockSpec(memory_space=pltpu.SMEM)
    dep, row_a, row_b, edge_a, edge_b = faces
    tiles, parts = pl.pallas_call(
        own_blocks,
        out_shape=[
            jax.ShapeDtypeStruct((3, planes + 9, blocks, 16, LANES), BF16),
            jax.ShapeDtypeStruct((hidden_planes + 1, blocks, 16, 2 * LANES), F32),
        ],
        in_specs=[smem] + [whole] * 7,
        out_specs=[whole] * 2,
        scratch_shapes=[pltpu.VMEM((2, blocks, 40, LANES), F32)],
        compiler_params=pltpu.CompilerParams(vmem_limit_bytes=16 * 1024 * 1024),
        cost_estimate=pl.CostEstimate(flops=2 * 10**9, bytes_accessed=10**7, transcendentals=0),
    )(flags, volume, *faces, weights[0])
    scratch = [
        pltpu.VMEM((rows, LANES), F32),
        pltpu.VMEM((4, 2, 40, LANES), F32),
        pltpu.VMEM((3, planes + 7, 2, 16, LANES), BF16),
        pltpu.VMEM((hidden_planes, 2, 16, 2 * LANES), F32),
        pltpu.VMEM((hidden_planes, blocks + 2, 16, LANES), F32),
        pltpu.VMEM((3, hidden_planes, blocks + 2, 8, LANES), F32),
        pltpu.VMEM((3, out_planes + 3, blocks + 2, 16, LANES), BF16),
        pltpu.VMEM((out_planes + 1, blocks + 1, 8, LANES), F32),
        pltpu.VMEM((out_planes // 2 + 1, blocks + 1, 16, LANES), F32),
        pltpu.VMEM((out_planes // 2 + 1, blocks + 1, 16, LANES), BF16),
    ]
    operands = (tiles, parts, *faces, *corners, cotangent, *weights)
    return pl.pallas_call(
        body,
        out_shape=[jax.ShapeDtypeStruct((squares, rows // (2 * squares), LANES), dtype) for dtype in (F32, BF16)],
        in_specs=[smem] * 2 + [whole] * len(operands),
        out_specs=[whole] * 2,
        scratch_shapes=scratch,
        compiler_params=pltpu.CompilerParams(vmem_limit_bytes=28 * 1024 * 1024),
        cost_estimate=pl.CostEstimate(flops=4 * 10**9, bytes_accessed=10**7, transcendentals=0),
    )(flags, place, *operands)


def shards(volume, first_weight, second_weight, cotangent):
    half = lax.axis_index("depth")
    row, col = lax.axis_index("row"), lax.axis_index("col")
    rows, cols = lax.axis_size("row"), lax.axis_size("col")
    inner = [jnp.logical_and(i > 0, i < n - 1).astype(jnp.int32) for i, n in ((row, rows), (col, cols))]
    flags = jnp.stack([half, row % 2, col % 2, *inner])
    whole = pl.BlockSpec(memory_space=pltpu.VMEM)
    smem = pl.BlockSpec(memory_space=pltpu.SMEM)
    small = pltpu.CompilerParams(vmem_limit_bytes=12 * 1024 * 1024)
    planes, high, width = volume.shape
    groups = planes + cotangent.shape[0] // 4
    in_hbm = pl.BlockSpec(memory_space=pltpu.HBM)

    def stay(argument):
        return pltpu.with_memory_space_constraint(argument, pltpu.HBM)

    volume, cotangent, dep = pl.pallas_call(
        bring,
        out_shape=[jax.ShapeDtypeStruct(shape, BF16) for shape in (volume.shape, cotangent.shape, (17, 4, width))],
        in_specs=[smem] + [in_hbm] * 2,
        out_specs=[whole] * 3,
        scratch_shapes=[pltpu.SemaphoreType.DMA((4,))],
        compiler_params=small,
    )(flags, stay(volume), stay(cotangent))
    row_b, row_a = pl.pallas_call(
        pack_rows,
        out_shape=[jax.ShapeDtypeStruct((groups, 4, width), BF16)] * 2,
        in_specs=[smem] + [whole] * 2,
        out_specs=[whole] * 2,
        compiler_params=small,
    )(flags, volume, cotangent)

    def to_col(block, kind):
        return lax.ppermute(block, ("row", "col"), pairs_of_lines(rows, cols, kind))

    dep = lax.ppermute(dep, "depth", [(0, 1), (1, 0)])
    route = []
    for i, j in pairs_on_line(rows, 1):
        route += [((d * rows + i) * cols + c, (d * rows + j) * cols + (c ^ 1 if i == j else c)) for d in (0, 1) for c in range(cols)]
    row_b = lax.ppermute(row_b, ("depth", "row", "col"), route)
    row_a = lax.ppermute(row_a, "row", pairs_on_line(rows, 0))
    row_a, volume, cotangent = lax.optimization_barrier((row_a, volume, cotangent))
    weights = (first_weight, second_weight.T)
    shapes = [(groups, high, LANES)] * 2 + [weight.shape for weight in weights]
    side_a, side_b, first_taps, second_taps = pl.pallas_call(
        pack_sides,
        out_shape=[jax.ShapeDtypeStruct(shape, BF16) for shape in shapes],
        in_specs=[smem] + [whole] * 2 + [in_hbm] * 2,
        out_specs=[whole] * len(shapes),
        scratch_shapes=[pltpu.SemaphoreType.DMA((2,))],
        compiler_params=small,
    )(flags, volume, cotangent, *[stay(weight) for weight in weights])

    side_a, side_b = to_col(side_a, 0), to_col(side_b, 1)
    low, top = [jnp.concatenate([dep[n : n + 1] for n in (*range(k, 16, 4), 16)], axis=0) for k in (0, 3)]
    even, ends = row % 2 == 0, jnp.logical_or(row == 0, row == rows - 1)
    edge_a = jnp.where(even, top, low)
    edge_b = jnp.where(ends, 0, jnp.where(even, low, top))
    edge_a = lax.ppermute(edge_a, "row", pairs_on_line(rows, 0))
    edge_b = lax.ppermute(edge_b, ("depth", "row"), pairs_of_lines(2, rows, 1))
    weights = pl.pallas_call(
        bands,
        out_shape=[jax.ShapeDtypeStruct(shape, BF16) for shape in ((1152, 256), (1152, 256), (9, 256, 128))],
        in_specs=[whole] * 2,
        out_specs=[whole] * 3,
        compiler_params=small,
    )(first_taps, second_taps)
    row_b, weights = lax.optimization_barrier((row_b, weights))
    col_a, col_b = pl.pallas_call(
        pack_corners,
        out_shape=[jax.ShapeDtypeStruct((planes + 14, 8, LANES), BF16)] * 2,
        in_specs=[smem] + [whole] * 5,
        out_specs=[whole] * 2,
        compiler_params=small,
    )(flags, row_b, row_a, dep, edge_a, edge_b)
    col_a, col_b, volume = lax.optimization_barrier((col_a, col_b, volume))
    col_a, col_b = to_col(col_a, 0), to_col(col_b, 1)

    spot = lax.axis_index(("depth", "row"))
    squares = lax.axis_size(("depth", "row")) // 2
    where = jnp.stack([spot % 2, spot // 2])
    faces, corners = (dep, row_a, row_b, edge_a, edge_b), (side_a, side_b, col_a, col_b)
    keep, give = local_grads(flags, where, squares, volume, faces, corners, cotangent, weights)

    def to_square(block, n):
        route = [(2 * i + c, 2 * (i ^ n) + c) for i in range(squares) for c in (0, 1)]
        return lax.ppermute(block, ("depth", "row"), route)

    def to_core(block):
        return lax.ppermute(block, ("depth", "row"), [(i, i ^ 1) for i in range(2 * squares)])

    def along_col(block, n):
        return lax.ppermute(block, "col", [(i, i ^ n) for i in range(cols)])

    both = keep + to_core(give).astype(F32)
    near = both.astype(BF16)
    share = add_up(both[0], *[to_square(near[n], n) for n in range(1, squares)])
    share = add_up(share, *[along_col(share, n) for n in range(1, cols)])
    mine = jnp.stack([share] + [to_square(share, n) for n in range(1, squares)])
    other = to_core(mine)
    grads = [jax.ShapeDtypeStruct(shape, F32) for shape in (first_weight.shape, second_weight.shape[::-1])]
    first_grad, second_grad = pl.pallas_call(
        unpack,
        out_shape=grads,
        in_specs=[smem] + [whole] * 2,
        out_specs=[in_hbm] * 2,
        scratch_shapes=[
            pltpu.VMEM((mine.shape[0] * mine.shape[1] * 2, LANES), F32),
            pltpu.VMEM(first_weight.shape, F32),
            pltpu.SemaphoreType.DMA((2,)),
        ],
        compiler_params=small,
    )(where, mine, other)
    return first_grad, second_grad.T


def solution(mesh):
    placed = (P("depth", "row", "col"), P(), P(), P("depth", "row", "col"))
    return jax.shard_map(shards, mesh=mesh, in_specs=placed, out_specs=(P(), P()), check_vma=False)
```

```python
import jax
import jax.numpy as jnp
from jax import lax
from jax.experimental import pallas as pl
from jax.experimental.pallas import tpu as pltpu
from jax.sharding import PartitionSpec as P

LANES = 128
SECOND_ROWS = 27 * 64
FIRST_BLOCKS = 7
F32 = jnp.float32
BF16 = jnp.bfloat16


def pairs_on_line(count, kind):
    firsts = range(kind, count - 1, 2)
    swapped = [(i, i + 1) for i in firsts] + [(i + 1, i) for i in firsts]
    met = {i for i, j in swapped}
    return swapped + [(i, i) for i in range(count) if i not in met]


def pairs_of_lines(lines, count, kind):
    route = []
    for line in range(lines):
        for i, j in pairs_on_line(count, kind):
            route.append((line * count + i, (line ^ 1 if i == j else line) * count + j))
    return route


def add_up(*terms):
    terms = [term.astype(F32) for term in terms]
    while len(terms) > 1:
        terms = [terms[n] + terms[n + 1] for n in range(0, len(terms), 2)]
    return terms[0].astype(BF16)


def matmul(left, right):
    return lax.dot_general(left, right, (((1,), (0,)), ((), ())), preferred_element_type=F32)


def bring(
    flag_ref, vol_hbm, cot_hbm, first_hbm, second_hbm, vol_ref, cot_ref, first_ref, second_ref, dep_ref, arrived
):
    first_plane = flag_ref[0] == 0
    planes, width = vol_ref.shape[0], vol_ref.shape[2]
    inner = pl.ds(4, planes - 8)
    copies = [pltpu.make_async_copy(cot_hbm, cot_ref, arrived.at[0])]
    for n, part in enumerate((pl.ds(0, 4), pl.ds(planes - 4, 4), inner)):
        copies.append(pltpu.make_async_copy(vol_hbm.at[part], vol_ref.at[part], arrived.at[1 + n]))
    copies.append(pltpu.make_async_copy(first_hbm, first_ref, arrived.at[4]))
    copies.append(pltpu.make_async_copy(second_hbm, second_ref, arrived.at[5]))
    for copy in copies:
        copy.start()
    for copy in copies[:3]:
        copy.wait()
    dep_ref[16] = cot_ref[0]
    for q in range(4):
        for m in range(width // LANES):
            lanes = slice(m * LANES, (m + 1) * LANES)
            last, start = vol_ref[planes - 4 + q, :, lanes].astype(F32), vol_ref[q, :, lanes].astype(F32)
            block = jnp.where(first_plane, last, start)
            for g in range(4):
                dep_ref[4 * q + g, :, lanes] = block[4 * g : 4 * g + 4].astype(BF16)
    for copy in copies[3:]:
        copy.wait()


def pack_rows(flag_ref, vol_ref, cot_ref, row_b_ref, row_a_ref):
    row_even, row_inner = flag_ref[1] == 0, flag_ref[3] != 0
    planes, high, width = vol_ref.shape
    cots = cot_ref.shape[0]

    def plane(d, carry):
        for m in range(width // LANES):
            lanes = slice(m * LANES, (m + 1) * LANES)
            block = vol_ref[d, :, lanes].astype(F32)
            low, top = block[:4], block[high - 4 :]
            row_a_ref[d, :, lanes] = jnp.where(row_even, top, low).astype(BF16)
            row_b_ref[d, :, lanes] = jnp.where(row_inner, jnp.where(row_even, low, top), 0.0).astype(BF16)
        return carry

    lax.fori_loop(0, planes, plane, 0, unroll=4)
    for g in range(cots // 4):
        tops = jnp.concatenate([cot_ref[4 * g + n].astype(F32)[:1] for n in range(4)], axis=0)
        row_a_ref[planes + g] = tops.astype(BF16)
        row_b_ref[planes + g] = jnp.where(row_inner, tops, 0.0).astype(BF16)


def pack_sides(flag_ref, vol_ref, cot_ref, col_a_ref, col_b_ref):
    col_even, col_inner = flag_ref[2] == 0, flag_ref[4] != 0
    planes, high, width = vol_ref.shape
    cots = cot_ref.shape[0]
    for g in range(cots // 4):
        side = jnp.concatenate([cot_ref[4 * g + n, :, :LANES].astype(F32) for n in range(4)], axis=0)
        col_a_ref[planes + g] = side.astype(BF16)
        col_b_ref[planes + g] = jnp.where(col_inner, side, 0.0).astype(BF16)

    def plane(d, carry):
        left = vol_ref[d, :, :LANES].astype(F32)
        right = vol_ref[d, :, width - LANES :].astype(F32)
        col_a_ref[d] = jnp.where(col_even, right, left).astype(BF16)
        col_b_ref[d] = jnp.where(col_inner, jnp.where(col_even, left, right), 0.0).astype(BF16)
        return carry

    lax.fori_loop(0, planes, plane, 0, unroll=4)


def pack_corners(flag_ref, row_b_ref, row_a_ref, dep_ref, edge_a_ref, edge_b_ref, col_a_ref, col_b_ref):
    row_even, col_even, col_inner = flag_ref[1] == 0, flag_ref[2] == 0, flag_ref[4] != 0
    width = dep_ref.shape[2]
    groups = row_a_ref.shape[0]
    planes = (groups * 16) // 17
    faces = (slice(0, LANES), slice(width - LANES, width))

    def store(n, left, right):
        col_a_ref[n] = jnp.where(col_even, right, left).astype(BF16)
        col_b_ref[n] = jnp.where(col_inner, jnp.where(col_even, left, right), 0.0).astype(BF16)

    def lower_upper(a_ref, b_ref, source, target):
        values = []
        for lanes in faces:
            a, b = a_ref[source, :, lanes].astype(F32), b_ref[source, :, lanes].astype(F32)
            values.append(jnp.concatenate([jnp.where(row_even, b, a), jnp.where(row_even, a, b)], axis=0))
        store(target, *values)

    def plane(d, carry):
        lower_upper(row_a_ref, row_b_ref, d, d)
        return carry

    lax.fori_loop(0, planes, plane, 0, unroll=4)
    for q in range(4):
        lower_upper(edge_a_ref, edge_b_ref, q, planes + q)
        for n in range(2):
            units = range(4 * q + 2 * n, 4 * q + 2 * n + 2)
            store(
                planes + 4 + 2 * q + n,
                *[jnp.concatenate([dep_ref[u, :, lanes].astype(F32) for u in units], axis=0) for lanes in faces],
            )
    lanes = faces[0]
    tops = [
        jnp.where(row_even, row_a_ref[g, :, lanes].astype(F32), row_b_ref[g, :, lanes].astype(F32))
        for g in range(planes, groups)
    ]
    corner = jnp.where(row_even, edge_a_ref[4, :, lanes].astype(F32), edge_b_ref[4, :, lanes].astype(F32))
    own = dep_ref[16, :, lanes].astype(F32)
    for n, values in enumerate((jnp.concatenate(tops, axis=0), jnp.concatenate([own, corner], axis=0))):
        col_a_ref[planes + 12 + n] = values.astype(BF16)
        col_b_ref[planes + 12 + n] = jnp.where(col_inner, values, 0.0).astype(BF16)


def bands(first_ref, second_ref, w1_ref, w2_ref, w2b_ref):
    out_chan = first_ref.shape[0]
    first = first_ref[...].astype(F32)
    blank = jnp.zeros((out_chan, LANES), F32)
    for tap in range(9):
        rows = slice(tap * LANES, (tap + 1) * LANES)
        taps = first[:, tap * 96 : (tap + 1) * 96]
        main_even = jnp.concatenate([taps[:, 32:], blank[:, :64]], axis=1)
        main_odd = jnp.concatenate([blank[:, :32], taps], axis=1)
        prev_even = jnp.concatenate([blank[:, :96], taps[:, :32]], axis=1)
        w1_ref[rows] = jnp.concatenate([main_even, main_odd, prev_even, blank], axis=0).T.astype(BF16)
        main = second_ref[tap * 192 + 64 : (tap + 1) * 192, :]
        prev = jnp.concatenate([jnp.zeros((64, LANES), BF16), second_ref[tap * 192 : tap * 192 + 64, :]], axis=0)
        both = jnp.concatenate([main, prev], axis=1)
        w2_ref[rows] = both
        w2b_ref[tap] = both.astype(F32).T.astype(BF16)


def split_rows(stage, tiles, index, blocks):
    for m in blocks:
        rows = [stage[m, pl.ds(4 + s, 8, stride=4), :] for s in range(-1, 4)]
        for b in range(3):
            tiles[b, index, m] = jnp.concatenate([rows[b], rows[b + 2]], axis=0).astype(BF16)


def clear_stage(stage):
    stage[:, :, 0:8, :] = jnp.zeros(stage.shape[:2] + (8, LANES), F32)
    stage[:, :, 24:40, :] = jnp.zeros(stage.shape[:2] + (16, LANES), F32)


def ahead(even, a, b):
    return jnp.where(even, a.astype(F32), b.astype(F32))


def behind(even, a, b):
    return jnp.where(even, b.astype(F32), a.astype(F32))


def own_blocks(
    flag_ref, vol_ref, dep_ref, row_a_ref, row_b_ref, edge_a_ref, edge_b_ref, w1_ref, tiles, parts, stage
):
    first_plane, row_even = flag_ref[0] == 0, flag_ref[1] == 0
    planes = vol_ref.shape[0]
    blocks = vol_ref.shape[2] // LANES
    clear_stage(stage)

    def place(n, target, own, a, b, keep):
        def kept(values):
            return values if keep is None else jnp.where(keep, values, 0.0)

        for m in range(blocks):
            lanes = slice(m * LANES, (m + 1) * LANES)
            stage[n, m, 8:24, :] = kept(own(lanes).astype(F32))
            stage[n, m, 4:8, :] = kept(behind(row_even, a(lanes), b(lanes)))
            stage[n, m, 24:28, :] = kept(ahead(row_even, a(lanes), b(lanes)))
        split_rows(stage.at[n], tiles, target, range(blocks))

    def place_own(pair, carry):
        for n in range(2):
            d = 2 * pair + n
            place(
                n, d + 3, lambda lanes: vol_ref[d, :, lanes],
                lambda lanes: row_a_ref[d, :, lanes], lambda lanes: row_b_ref[d, :, lanes], None,
            )
        return carry

    def place_halo(target, q, keep):
        place(
            target % 2, target,
            lambda lanes: jnp.concatenate([dep_ref[4 * q + g, :, lanes].astype(F32) for g in range(4)], axis=0),
            lambda lanes: edge_a_ref[q, :, lanes], lambda lanes: edge_b_ref[q, :, lanes], keep,
        )

    lax.fori_loop(0, planes // 2, place_own, 0)
    for q in range(3):
        place_halo(q, q + 1, jnp.logical_not(first_plane))
    for q in range(4):
        place_halo(planes + 3 + q, q, first_plane)
    tiles[:, planes + 7 :] = jnp.zeros((3, 2, blocks, 16, LANES), BF16)

    group = 5

    def product(step, carry):
        taps = []
        for a in range(3):
            for b in range(3):
                start = 2 * group * step + a
                found = [tiles[b, start + 2 * n].reshape(blocks * 16, LANES) for n in range(group)]
                taps.append(jnp.concatenate(found, axis=0))
        found = matmul(jnp.concatenate(taps, axis=1), w1_ref[...])
        parts[pl.ds(group * step, group)] = found.reshape(group, blocks, 16, 2 * LANES)
        return carry

    lax.fori_loop(0, parts.shape[0] // group, product, 0)


def body(
    flag_ref, place_ref, tiles, parts, dep_ref, row_a_ref, row_b_ref, edge_a_ref, edge_b_ref,
    side_a_ref, side_b_ref, col_a_ref, col_b_ref, cot_ref, w1_ref, w2_ref, w2b_ref, keep_ref, give_ref,
    out_ref, stage, rim_tiles, rim_parts, slopes, hid, pairs, ups, deltas, shifted,
):
    first_plane, row_even, col_even = flag_ref[0] == 0, flag_ref[1] == 0, flag_ref[2] == 0
    planes = tiles.shape[1] - 9
    blocks = tiles.shape[2]
    half_planes = planes // 4
    hidden_planes = planes // 2 + 3

    clear_stage(stage)

    def place(n, target, source, side_a, side_b, keep):
        for m, choose in ((0, behind), (1, ahead)):
            corners = choose(col_even, col_a_ref[source], col_b_ref[source])
            own = choose(col_even, side_a, side_b)
            if keep is not None:
                corners, own = jnp.where(keep, corners, 0.0), jnp.where(keep, own, 0.0)
            stage[n, m, 4:8, :] = corners[:4]
            stage[n, m, 8:24, :] = own
            stage[n, m, 24:28, :] = corners[4:]
        split_rows(stage.at[n], rim_tiles, target, range(2))

    def place_own(group, carry):
        for n in range(4):
            d = 4 * group + n
            place(n, d + 3, d, side_a_ref[d], side_b_ref[d], None)
        return carry

    def place_halo(target, q, keep):
        start = planes + 4 + 2 * q
        side_a = jnp.concatenate([col_a_ref[start].astype(F32), col_a_ref[start + 1].astype(F32)], axis=0)
        side_b = jnp.concatenate([col_b_ref[start].astype(F32), col_b_ref[start + 1].astype(F32)], axis=0)
        place(target % 4, target, planes + q, side_a, side_b, keep)

    lax.fori_loop(0, planes // 4, place_own, 0)
    for q in range(3):
        place_halo(q, q + 1, jnp.logical_not(first_plane))
    for q in range(4):
        place_halo(planes + 3 + q, q, first_plane)

    taps = []
    for a in range(3):
        for b in range(3):
            rows = [rim_tiles[b, 2 * i + a].reshape(32, LANES) for i in range(hidden_planes)]
            taps.append(jnp.concatenate(rows, axis=0))
    found = matmul(jnp.concatenate(taps, axis=1), w1_ref[...])
    rim_parts[...] = found.reshape(hidden_planes, 2, 16, 2 * LANES)

    def conv_one(i, carry):
        main, prev = parts[i, :, :, :LANES], parts[i, :, :, LANES:]
        rim, rim_prev = rim_parts[i, :, :, :LANES], rim_parts[i, 0:1, :, LANES:]
        blank = jnp.zeros((1, 16, LANES), F32)
        pre = jnp.concatenate([rim[:1], main, rim[1:]], axis=0) + jnp.concatenate([blank, rim_prev, prev], axis=0)
        square = pre * pre + 1.0
        inverse = lax.rsqrt(square)
        slopes[i] = 0.6 + 0.4 * (pre * inverse)
        hidden = (0.6 * pre + 0.4 * (square * inverse - 1.0)).astype(BF16).astype(F32)
        odd = hidden[:, 8:, :]
        hid[0, i] = pltpu.roll(odd, 1, 1)
        hid[1, i] = hidden[:, :8, :]
        hid[2, i] = odd
        return carry

    lax.fori_loop(0, hidden_planes, conv_one, 0)

    wide = (blocks + 2) * 16

    def pair(i, carry):
        for b in range(3):
            pairs[b, i] = jnp.concatenate([hid[b, i], hid[b, i + half_planes]], axis=1).astype(BF16)
        return carry

    lax.fori_loop(0, half_planes + 3, pair, 0)

    ups[...] = jnp.zeros_like(ups)
    for k in range(blocks):
        lanes = slice(k * LANES, (k + 1) * LANES)
        ups[0:half_planes, k, 1:5, :] = cot_ref[:, :, lanes].astype(F32)
        ups[half_planes, k, 1:5, :] = jnp.where(first_plane, dep_ref[16, :, lanes].astype(F32), 0.0)
        for g in range(half_planes // 4):
            tops = ahead(row_even, row_a_ref[planes + g, :, lanes], row_b_ref[planes + g, :, lanes])
            for n in range(4):
                ups[4 * g + n, k, 5:6, :] = tops[n : n + 1]
        corner = ahead(row_even, edge_a_ref[4, :, lanes], edge_b_ref[4, :, lanes])[:1]
        ups[half_planes, k, 5:6, :] = jnp.where(first_plane, corner, 0.0)
    for g in range(half_planes // 4):
        side = ahead(col_even, side_a_ref[planes + g], side_b_ref[planes + g])
        for n in range(4):
            ups[4 * g + n, blocks, 1:5, :] = side[4 * n : 4 * n + 4]
    tops = ahead(col_even, col_a_ref[planes + 12], col_b_ref[planes + 12])
    for n in range(half_planes):
        ups[n, blocks, 5:6, :] = tops[n : n + 1]
    beyond = jnp.where(first_plane, ahead(col_even, col_a_ref[planes + 13], col_b_ref[planes + 13]), 0.0)
    ups[half_planes, blocks, 1:6, :] = beyond[:5]

    quarter = half_planes // 2

    taps = []
    for a in range(3):
        for b in range(3):
            rows = [pairs[b, 2 * t + a].reshape(wide, LANES) for t in range(quarter + 1)]
            taps.append(jnp.concatenate(rows, axis=0))
    found = matmul(jnp.concatenate(taps, axis=1), w2_ref[...]).reshape(quarter + 1, blocks + 2, 16, 2 * LANES)
    for t in range(quarter + 1):
        pre = found[t, 1:, :, :LANES] + found[t, :-1, :, LANES:]
        slope = 0.6 + 0.4 * (pre * lax.rsqrt(pre * pre + 1.0))
        upstream = jnp.concatenate([ups[t], ups[t + quarter]], axis=1)
        delta = (upstream * slope).astype(BF16).astype(F32)
        moved = jnp.concatenate([pltpu.roll(delta[:, :8], 7, 1), pltpu.roll(delta[:, 8:], 7, 1)], axis=1)
        deltas[t] = delta
        shifted[t] = moved.astype(BF16)

    sublane = lax.broadcasted_iota(jnp.int32, (1, 1, 16, 1), 2) % 8
    own_rows = jnp.logical_and(sublane >= 1, sublane <= 4)

    def with_next(values, needed):
        values = values.T
        edge = jnp.zeros((LANES, values.shape[1] // blocks), values.dtype)
        here = jnp.concatenate([edge, values], axis=1)
        after = jnp.concatenate([values, edge], axis=1)[:needed]
        return jnp.concatenate([here, after], axis=0)

    own_delta = [jnp.where(own_rows[0], deltas[t, 0:blocks], 0.0) for t in range(quarter)]
    left = with_next(jnp.stack(own_delta, axis=1).reshape(blocks * quarter * 16, LANES), LANES).astype(BF16)

    def second_taps(tap):
        a, b = tap // 3, tap % 3
        found = [pairs[b, 2 * t + a, 0 : blocks + 1] for t in range(quarter)]
        return jnp.stack(found, axis=1).reshape((blocks + 1) * quarter * 16, LANES)

    for tap in range(0, 9, 2):
        right = [second_taps(x) for x in range(tap, min(tap + 2, 9))]
        found = matmul(left, jnp.concatenate(right, axis=1))
        for n in range(len(right)):
            row = (tap + n) * 192
            lanes = slice(n * LANES, (n + 1) * LANES)
            out_ref[row : row + 64, :] = found[LANES:, lanes].T[64:]
            out_ref[row + 64 : row + 192, :] = found[:LANES, lanes].T

    def pack(values):
        both = jnp.concatenate([values[:, :-1], values[:, 1:]], axis=3)
        return both.reshape(quarter * blocks * 16, 2 * LANES)

    plain = deltas[...].astype(BF16)
    moved = shifted[...]
    here, after = pack(plain[:-1]), pack(plain[1:])
    here_up, after_up = pack(moved[:-1]), pack(moved[1:])

    def back(terms):
        joined = jnp.concatenate([values for values, a, b in terms], axis=1)
        weights = jnp.concatenate([w2b_ref[3 * a + b] for values, a, b in terms], axis=0)
        return matmul(joined, weights).reshape(quarter, blocks, 16, LANES)

    rows = [
        [back([(here, 1, 1)]), back([(here_up, 1, 0), (here, 1, 2)])],
        [
            back([(after, 0, 1), (here, 2, 1)]),
            back([(after_up, 0, 0), (after, 0, 2), (here_up, 2, 0), (here, 2, 2)]),
        ],
    ]
    own_list = []
    for i in range(planes // 2):
        t, parity = i // 2, i % 2
        half = slice(0, 8) if t < quarter else slice(8, 16)
        back_one = jnp.concatenate([rows[parity][p][t % quarter, :, half, :] for p in (0, 1)], axis=1)
        delta = back_one * slopes[i + 1, 1 : blocks + 1]
        own_list.append(jnp.where(own_rows[0], delta, 0.0).astype(BF16))
    left_one = with_next(jnp.stack(own_list, axis=1).reshape(blocks * (planes // 2) * 16, LANES), 64)

    def first_taps(tap):
        a, b = tap // 3, tap % 3
        found = []
        for m in range(blocks + 1):
            for i in range(planes // 2):
                index = 2 * (i + 1) + a
                found.append(rim_tiles[b, index, 0] if m == 0 else tiles[b, index, m - 1])
        return jnp.concatenate(found, axis=0)

    grads = []
    for tap in range(0, 9, 2):
        right = [first_taps(x) for x in range(tap, min(tap + 2, 9))]
        found = matmul(left_one, jnp.concatenate(right, axis=1))
        for n in range(len(right)):
            main = found[:LANES, n * LANES : (n + 1) * LANES]
            prev = found[LANES:, n * LANES : (n + 1) * LANES]
            even = jnp.concatenate([prev[:, 96:], main[:64, :64]], axis=1)
            grads.append(even + main[64:, 32:])
    grads.append(jnp.zeros((64, FIRST_BLOCKS * LANES - 9 * 96), F32))
    first = jnp.concatenate(grads, axis=1)
    for n in range(FIRST_BLOCKS):
        row = SECOND_ROWS + 64 * n
        out_ref[row : row + 64, :] = first[:, n * LANES : (n + 1) * LANES]
    used = SECOND_ROWS + 64 * FIRST_BLOCKS
    if out_ref.shape[0] > used:
        out_ref[used:, :] = jnp.zeros((out_ref.shape[0] - used, LANES), F32)

    core, square = place_ref[0], place_ref[1]
    squares, size = keep_ref.shape[0], keep_ref.shape[1]
    for n in range(squares):
        for ref, half in ((keep_ref, core), (give_ref, 1 - core)):
            start = pl.multiple_of((half * squares + (square ^ n)) * size, 8)
            ref[n] = out_ref[pl.ds(start, size), :].astype(ref.dtype)


def unpack(place_ref, keep_ref, got_ref, g1_hbm, g2_hbm, sums, first, sent):
    core, square = place_ref[0], place_ref[1]
    squares, size = keep_ref.shape[0], keep_ref.shape[1]
    for n in range(squares):
        for ref, half in ((keep_ref, core), (got_ref, 1 - core)):
            start = pl.multiple_of((half * squares + (square ^ n)) * size, 8)
            sums[pl.ds(start, size), :] = ref[n].astype(F32)
    second = pltpu.make_async_copy(sums.at[pl.ds(0, SECOND_ROWS)], g2_hbm, sent.at[0])
    second.start()
    found = [sums[SECOND_ROWS + 64 * n : SECOND_ROWS + 64 * (n + 1), :] for n in range(FIRST_BLOCKS)]
    first[...] = jnp.concatenate(found, axis=1)[:, : first.shape[1]]
    copy = pltpu.make_async_copy(first, g1_hbm, sent.at[1])
    copy.start()
    copy.wait()
    second.wait()


def local_grads(flags, place, squares, volume, faces, corners, cotangent, weights):
    planes = volume.shape[0]
    blocks = volume.shape[2] // LANES
    hidden_planes = planes // 2 + 3
    out_planes = planes // 4
    unit = 2 * squares * 16
    rows = -(-(SECOND_ROWS + 64 * FIRST_BLOCKS) // unit) * unit
    whole = pl.BlockSpec(memory_space=pltpu.VMEM)
    smem = pl.BlockSpec(memory_space=pltpu.SMEM)
    dep, row_a, row_b, edge_a, edge_b = faces
    tiles, parts = pl.pallas_call(
        own_blocks,
        out_shape=[
            jax.ShapeDtypeStruct((3, planes + 9, blocks, 16, LANES), BF16),
            jax.ShapeDtypeStruct((hidden_planes + 1, blocks, 16, 2 * LANES), F32),
        ],
        in_specs=[smem] + [whole] * 7,
        out_specs=[whole] * 2,
        scratch_shapes=[pltpu.VMEM((2, blocks, 40, LANES), F32)],
        compiler_params=pltpu.CompilerParams(vmem_limit_bytes=16 * 1024 * 1024),
        cost_estimate=pl.CostEstimate(flops=2 * 10**9, bytes_accessed=10**7, transcendentals=0),
    )(flags, volume, *faces, weights[0])
    scratch = [
        pltpu.VMEM((rows, LANES), F32),
        pltpu.VMEM((4, 2, 40, LANES), F32),
        pltpu.VMEM((3, planes + 7, 2, 16, LANES), BF16),
        pltpu.VMEM((hidden_planes, 2, 16, 2 * LANES), F32),
        pltpu.VMEM((hidden_planes, blocks + 2, 16, LANES), F32),
        pltpu.VMEM((3, hidden_planes, blocks + 2, 8, LANES), F32),
        pltpu.VMEM((3, out_planes + 3, blocks + 2, 16, LANES), BF16),
        pltpu.VMEM((out_planes + 1, blocks + 1, 8, LANES), F32),
        pltpu.VMEM((out_planes // 2 + 1, blocks + 1, 16, LANES), F32),
        pltpu.VMEM((out_planes // 2 + 1, blocks + 1, 16, LANES), BF16),
    ]
    operands = (tiles, parts, *faces, *corners, cotangent, *weights)
    return pl.pallas_call(
        body,
        out_shape=[jax.ShapeDtypeStruct((squares, rows // (2 * squares), LANES), dtype) for dtype in (F32, BF16)],
        in_specs=[smem] * 2 + [whole] * len(operands),
        out_specs=[whole] * 2,
        scratch_shapes=scratch,
        compiler_params=pltpu.CompilerParams(vmem_limit_bytes=28 * 1024 * 1024),
        cost_estimate=pl.CostEstimate(flops=4 * 10**9, bytes_accessed=10**7, transcendentals=0),
    )(flags, place, *operands)


def shards(volume, first_weight, second_weight, cotangent):
    half = lax.axis_index("depth")
    row, col = lax.axis_index("row"), lax.axis_index("col")
    rows, cols = lax.axis_size("row"), lax.axis_size("col")
    inner = [jnp.logical_and(i > 0, i < n - 1).astype(jnp.int32) for i, n in ((row, rows), (col, cols))]
    flags = jnp.stack([half, row % 2, col % 2, *inner])
    whole = pl.BlockSpec(memory_space=pltpu.VMEM)
    smem = pl.BlockSpec(memory_space=pltpu.SMEM)
    small = pltpu.CompilerParams(vmem_limit_bytes=12 * 1024 * 1024)
    planes, high, width = volume.shape
    groups = planes + cotangent.shape[0] // 4
    in_hbm = pl.BlockSpec(memory_space=pltpu.HBM)

    def stay(argument):
        return pltpu.with_memory_space_constraint(argument, pltpu.HBM)

    arguments = (volume, cotangent, first_weight, second_weight.T)
    shapes = [argument.shape for argument in arguments] + [(17, 4, width)]
    volume, cotangent, first_taps, second_taps, dep = pl.pallas_call(
        bring,
        out_shape=[jax.ShapeDtypeStruct(shape, BF16) for shape in shapes],
        in_specs=[smem] + [in_hbm] * 4,
        out_specs=[whole] * len(shapes),
        scratch_shapes=[pltpu.SemaphoreType.DMA((6,))],
        compiler_params=small,
    )(flags, *[stay(argument) for argument in arguments])
    row_b, row_a = pl.pallas_call(
        pack_rows,
        out_shape=[jax.ShapeDtypeStruct((groups, 4, width), BF16)] * 2,
        in_specs=[smem] + [whole] * 2,
        out_specs=[whole] * 2,
        compiler_params=small,
    )(flags, volume, cotangent)

    def to_col(block, kind):
        return lax.ppermute(block, ("row", "col"), pairs_of_lines(rows, cols, kind))

    dep = lax.ppermute(dep, "depth", [(0, 1), (1, 0)])
    route = []
    for i, j in pairs_on_line(rows, 1):
        route += [((d * rows + i) * cols + c, (d * rows + j) * cols + (c ^ 1 if i == j else c)) for d in (0, 1) for c in range(cols)]
    row_b = lax.ppermute(row_b, ("depth", "row", "col"), route)
    row_a = lax.ppermute(row_a, "row", pairs_on_line(rows, 0))
    row_a, volume, cotangent = lax.optimization_barrier((row_a, volume, cotangent))
    side_a, side_b = pl.pallas_call(
        pack_sides,
        out_shape=[jax.ShapeDtypeStruct((groups, high, LANES), BF16)] * 2,
        in_specs=[smem] + [whole] * 2,
        out_specs=[whole] * 2,
        compiler_params=small,
    )(flags, volume, cotangent)
    side_a, side_b = to_col(side_a, 0), to_col(side_b, 1)
    low, top = [jnp.concatenate([dep[n : n + 1] for n in (*range(k, 16, 4), 16)], axis=0) for k in (0, 3)]
    even, ends = row % 2 == 0, jnp.logical_or(row == 0, row == rows - 1)
    edge_a = jnp.where(even, top, low)
    edge_b = jnp.where(ends, 0, jnp.where(even, low, top))
    edge_a = lax.ppermute(edge_a, "row", pairs_on_line(rows, 0))
    edge_b = lax.ppermute(edge_b, ("depth", "row"), pairs_of_lines(2, rows, 1))
    weights = pl.pallas_call(
        bands,
        out_shape=[jax.ShapeDtypeStruct(shape, BF16) for shape in ((1152, 256), (1152, 256), (9, 256, 128))],
        in_specs=[whole] * 2,
        out_specs=[whole] * 3,
        compiler_params=small,
    )(first_taps, second_taps)
    row_b, weights = lax.optimization_barrier((row_b, weights))
    col_a, col_b = pl.pallas_call(
        pack_corners,
        out_shape=[jax.ShapeDtypeStruct((planes + 14, 8, LANES), BF16)] * 2,
        in_specs=[smem] + [whole] * 5,
        out_specs=[whole] * 2,
        compiler_params=small,
    )(flags, row_b, row_a, dep, edge_a, edge_b)
    col_a, col_b, volume = lax.optimization_barrier((col_a, col_b, volume))
    col_a, col_b = to_col(col_a, 0), to_col(col_b, 1)

    spot = lax.axis_index(("depth", "row"))
    squares = lax.axis_size(("depth", "row")) // 2
    where = jnp.stack([spot % 2, spot // 2])
    faces, corners = (dep, row_a, row_b, edge_a, edge_b), (side_a, side_b, col_a, col_b)
    keep, give = local_grads(flags, where, squares, volume, faces, corners, cotangent, weights)

    def to_square(block, n):
        route = [(2 * i + c, 2 * (i ^ n) + c) for i in range(squares) for c in (0, 1)]
        return lax.ppermute(block, ("depth", "row"), route)

    def to_core(block):
        return lax.ppermute(block, ("depth", "row"), [(i, i ^ 1) for i in range(2 * squares)])

    def along_col(block, n):
        return lax.ppermute(block, "col", [(i, i ^ n) for i in range(cols)])

    both = keep + to_core(give).astype(F32)
    near = both.astype(BF16)
    share = add_up(both[0], *[to_square(near[n], n) for n in range(1, squares)])
    share = add_up(share, *[along_col(share, n) for n in range(1, cols)])
    mine = jnp.stack([share] + [to_square(share, n) for n in range(1, squares)])
    other = to_core(mine)
    grads = [jax.ShapeDtypeStruct(shape, F32) for shape in (first_weight.shape, second_weight.shape[::-1])]
    first_grad, second_grad = pl.pallas_call(
        unpack,
        out_shape=grads,
        in_specs=[smem] + [whole] * 2,
        out_specs=[in_hbm] * 2,
        scratch_shapes=[
            pltpu.VMEM((mine.shape[0] * mine.shape[1] * 2, LANES), F32),
            pltpu.VMEM(first_weight.shape, F32),
            pltpu.SemaphoreType.DMA((2,)),
        ],
        compiler_params=small,
    )(where, mine, other)
    return first_grad, second_grad.T


def solution(mesh):
    placed = (P("depth", "row", "col"), P(), P(), P("depth", "row", "col"))
    return jax.shard_map(shards, mesh=mesh, in_specs=placed, out_specs=(P(), P()), check_vma=False)
```

```python
import jax
import jax.numpy as jnp
from jax import lax
from jax.experimental import pallas as pl
from jax.experimental.pallas import tpu as pltpu
from jax.sharding import PartitionSpec as P

LANES = 128
SECOND_ROWS = 27 * 64
FIRST_BLOCKS = 7
F32 = jnp.float32
BF16 = jnp.bfloat16


def pairs_on_line(count, kind):
    firsts = range(kind, count - 1, 2)
    swapped = [(i, i + 1) for i in firsts] + [(i + 1, i) for i in firsts]
    met = {i for i, j in swapped}
    return swapped + [(i, i) for i in range(count) if i not in met]


def pairs_of_lines(lines, count, kind):
    route = []
    for line in range(lines):
        for i, j in pairs_on_line(count, kind):
            route.append((line * count + i, (line ^ 1 if i == j else line) * count + j))
    return route


def add_up(*terms):
    terms = [term.astype(F32) for term in terms]
    while len(terms) > 1:
        terms = [terms[n] + terms[n + 1] for n in range(0, len(terms), 2)]
    return terms[0].astype(BF16)


def matmul(left, right):
    return lax.dot_general(left, right, (((1,), (0,)), ((), ())), preferred_element_type=F32)


def bring(
    flag_ref, vol_hbm, cot_hbm, first_hbm, second_hbm, vol_ref, cot_ref, first_ref, second_ref, dep_ref, arrived
):
    first_plane = flag_ref[0] == 0
    planes, width = vol_ref.shape[0], vol_ref.shape[2]
    inner = pl.ds(4, planes - 8)
    copies = [pltpu.make_async_copy(cot_hbm, cot_ref, arrived.at[0])]
    for n, part in enumerate((pl.ds(0, 4), pl.ds(planes - 4, 4), inner)):
        copies.append(pltpu.make_async_copy(vol_hbm.at[part], vol_ref.at[part], arrived.at[1 + n]))
    copies.append(pltpu.make_async_copy(first_hbm, first_ref, arrived.at[4]))
    copies.append(pltpu.make_async_copy(second_hbm, second_ref, arrived.at[5]))
    for copy in copies:
        copy.start()
    for copy in copies[:3]:
        copy.wait()
    dep_ref[16] = cot_ref[0]
    for q in range(4):
        for m in range(width // LANES):
            lanes = slice(m * LANES, (m + 1) * LANES)
            last, start = vol_ref[planes - 4 + q, :, lanes].astype(F32), vol_ref[q, :, lanes].astype(F32)
            block = jnp.where(first_plane, last, start)
            for g in range(4):
                dep_ref[4 * q + g, :, lanes] = block[4 * g : 4 * g + 4].astype(BF16)
    for copy in copies[3:]:
        copy.wait()


def pack_rows(flag_ref, vol_ref, cot_ref, row_b_ref, row_a_ref):
    row_even, row_inner = flag_ref[1] == 0, flag_ref[3] != 0
    planes, high, width = vol_ref.shape
    cots = cot_ref.shape[0]

    def plane(d, carry):
        for m in range(width // LANES):
            lanes = slice(m * LANES, (m + 1) * LANES)
            block = vol_ref[d, :, lanes].astype(F32)
            low, top = block[:4], block[high - 4 :]
            row_a_ref[d, :, lanes] = jnp.where(row_even, top, low).astype(BF16)
            row_b_ref[d, :, lanes] = jnp.where(row_inner, jnp.where(row_even, low, top), 0.0).astype(BF16)
        return carry

    lax.fori_loop(0, planes, plane, 0, unroll=4)
    for g in range(cots // 4):
        tops = jnp.concatenate([cot_ref[4 * g + n].astype(F32)[:1] for n in range(4)], axis=0)
        row_a_ref[planes + g] = tops.astype(BF16)
        row_b_ref[planes + g] = jnp.where(row_inner, tops, 0.0).astype(BF16)


def pack_sides(flag_ref, vol_ref, cot_ref, col_a_ref, col_b_ref):
    col_even, col_inner = flag_ref[2] == 0, flag_ref[4] != 0
    planes, high, width = vol_ref.shape
    cots = cot_ref.shape[0]
    for g in range(cots // 4):
        side = jnp.concatenate([cot_ref[4 * g + n, :, :LANES].astype(F32) for n in range(4)], axis=0)
        col_a_ref[planes + g] = side.astype(BF16)
        col_b_ref[planes + g] = jnp.where(col_inner, side, 0.0).astype(BF16)

    def plane(d, carry):
        left = vol_ref[d, :, :LANES].astype(F32)
        right = vol_ref[d, :, width - LANES :].astype(F32)
        col_a_ref[d] = jnp.where(col_even, right, left).astype(BF16)
        col_b_ref[d] = jnp.where(col_inner, jnp.where(col_even, left, right), 0.0).astype(BF16)
        return carry

    lax.fori_loop(0, planes, plane, 0, unroll=4)


def pack_corners(flag_ref, row_b_ref, row_a_ref, dep_ref, edge_a_ref, edge_b_ref, col_a_ref, col_b_ref):
    row_even, col_even, col_inner = flag_ref[1] == 0, flag_ref[2] == 0, flag_ref[4] != 0
    width = dep_ref.shape[2]
    groups = row_a_ref.shape[0]
    planes = (groups * 16) // 17
    faces = (slice(0, LANES), slice(width - LANES, width))

    def store(n, left, right):
        col_a_ref[n] = jnp.where(col_even, right, left).astype(BF16)
        col_b_ref[n] = jnp.where(col_inner, jnp.where(col_even, left, right), 0.0).astype(BF16)

    def lower_upper(a_ref, b_ref, source, target):
        values = []
        for lanes in faces:
            a, b = a_ref[source, :, lanes].astype(F32), b_ref[source, :, lanes].astype(F32)
            values.append(jnp.concatenate([jnp.where(row_even, b, a), jnp.where(row_even, a, b)], axis=0))
        store(target, *values)

    def plane(d, carry):
        lower_upper(row_a_ref, row_b_ref, d, d)
        return carry

    lax.fori_loop(0, planes, plane, 0, unroll=4)
    for q in range(4):
        lower_upper(edge_a_ref, edge_b_ref, q, planes + q)
        for n in range(2):
            units = range(4 * q + 2 * n, 4 * q + 2 * n + 2)
            store(
                planes + 4 + 2 * q + n,
                *[jnp.concatenate([dep_ref[u, :, lanes].astype(F32) for u in units], axis=0) for lanes in faces],
            )
    lanes = faces[0]
    tops = [
        jnp.where(row_even, row_a_ref[g, :, lanes].astype(F32), row_b_ref[g, :, lanes].astype(F32))
        for g in range(planes, groups)
    ]
    corner = jnp.where(row_even, edge_a_ref[4, :, lanes].astype(F32), edge_b_ref[4, :, lanes].astype(F32))
    own = dep_ref[16, :, lanes].astype(F32)
    for n, values in enumerate((jnp.concatenate(tops, axis=0), jnp.concatenate([own, corner], axis=0))):
        col_a_ref[planes + 12 + n] = values.astype(BF16)
        col_b_ref[planes + 12 + n] = jnp.where(col_inner, values, 0.0).astype(BF16)


def bands(first_ref, second_ref, w1_ref, w2_ref, w2b_ref):
    out_chan = first_ref.shape[0]
    first = first_ref[...].astype(F32)
    blank = jnp.zeros((out_chan, LANES), F32)
    for tap in range(9):
        rows = slice(tap * LANES, (tap + 1) * LANES)
        taps = first[:, tap * 96 : (tap + 1) * 96]
        main_even = jnp.concatenate([taps[:, 32:], blank[:, :64]], axis=1)
        main_odd = jnp.concatenate([blank[:, :32], taps], axis=1)
        prev_even = jnp.concatenate([blank[:, :96], taps[:, :32]], axis=1)
        w1_ref[rows] = jnp.concatenate([main_even, main_odd, prev_even, blank], axis=0).T.astype(BF16)
        main = second_ref[tap * 192 + 64 : (tap + 1) * 192, :]
        prev = jnp.concatenate([jnp.zeros((64, LANES), BF16), second_ref[tap * 192 : tap * 192 + 64, :]], axis=0)
        both = jnp.concatenate([main, prev], axis=1)
        w2_ref[rows] = both
        w2b_ref[tap] = both.astype(F32).T.astype(BF16)


def split_rows(stage, tiles, index, blocks):
    for m in blocks:
        rows = [stage[m, pl.ds(4 + s, 8, stride=4), :] for s in range(-1, 4)]
        for b in range(3):
            tiles[b, index, m] = jnp.concatenate([rows[b], rows[b + 2]], axis=0).astype(BF16)


def clear_stage(stage):
    stage[:, :, 0:8, :] = jnp.zeros(stage.shape[:2] + (8, LANES), F32)
    stage[:, :, 24:40, :] = jnp.zeros(stage.shape[:2] + (16, LANES), F32)


def ahead(even, a, b):
    return jnp.where(even, a.astype(F32), b.astype(F32))


def behind(even, a, b):
    return jnp.where(even, b.astype(F32), a.astype(F32))


def own_blocks(
    flag_ref, vol_ref, dep_ref, row_a_ref, row_b_ref, edge_a_ref, edge_b_ref, w1_ref, tiles, parts, stage
):
    first_plane, row_even = flag_ref[0] == 0, flag_ref[1] == 0
    planes = vol_ref.shape[0]
    blocks = vol_ref.shape[2] // LANES
    clear_stage(stage)

    def place(n, target, own, a, b, keep):
        def kept(values):
            return values if keep is None else jnp.where(keep, values, 0.0)

        for m in range(blocks):
            lanes = slice(m * LANES, (m + 1) * LANES)
            stage[n, m, 8:24, :] = kept(own(lanes).astype(F32))
            stage[n, m, 4:8, :] = kept(behind(row_even, a(lanes), b(lanes)))
            stage[n, m, 24:28, :] = kept(ahead(row_even, a(lanes), b(lanes)))
        split_rows(stage.at[n], tiles, target, range(blocks))

    def place_own(group, carry):
        for n in range(4):
            d = 4 * group + n
            place(
                n, d + 3, lambda lanes: vol_ref[d, :, lanes],
                lambda lanes: row_a_ref[d, :, lanes], lambda lanes: row_b_ref[d, :, lanes], None,
            )
        return carry

    def place_halo(target, q, keep):
        place(
            target % 4, target,
            lambda lanes: jnp.concatenate([dep_ref[4 * q + g, :, lanes].astype(F32) for g in range(4)], axis=0),
            lambda lanes: edge_a_ref[q, :, lanes], lambda lanes: edge_b_ref[q, :, lanes], keep,
        )

    lax.fori_loop(0, planes // 4, place_own, 0)
    for q in range(3):
        place_halo(q, q + 1, jnp.logical_not(first_plane))
    for q in range(4):
        place_halo(planes + 3 + q, q, first_plane)
    tiles[:, planes + 7 :] = jnp.zeros((3, 2, blocks, 16, LANES), BF16)

    group = 5

    def product(step, carry):
        taps = []
        for a in range(3):
            for b in range(3):
                start = 2 * group * step + a
                found = [tiles[b, start + 2 * n].reshape(blocks * 16, LANES) for n in range(group)]
                taps.append(jnp.concatenate(found, axis=0))
        found = matmul(jnp.concatenate(taps, axis=1), w1_ref[...])
        parts[pl.ds(group * step, group)] = found.reshape(group, blocks, 16, 2 * LANES)
        return carry

    lax.fori_loop(0, parts.shape[0] // group, product, 0)


def body(
    flag_ref, place_ref, tiles, parts, dep_ref, row_a_ref, row_b_ref, edge_a_ref, edge_b_ref,
    side_a_ref, side_b_ref, col_a_ref, col_b_ref, cot_ref, w1_ref, w2_ref, w2b_ref, keep_ref, give_ref,
    out_ref, stage, rim_tiles, rim_parts, slopes, hid, pairs, ups, deltas, shifted,
):
    first_plane, row_even, col_even = flag_ref[0] == 0, flag_ref[1] == 0, flag_ref[2] == 0
    planes = tiles.shape[1] - 9
    blocks = tiles.shape[2]
    half_planes = planes // 4
    hidden_planes = planes // 2 + 3

    clear_stage(stage)

    def place(n, target, source, side_a, side_b, keep):
        for m, choose in ((0, behind), (1, ahead)):
            corners = choose(col_even, col_a_ref[source], col_b_ref[source])
            own = choose(col_even, side_a, side_b)
            if keep is not None:
                corners, own = jnp.where(keep, corners, 0.0), jnp.where(keep, own, 0.0)
            stage[n, m, 4:8, :] = corners[:4]
            stage[n, m, 8:24, :] = own
            stage[n, m, 24:28, :] = corners[4:]
        split_rows(stage.at[n], rim_tiles, target, range(2))

    def place_own(group, carry):
        for n in range(4):
            d = 4 * group + n
            place(n, d + 3, d, side_a_ref[d], side_b_ref[d], None)
        return carry

    def place_halo(target, q, keep):
        start = planes + 4 + 2 * q
        side_a = jnp.concatenate([col_a_ref[start].astype(F32), col_a_ref[start + 1].astype(F32)], axis=0)
        side_b = jnp.concatenate([col_b_ref[start].astype(F32), col_b_ref[start + 1].astype(F32)], axis=0)
        place(target % 4, target, planes + q, side_a, side_b, keep)

    lax.fori_loop(0, planes // 4, place_own, 0, unroll=2)
    for q in range(3):
        place_halo(q, q + 1, jnp.logical_not(first_plane))
    for q in range(4):
        place_halo(planes + 3 + q, q, first_plane)

    taps = []
    for a in range(3):
        for b in range(3):
            rows = [rim_tiles[b, 2 * i + a].reshape(32, LANES) for i in range(hidden_planes)]
            taps.append(jnp.concatenate(rows, axis=0))
    found = matmul(jnp.concatenate(taps, axis=1), w1_ref[...])
    rim_parts[...] = found.reshape(hidden_planes, 2, 16, 2 * LANES)

    def conv_one(i, carry):
        main, prev = parts[i, :, :, :LANES], parts[i, :, :, LANES:]
        rim, rim_prev = rim_parts[i, :, :, :LANES], rim_parts[i, 0:1, :, LANES:]
        blank = jnp.zeros((1, 16, LANES), F32)
        pre = jnp.concatenate([rim[:1], main, rim[1:]], axis=0) + jnp.concatenate([blank, rim_prev, prev], axis=0)
        square = pre * pre + 1.0
        inverse = lax.rsqrt(square)
        slopes[i] = 0.6 + 0.4 * (pre * inverse)
        hidden = (0.6 * pre + 0.4 * (square * inverse - 1.0)).astype(BF16).astype(F32)
        odd = hidden[:, 8:, :]
        hid[0, i] = pltpu.roll(odd, 1, 1)
        hid[1, i] = hidden[:, :8, :]
        hid[2, i] = odd
        return carry

    lax.fori_loop(0, hidden_planes, conv_one, 0, unroll=True)

    wide = (blocks + 2) * 16

    def pair(i, carry):
        for b in range(3):
            pairs[b, i] = jnp.concatenate([hid[b, i], hid[b, i + half_planes]], axis=1).astype(BF16)
        return carry

    lax.fori_loop(0, half_planes + 3, pair, 0, unroll=True)

    ups[...] = jnp.zeros_like(ups)
    for k in range(blocks):
        lanes = slice(k * LANES, (k + 1) * LANES)
        ups[0:half_planes, k, 1:5, :] = cot_ref[:, :, lanes].astype(F32)
        ups[half_planes, k, 1:5, :] = jnp.where(first_plane, dep_ref[16, :, lanes].astype(F32), 0.0)
        for g in range(half_planes // 4):
            tops = ahead(row_even, row_a_ref[planes + g, :, lanes], row_b_ref[planes + g, :, lanes])
            for n in range(4):
                ups[4 * g + n, k, 5:6, :] = tops[n : n + 1]
        corner = ahead(row_even, edge_a_ref[4, :, lanes], edge_b_ref[4, :, lanes])[:1]
        ups[half_planes, k, 5:6, :] = jnp.where(first_plane, corner, 0.0)
    for g in range(half_planes // 4):
        side = ahead(col_even, side_a_ref[planes + g], side_b_ref[planes + g])
        for n in range(4):
            ups[4 * g + n, blocks, 1:5, :] = side[4 * n : 4 * n + 4]
    tops = ahead(col_even, col_a_ref[planes + 12], col_b_ref[planes + 12])
    for n in range(half_planes):
        ups[n, blocks, 5:6, :] = tops[n : n + 1]
    beyond = jnp.where(first_plane, ahead(col_even, col_a_ref[planes + 13], col_b_ref[planes + 13]), 0.0)
    ups[half_planes, blocks, 1:6, :] = beyond[:5]

    quarter = half_planes // 2

    taps = []
    for a in range(3):
        for b in range(3):
            rows = [pairs[b, 2 * t + a].reshape(wide, LANES) for t in range(quarter + 1)]
            taps.append(jnp.concatenate(rows, axis=0))
    found = matmul(jnp.concatenate(taps, axis=1), w2_ref[...]).reshape(quarter + 1, blocks + 2, 16, 2 * LANES)
    for t in range(quarter + 1):
        pre = found[t, 1:, :, :LANES] + found[t, :-1, :, LANES:]
        slope = 0.6 + 0.4 * (pre * lax.rsqrt(pre * pre + 1.0))
        upstream = jnp.concatenate([ups[t], ups[t + quarter]], axis=1)
        delta = (upstream * slope).astype(BF16).astype(F32)
        moved = jnp.concatenate([pltpu.roll(delta[:, :8], 7, 1), pltpu.roll(delta[:, 8:], 7, 1)], axis=1)
        deltas[t] = delta
        shifted[t] = moved.astype(BF16)

    sublane = lax.broadcasted_iota(jnp.int32, (1, 1, 16, 1), 2) % 8
    own_rows = jnp.logical_and(sublane >= 1, sublane <= 4)

    def with_next(values, needed):
        values = values.T
        edge = jnp.zeros((LANES, values.shape[1] // blocks), values.dtype)
        here = jnp.concatenate([edge, values], axis=1)
        after = jnp.concatenate([values, edge], axis=1)[:needed]
        return jnp.concatenate([here, after], axis=0)

    own_delta = [jnp.where(own_rows[0], deltas[t, 0:blocks], 0.0) for t in range(quarter)]
    left = with_next(jnp.stack(own_delta, axis=1).reshape(blocks * quarter * 16, LANES), LANES).astype(BF16)

    def second_taps(tap):
        a, b = tap // 3, tap % 3
        found = [pairs[b, 2 * t + a, 0 : blocks + 1] for t in range(quarter)]
        return jnp.stack(found, axis=1).reshape((blocks + 1) * quarter * 16, LANES)

    for tap in range(0, 9, 2):
        right = [second_taps(x) for x in range(tap, min(tap + 2, 9))]
        found = matmul(left, jnp.concatenate(right, axis=1))
        for n in range(len(right)):
            row = (tap + n) * 192
            lanes = slice(n * LANES, (n + 1) * LANES)
            out_ref[row : row + 64, :] = found[LANES:, lanes].T[64:]
            out_ref[row + 64 : row + 192, :] = found[:LANES, lanes].T

    def pack(values):
        both = jnp.concatenate([values[:, :-1], values[:, 1:]], axis=3)
        return both.reshape(quarter * blocks * 16, 2 * LANES)

    plain = deltas[...].astype(BF16)
    moved = shifted[...]
    here, after = pack(plain[:-1]), pack(plain[1:])
    here_up, after_up = pack(moved[:-1]), pack(moved[1:])

    def back(terms):
        joined = jnp.concatenate([values for values, a, b in terms], axis=1)
        weights = jnp.concatenate([w2b_ref[3 * a + b] for values, a, b in terms], axis=0)
        return matmul(joined, weights).reshape(quarter, blocks, 16, LANES)

    rows = [
        [back([(here, 1, 1)]), back([(here_up, 1, 0), (here, 1, 2)])],
        [
            back([(after, 0, 1), (here, 2, 1)]),
            back([(after_up, 0, 0), (after, 0, 2), (here_up, 2, 0), (here, 2, 2)]),
        ],
    ]
    own_list = []
    for i in range(planes // 2):
        t, parity = i // 2, i % 2
        half = slice(0, 8) if t < quarter else slice(8, 16)
        back_one = jnp.concatenate([rows[parity][p][t % quarter, :, half, :] for p in (0, 1)], axis=1)
        delta = back_one * slopes[i + 1, 1 : blocks + 1]
        own_list.append(jnp.where(own_rows[0], delta, 0.0).astype(BF16))
    left_one = with_next(jnp.stack(own_list, axis=1).reshape(blocks * (planes // 2) * 16, LANES), 64)

    def first_taps(tap):
        a, b = tap // 3, tap % 3
        found = []
        for m in range(blocks + 1):
            for i in range(planes // 2):
                index = 2 * (i + 1) + a
                found.append(rim_tiles[b, index, 0] if m == 0 else tiles[b, index, m - 1])
        return jnp.concatenate(found, axis=0)

    grads = []
    for tap in range(0, 9, 2):
        right = [first_taps(x) for x in range(tap, min(tap + 2, 9))]
        found = matmul(left_one, jnp.concatenate(right, axis=1))
        for n in range(len(right)):
            main = found[:LANES, n * LANES : (n + 1) * LANES]
            prev = found[LANES:, n * LANES : (n + 1) * LANES]
            even = jnp.concatenate([prev[:, 96:], main[:64, :64]], axis=1)
            grads.append(even + main[64:, 32:])
    grads.append(jnp.zeros((64, FIRST_BLOCKS * LANES - 9 * 96), F32))
    first = jnp.concatenate(grads, axis=1)
    for n in range(FIRST_BLOCKS):
        row = SECOND_ROWS + 64 * n
        out_ref[row : row + 64, :] = first[:, n * LANES : (n + 1) * LANES]
    used = SECOND_ROWS + 64 * FIRST_BLOCKS
    if out_ref.shape[0] > used:
        out_ref[used:, :] = jnp.zeros((out_ref.shape[0] - used, LANES), F32)

    core, square = place_ref[0], place_ref[1]
    squares, size = keep_ref.shape[0], keep_ref.shape[1]
    for n in range(squares):
        for ref, half in ((keep_ref, core), (give_ref, 1 - core)):
            start = pl.multiple_of((half * squares + (square ^ n)) * size, 8)
            ref[n] = out_ref[pl.ds(start, size), :].astype(ref.dtype)


def unpack(place_ref, keep_ref, got_ref, g1_hbm, g2_hbm, sums, first, sent):
    core, square = place_ref[0], place_ref[1]
    squares, size = keep_ref.shape[0], keep_ref.shape[1]
    for n in range(squares):
        for ref, half in ((keep_ref, core), (got_ref, 1 - core)):
            start = pl.multiple_of((half * squares + (square ^ n)) * size, 8)
            sums[pl.ds(start, size), :] = ref[n].astype(F32)
    second = pltpu.make_async_copy(sums.at[pl.ds(0, SECOND_ROWS)], g2_hbm, sent.at[0])
    second.start()
    found = [sums[SECOND_ROWS + 64 * n : SECOND_ROWS + 64 * (n + 1), :] for n in range(FIRST_BLOCKS)]
    first[...] = jnp.concatenate(found, axis=1)[:, : first.shape[1]]
    copy = pltpu.make_async_copy(first, g1_hbm, sent.at[1])
    copy.start()
    copy.wait()
    second.wait()


def local_grads(flags, place, squares, volume, faces, corners, cotangent, weights):
    planes = volume.shape[0]
    blocks = volume.shape[2] // LANES
    hidden_planes = planes // 2 + 3
    out_planes = planes // 4
    unit = 2 * squares * 16
    rows = -(-(SECOND_ROWS + 64 * FIRST_BLOCKS) // unit) * unit
    whole = pl.BlockSpec(memory_space=pltpu.VMEM)
    smem = pl.BlockSpec(memory_space=pltpu.SMEM)
    dep, row_a, row_b, edge_a, edge_b = faces
    tiles, parts = pl.pallas_call(
        own_blocks,
        out_shape=[
            jax.ShapeDtypeStruct((3, planes + 9, blocks, 16, LANES), BF16),
            jax.ShapeDtypeStruct((hidden_planes + 1, blocks, 16, 2 * LANES), F32),
        ],
        in_specs=[smem] + [whole] * 7,
        out_specs=[whole] * 2,
        scratch_shapes=[pltpu.VMEM((4, blocks, 40, LANES), F32)],
        compiler_params=pltpu.CompilerParams(vmem_limit_bytes=16 * 1024 * 1024),
        cost_estimate=pl.CostEstimate(flops=2 * 10**9, bytes_accessed=10**7, transcendentals=0),
    )(flags, volume, *faces, weights[0])
    scratch = [
        pltpu.VMEM((rows, LANES), F32),
        pltpu.VMEM((4, 2, 40, LANES), F32),
        pltpu.VMEM((3, planes + 7, 2, 16, LANES), BF16),
        pltpu.VMEM((hidden_planes, 2, 16, 2 * LANES), F32),
        pltpu.VMEM((hidden_planes, blocks + 2, 16, LANES), F32),
        pltpu.VMEM((3, hidden_planes, blocks + 2, 8, LANES), F32),
        pltpu.VMEM((3, out_planes + 3, blocks + 2, 16, LANES), BF16),
        pltpu.VMEM((out_planes + 1, blocks + 1, 8, LANES), F32),
        pltpu.VMEM((out_planes // 2 + 1, blocks + 1, 16, LANES), F32),
        pltpu.VMEM((out_planes // 2 + 1, blocks + 1, 16, LANES), BF16),
    ]
    operands = (tiles, parts, *faces, *corners, cotangent, *weights)
    return pl.pallas_call(
        body,
        out_shape=[jax.ShapeDtypeStruct((squares, rows // (2 * squares), LANES), dtype) for dtype in (F32, BF16)],
        in_specs=[smem] * 2 + [whole] * len(operands),
        out_specs=[whole] * 2,
        scratch_shapes=scratch,
        compiler_params=pltpu.CompilerParams(vmem_limit_bytes=28 * 1024 * 1024),
        cost_estimate=pl.CostEstimate(flops=4 * 10**9, bytes_accessed=10**7, transcendentals=0),
    )(flags, place, *operands)


def shards(volume, first_weight, second_weight, cotangent):
    half = lax.axis_index("depth")
    row, col = lax.axis_index("row"), lax.axis_index("col")
    rows, cols = lax.axis_size("row"), lax.axis_size("col")
    inner = [jnp.logical_and(i > 0, i < n - 1).astype(jnp.int32) for i, n in ((row, rows), (col, cols))]
    flags = jnp.stack([half, row % 2, col % 2, *inner])
    whole = pl.BlockSpec(memory_space=pltpu.VMEM)
    smem = pl.BlockSpec(memory_space=pltpu.SMEM)
    small = pltpu.CompilerParams(vmem_limit_bytes=12 * 1024 * 1024)
    planes, high, width = volume.shape
    groups = planes + cotangent.shape[0] // 4
    in_hbm = pl.BlockSpec(memory_space=pltpu.HBM)

    def stay(argument):
        return pltpu.with_memory_space_constraint(argument, pltpu.HBM)

    arguments = (volume, cotangent, first_weight, second_weight.T)
    shapes = [argument.shape for argument in arguments] + [(17, 4, width)]
    volume, cotangent, first_taps, second_taps, dep = pl.pallas_call(
        bring,
        out_shape=[jax.ShapeDtypeStruct(shape, BF16) for shape in shapes],
        in_specs=[smem] + [in_hbm] * 4,
        out_specs=[whole] * len(shapes),
        scratch_shapes=[pltpu.SemaphoreType.DMA((6,))],
        compiler_params=small,
    )(flags, *[stay(argument) for argument in arguments])
    row_b, row_a = pl.pallas_call(
        pack_rows,
        out_shape=[jax.ShapeDtypeStruct((groups, 4, width), BF16)] * 2,
        in_specs=[smem] + [whole] * 2,
        out_specs=[whole] * 2,
        compiler_params=small,
    )(flags, volume, cotangent)

    def to_col(block, kind):
        return lax.ppermute(block, ("row", "col"), pairs_of_lines(rows, cols, kind))

    dep = lax.ppermute(dep, "depth", [(0, 1), (1, 0)])
    route = []
    for i, j in pairs_on_line(rows, 1):
        route += [((d * rows + i) * cols + c, (d * rows + j) * cols + (c ^ 1 if i == j else c)) for d in (0, 1) for c in range(cols)]
    row_b = lax.ppermute(row_b, ("depth", "row", "col"), route)
    row_a = lax.ppermute(row_a, "row", pairs_on_line(rows, 0))
    row_a, volume, cotangent = lax.optimization_barrier((row_a, volume, cotangent))
    side_a, side_b = pl.pallas_call(
        pack_sides,
        out_shape=[jax.ShapeDtypeStruct((groups, high, LANES), BF16)] * 2,
        in_specs=[smem] + [whole] * 2,
        out_specs=[whole] * 2,
        compiler_params=small,
    )(flags, volume, cotangent)
    side_a, side_b = to_col(side_a, 0), to_col(side_b, 1)
    low, top = [jnp.concatenate([dep[n : n + 1] for n in (*range(k, 16, 4), 16)], axis=0) for k in (0, 3)]
    even, ends = row % 2 == 0, jnp.logical_or(row == 0, row == rows - 1)
    edge_a = jnp.where(even, top, low)
    edge_b = jnp.where(ends, 0, jnp.where(even, low, top))
    edge_a = lax.ppermute(edge_a, "row", pairs_on_line(rows, 0))
    edge_b = lax.ppermute(edge_b, ("depth", "row"), pairs_of_lines(2, rows, 1))
    weights = pl.pallas_call(
        bands,
        out_shape=[jax.ShapeDtypeStruct(shape, BF16) for shape in ((1152, 256), (1152, 256), (9, 256, 128))],
        in_specs=[whole] * 2,
        out_specs=[whole] * 3,
        compiler_params=small,
    )(first_taps, second_taps)
    row_b, weights = lax.optimization_barrier((row_b, weights))
    col_a, col_b = pl.pallas_call(
        pack_corners,
        out_shape=[jax.ShapeDtypeStruct((planes + 14, 8, LANES), BF16)] * 2,
        in_specs=[smem] + [whole] * 5,
        out_specs=[whole] * 2,
        compiler_params=small,
    )(flags, row_b, row_a, dep, edge_a, edge_b)
    col_a, col_b, volume = lax.optimization_barrier((col_a, col_b, volume))
    col_a, col_b = to_col(col_a, 0), to_col(col_b, 1)

    spot = lax.axis_index(("depth", "row"))
    squares = lax.axis_size(("depth", "row")) // 2
    where = jnp.stack([spot % 2, spot // 2])
    faces, corners = (dep, row_a, row_b, edge_a, edge_b), (side_a, side_b, col_a, col_b)
    keep, give = local_grads(flags, where, squares, volume, faces, corners, cotangent, weights)

    def to_square(block, n):
        route = [(2 * i + c, 2 * (i ^ n) + c) for i in range(squares) for c in (0, 1)]
        return lax.ppermute(block, ("depth", "row"), route)

    def to_core(block):
        return lax.ppermute(block, ("depth", "row"), [(i, i ^ 1) for i in range(2 * squares)])

    def along_col(block, n):
        return lax.ppermute(block, "col", [(i, i ^ n) for i in range(cols)])

    both = keep + to_core(give).astype(F32)
    near = both.astype(BF16)
    share = add_up(both[0], *[to_square(near[n], n) for n in range(1, squares)])
    share = add_up(share, *[along_col(share, n) for n in range(1, cols)])
    mine = jnp.stack([share] + [to_square(share, n) for n in range(1, squares)])
    other = to_core(mine)
    grads = [jax.ShapeDtypeStruct(shape, F32) for shape in (first_weight.shape, second_weight.shape[::-1])]
    first_grad, second_grad = pl.pallas_call(
        unpack,
        out_shape=grads,
        in_specs=[smem] + [whole] * 2,
        out_specs=[in_hbm] * 2,
        scratch_shapes=[
            pltpu.VMEM((mine.shape[0] * mine.shape[1] * 2, LANES), F32),
            pltpu.VMEM(first_weight.shape, F32),
            pltpu.SemaphoreType.DMA((2,)),
        ],
        compiler_params=small,
    )(where, mine, other)
    return first_grad, second_grad.T


def solution(mesh):
    placed = (P("depth", "row", "col"), P(), P(), P("depth", "row", "col"))
    return jax.shard_map(shards, mesh=mesh, in_specs=placed, out_specs=(P(), P()), check_vma=False)
```

```python
import jax
import jax.numpy as jnp
from jax import lax
from jax.experimental import pallas as pl
from jax.experimental.pallas import tpu as pltpu
from jax.sharding import PartitionSpec as P

LANES = 128
SECOND_ROWS = 27 * 64
FIRST_BLOCKS = 7
F32 = jnp.float32
BF16 = jnp.bfloat16


def pairs_on_line(count, kind):
    firsts = range(kind, count - 1, 2)
    swapped = [(i, i + 1) for i in firsts] + [(i + 1, i) for i in firsts]
    met = {i for i, j in swapped}
    return swapped + [(i, i) for i in range(count) if i not in met]


def pairs_of_lines(lines, count, kind):
    route = []
    for line in range(lines):
        for i, j in pairs_on_line(count, kind):
            route.append((line * count + i, (line ^ 1 if i == j else line) * count + j))
    return route


def add_up(*terms):
    terms = [term.astype(F32) for term in terms]
    while len(terms) > 1:
        terms = [terms[n] + terms[n + 1] for n in range(0, len(terms), 2)]
    return terms[0].astype(BF16)


def matmul(left, right):
    return lax.dot_general(left, right, (((1,), (0,)), ((), ())), preferred_element_type=F32)


def bring(
    flag_ref, vol_hbm, cot_hbm, first_hbm, second_hbm, vol_ref, cot_ref, first_ref, second_ref, dep_ref, arrived
):
    first_plane = flag_ref[0] == 0
    planes, width = vol_ref.shape[0], vol_ref.shape[2]
    inner = pl.ds(4, planes - 8)
    copies = [pltpu.make_async_copy(cot_hbm, cot_ref, arrived.at[0])]
    for n, part in enumerate((pl.ds(0, 4), pl.ds(planes - 4, 4), inner)):
        copies.append(pltpu.make_async_copy(vol_hbm.at[part], vol_ref.at[part], arrived.at[1 + n]))
    copies.append(pltpu.make_async_copy(first_hbm, first_ref, arrived.at[4]))
    copies.append(pltpu.make_async_copy(second_hbm, second_ref, arrived.at[5]))
    for copy in copies:
        copy.start()
    for copy in copies[:3]:
        copy.wait()
    dep_ref[16] = cot_ref[0]
    for q in range(4):
        for m in range(width // LANES):
            lanes = slice(m * LANES, (m + 1) * LANES)
            last, start = vol_ref[planes - 4 + q, :, lanes].astype(F32), vol_ref[q, :, lanes].astype(F32)
            block = jnp.where(first_plane, last, start)
            for g in range(4):
                dep_ref[4 * q + g, :, lanes] = block[4 * g : 4 * g + 4].astype(BF16)
    for copy in copies[3:]:
        copy.wait()


def pack_rows(flag_ref, vol_ref, cot_ref, row_b_ref, row_a_ref):
    row_even, row_inner = flag_ref[1] == 0, flag_ref[3] != 0
    planes, high, width = vol_ref.shape
    cots = cot_ref.shape[0]

    def plane(d, carry):
        for m in range(width // LANES):
            lanes = slice(m * LANES, (m + 1) * LANES)
            block = vol_ref[d, :, lanes].astype(F32)
            low, top = block[:4], block[high - 4 :]
            row_a_ref[d, :, lanes] = jnp.where(row_even, top, low).astype(BF16)
            row_b_ref[d, :, lanes] = jnp.where(row_inner, jnp.where(row_even, low, top), 0.0).astype(BF16)
        return carry

    lax.fori_loop(0, planes, plane, 0, unroll=4)
    for g in range(cots // 4):
        tops = jnp.concatenate([cot_ref[4 * g + n].astype(F32)[:1] for n in range(4)], axis=0)
        row_a_ref[planes + g] = tops.astype(BF16)
        row_b_ref[planes + g] = jnp.where(row_inner, tops, 0.0).astype(BF16)


def pack_sides(flag_ref, vol_ref, cot_ref, col_a_ref, col_b_ref):
    col_even, col_inner = flag_ref[2] == 0, flag_ref[4] != 0
    planes, high, width = vol_ref.shape
    cots = cot_ref.shape[0]
    for g in range(cots // 4):
        side = jnp.concatenate([cot_ref[4 * g + n, :, :LANES].astype(F32) for n in range(4)], axis=0)
        col_a_ref[planes + g] = side.astype(BF16)
        col_b_ref[planes + g] = jnp.where(col_inner, side, 0.0).astype(BF16)

    def plane(d, carry):
        left = vol_ref[d, :, :LANES].astype(F32)
        right = vol_ref[d, :, width - LANES :].astype(F32)
        col_a_ref[d] = jnp.where(col_even, right, left).astype(BF16)
        col_b_ref[d] = jnp.where(col_inner, jnp.where(col_even, left, right), 0.0).astype(BF16)
        return carry

    lax.fori_loop(0, planes, plane, 0, unroll=4)


def pack_corners(flag_ref, row_b_ref, row_a_ref, dep_ref, edge_a_ref, edge_b_ref, col_a_ref, col_b_ref):
    row_even, col_even, col_inner = flag_ref[1] == 0, flag_ref[2] == 0, flag_ref[4] != 0
    width = dep_ref.shape[2]
    groups = row_a_ref.shape[0]
    planes = (groups * 16) // 17
    faces = (slice(0, LANES), slice(width - LANES, width))

    def store(n, left, right):
        col_a_ref[n] = jnp.where(col_even, right, left).astype(BF16)
        col_b_ref[n] = jnp.where(col_inner, jnp.where(col_even, left, right), 0.0).astype(BF16)

    def lower_upper(a_ref, b_ref, source, target):
        values = []
        for lanes in faces:
            a, b = a_ref[source, :, lanes].astype(F32), b_ref[source, :, lanes].astype(F32)
            values.append(jnp.concatenate([jnp.where(row_even, b, a), jnp.where(row_even, a, b)], axis=0))
        store(target, *values)

    def plane(d, carry):
        lower_upper(row_a_ref, row_b_ref, d, d)
        return carry

    lax.fori_loop(0, planes, plane, 0, unroll=4)
    for q in range(4):
        lower_upper(edge_a_ref, edge_b_ref, q, planes + q)
        for n in range(2):
            units = range(4 * q + 2 * n, 4 * q + 2 * n + 2)
            store(
                planes + 4 + 2 * q + n,
                *[jnp.concatenate([dep_ref[u, :, lanes].astype(F32) for u in units], axis=0) for lanes in faces],
            )
    lanes = faces[0]
    tops = [
        jnp.where(row_even, row_a_ref[g, :, lanes].astype(F32), row_b_ref[g, :, lanes].astype(F32))
        for g in range(planes, groups)
    ]
    corner = jnp.where(row_even, edge_a_ref[4, :, lanes].astype(F32), edge_b_ref[4, :, lanes].astype(F32))
    own = dep_ref[16, :, lanes].astype(F32)
    for n, values in enumerate((jnp.concatenate(tops, axis=0), jnp.concatenate([own, corner], axis=0))):
        col_a_ref[planes + 12 + n] = values.astype(BF16)
        col_b_ref[planes + 12 + n] = jnp.where(col_inner, values, 0.0).astype(BF16)


def bands(first_ref, second_ref, w1_ref, w2_ref, w2b_ref):
    out_chan = first_ref.shape[0]
    first = first_ref[...].astype(F32)
    blank = jnp.zeros((out_chan, LANES), F32)
    for tap in range(9):
        rows = slice(tap * LANES, (tap + 1) * LANES)
        taps = first[:, tap * 96 : (tap + 1) * 96]
        main_even = jnp.concatenate([taps[:, 32:], blank[:, :64]], axis=1)
        main_odd = jnp.concatenate([blank[:, :32], taps], axis=1)
        prev_even = jnp.concatenate([blank[:, :96], taps[:, :32]], axis=1)
        w1_ref[rows] = jnp.concatenate([main_even, main_odd, prev_even, blank], axis=0).T.astype(BF16)
        main = second_ref[tap * 192 + 64 : (tap + 1) * 192, :]
        prev = jnp.concatenate([jnp.zeros((64, LANES), BF16), second_ref[tap * 192 : tap * 192 + 64, :]], axis=0)
        both = jnp.concatenate([main, prev], axis=1)
        w2_ref[rows] = both
        w2b_ref[tap] = both.astype(F32).T.astype(BF16)


def split_rows(stage, tiles, index, blocks):
    for m in blocks:
        rows = [stage[m, pl.ds(4 + s, 8, stride=4), :] for s in range(-1, 4)]
        for b in range(3):
            tiles[b, index, m] = jnp.concatenate([rows[b], rows[b + 2]], axis=0).astype(BF16)


def clear_stage(stage):
    stage[:, :, 0:8, :] = jnp.zeros(stage.shape[:2] + (8, LANES), F32)
    stage[:, :, 24:40, :] = jnp.zeros(stage.shape[:2] + (16, LANES), F32)


def ahead(even, a, b):
    return jnp.where(even, a.astype(F32), b.astype(F32))


def behind(even, a, b):
    return jnp.where(even, b.astype(F32), a.astype(F32))


def own_blocks(
    flag_ref, vol_ref, dep_ref, row_a_ref, row_b_ref, edge_a_ref, edge_b_ref, w1_ref, tiles, parts, stage
):
    first_plane, row_even = flag_ref[0] == 0, flag_ref[1] == 0
    planes = vol_ref.shape[0]
    blocks = vol_ref.shape[2] // LANES
    clear_stage(stage)

    def place(n, target, own, a, b, keep):
        def kept(values):
            return values if keep is None else jnp.where(keep, values, 0.0)

        for m in range(blocks):
            lanes = slice(m * LANES, (m + 1) * LANES)
            stage[n, m, 8:24, :] = kept(own(lanes).astype(F32))
            stage[n, m, 4:8, :] = kept(behind(row_even, a(lanes), b(lanes)))
            stage[n, m, 24:28, :] = kept(ahead(row_even, a(lanes), b(lanes)))
        split_rows(stage.at[n], tiles, target, range(blocks))

    def place_own(group, carry):
        for n in range(4):
            d = 4 * group + n
            place(
                n, d + 3, lambda lanes: vol_ref[d, :, lanes],
                lambda lanes: row_a_ref[d, :, lanes], lambda lanes: row_b_ref[d, :, lanes], None,
            )
        return carry

    def place_halo(target, q, keep):
        place(
            target % 4, target,
            lambda lanes: jnp.concatenate([dep_ref[4 * q + g, :, lanes].astype(F32) for g in range(4)], axis=0),
            lambda lanes: edge_a_ref[q, :, lanes], lambda lanes: edge_b_ref[q, :, lanes], keep,
        )

    lax.fori_loop(0, planes // 4, place_own, 0)
    for q in range(3):
        place_halo(q, q + 1, jnp.logical_not(first_plane))
    for q in range(4):
        place_halo(planes + 3 + q, q, first_plane)
    tiles[:, planes + 7 :] = jnp.zeros((3, 2, blocks, 16, LANES), BF16)

    group = 5

    def product(step, carry):
        taps = []
        for a in range(3):
            for b in range(3):
                start = 2 * group * step + a
                found = [tiles[b, start + 2 * n].reshape(blocks * 16, LANES) for n in range(group)]
                taps.append(jnp.concatenate(found, axis=0))
        found = matmul(jnp.concatenate(taps, axis=1), w1_ref[...])
        parts[pl.ds(group * step, group)] = found.reshape(group, blocks, 16, 2 * LANES)
        return carry

    lax.fori_loop(0, parts.shape[0] // group, product, 0)


def body(
    flag_ref, place_ref, tiles, parts, dep_ref, row_a_ref, row_b_ref, edge_a_ref, edge_b_ref,
    side_a_ref, side_b_ref, col_a_ref, col_b_ref, cot_ref, w1_ref, w2_ref, w2b_ref, keep_ref, give_ref,
    out_ref, stage, rim_tiles, rim_parts, slopes, hid, pairs, ups, deltas, shifted,
):
    first_plane, row_even, col_even = flag_ref[0] == 0, flag_ref[1] == 0, flag_ref[2] == 0
    planes = tiles.shape[1] - 9
    blocks = tiles.shape[2]
    half_planes = planes // 4
    hidden_planes = planes // 2 + 3

    clear_stage(stage)

    def place(n, target, source, side_a, side_b, keep):
        for m, choose in ((0, behind), (1, ahead)):
            corners = choose(col_even, col_a_ref[source], col_b_ref[source])
            own = choose(col_even, side_a, side_b)
            if keep is not None:
                corners, own = jnp.where(keep, corners, 0.0), jnp.where(keep, own, 0.0)
            stage[n, m, 4:8, :] = corners[:4]
            stage[n, m, 8:24, :] = own
            stage[n, m, 24:28, :] = corners[4:]
        split_rows(stage.at[n], rim_tiles, target, range(2))

    def place_own(group, carry):
        for n in range(4):
            d = 4 * group + n
            place(n, d + 3, d, side_a_ref[d], side_b_ref[d], None)
        return carry

    def place_halo(target, q, keep):
        start = planes + 4 + 2 * q
        side_a = jnp.concatenate([col_a_ref[start].astype(F32), col_a_ref[start + 1].astype(F32)], axis=0)
        side_b = jnp.concatenate([col_b_ref[start].astype(F32), col_b_ref[start + 1].astype(F32)], axis=0)
        place(target % 4, target, planes + q, side_a, side_b, keep)

    lax.fori_loop(0, planes // 4, place_own, 0, unroll=2)
    for q in range(3):
        place_halo(q, q + 1, jnp.logical_not(first_plane))
    for q in range(4):
        place_halo(planes + 3 + q, q, first_plane)

    taps = []
    for a in range(3):
        for b in range(3):
            rows = [rim_tiles[b, 2 * i + a].reshape(32, LANES) for i in range(hidden_planes)]
            taps.append(jnp.concatenate(rows, axis=0))
    found = matmul(jnp.concatenate(taps, axis=1), w1_ref[...])
    rim_parts[...] = found.reshape(hidden_planes, 2, 16, 2 * LANES)

    def conv_one(i, carry):
        main, prev = parts[i, :, :, :LANES], parts[i, :, :, LANES:]
        rim, rim_prev = rim_parts[i, :, :, :LANES], rim_parts[i, 0:1, :, LANES:]
        blank = jnp.zeros((1, 16, LANES), F32)
        pre = jnp.concatenate([rim[:1], main, rim[1:]], axis=0) + jnp.concatenate([blank, rim_prev, prev], axis=0)
        square = pre * pre + 1.0
        inverse = lax.rsqrt(square)
        slopes[i] = 0.6 + 0.4 * (pre * inverse)
        hidden = (0.6 * pre + 0.4 * (square * inverse - 1.0)).astype(BF16).astype(F32)
        odd = hidden[:, 8:, :]
        hid[0, i] = pltpu.roll(odd, 1, 1)
        hid[1, i] = hidden[:, :8, :]
        hid[2, i] = odd
        return carry

    lax.fori_loop(0, hidden_planes, conv_one, 0, unroll=True)

    wide = (blocks + 2) * 16

    def pair(i, carry):
        for b in range(3):
            pairs[b, i] = jnp.concatenate([hid[b, i], hid[b, i + half_planes]], axis=1).astype(BF16)
        return carry

    lax.fori_loop(0, half_planes + 3, pair, 0, unroll=True)

    ups[...] = jnp.zeros_like(ups)
    for k in range(blocks):
        lanes = slice(k * LANES, (k + 1) * LANES)
        ups[0:half_planes, k, 1:5, :] = cot_ref[:, :, lanes].astype(F32)
        ups[half_planes, k, 1:5, :] = jnp.where(first_plane, dep_ref[16, :, lanes].astype(F32), 0.0)
        for g in range(half_planes // 4):
            tops = ahead(row_even, row_a_ref[planes + g, :, lanes], row_b_ref[planes + g, :, lanes])
            for n in range(4):
                ups[4 * g + n, k, 5:6, :] = tops[n : n + 1]
        corner = ahead(row_even, edge_a_ref[4, :, lanes], edge_b_ref[4, :, lanes])[:1]
        ups[half_planes, k, 5:6, :] = jnp.where(first_plane, corner, 0.0)
    for g in range(half_planes // 4):
        side = ahead(col_even, side_a_ref[planes + g], side_b_ref[planes + g])
        for n in range(4):
            ups[4 * g + n, blocks, 1:5, :] = side[4 * n : 4 * n + 4]
    tops = ahead(col_even, col_a_ref[planes + 12], col_b_ref[planes + 12])
    for n in range(half_planes):
        ups[n, blocks, 5:6, :] = tops[n : n + 1]
    beyond = jnp.where(first_plane, ahead(col_even, col_a_ref[planes + 13], col_b_ref[planes + 13]), 0.0)
    ups[half_planes, blocks, 1:6, :] = beyond[:5]

    quarter = half_planes // 2

    taps = []
    for a in range(3):
        for b in range(3):
            rows = [pairs[b, 2 * t + a].reshape(wide, LANES) for t in range(quarter + 1)]
            taps.append(jnp.concatenate(rows, axis=0))
    found = matmul(jnp.concatenate(taps, axis=1), w2_ref[...]).reshape(quarter + 1, blocks + 2, 16, 2 * LANES)
    for t in range(quarter + 1):
        pre = found[t, 1:, :, :LANES] + found[t, :-1, :, LANES:]
        slope = 0.6 + 0.4 * (pre * lax.rsqrt(pre * pre + 1.0))
        upstream = jnp.concatenate([ups[t], ups[t + quarter]], axis=1)
        delta = (upstream * slope).astype(BF16).astype(F32)
        moved = jnp.concatenate([pltpu.roll(delta[:, :8], 7, 1), pltpu.roll(delta[:, 8:], 7, 1)], axis=1)
        deltas[t] = delta
        shifted[t] = moved.astype(BF16)

    sublane = lax.broadcasted_iota(jnp.int32, (1, 1, 16, 1), 2) % 8
    own_rows = jnp.logical_and(sublane >= 1, sublane <= 4)

    def with_next(values, needed):
        values = values.T
        edge = jnp.zeros((LANES, values.shape[1] // blocks), values.dtype)
        here = jnp.concatenate([edge, values], axis=1)
        after = jnp.concatenate([values, edge], axis=1)[:needed]
        return jnp.concatenate([here, after], axis=0)

    own_delta = [jnp.where(own_rows[0], deltas[t, 0:blocks], 0.0) for t in range(quarter)]
    left = with_next(jnp.stack(own_delta, axis=1).reshape(blocks * quarter * 16, LANES), LANES).astype(BF16)

    def second_taps(tap):
        a, b = tap // 3, tap % 3
        found = [pairs[b, 2 * t + a, 0 : blocks + 1] for t in range(quarter)]
        return jnp.stack(found, axis=1).reshape((blocks + 1) * quarter * 16, LANES)

    for tap in range(0, 9, 2):
        right = [second_taps(x) for x in range(tap, min(tap + 2, 9))]
        found = matmul(left, jnp.concatenate(right, axis=1))
        for n in range(len(right)):
            row = (tap + n) * 192
            lanes = slice(n * LANES, (n + 1) * LANES)
            out_ref[row : row + 64, :] = found[LANES:, lanes].T[64:]
            out_ref[row + 64 : row + 192, :] = found[:LANES, lanes].T

    def pack(values):
        both = jnp.concatenate([values[:, :-1], values[:, 1:]], axis=3)
        return both.reshape(quarter * blocks * 16, 2 * LANES)

    plain = deltas[...].astype(BF16)
    moved = shifted[...]
    here, after = pack(plain[:-1]), pack(plain[1:])
    here_up, after_up = pack(moved[:-1]), pack(moved[1:])

    def back(terms):
        joined = jnp.concatenate([values for values, a, b in terms], axis=1)
        weights = jnp.concatenate([w2b_ref[3 * a + b] for values, a, b in terms], axis=0)
        return matmul(joined, weights).reshape(quarter, blocks, 16, LANES)

    rows = [
        [back([(here, 1, 1)]), back([(here_up, 1, 0), (here, 1, 2)])],
        [
            back([(after, 0, 1), (here, 2, 1)]),
            back([(after_up, 0, 0), (after, 0, 2), (here_up, 2, 0), (here, 2, 2)]),
        ],
    ]
    own_list = []
    for i in range(planes // 2):
        t, parity = i // 2, i % 2
        half = slice(0, 8) if t < quarter else slice(8, 16)
        back_one = jnp.concatenate([rows[parity][p][t % quarter, :, half, :] for p in (0, 1)], axis=1)
        delta = back_one * slopes[i + 1, 1 : blocks + 1]
        own_list.append(jnp.where(own_rows[0], delta, 0.0).astype(BF16))
    left_one = with_next(jnp.stack(own_list, axis=1).reshape(blocks * (planes // 2) * 16, LANES), 64)

    def first_taps(tap):
        a, b = tap // 3, tap % 3
        found = []
        for m in range(blocks + 1):
            for i in range(planes // 2):
                index = 2 * (i + 1) + a
                found.append(rim_tiles[b, index, 0] if m == 0 else tiles[b, index, m - 1])
        return jnp.concatenate(found, axis=0)

    grads = []
    for tap in range(0, 9, 2):
        right = [first_taps(x) for x in range(tap, min(tap + 2, 9))]
        found = matmul(left_one, jnp.concatenate(right, axis=1))
        for n in range(len(right)):
            main = found[:LANES, n * LANES : (n + 1) * LANES]
            prev = found[LANES:, n * LANES : (n + 1) * LANES]
            even = jnp.concatenate([prev[:, 96:], main[:64, :64]], axis=1)
            grads.append(even + main[64:, 32:])
    grads.append(jnp.zeros((64, FIRST_BLOCKS * LANES - 9 * 96), F32))
    first = jnp.concatenate(grads, axis=1)
    for n in range(FIRST_BLOCKS):
        row = SECOND_ROWS + 64 * n
        out_ref[row : row + 64, :] = first[:, n * LANES : (n + 1) * LANES]
    used = SECOND_ROWS + 64 * FIRST_BLOCKS
    if out_ref.shape[0] > used:
        out_ref[used:, :] = jnp.zeros((out_ref.shape[0] - used, LANES), F32)

    core, square = place_ref[0], place_ref[1]
    squares, size = keep_ref.shape[0], keep_ref.shape[1]
    for n in range(squares):
        for ref, half in ((keep_ref, core), (give_ref, 1 - core)):
            start = pl.multiple_of((half * squares + (square ^ n)) * size, 8)
            ref[n] = out_ref[pl.ds(start, size), :].astype(ref.dtype)


def unpack(place_ref, keep_ref, got_ref, g1_hbm, g2_hbm, sums, first, sent):
    core, square = place_ref[0], place_ref[1]
    squares, size = keep_ref.shape[0], keep_ref.shape[1]
    for n in range(squares):
        for ref, half in ((keep_ref, core), (got_ref, 1 - core)):
            start = pl.multiple_of((half * squares + (square ^ n)) * size, 8)
            sums[pl.ds(start, size), :] = ref[-n % squares].astype(F32)
    second = pltpu.make_async_copy(sums.at[pl.ds(0, SECOND_ROWS)], g2_hbm, sent.at[0])
    second.start()
    found = [sums[SECOND_ROWS + 64 * n : SECOND_ROWS + 64 * (n + 1), :] for n in range(FIRST_BLOCKS)]
    first[...] = jnp.concatenate(found, axis=1)[:, : first.shape[1]]
    copy = pltpu.make_async_copy(first, g1_hbm, sent.at[1])
    copy.start()
    copy.wait()
    second.wait()


def local_grads(flags, place, squares, volume, faces, corners, cotangent, weights):
    planes = volume.shape[0]
    blocks = volume.shape[2] // LANES
    hidden_planes = planes // 2 + 3
    out_planes = planes // 4
    unit = 2 * squares * 16
    rows = -(-(SECOND_ROWS + 64 * FIRST_BLOCKS) // unit) * unit
    whole = pl.BlockSpec(memory_space=pltpu.VMEM)
    smem = pl.BlockSpec(memory_space=pltpu.SMEM)
    dep, row_a, row_b, edge_a, edge_b = faces
    tiles, parts = pl.pallas_call(
        own_blocks,
        out_shape=[
            jax.ShapeDtypeStruct((3, planes + 9, blocks, 16, LANES), BF16),
            jax.ShapeDtypeStruct((hidden_planes + 1, blocks, 16, 2 * LANES), F32),
        ],
        in_specs=[smem] + [whole] * 7,
        out_specs=[whole] * 2,
        scratch_shapes=[pltpu.VMEM((4, blocks, 40, LANES), F32)],
        compiler_params=pltpu.CompilerParams(vmem_limit_bytes=16 * 1024 * 1024),
        cost_estimate=pl.CostEstimate(flops=2 * 10**9, bytes_accessed=10**7, transcendentals=0),
    )(flags, volume, *faces, weights[0])
    scratch = [
        pltpu.VMEM((rows, LANES), F32),
        pltpu.VMEM((4, 2, 40, LANES), F32),
        pltpu.VMEM((3, planes + 7, 2, 16, LANES), BF16),
        pltpu.VMEM((hidden_planes, 2, 16, 2 * LANES), F32),
        pltpu.VMEM((hidden_planes, blocks + 2, 16, LANES), F32),
        pltpu.VMEM((3, hidden_planes, blocks + 2, 8, LANES), F32),
        pltpu.VMEM((3, out_planes + 3, blocks + 2, 16, LANES), BF16),
        pltpu.VMEM((out_planes + 1, blocks + 1, 8, LANES), F32),
        pltpu.VMEM((out_planes // 2 + 1, blocks + 1, 16, LANES), F32),
        pltpu.VMEM((out_planes // 2 + 1, blocks + 1, 16, LANES), BF16),
    ]
    operands = (tiles, parts, *faces, *corners, cotangent, *weights)
    return pl.pallas_call(
        body,
        out_shape=[jax.ShapeDtypeStruct((squares, rows // (2 * squares), LANES), dtype) for dtype in (F32, BF16)],
        in_specs=[smem] * 2 + [whole] * len(operands),
        out_specs=[whole] * 2,
        scratch_shapes=scratch,
        compiler_params=pltpu.CompilerParams(vmem_limit_bytes=28 * 1024 * 1024),
        cost_estimate=pl.CostEstimate(flops=4 * 10**9, bytes_accessed=10**7, transcendentals=0),
    )(flags, place, *operands)


def shards(volume, first_weight, second_weight, cotangent):
    half = lax.axis_index("depth")
    row, col = lax.axis_index("row"), lax.axis_index("col")
    rows, cols = lax.axis_size("row"), lax.axis_size("col")
    inner = [jnp.logical_and(i > 0, i < n - 1).astype(jnp.int32) for i, n in ((row, rows), (col, cols))]
    flags = jnp.stack([half, row % 2, col % 2, *inner])
    whole = pl.BlockSpec(memory_space=pltpu.VMEM)
    smem = pl.BlockSpec(memory_space=pltpu.SMEM)
    small = pltpu.CompilerParams(vmem_limit_bytes=12 * 1024 * 1024)
    planes, high, width = volume.shape
    groups = planes + cotangent.shape[0] // 4
    in_hbm = pl.BlockSpec(memory_space=pltpu.HBM)

    def stay(argument):
        return pltpu.with_memory_space_constraint(argument, pltpu.HBM)

    arguments = (volume, cotangent, first_weight, second_weight.T)
    shapes = [argument.shape for argument in arguments] + [(17, 4, width)]
    volume, cotangent, first_taps, second_taps, dep = pl.pallas_call(
        bring,
        out_shape=[jax.ShapeDtypeStruct(shape, BF16) for shape in shapes],
        in_specs=[smem] + [in_hbm] * 4,
        out_specs=[whole] * len(shapes),
        scratch_shapes=[pltpu.SemaphoreType.DMA((6,))],
        compiler_params=small,
    )(flags, *[stay(argument) for argument in arguments])
    row_b, row_a = pl.pallas_call(
        pack_rows,
        out_shape=[jax.ShapeDtypeStruct((groups, 4, width), BF16)] * 2,
        in_specs=[smem] + [whole] * 2,
        out_specs=[whole] * 2,
        compiler_params=small,
    )(flags, volume, cotangent)

    def to_col(block, kind):
        return lax.ppermute(block, ("row", "col"), pairs_of_lines(rows, cols, kind))

    dep = lax.ppermute(dep, "depth", [(0, 1), (1, 0)])
    route = []
    for i, j in pairs_on_line(rows, 1):
        route += [((d * rows + i) * cols + c, (d * rows + j) * cols + (c ^ 1 if i == j else c)) for d in (0, 1) for c in range(cols)]
    row_b = lax.ppermute(row_b, ("depth", "row", "col"), route)
    row_a = lax.ppermute(row_a, "row", pairs_on_line(rows, 0))
    row_a, volume, cotangent = lax.optimization_barrier((row_a, volume, cotangent))
    side_a, side_b = pl.pallas_call(
        pack_sides,
        out_shape=[jax.ShapeDtypeStruct((groups, high, LANES), BF16)] * 2,
        in_specs=[smem] + [whole] * 2,
        out_specs=[whole] * 2,
        compiler_params=small,
    )(flags, volume, cotangent)
    side_a, side_b = to_col(side_a, 0), to_col(side_b, 1)
    low, top = [jnp.concatenate([dep[n : n + 1] for n in (*range(k, 16, 4), 16)], axis=0) for k in (0, 3)]
    even, ends = row % 2 == 0, jnp.logical_or(row == 0, row == rows - 1)
    edge_a = jnp.where(even, top, low)
    edge_b = jnp.where(ends, 0, jnp.where(even, low, top))
    edge_a = lax.ppermute(edge_a, "row", pairs_on_line(rows, 0))
    edge_b = lax.ppermute(edge_b, ("depth", "row"), pairs_of_lines(2, rows, 1))
    weights = pl.pallas_call(
        bands,
        out_shape=[jax.ShapeDtypeStruct(shape, BF16) for shape in ((1152, 256), (1152, 256), (9, 256, 128))],
        in_specs=[whole] * 2,
        out_specs=[whole] * 3,
        compiler_params=small,
    )(first_taps, second_taps)
    row_b, weights = lax.optimization_barrier((row_b, weights))
    col_a, col_b = pl.pallas_call(
        pack_corners,
        out_shape=[jax.ShapeDtypeStruct((planes + 14, 8, LANES), BF16)] * 2,
        in_specs=[smem] + [whole] * 5,
        out_specs=[whole] * 2,
        compiler_params=small,
    )(flags, row_b, row_a, dep, edge_a, edge_b)
    col_a, col_b, volume = lax.optimization_barrier((col_a, col_b, volume))
    col_a, col_b = to_col(col_a, 0), to_col(col_b, 1)

    spot = lax.axis_index(("depth", "row"))
    squares = lax.axis_size(("depth", "row")) // 2
    where = jnp.stack([spot % 2, spot // 2])
    faces, corners = (dep, row_a, row_b, edge_a, edge_b), (side_a, side_b, col_a, col_b)
    keep, give = local_grads(flags, where, squares, volume, faces, corners, cotangent, weights)

    def to_square(block, n):
        route = [(2 * i + c, 2 * (i ^ n) + c) for i in range(squares) for c in (0, 1)]
        return lax.ppermute(block, ("depth", "row"), route)

    def to_core(block):
        return lax.ppermute(block, ("depth", "row"), [(i, i ^ 1) for i in range(2 * squares)])

    def along_col(block, n):
        return lax.ppermute(block, "col", [(i, i ^ n) for i in range(cols)])

    both = keep + to_core(give).astype(F32)
    near = both.astype(BF16)
    order = [1, *reversed(range(2, squares))]
    share = add_up(both[0], *[to_square(near[n], n) for n in order])
    share = add_up(share, *[along_col(share, n) for n in range(1, cols)])
    mine = jnp.stack([share] + [to_square(share, n) for n in reversed(range(1, squares))])
    other = to_core(mine)
    grads = [jax.ShapeDtypeStruct(shape, F32) for shape in (first_weight.shape, second_weight.shape[::-1])]
    first_grad, second_grad = pl.pallas_call(
        unpack,
        out_shape=grads,
        in_specs=[smem] + [whole] * 2,
        out_specs=[in_hbm] * 2,
        scratch_shapes=[
            pltpu.VMEM((mine.shape[0] * mine.shape[1] * 2, LANES), F32),
            pltpu.VMEM(first_weight.shape, F32),
            pltpu.SemaphoreType.DMA((2,)),
        ],
        compiler_params=small,
    )(where, mine, other)
    return first_grad, second_grad.T


def solution(mesh):
    placed = (P("depth", "row", "col"), P(), P(), P("depth", "row", "col"))
    return jax.shard_map(shards, mesh=mesh, in_specs=placed, out_specs=(P(), P()), check_vma=False)
```

```python
import jax
import jax.numpy as jnp
from jax import lax
from jax.experimental import pallas as pl
from jax.experimental.pallas import tpu as pltpu
from jax.sharding import PartitionSpec as P

LANES = 128
SECOND_ROWS = 27 * 64
FIRST_BLOCKS = 7
F32 = jnp.float32
BF16 = jnp.bfloat16


def pairs_on_line(count, kind):
    firsts = range(kind, count - 1, 2)
    swapped = [(i, i + 1) for i in firsts] + [(i + 1, i) for i in firsts]
    met = {i for i, j in swapped}
    return swapped + [(i, i) for i in range(count) if i not in met]


def pairs_of_lines(lines, count, kind):
    route = []
    for line in range(lines):
        for i, j in pairs_on_line(count, kind):
            route.append((line * count + i, (line ^ 1 if i == j else line) * count + j))
    return route


def add_up(*terms):
    terms = [term.astype(F32) for term in terms]
    while len(terms) > 1:
        terms = [terms[n] + terms[n + 1] for n in range(0, len(terms), 2)]
    return terms[0].astype(BF16)


def matmul(left, right):
    return lax.dot_general(left, right, (((1,), (0,)), ((), ())), preferred_element_type=F32)


def bring(
    flag_ref, vol_hbm, cot_hbm, first_hbm, second_hbm, vol_ref, cot_ref, first_ref, second_ref, dep_ref, arrived
):
    first_plane = flag_ref[0] == 0
    planes, width = vol_ref.shape[0], vol_ref.shape[2]
    inner = pl.ds(4, planes - 8)
    copies = [pltpu.make_async_copy(cot_hbm, cot_ref, arrived.at[0])]
    for n, part in enumerate((pl.ds(0, 4), pl.ds(planes - 4, 4), inner)):
        copies.append(pltpu.make_async_copy(vol_hbm.at[part], vol_ref.at[part], arrived.at[1 + n]))
    copies.append(pltpu.make_async_copy(first_hbm, first_ref, arrived.at[4]))
    copies.append(pltpu.make_async_copy(second_hbm, second_ref, arrived.at[5]))
    for copy in copies:
        copy.start()
    for copy in copies[:3]:
        copy.wait()
    dep_ref[16] = cot_ref[0]
    for q in range(4):
        for m in range(width // LANES):
            lanes = slice(m * LANES, (m + 1) * LANES)
            last, start = vol_ref[planes - 4 + q, :, lanes].astype(F32), vol_ref[q, :, lanes].astype(F32)
            block = jnp.where(first_plane, last, start)
            for g in range(4):
                dep_ref[4 * q + g, :, lanes] = block[4 * g : 4 * g + 4].astype(BF16)
    for copy in copies[3:]:
        copy.wait()


def pack_rows(flag_ref, vol_ref, cot_ref, row_b_ref, row_a_ref):
    row_even, row_inner = flag_ref[1] == 0, flag_ref[3] != 0
    planes, high, width = vol_ref.shape
    cots = cot_ref.shape[0]

    def plane(d, carry):
        for m in range(width // LANES):
            lanes = slice(m * LANES, (m + 1) * LANES)
            block = vol_ref[d, :, lanes].astype(F32)
            low, top = block[:4], block[high - 4 :]
            row_a_ref[d, :, lanes] = jnp.where(row_even, top, low).astype(BF16)
            row_b_ref[d, :, lanes] = jnp.where(row_inner, jnp.where(row_even, low, top), 0.0).astype(BF16)
        return carry

    lax.fori_loop(0, planes, plane, 0, unroll=4)
    for g in range(cots // 4):
        tops = jnp.concatenate([cot_ref[4 * g + n].astype(F32)[:1] for n in range(4)], axis=0)
        row_a_ref[planes + g] = tops.astype(BF16)
        row_b_ref[planes + g] = jnp.where(row_inner, tops, 0.0).astype(BF16)


def pack_sides(flag_ref, vol_ref, cot_ref, col_a_ref, col_b_ref):
    col_even, col_inner = flag_ref[2] == 0, flag_ref[4] != 0
    planes, high, width = vol_ref.shape
    cots = cot_ref.shape[0]
    for g in range(cots // 4):
        side = jnp.concatenate([cot_ref[4 * g + n, :, :LANES].astype(F32) for n in range(4)], axis=0)
        col_a_ref[planes + g] = side.astype(BF16)
        col_b_ref[planes + g] = jnp.where(col_inner, side, 0.0).astype(BF16)

    def plane(d, carry):
        left = vol_ref[d, :, :LANES].astype(F32)
        right = vol_ref[d, :, width - LANES :].astype(F32)
        col_a_ref[d] = jnp.where(col_even, right, left).astype(BF16)
        col_b_ref[d] = jnp.where(col_inner, jnp.where(col_even, left, right), 0.0).astype(BF16)
        return carry

    lax.fori_loop(0, planes, plane, 0, unroll=4)


def pack_corners(flag_ref, row_b_ref, row_a_ref, dep_ref, edge_a_ref, edge_b_ref, col_a_ref, col_b_ref):
    row_even, col_even, col_inner = flag_ref[1] == 0, flag_ref[2] == 0, flag_ref[4] != 0
    width = dep_ref.shape[2]
    groups = row_a_ref.shape[0]
    planes = (groups * 16) // 17
    faces = (slice(0, LANES), slice(width - LANES, width))

    def store(n, left, right):
        col_a_ref[n] = jnp.where(col_even, right, left).astype(BF16)
        col_b_ref[n] = jnp.where(col_inner, jnp.where(col_even, left, right), 0.0).astype(BF16)

    def lower_upper(a_ref, b_ref, source, target):
        values = []
        for lanes in faces:
            a, b = a_ref[source, :, lanes].astype(F32), b_ref[source, :, lanes].astype(F32)
            values.append(jnp.concatenate([jnp.where(row_even, b, a), jnp.where(row_even, a, b)], axis=0))
        store(target, *values)

    def plane(d, carry):
        lower_upper(row_a_ref, row_b_ref, d, d)
        return carry

    lax.fori_loop(0, planes, plane, 0, unroll=4)
    for q in range(4):
        lower_upper(edge_a_ref, edge_b_ref, q, planes + q)
        for n in range(2):
            units = range(4 * q + 2 * n, 4 * q + 2 * n + 2)
            store(
                planes + 4 + 2 * q + n,
                *[jnp.concatenate([dep_ref[u, :, lanes].astype(F32) for u in units], axis=0) for lanes in faces],
            )
    lanes = faces[0]
    tops = [
        jnp.where(row_even, row_a_ref[g, :, lanes].astype(F32), row_b_ref[g, :, lanes].astype(F32))
        for g in range(planes, groups)
    ]
    corner = jnp.where(row_even, edge_a_ref[4, :, lanes].astype(F32), edge_b_ref[4, :, lanes].astype(F32))
    own = dep_ref[16, :, lanes].astype(F32)
    for n, values in enumerate((jnp.concatenate(tops, axis=0), jnp.concatenate([own, corner], axis=0))):
        col_a_ref[planes + 12 + n] = values.astype(BF16)
        col_b_ref[planes + 12 + n] = jnp.where(col_inner, values, 0.0).astype(BF16)


def bands(first_ref, second_ref, w1_ref, w2_ref, w2b_ref):
    out_chan = first_ref.shape[0]
    first = first_ref[...].astype(F32)
    blank = jnp.zeros((out_chan, LANES), F32)
    for tap in range(9):
        rows = slice(tap * LANES, (tap + 1) * LANES)
        taps = first[:, tap * 96 : (tap + 1) * 96]
        main_even = jnp.concatenate([taps[:, 32:], blank[:, :64]], axis=1)
        main_odd = jnp.concatenate([blank[:, :32], taps], axis=1)
        prev_even = jnp.concatenate([blank[:, :96], taps[:, :32]], axis=1)
        w1_ref[rows] = jnp.concatenate([main_even, main_odd, prev_even, blank], axis=0).T.astype(BF16)
        main = second_ref[tap * 192 + 64 : (tap + 1) * 192, :]
        prev = jnp.concatenate([jnp.zeros((64, LANES), BF16), second_ref[tap * 192 : tap * 192 + 64, :]], axis=0)
        both = jnp.concatenate([main, prev], axis=1)
        w2_ref[rows] = both
        w2b_ref[tap] = both.astype(F32).T.astype(BF16)


def split_rows(stage, tiles, index, blocks):
    for m in blocks:
        rows = [stage[m, pl.ds(4 + s, 8, stride=4), :] for s in range(-1, 4)]
        for b in range(3):
            tiles[b, index, m] = jnp.concatenate([rows[b], rows[b + 2]], axis=0).astype(BF16)


def clear_stage(stage):
    stage[:, :, 0:8, :] = jnp.zeros(stage.shape[:2] + (8, LANES), F32)
    stage[:, :, 24:40, :] = jnp.zeros(stage.shape[:2] + (16, LANES), F32)


def ahead(even, a, b):
    return jnp.where(even, a.astype(F32), b.astype(F32))


def behind(even, a, b):
    return jnp.where(even, b.astype(F32), a.astype(F32))


def own_blocks(
    flag_ref, vol_ref, dep_ref, row_a_ref, row_b_ref, edge_a_ref, edge_b_ref, w1_ref, tiles, parts, stage
):
    first_plane, row_even = flag_ref[0] == 0, flag_ref[1] == 0
    planes = vol_ref.shape[0]
    blocks = vol_ref.shape[2] // LANES
    clear_stage(stage)

    def place(n, target, own, a, b, keep):
        def kept(values):
            return values if keep is None else jnp.where(keep, values, 0.0)

        for m in range(blocks):
            lanes = slice(m * LANES, (m + 1) * LANES)
            stage[n, m, 8:24, :] = kept(own(lanes).astype(F32))
            stage[n, m, 4:8, :] = kept(behind(row_even, a(lanes), b(lanes)))
            stage[n, m, 24:28, :] = kept(ahead(row_even, a(lanes), b(lanes)))
        split_rows(stage.at[n], tiles, target, range(blocks))

    def place_own(group, carry):
        for n in range(4):
            d = 4 * group + n
            place(
                n, d + 3, lambda lanes: vol_ref[d, :, lanes],
                lambda lanes: row_a_ref[d, :, lanes], lambda lanes: row_b_ref[d, :, lanes], None,
            )
        return carry

    def place_halo(target, q, keep):
        place(
            target % 4, target,
            lambda lanes: jnp.concatenate([dep_ref[4 * q + g, :, lanes].astype(F32) for g in range(4)], axis=0),
            lambda lanes: edge_a_ref[q, :, lanes], lambda lanes: edge_b_ref[q, :, lanes], keep,
        )

    lax.fori_loop(0, planes // 4, place_own, 0)
    for q in range(3):
        place_halo(q, q + 1, jnp.logical_not(first_plane))
    for q in range(4):
        place_halo(planes + 3 + q, q, first_plane)
    tiles[:, planes + 7 :] = jnp.zeros((3, 2, blocks, 16, LANES), BF16)

    group = 5

    def product(step, carry):
        taps = []
        for a in range(3):
            for b in range(3):
                start = 2 * group * step + a
                found = [tiles[b, start + 2 * n].reshape(blocks * 16, LANES) for n in range(group)]
                taps.append(jnp.concatenate(found, axis=0))
        found = matmul(jnp.concatenate(taps, axis=1), w1_ref[...])
        parts[pl.ds(group * step, group)] = found.reshape(group, blocks, 16, 2 * LANES)
        return carry

    lax.fori_loop(0, parts.shape[0] // group, product, 0)


def body(
    flag_ref, place_ref, tiles, parts, dep_ref, row_a_ref, row_b_ref, edge_a_ref, edge_b_ref,
    side_a_ref, side_b_ref, col_a_ref, col_b_ref, cot_ref, w1_ref, w2_ref, w2b_ref, keep_ref, give_ref,
    out_ref, stage, rim_tiles, rim_parts, slopes, hid, pairs, ups, deltas, shifted,
):
    first_plane, row_even, col_even = flag_ref[0] == 0, flag_ref[1] == 0, flag_ref[2] == 0
    planes = tiles.shape[1] - 9
    blocks = tiles.shape[2]
    half_planes = planes // 4
    hidden_planes = planes // 2 + 3

    clear_stage(stage)

    def place(n, target, source, side_a, side_b, keep):
        for m, choose in ((0, behind), (1, ahead)):
            corners = choose(col_even, col_a_ref[source], col_b_ref[source])
            own = choose(col_even, side_a, side_b)
            if keep is not None:
                corners, own = jnp.where(keep, corners, 0.0), jnp.where(keep, own, 0.0)
            stage[n, m, 4:8, :] = corners[:4]
            stage[n, m, 8:24, :] = own
            stage[n, m, 24:28, :] = corners[4:]
        split_rows(stage.at[n], rim_tiles, target, range(2))

    def place_own(group, carry):
        for n in range(4):
            d = 4 * group + n
            place(n, d + 3, d, side_a_ref[d], side_b_ref[d], None)
        return carry

    def place_halo(target, q, keep):
        start = planes + 4 + 2 * q
        side_a = jnp.concatenate([col_a_ref[start].astype(F32), col_a_ref[start + 1].astype(F32)], axis=0)
        side_b = jnp.concatenate([col_b_ref[start].astype(F32), col_b_ref[start + 1].astype(F32)], axis=0)
        place(target % 4, target, planes + q, side_a, side_b, keep)

    lax.fori_loop(0, planes // 4, place_own, 0, unroll=2)
    for q in range(3):
        place_halo(q, q + 1, jnp.logical_not(first_plane))
    for q in range(4):
        place_halo(planes + 3 + q, q, first_plane)

    taps = []
    for a in range(3):
        for b in range(3):
            rows = [rim_tiles[b, 2 * i + a].reshape(32, LANES) for i in range(hidden_planes)]
            taps.append(jnp.concatenate(rows, axis=0))
    found = matmul(jnp.concatenate(taps, axis=1), w1_ref[...])
    rim_parts[...] = found.reshape(hidden_planes, 2, 16, 2 * LANES)

    def conv_one(i, carry):
        main, prev = parts[i, :, :, :LANES], parts[i, :, :, LANES:]
        rim, rim_prev = rim_parts[i, :, :, :LANES], rim_parts[i, 0:1, :, LANES:]
        blank = jnp.zeros((1, 16, LANES), F32)
        pre = jnp.concatenate([rim[:1], main, rim[1:]], axis=0) + jnp.concatenate([blank, rim_prev, prev], axis=0)
        square = pre * pre + 1.0
        inverse = lax.rsqrt(square)
        slopes[i] = 0.6 + 0.4 * (pre * inverse)
        hidden = (0.6 * pre + 0.4 * (square * inverse - 1.0)).astype(BF16).astype(F32)
        odd = hidden[:, 8:, :]
        hid[0, i] = pltpu.roll(odd, 1, 1)
        hid[1, i] = hidden[:, :8, :]
        hid[2, i] = odd
        return carry

    lax.fori_loop(0, hidden_planes, conv_one, 0, unroll=True)

    wide = (blocks + 2) * 16

    def pair(i, carry):
        for b in range(3):
            pairs[b, i] = jnp.concatenate([hid[b, i], hid[b, i + half_planes]], axis=1).astype(BF16)
        return carry

    lax.fori_loop(0, half_planes + 3, pair, 0, unroll=True)

    ups[...] = jnp.zeros_like(ups)
    for k in range(blocks):
        lanes = slice(k * LANES, (k + 1) * LANES)
        ups[0:half_planes, k, 1:5, :] = cot_ref[:, :, lanes].astype(F32)
        ups[half_planes, k, 1:5, :] = jnp.where(first_plane, dep_ref[16, :, lanes].astype(F32), 0.0)
        for g in range(half_planes // 4):
            tops = ahead(row_even, row_a_ref[planes + g, :, lanes], row_b_ref[planes + g, :, lanes])
            for n in range(4):
                ups[4 * g + n, k, 5:6, :] = tops[n : n + 1]
        corner = ahead(row_even, edge_a_ref[4, :, lanes], edge_b_ref[4, :, lanes])[:1]
        ups[half_planes, k, 5:6, :] = jnp.where(first_plane, corner, 0.0)
    for g in range(half_planes // 4):
        side = ahead(col_even, side_a_ref[planes + g], side_b_ref[planes + g])
        for n in range(4):
            ups[4 * g + n, blocks, 1:5, :] = side[4 * n : 4 * n + 4]
    tops = ahead(col_even, col_a_ref[planes + 12], col_b_ref[planes + 12])
    for n in range(half_planes):
        ups[n, blocks, 5:6, :] = tops[n : n + 1]
    beyond = jnp.where(first_plane, ahead(col_even, col_a_ref[planes + 13], col_b_ref[planes + 13]), 0.0)
    ups[half_planes, blocks, 1:6, :] = beyond[:5]

    quarter = half_planes // 2

    taps = []
    for a in range(3):
        for b in range(3):
            rows = [pairs[b, 2 * t + a].reshape(wide, LANES) for t in range(quarter + 1)]
            taps.append(jnp.concatenate(rows, axis=0))
    found = matmul(jnp.concatenate(taps, axis=1), w2_ref[...]).reshape(quarter + 1, blocks + 2, 16, 2 * LANES)
    for t in range(quarter + 1):
        pre = found[t, 1:, :, :LANES] + found[t, :-1, :, LANES:]
        slope = 0.6 + 0.4 * (pre * lax.rsqrt(pre * pre + 1.0))
        upstream = jnp.concatenate([ups[t], ups[t + quarter]], axis=1)
        delta = (upstream * slope).astype(BF16).astype(F32)
        moved = jnp.concatenate([pltpu.roll(delta[:, :8], 7, 1), pltpu.roll(delta[:, 8:], 7, 1)], axis=1)
        deltas[t] = delta
        shifted[t] = moved.astype(BF16)

    sublane = lax.broadcasted_iota(jnp.int32, (1, 1, 16, 1), 2) % 8
    own_rows = jnp.logical_and(sublane >= 1, sublane <= 4)

    def with_next(values, needed):
        values = values.T
        edge = jnp.zeros((LANES, values.shape[1] // blocks), values.dtype)
        here = jnp.concatenate([edge, values], axis=1)
        after = jnp.concatenate([values, edge], axis=1)[:needed]
        return jnp.concatenate([here, after], axis=0)

    own_delta = [jnp.where(own_rows[0], deltas[t, 0:blocks], 0.0) for t in range(quarter)]
    left = with_next(jnp.stack(own_delta, axis=1).reshape(blocks * quarter * 16, LANES), LANES).astype(BF16)

    def second_taps(tap):
        a, b = tap // 3, tap % 3
        found = [pairs[b, 2 * t + a, 0 : blocks + 1] for t in range(quarter)]
        return jnp.stack(found, axis=1).reshape((blocks + 1) * quarter * 16, LANES)

    for tap in range(0, 9, 2):
        right = [second_taps(x) for x in range(tap, min(tap + 2, 9))]
        found = matmul(left, jnp.concatenate(right, axis=1))
        for n in range(len(right)):
            row = (tap + n) * 192
            lanes = slice(n * LANES, (n + 1) * LANES)
            out_ref[row : row + 64, :] = found[LANES:, lanes].T[64:]
            out_ref[row + 64 : row + 192, :] = found[:LANES, lanes].T

    def pack(values):
        both = jnp.concatenate([values[:, :-1], values[:, 1:]], axis=3)
        return both.reshape(quarter * blocks * 16, 2 * LANES)

    plain = deltas[...].astype(BF16)
    moved = shifted[...]
    here, after = pack(plain[:-1]), pack(plain[1:])
    here_up, after_up = pack(moved[:-1]), pack(moved[1:])

    def back(values, taps):
        weights = jnp.concatenate([w2b_ref[3 * a + b] for a, b in taps], axis=1)
        found = matmul(values, weights)
        found = [found[:, n * LANES : (n + 1) * LANES] for n in range(len(taps))]
        return [part.reshape(quarter, blocks, 16, LANES) for part in found]

    here_11, here_12, here_21, here_22 = back(here, ((1, 1), (1, 2), (2, 1), (2, 2)))
    up_10, up_20 = back(here_up, ((1, 0), (2, 0)))
    after_01, after_02 = back(after, ((0, 1), (0, 2)))
    (after_00,) = back(after_up, ((0, 0),))
    rows = [[here_11, up_10 + here_12], [after_01 + here_21, after_00 + after_02 + up_20 + here_22]]
    own_list = []
    for i in range(planes // 2):
        t, parity = i // 2, i % 2
        half = slice(0, 8) if t < quarter else slice(8, 16)
        back_one = jnp.concatenate([rows[parity][p][t % quarter, :, half, :] for p in (0, 1)], axis=1)
        delta = back_one * slopes[i + 1, 1 : blocks + 1]
        own_list.append(jnp.where(own_rows[0], delta, 0.0).astype(BF16))
    left_one = with_next(jnp.stack(own_list, axis=1).reshape(blocks * (planes // 2) * 16, LANES), 64)

    def first_taps(tap):
        a, b = tap // 3, tap % 3
        found = []
        for m in range(blocks + 1):
            for i in range(planes // 2):
                index = 2 * (i + 1) + a
                found.append(rim_tiles[b, index, 0] if m == 0 else tiles[b, index, m - 1])
        return jnp.concatenate(found, axis=0)

    grads = []
    for tap in range(0, 9, 2):
        right = [first_taps(x) for x in range(tap, min(tap + 2, 9))]
        found = matmul(left_one, jnp.concatenate(right, axis=1))
        for n in range(len(right)):
            main = found[:LANES, n * LANES : (n + 1) * LANES]
            prev = found[LANES:, n * LANES : (n + 1) * LANES]
            even = jnp.concatenate([prev[:, 96:], main[:64, :64]], axis=1)
            grads.append(even + main[64:, 32:])
    grads.append(jnp.zeros((64, FIRST_BLOCKS * LANES - 9 * 96), F32))
    first = jnp.concatenate(grads, axis=1)
    for n in range(FIRST_BLOCKS):
        row = SECOND_ROWS + 64 * n
        out_ref[row : row + 64, :] = first[:, n * LANES : (n + 1) * LANES]
    used = SECOND_ROWS + 64 * FIRST_BLOCKS
    if out_ref.shape[0] > used:
        out_ref[used:, :] = jnp.zeros((out_ref.shape[0] - used, LANES), F32)

    core, square = place_ref[0], place_ref[1]
    squares, size = keep_ref.shape[0], keep_ref.shape[1]
    for n in range(squares):
        for ref, half in ((keep_ref, core), (give_ref, 1 - core)):
            start = pl.multiple_of((half * squares + (square ^ n)) * size, 8)
            ref[n] = out_ref[pl.ds(start, size), :].astype(ref.dtype)


def unpack(place_ref, keep_ref, got_ref, g1_hbm, g2_hbm, sums, first, sent):
    core, square = place_ref[0], place_ref[1]
    squares, size = keep_ref.shape[0], keep_ref.shape[1]
    for n in range(squares):
        for ref, half in ((keep_ref, core), (got_ref, 1 - core)):
            start = pl.multiple_of((half * squares + (square ^ n)) * size, 8)
            sums[pl.ds(start, size), :] = ref[-n % squares].astype(F32)
    second = pltpu.make_async_copy(sums.at[pl.ds(0, SECOND_ROWS)], g2_hbm, sent.at[0])
    second.start()
    found = [sums[SECOND_ROWS + 64 * n : SECOND_ROWS + 64 * (n + 1), :] for n in range(FIRST_BLOCKS)]
    first[...] = jnp.concatenate(found, axis=1)[:, : first.shape[1]]
    copy = pltpu.make_async_copy(first, g1_hbm, sent.at[1])
    copy.start()
    copy.wait()
    second.wait()


def local_grads(flags, place, squares, volume, faces, corners, cotangent, weights):
    planes = volume.shape[0]
    blocks = volume.shape[2] // LANES
    hidden_planes = planes // 2 + 3
    out_planes = planes // 4
    unit = 2 * squares * 16
    rows = -(-(SECOND_ROWS + 64 * FIRST_BLOCKS) // unit) * unit
    whole = pl.BlockSpec(memory_space=pltpu.VMEM)
    smem = pl.BlockSpec(memory_space=pltpu.SMEM)
    dep, row_a, row_b, edge_a, edge_b = faces
    tiles, parts = pl.pallas_call(
        own_blocks,
        out_shape=[
            jax.ShapeDtypeStruct((3, planes + 9, blocks, 16, LANES), BF16),
            jax.ShapeDtypeStruct((hidden_planes + 1, blocks, 16, 2 * LANES), F32),
        ],
        in_specs=[smem] + [whole] * 7,
        out_specs=[whole] * 2,
        scratch_shapes=[pltpu.VMEM((4, blocks, 40, LANES), F32)],
        compiler_params=pltpu.CompilerParams(vmem_limit_bytes=16 * 1024 * 1024),
        cost_estimate=pl.CostEstimate(flops=2 * 10**9, bytes_accessed=10**7, transcendentals=0),
    )(flags, volume, *faces, weights[0])
    scratch = [
        pltpu.VMEM((rows, LANES), F32),
        pltpu.VMEM((4, 2, 40, LANES), F32),
        pltpu.VMEM((3, planes + 7, 2, 16, LANES), BF16),
        pltpu.VMEM((hidden_planes, 2, 16, 2 * LANES), F32),
        pltpu.VMEM((hidden_planes, blocks + 2, 16, LANES), F32),
        pltpu.VMEM((3, hidden_planes, blocks + 2, 8, LANES), F32),
        pltpu.VMEM((3, out_planes + 3, blocks + 2, 16, LANES), BF16),
        pltpu.VMEM((out_planes + 1, blocks + 1, 8, LANES), F32),
        pltpu.VMEM((out_planes // 2 + 1, blocks + 1, 16, LANES), F32),
        pltpu.VMEM((out_planes // 2 + 1, blocks + 1, 16, LANES), BF16),
    ]
    operands = (tiles, parts, *faces, *corners, cotangent, *weights)
    return pl.pallas_call(
        body,
        out_shape=[jax.ShapeDtypeStruct((squares, rows // (2 * squares), LANES), dtype) for dtype in (F32, BF16)],
        in_specs=[smem] * 2 + [whole] * len(operands),
        out_specs=[whole] * 2,
        scratch_shapes=scratch,
        compiler_params=pltpu.CompilerParams(vmem_limit_bytes=28 * 1024 * 1024),
        cost_estimate=pl.CostEstimate(flops=4 * 10**9, bytes_accessed=10**7, transcendentals=0),
    )(flags, place, *operands)


def shards(volume, first_weight, second_weight, cotangent):
    half = lax.axis_index("depth")
    row, col = lax.axis_index("row"), lax.axis_index("col")
    rows, cols = lax.axis_size("row"), lax.axis_size("col")
    inner = [jnp.logical_and(i > 0, i < n - 1).astype(jnp.int32) for i, n in ((row, rows), (col, cols))]
    flags = jnp.stack([half, row % 2, col % 2, *inner])
    whole = pl.BlockSpec(memory_space=pltpu.VMEM)
    smem = pl.BlockSpec(memory_space=pltpu.SMEM)
    small = pltpu.CompilerParams(vmem_limit_bytes=12 * 1024 * 1024)
    planes, high, width = volume.shape
    groups = planes + cotangent.shape[0] // 4
    in_hbm = pl.BlockSpec(memory_space=pltpu.HBM)

    def stay(argument):
        return pltpu.with_memory_space_constraint(argument, pltpu.HBM)

    arguments = (volume, cotangent, first_weight, second_weight.T)
    shapes = [argument.shape for argument in arguments] + [(17, 4, width)]
    volume, cotangent, first_taps, second_taps, dep = pl.pallas_call(
        bring,
        out_shape=[jax.ShapeDtypeStruct(shape, BF16) for shape in shapes],
        in_specs=[smem] + [in_hbm] * 4,
        out_specs=[whole] * len(shapes),
        scratch_shapes=[pltpu.SemaphoreType.DMA((6,))],
        compiler_params=small,
    )(flags, *[stay(argument) for argument in arguments])
    row_b, row_a = pl.pallas_call(
        pack_rows,
        out_shape=[jax.ShapeDtypeStruct((groups, 4, width), BF16)] * 2,
        in_specs=[smem] + [whole] * 2,
        out_specs=[whole] * 2,
        compiler_params=small,
    )(flags, volume, cotangent)

    def to_col(block, kind):
        return lax.ppermute(block, ("row", "col"), pairs_of_lines(rows, cols, kind))

    dep = lax.ppermute(dep, "depth", [(0, 1), (1, 0)])
    route = []
    for i, j in pairs_on_line(rows, 1):
        route += [((d * rows + i) * cols + c, (d * rows + j) * cols + (c ^ 1 if i == j else c)) for d in (0, 1) for c in range(cols)]
    row_b = lax.ppermute(row_b, ("depth", "row", "col"), route)
    row_a = lax.ppermute(row_a, "row", pairs_on_line(rows, 0))
    side_a, side_b = pl.pallas_call(
        pack_sides,
        out_shape=[jax.ShapeDtypeStruct((groups, high, LANES), BF16)] * 2,
        in_specs=[smem] + [whole] * 2,
        out_specs=[whole] * 2,
        compiler_params=small,
    )(flags, volume, cotangent)
    dep, side_a, side_b, first_taps = lax.optimization_barrier((dep, side_a, side_b, first_taps))
    row_a, side_b = lax.optimization_barrier((row_a, side_b))
    side_a, side_b = to_col(side_a, 0), to_col(side_b, 1)
    low, top = [jnp.concatenate([dep[n : n + 1] for n in (*range(k, 16, 4), 16)], axis=0) for k in (0, 3)]
    even, ends = row % 2 == 0, jnp.logical_or(row == 0, row == rows - 1)
    edge_a = jnp.where(even, top, low)
    edge_b = jnp.where(ends, 0, jnp.where(even, low, top))
    edge_a = lax.ppermute(edge_a, "row", pairs_on_line(rows, 0))
    edge_b = lax.ppermute(edge_b, ("depth", "row"), pairs_of_lines(2, rows, 1))
    weights = pl.pallas_call(
        bands,
        out_shape=[jax.ShapeDtypeStruct(shape, BF16) for shape in ((1152, 256), (1152, 256), (9, 256, 128))],
        in_specs=[whole] * 2,
        out_specs=[whole] * 3,
        compiler_params=small,
    )(first_taps, second_taps)
    row_b, weights = lax.optimization_barrier((row_b, weights))
    col_a, col_b = pl.pallas_call(
        pack_corners,
        out_shape=[jax.ShapeDtypeStruct((planes + 14, 8, LANES), BF16)] * 2,
        in_specs=[smem] + [whole] * 5,
        out_specs=[whole] * 2,
        compiler_params=small,
    )(flags, row_b, row_a, dep, edge_a, edge_b)
    col_a, col_b, volume = lax.optimization_barrier((col_a, col_b, volume))
    col_a, col_b = to_col(col_a, 0), to_col(col_b, 1)

    spot = lax.axis_index(("depth", "row"))
    squares = lax.axis_size(("depth", "row")) // 2
    where = jnp.stack([spot % 2, spot // 2])
    faces, corners = (dep, row_a, row_b, edge_a, edge_b), (side_a, side_b, col_a, col_b)
    keep, give = local_grads(flags, where, squares, volume, faces, corners, cotangent, weights)

    def to_square(block, n):
        route = [(2 * i + c, 2 * (i ^ n) + c) for i in range(squares) for c in (0, 1)]
        return lax.ppermute(block, ("depth", "row"), route)

    def to_core(block):
        return lax.ppermute(block, ("depth", "row"), [(i, i ^ 1) for i in range(2 * squares)])

    def along_col(block, n):
        return lax.ppermute(block, "col", [(i, i ^ n) for i in range(cols)])

    both = keep + to_core(give).astype(F32)
    near = both.astype(BF16)
    order = [1, *reversed(range(2, squares))]
    share = add_up(both[0], *[to_square(near[n], n) for n in order])
    share = add_up(share, *[along_col(share, n) for n in range(1, cols)])
    mine = jnp.stack([share] + [to_square(share, n) for n in reversed(range(1, squares))])
    other = to_core(mine)
    grads = [jax.ShapeDtypeStruct(shape, F32) for shape in (first_weight.shape, second_weight.shape[::-1])]
    first_grad, second_grad = pl.pallas_call(
        unpack,
        out_shape=grads,
        in_specs=[smem] + [whole] * 2,
        out_specs=[in_hbm] * 2,
        scratch_shapes=[
            pltpu.VMEM((mine.shape[0] * mine.shape[1] * 2, LANES), F32),
            pltpu.VMEM(first_weight.shape, F32),
            pltpu.SemaphoreType.DMA((2,)),
        ],
        compiler_params=small,
    )(where, mine, other)
    return first_grad, second_grad.T


def solution(mesh):
    placed = (P("depth", "row", "col"), P(), P(), P("depth", "row", "col"))
    return jax.shard_map(shards, mesh=mesh, in_specs=placed, out_specs=(P(), P()), check_vma=False)
```

```python
import functools

import jax
import jax.numpy as jnp
from jax import lax
from jax.experimental import pallas as pl
from jax.experimental.pallas import tpu as pltpu
from jax.sharding import PartitionSpec as P

LANES = 128
SECOND_ROWS = 27 * 64
FIRST_BLOCKS = 7
F32 = jnp.float32
BF16 = jnp.bfloat16


def pairs_on_line(count, kind):
    firsts = range(kind, count - 1, 2)
    swapped = [(i, i + 1) for i in firsts] + [(i + 1, i) for i in firsts]
    met = {i for i, j in swapped}
    return swapped + [(i, i) for i in range(count) if i not in met]


def pairs_of_lines(lines, count, kind):
    route = []
    for line in range(lines):
        for i, j in pairs_on_line(count, kind):
            route.append((line * count + i, (line ^ 1 if i == j else line) * count + j))
    return route


def add_up(*terms):
    terms = [term.astype(F32) for term in terms]
    while len(terms) > 1:
        terms = [terms[n] + terms[n + 1] for n in range(0, len(terms), 2)]
    return terms[0].astype(BF16)


def matmul(left, right):
    return lax.dot_general(left, right, (((1,), (0,)), ((), ())), preferred_element_type=F32)


def bring(
    flag_ref, vol_hbm, cot_hbm, first_hbm, second_hbm, vol_ref, cot_ref, first_ref, second_ref, dep_ref, arrived
):
    first_plane = flag_ref[0] == 0
    planes, width = vol_ref.shape[0], vol_ref.shape[2]
    inner = pl.ds(4, planes - 8)
    copies = [pltpu.make_async_copy(cot_hbm, cot_ref, arrived.at[0])]
    for n, part in enumerate((pl.ds(0, 4), pl.ds(planes - 4, 4), inner)):
        copies.append(pltpu.make_async_copy(vol_hbm.at[part], vol_ref.at[part], arrived.at[1 + n]))
    copies.append(pltpu.make_async_copy(first_hbm, first_ref, arrived.at[4]))
    copies.append(pltpu.make_async_copy(second_hbm, second_ref, arrived.at[5]))
    for copy in copies:
        copy.start()
    for copy in copies[:3]:
        copy.wait()
    dep_ref[16] = cot_ref[0]
    for q in range(4):
        for m in range(width // LANES):
            lanes = slice(m * LANES, (m + 1) * LANES)
            last, start = vol_ref[planes - 4 + q, :, lanes].astype(F32), vol_ref[q, :, lanes].astype(F32)
            block = jnp.where(first_plane, last, start)
            for g in range(4):
                dep_ref[4 * q + g, :, lanes] = block[4 * g : 4 * g + 4].astype(BF16)
    for copy in copies[3:]:
        copy.wait()


def pack_rows(flag_ref, vol_ref, cot_ref, row_b_ref, row_a_ref):
    row_even, row_inner = flag_ref[1] == 0, flag_ref[3] != 0
    planes, high, width = vol_ref.shape
    cots = cot_ref.shape[0]

    def run(even, inner):
        def plane(d, carry):
            for m in range(width // LANES):
                lanes = slice(m * LANES, (m + 1) * LANES)
                low, top = vol_ref[d, :4, lanes], vol_ref[d, high - 4 :, lanes]
                row_a_ref[d, :, lanes] = top if even else low
                if inner:
                    row_b_ref[d, :, lanes] = low if even else top
                else:
                    row_b_ref[d, :, lanes] = jnp.zeros_like(low)
            return carry

        lax.fori_loop(0, planes, plane, 0, unroll=4)

    for even in (True, False):
        for inner in (True, False):
            here = jnp.logical_and(row_even == even, row_inner == inner)
            pl.when(here)(functools.partial(run, even, inner))
    for g in range(cots // 4):
        tops = jnp.concatenate([cot_ref[4 * g + n].astype(F32)[:1] for n in range(4)], axis=0)
        row_a_ref[planes + g] = tops.astype(BF16)
        row_b_ref[planes + g] = jnp.where(row_inner, tops, 0.0).astype(BF16)


def pack_sides(flag_ref, vol_ref, cot_ref, col_a_ref, col_b_ref):
    col_even, col_inner = flag_ref[2] == 0, flag_ref[4] != 0
    planes, high, width = vol_ref.shape
    cots = cot_ref.shape[0]
    for g in range(cots // 4):
        side = jnp.concatenate([cot_ref[4 * g + n, :, :LANES].astype(F32) for n in range(4)], axis=0)
        col_a_ref[planes + g] = side.astype(BF16)
        col_b_ref[planes + g] = jnp.where(col_inner, side, 0.0).astype(BF16)

    def plane(d, carry):
        left = vol_ref[d, :, :LANES].astype(F32)
        right = vol_ref[d, :, width - LANES :].astype(F32)
        col_a_ref[d] = jnp.where(col_even, right, left).astype(BF16)
        col_b_ref[d] = jnp.where(col_inner, jnp.where(col_even, left, right), 0.0).astype(BF16)
        return carry

    lax.fori_loop(0, planes, plane, 0, unroll=4)


def pack_corners(flag_ref, row_b_ref, row_a_ref, dep_ref, edge_a_ref, edge_b_ref, col_a_ref, col_b_ref):
    row_even, col_even, col_inner = flag_ref[1] == 0, flag_ref[2] == 0, flag_ref[4] != 0
    width = dep_ref.shape[2]
    groups = row_a_ref.shape[0]
    planes = (groups * 16) // 17
    faces = (slice(0, LANES), slice(width - LANES, width))

    def store(n, left, right):
        col_a_ref[n] = jnp.where(col_even, right, left).astype(BF16)
        col_b_ref[n] = jnp.where(col_inner, jnp.where(col_even, left, right), 0.0).astype(BF16)

    def lower_upper(a_ref, b_ref, source, target):
        values = []
        for lanes in faces:
            a, b = a_ref[source, :, lanes].astype(F32), b_ref[source, :, lanes].astype(F32)
            values.append(jnp.concatenate([jnp.where(row_even, b, a), jnp.where(row_even, a, b)], axis=0))
        store(target, *values)

    def plane(d, carry):
        lower_upper(row_a_ref, row_b_ref, d, d)
        return carry

    lax.fori_loop(0, planes, plane, 0, unroll=4)
    for q in range(4):
        lower_upper(edge_a_ref, edge_b_ref, q, planes + q)
        for n in range(2):
            units = range(4 * q + 2 * n, 4 * q + 2 * n + 2)
            store(
                planes + 4 + 2 * q + n,
                *[jnp.concatenate([dep_ref[u, :, lanes].astype(F32) for u in units], axis=0) for lanes in faces],
            )
    lanes = faces[0]
    tops = [
        jnp.where(row_even, row_a_ref[g, :, lanes].astype(F32), row_b_ref[g, :, lanes].astype(F32))
        for g in range(planes, groups)
    ]
    corner = jnp.where(row_even, edge_a_ref[4, :, lanes].astype(F32), edge_b_ref[4, :, lanes].astype(F32))
    own = dep_ref[16, :, lanes].astype(F32)
    for n, values in enumerate((jnp.concatenate(tops, axis=0), jnp.concatenate([own, corner], axis=0))):
        col_a_ref[planes + 12 + n] = values.astype(BF16)
        col_b_ref[planes + 12 + n] = jnp.where(col_inner, values, 0.0).astype(BF16)


def bands(first_ref, second_ref, w1_ref, w2_ref, w2b_ref):
    out_chan = first_ref.shape[0]
    first = first_ref[...].astype(F32)
    blank = jnp.zeros((out_chan, LANES), F32)
    for tap in range(9):
        rows = slice(tap * LANES, (tap + 1) * LANES)
        taps = first[:, tap * 96 : (tap + 1) * 96]
        main_even = jnp.concatenate([taps[:, 32:], blank[:, :64]], axis=1)
        main_odd = jnp.concatenate([blank[:, :32], taps], axis=1)
        prev_even = jnp.concatenate([blank[:, :96], taps[:, :32]], axis=1)
        w1_ref[rows] = jnp.concatenate([main_even, main_odd, prev_even, blank], axis=0).T.astype(BF16)
        main = second_ref[tap * 192 + 64 : (tap + 1) * 192, :]
        prev = jnp.concatenate([jnp.zeros((64, LANES), BF16), second_ref[tap * 192 : tap * 192 + 64, :]], axis=0)
        both = jnp.concatenate([main, prev], axis=1)
        w2_ref[rows] = both
        w2b_ref[tap] = both.astype(F32).T.astype(BF16)


def split_rows(stage, tiles, index, blocks):
    for m in blocks:
        rows = [stage[m, pl.ds(4 + s, 8, stride=4), :] for s in range(-1, 4)]
        for b in range(3):
            tiles[b, index, m] = jnp.concatenate([rows[b], rows[b + 2]], axis=0).astype(BF16)


def clear_stage(stage):
    stage[:, :, 0:8, :] = jnp.zeros(stage.shape[:2] + (8, LANES), F32)
    stage[:, :, 24:40, :] = jnp.zeros(stage.shape[:2] + (16, LANES), F32)


def ahead(even, a, b):
    return jnp.where(even, a.astype(F32), b.astype(F32))


def behind(even, a, b):
    return jnp.where(even, b.astype(F32), a.astype(F32))


def own_blocks(
    flag_ref, vol_ref, dep_ref, row_a_ref, row_b_ref, edge_a_ref, edge_b_ref, w1_ref, tiles, parts, stage
):
    first_plane, row_even = flag_ref[0] == 0, flag_ref[1] == 0
    planes = vol_ref.shape[0]
    blocks = vol_ref.shape[2] // LANES
    clear_stage(stage)

    def run(even):
        def place(n, target, own, a, b, keep):
            def kept(values):
                return values if keep is None else jnp.where(keep, values, 0.0)

            for m in range(blocks):
                lanes = slice(m * LANES, (m + 1) * LANES)
                stage[n, m, 8:24, :] = kept(own(lanes).astype(F32))
                stage[n, m, 4:8, :] = kept((b if even else a)(lanes).astype(F32))
                stage[n, m, 24:28, :] = kept((a if even else b)(lanes).astype(F32))
            split_rows(stage.at[n], tiles, target, range(blocks))

        def place_own(group, carry):
            for n in range(4):
                d = 4 * group + n
                place(
                    n, d + 3, lambda lanes: vol_ref[d, :, lanes],
                    lambda lanes: row_a_ref[d, :, lanes], lambda lanes: row_b_ref[d, :, lanes], None,
                )
            return carry

        def place_halo(target, q, keep):
            place(
                target % 4, target,
                lambda lanes: jnp.concatenate([dep_ref[4 * q + g, :, lanes].astype(F32) for g in range(4)], axis=0),
                lambda lanes: edge_a_ref[q, :, lanes], lambda lanes: edge_b_ref[q, :, lanes], keep,
            )

        lax.fori_loop(0, planes // 4, place_own, 0)
        for q in range(3):
            place_halo(q, q + 1, jnp.logical_not(first_plane))
        for q in range(4):
            place_halo(planes + 3 + q, q, first_plane)

    for even in (True, False):
        pl.when(row_even == even)(functools.partial(run, even))
    tiles[:, planes + 7 :] = jnp.zeros((3, 2, blocks, 16, LANES), BF16)

    group = 5

    def product(step, carry):
        taps = []
        for a in range(3):
            for b in range(3):
                start = 2 * group * step + a
                found = [tiles[b, start + 2 * n].reshape(blocks * 16, LANES) for n in range(group)]
                taps.append(jnp.concatenate(found, axis=0))
        found = matmul(jnp.concatenate(taps, axis=1), w1_ref[...])
        parts[pl.ds(group * step, group)] = found.reshape(group, blocks, 16, 2 * LANES)
        return carry

    lax.fori_loop(0, parts.shape[0] // group, product, 0)


def body(
    flag_ref, place_ref, tiles, parts, dep_ref, row_a_ref, row_b_ref, edge_a_ref, edge_b_ref,
    side_a_ref, side_b_ref, col_a_ref, col_b_ref, cot_ref, w1_ref, w2_ref, w2b_ref, keep_ref, give_ref,
    out_ref, stage, rim_tiles, rim_parts, slopes, hid, pairs, ups, deltas, shifted,
):
    first_plane, row_even, col_even = flag_ref[0] == 0, flag_ref[1] == 0, flag_ref[2] == 0
    planes = tiles.shape[1] - 9
    blocks = tiles.shape[2]
    half_planes = planes // 4
    hidden_planes = planes // 2 + 3

    clear_stage(stage)

    def run(even):
        def place(n, target, source, side_a, side_b, keep):
            for m in range(2):
                first = even == (m == 1)
                corners = (col_a_ref if first else col_b_ref)[source].astype(F32)
                own = (side_a if first else side_b).astype(F32)
                if keep is not None:
                    corners, own = jnp.where(keep, corners, 0.0), jnp.where(keep, own, 0.0)
                stage[n, m, 4:8, :] = corners[:4]
                stage[n, m, 8:24, :] = own
                stage[n, m, 24:28, :] = corners[4:]
            split_rows(stage.at[n], rim_tiles, target, range(2))

        def place_own(group, carry):
            for n in range(4):
                d = 4 * group + n
                place(n, d + 3, d, side_a_ref[d], side_b_ref[d], None)
            return carry

        def place_halo(target, q, keep):
            start = planes + 4 + 2 * q
            side_a = jnp.concatenate([col_a_ref[start].astype(F32), col_a_ref[start + 1].astype(F32)], axis=0)
            side_b = jnp.concatenate([col_b_ref[start].astype(F32), col_b_ref[start + 1].astype(F32)], axis=0)
            place(target % 4, target, planes + q, side_a, side_b, keep)

        lax.fori_loop(0, planes // 4, place_own, 0, unroll=2)
        for q in range(3):
            place_halo(q, q + 1, jnp.logical_not(first_plane))
        for q in range(4):
            place_halo(planes + 3 + q, q, first_plane)

    for even in (True, False):
        pl.when(col_even == even)(functools.partial(run, even))

    taps = []
    for a in range(3):
        for b in range(3):
            rows = [rim_tiles[b, 2 * i + a].reshape(32, LANES) for i in range(hidden_planes)]
            taps.append(jnp.concatenate(rows, axis=0))
    found = matmul(jnp.concatenate(taps, axis=1), w1_ref[...])
    rim_parts[...] = found.reshape(hidden_planes, 2, 16, 2 * LANES)

    def conv_one(i, carry):
        main, prev = parts[i, :, :, :LANES], parts[i, :, :, LANES:]
        rim, rim_prev = rim_parts[i, :, :, :LANES], rim_parts[i, 0:1, :, LANES:]
        blank = jnp.zeros((1, 16, LANES), F32)
        pre = jnp.concatenate([rim[:1], main, rim[1:]], axis=0) + jnp.concatenate([blank, rim_prev, prev], axis=0)
        square = pre * pre + 1.0
        inverse = lax.rsqrt(square)
        slopes[i] = 0.6 + 0.4 * (pre * inverse)
        hidden = (0.6 * pre + 0.4 * (square * inverse - 1.0)).astype(BF16).astype(F32)
        odd = hidden[:, 8:, :]
        hid[0, i] = pltpu.roll(odd, 1, 1)
        hid[1, i] = hidden[:, :8, :]
        hid[2, i] = odd
        return carry

    lax.fori_loop(0, hidden_planes, conv_one, 0, unroll=True)

    wide = (blocks + 2) * 16

    def pair(i, carry):
        for b in range(3):
            pairs[b, i] = jnp.concatenate([hid[b, i], hid[b, i + half_planes]], axis=1).astype(BF16)
        return carry

    lax.fori_loop(0, half_planes + 3, pair, 0, unroll=True)

    ups[...] = jnp.zeros_like(ups)
    for k in range(blocks):
        lanes = slice(k * LANES, (k + 1) * LANES)
        ups[0:half_planes, k, 1:5, :] = cot_ref[:, :, lanes].astype(F32)
        ups[half_planes, k, 1:5, :] = jnp.where(first_plane, dep_ref[16, :, lanes].astype(F32), 0.0)
        for g in range(half_planes // 4):
            tops = ahead(row_even, row_a_ref[planes + g, :, lanes], row_b_ref[planes + g, :, lanes])
            for n in range(4):
                ups[4 * g + n, k, 5:6, :] = tops[n : n + 1]
        corner = ahead(row_even, edge_a_ref[4, :, lanes], edge_b_ref[4, :, lanes])[:1]
        ups[half_planes, k, 5:6, :] = jnp.where(first_plane, corner, 0.0)
    for g in range(half_planes // 4):
        side = ahead(col_even, side_a_ref[planes + g], side_b_ref[planes + g])
        for n in range(4):
            ups[4 * g + n, blocks, 1:5, :] = side[4 * n : 4 * n + 4]
    tops = ahead(col_even, col_a_ref[planes + 12], col_b_ref[planes + 12])
    for n in range(half_planes):
        ups[n, blocks, 5:6, :] = tops[n : n + 1]
    beyond = jnp.where(first_plane, ahead(col_even, col_a_ref[planes + 13], col_b_ref[planes + 13]), 0.0)
    ups[half_planes, blocks, 1:6, :] = beyond[:5]

    quarter = half_planes // 2

    taps = []
    for a in range(3):
        for b in range(3):
            rows = [pairs[b, 2 * t + a].reshape(wide, LANES) for t in range(quarter + 1)]
            taps.append(jnp.concatenate(rows, axis=0))
    found = matmul(jnp.concatenate(taps, axis=1), w2_ref[...]).reshape(quarter + 1, blocks + 2, 16, 2 * LANES)
    for t in range(quarter + 1):
        pre = found[t, 1:, :, :LANES] + found[t, :-1, :, LANES:]
        slope = 0.6 + 0.4 * (pre * lax.rsqrt(pre * pre + 1.0))
        upstream = jnp.concatenate([ups[t], ups[t + quarter]], axis=1)
        delta = (upstream * slope).astype(BF16).astype(F32)
        moved = jnp.concatenate([pltpu.roll(delta[:, :8], 7, 1), pltpu.roll(delta[:, 8:], 7, 1)], axis=1)
        deltas[t] = delta
        shifted[t] = moved.astype(BF16)

    sublane = lax.broadcasted_iota(jnp.int32, (1, 1, 16, 1), 2) % 8
    own_rows = jnp.logical_and(sublane >= 1, sublane <= 4)

    def with_next(values, needed):
        values = values.T
        edge = jnp.zeros((LANES, values.shape[1] // blocks), values.dtype)
        here = jnp.concatenate([edge, values], axis=1)
        after = jnp.concatenate([values, edge], axis=1)[:needed]
        return jnp.concatenate([here, after], axis=0)

    own_delta = [jnp.where(own_rows[0], deltas[t, 0:blocks], 0.0) for t in range(quarter)]
    left = with_next(jnp.stack(own_delta, axis=1).reshape(blocks * quarter * 16, LANES), LANES).astype(BF16)

    def second_taps(tap):
        a, b = tap // 3, tap % 3
        found = [pairs[b, 2 * t + a, 0 : blocks + 1] for t in range(quarter)]
        return jnp.stack(found, axis=1).reshape((blocks + 1) * quarter * 16, LANES)

    for tap in range(0, 9, 2):
        right = [second_taps(x) for x in range(tap, min(tap + 2, 9))]
        found = matmul(left, jnp.concatenate(right, axis=1))
        for n in range(len(right)):
            row = (tap + n) * 192
            lanes = slice(n * LANES, (n + 1) * LANES)
            out_ref[row : row + 64, :] = found[LANES:, lanes].T[64:]
            out_ref[row + 64 : row + 192, :] = found[:LANES, lanes].T

    def pack(values):
        both = jnp.concatenate([values[:, :-1], values[:, 1:]], axis=3)
        return both.reshape(quarter * blocks * 16, 2 * LANES)

    plain = deltas[...].astype(BF16)
    moved = shifted[...]
    here, after = pack(plain[:-1]), pack(plain[1:])
    here_up, after_up = pack(moved[:-1]), pack(moved[1:])

    def back(values, taps):
        weights = jnp.concatenate([w2b_ref[3 * a + b] for a, b in taps], axis=1)
        found = matmul(values, weights)
        found = [found[:, n * LANES : (n + 1) * LANES] for n in range(len(taps))]
        return [part.reshape(quarter, blocks, 16, LANES) for part in found]

    here_11, here_12, here_21, here_22 = back(here, ((1, 1), (1, 2), (2, 1), (2, 2)))
    up_10, up_20 = back(here_up, ((1, 0), (2, 0)))
    after_01, after_02 = back(after, ((0, 1), (0, 2)))
    (after_00,) = back(after_up, ((0, 0),))
    rows = [[here_11, up_10 + here_12], [after_01 + here_21, after_00 + after_02 + up_20 + here_22]]
    own_list = []
    for i in range(planes // 2):
        t, parity = i // 2, i % 2
        half = slice(0, 8) if t < quarter else slice(8, 16)
        back_one = jnp.concatenate([rows[parity][p][t % quarter, :, half, :] for p in (0, 1)], axis=1)
        delta = back_one * slopes[i + 1, 1 : blocks + 1]
        own_list.append(jnp.where(own_rows[0], delta, 0.0).astype(BF16))
    left_one = with_next(jnp.stack(own_list, axis=1).reshape(blocks * (planes // 2) * 16, LANES), 64)

    def first_taps(tap):
        a, b = tap // 3, tap % 3
        found = []
        for m in range(blocks + 1):
            for i in range(planes // 2):
                index = 2 * (i + 1) + a
                found.append(rim_tiles[b, index, 0] if m == 0 else tiles[b, index, m - 1])
        return jnp.concatenate(found, axis=0)

    grads = []
    for tap in range(0, 9, 2):
        right = [first_taps(x) for x in range(tap, min(tap + 2, 9))]
        found = matmul(left_one, jnp.concatenate(right, axis=1))
        for n in range(len(right)):
            main = found[:LANES, n * LANES : (n + 1) * LANES]
            prev = found[LANES:, n * LANES : (n + 1) * LANES]
            even = jnp.concatenate([prev[:, 96:], main[:64, :64]], axis=1)
            grads.append(even + main[64:, 32:])
    grads.append(jnp.zeros((64, FIRST_BLOCKS * LANES - 9 * 96), F32))
    first = jnp.concatenate(grads, axis=1)
    for n in range(FIRST_BLOCKS):
        row = SECOND_ROWS + 64 * n
        out_ref[row : row + 64, :] = first[:, n * LANES : (n + 1) * LANES]
    used = SECOND_ROWS + 64 * FIRST_BLOCKS
    if out_ref.shape[0] > used:
        out_ref[used:, :] = jnp.zeros((out_ref.shape[0] - used, LANES), F32)

    core, square = place_ref[0], place_ref[1]
    squares, size = keep_ref.shape[0], keep_ref.shape[1]
    for n in range(squares):
        for ref, half in ((keep_ref, core), (give_ref, 1 - core)):
            start = pl.multiple_of((half * squares + (square ^ n)) * size, 8)
            ref[n] = out_ref[pl.ds(start, size), :].astype(ref.dtype)


def unpack(place_ref, keep_ref, got_ref, g1_hbm, g2_hbm, sums, first, sent):
    core, square = place_ref[0], place_ref[1]
    squares, size = keep_ref.shape[0], keep_ref.shape[1]
    for n in range(squares):
        for ref, half in ((keep_ref, core), (got_ref, 1 - core)):
            start = pl.multiple_of((half * squares + (square ^ n)) * size, 8)
            sums[pl.ds(start, size), :] = ref[-n % squares].astype(F32)
    second = pltpu.make_async_copy(sums.at[pl.ds(0, SECOND_ROWS)], g2_hbm, sent.at[0])
    second.start()
    found = [sums[SECOND_ROWS + 64 * n : SECOND_ROWS + 64 * (n + 1), :] for n in range(FIRST_BLOCKS)]
    first[...] = jnp.concatenate(found, axis=1)[:, : first.shape[1]]
    copy = pltpu.make_async_copy(first, g1_hbm, sent.at[1])
    copy.start()
    copy.wait()
    second.wait()


def local_grads(flags, place, squares, volume, faces, corners, cotangent, weights):
    planes = volume.shape[0]
    blocks = volume.shape[2] // LANES
    hidden_planes = planes // 2 + 3
    out_planes = planes // 4
    unit = 2 * squares * 16
    rows = -(-(SECOND_ROWS + 64 * FIRST_BLOCKS) // unit) * unit
    whole = pl.BlockSpec(memory_space=pltpu.VMEM)
    smem = pl.BlockSpec(memory_space=pltpu.SMEM)
    dep, row_a, row_b, edge_a, edge_b = faces
    tiles, parts = pl.pallas_call(
        own_blocks,
        out_shape=[
            jax.ShapeDtypeStruct((3, planes + 9, blocks, 16, LANES), BF16),
            jax.ShapeDtypeStruct((hidden_planes + 1, blocks, 16, 2 * LANES), F32),
        ],
        in_specs=[smem] + [whole] * 7,
        out_specs=[whole] * 2,
        scratch_shapes=[pltpu.VMEM((4, blocks, 40, LANES), F32)],
        compiler_params=pltpu.CompilerParams(vmem_limit_bytes=16 * 1024 * 1024),
        cost_estimate=pl.CostEstimate(flops=2 * 10**9, bytes_accessed=10**7, transcendentals=0),
    )(flags, volume, *faces, weights[0])
    scratch = [
        pltpu.VMEM((rows, LANES), F32),
        pltpu.VMEM((4, 2, 40, LANES), F32),
        pltpu.VMEM((3, planes + 7, 2, 16, LANES), BF16),
        pltpu.VMEM((hidden_planes, 2, 16, 2 * LANES), F32),
        pltpu.VMEM((hidden_planes, blocks + 2, 16, LANES), F32),
        pltpu.VMEM((3, hidden_planes, blocks + 2, 8, LANES), F32),
        pltpu.VMEM((3, out_planes + 3, blocks + 2, 16, LANES), BF16),
        pltpu.VMEM((out_planes + 1, blocks + 1, 8, LANES), F32),
        pltpu.VMEM((out_planes // 2 + 1, blocks + 1, 16, LANES), F32),
        pltpu.VMEM((out_planes // 2 + 1, blocks + 1, 16, LANES), BF16),
    ]
    operands = (tiles, parts, *faces, *corners, cotangent, *weights)
    return pl.pallas_call(
        body,
        out_shape=[jax.ShapeDtypeStruct((squares, rows // (2 * squares), LANES), dtype) for dtype in (F32, BF16)],
        in_specs=[smem] * 2 + [whole] * len(operands),
        out_specs=[whole] * 2,
        scratch_shapes=scratch,
        compiler_params=pltpu.CompilerParams(vmem_limit_bytes=28 * 1024 * 1024),
        cost_estimate=pl.CostEstimate(flops=4 * 10**9, bytes_accessed=10**7, transcendentals=0),
    )(flags, place, *operands)


def shards(volume, first_weight, second_weight, cotangent):
    half = lax.axis_index("depth")
    row, col = lax.axis_index("row"), lax.axis_index("col")
    rows, cols = lax.axis_size("row"), lax.axis_size("col")
    inner = [jnp.logical_and(i > 0, i < n - 1).astype(jnp.int32) for i, n in ((row, rows), (col, cols))]
    flags = jnp.stack([half, row % 2, col % 2, *inner])
    whole = pl.BlockSpec(memory_space=pltpu.VMEM)
    smem = pl.BlockSpec(memory_space=pltpu.SMEM)
    small = pltpu.CompilerParams(vmem_limit_bytes=12 * 1024 * 1024)
    planes, high, width = volume.shape
    groups = planes + cotangent.shape[0] // 4
    in_hbm = pl.BlockSpec(memory_space=pltpu.HBM)

    def stay(argument):
        return pltpu.with_memory_space_constraint(argument, pltpu.HBM)

    arguments = (volume, cotangent, first_weight, second_weight.T)
    shapes = [argument.shape for argument in arguments] + [(17, 4, width)]
    volume, cotangent, first_taps, second_taps, dep = pl.pallas_call(
        bring,
        out_shape=[jax.ShapeDtypeStruct(shape, BF16) for shape in shapes],
        in_specs=[smem] + [in_hbm] * 4,
        out_specs=[whole] * len(shapes),
        scratch_shapes=[pltpu.SemaphoreType.DMA((6,))],
        compiler_params=small,
    )(flags, *[stay(argument) for argument in arguments])
    row_b, row_a = pl.pallas_call(
        pack_rows,
        out_shape=[jax.ShapeDtypeStruct((groups, 4, width), BF16)] * 2,
        in_specs=[smem] + [whole] * 2,
        out_specs=[whole] * 2,
        compiler_params=small,
    )(flags, volume, cotangent)

    def to_col(block, kind):
        return lax.ppermute(block, ("row", "col"), pairs_of_lines(rows, cols, kind))

    dep = lax.ppermute(dep, "depth", [(0, 1), (1, 0)])
    route = []
    for i, j in pairs_on_line(rows, 1):
        route += [((d * rows + i) * cols + c, (d * rows + j) * cols + (c ^ 1 if i == j else c)) for d in (0, 1) for c in range(cols)]
    row_b = lax.ppermute(row_b, ("depth", "row", "col"), route)
    row_a = lax.ppermute(row_a, "row", pairs_on_line(rows, 0))
    side_a, side_b = pl.pallas_call(
        pack_sides,
        out_shape=[jax.ShapeDtypeStruct((groups, high, LANES), BF16)] * 2,
        in_specs=[smem] + [whole] * 2,
        out_specs=[whole] * 2,
        compiler_params=small,
    )(flags, volume, cotangent)
    dep, side_a, side_b, first_taps = lax.optimization_barrier((dep, side_a, side_b, first_taps))
    row_a, side_b = lax.optimization_barrier((row_a, side_b))
    side_a, side_b = to_col(side_a, 0), to_col(side_b, 1)
    low, top = [jnp.concatenate([dep[n : n + 1] for n in (*range(k, 16, 4), 16)], axis=0) for k in (0, 3)]
    even, ends = row % 2 == 0, jnp.logical_or(row == 0, row == rows - 1)
    edge_a = jnp.where(even, top, low)
    edge_b = jnp.where(ends, 0, jnp.where(even, low, top))
    edge_a = lax.ppermute(edge_a, "row", pairs_on_line(rows, 0))
    edge_b = lax.ppermute(edge_b, ("depth", "row"), pairs_of_lines(2, rows, 1))
    weights = pl.pallas_call(
        bands,
        out_shape=[jax.ShapeDtypeStruct(shape, BF16) for shape in ((1152, 256), (1152, 256), (9, 256, 128))],
        in_specs=[whole] * 2,
        out_specs=[whole] * 3,
        compiler_params=small,
    )(first_taps, second_taps)
    row_b, weights = lax.optimization_barrier((row_b, weights))
    col_a, col_b = pl.pallas_call(
        pack_corners,
        out_shape=[jax.ShapeDtypeStruct((planes + 14, 8, LANES), BF16)] * 2,
        in_specs=[smem] + [whole] * 5,
        out_specs=[whole] * 2,
        compiler_params=small,
    )(flags, row_b, row_a, dep, edge_a, edge_b)
    col_a, col_b, volume = lax.optimization_barrier((col_a, col_b, volume))
    col_a, col_b = to_col(col_a, 0), to_col(col_b, 1)

    spot = lax.axis_index(("depth", "row"))
    squares = lax.axis_size(("depth", "row")) // 2
    where = jnp.stack([spot % 2, spot // 2])
    faces, corners = (dep, row_a, row_b, edge_a, edge_b), (side_a, side_b, col_a, col_b)
    keep, give = local_grads(flags, where, squares, volume, faces, corners, cotangent, weights)

    def to_square(block, n):
        route = [(2 * i + c, 2 * (i ^ n) + c) for i in range(squares) for c in (0, 1)]
        return lax.ppermute(block, ("depth", "row"), route)

    def to_core(block):
        return lax.ppermute(block, ("depth", "row"), [(i, i ^ 1) for i in range(2 * squares)])

    def along_col(block, n):
        return lax.ppermute(block, "col", [(i, i ^ n) for i in range(cols)])

    both = keep + to_core(give).astype(F32)
    near = both.astype(BF16)
    order = [1, *reversed(range(2, squares))]
    share = add_up(both[0], *[to_square(near[n], n) for n in order])
    share = add_up(share, *[along_col(share, n) for n in range(1, cols)])
    mine = jnp.stack([share] + [to_square(share, n) for n in reversed(range(1, squares))])
    other = to_core(mine)
    grads = [jax.ShapeDtypeStruct(shape, F32) for shape in (first_weight.shape, second_weight.shape[::-1])]
    first_grad, second_grad = pl.pallas_call(
        unpack,
        out_shape=grads,
        in_specs=[smem] + [whole] * 2,
        out_specs=[in_hbm] * 2,
        scratch_shapes=[
            pltpu.VMEM((mine.shape[0] * mine.shape[1] * 2, LANES), F32),
            pltpu.VMEM(first_weight.shape, F32),
            pltpu.SemaphoreType.DMA((2,)),
        ],
        compiler_params=small,
    )(where, mine, other)
    return first_grad, second_grad.T


def solution(mesh):
    placed = (P("depth", "row", "col"), P(), P(), P("depth", "row", "col"))
    return jax.shard_map(shards, mesh=mesh, in_specs=placed, out_specs=(P(), P()), check_vma=False)
```

```python
import functools

import jax
import jax.numpy as jnp
from jax import lax
from jax.experimental import pallas as pl
from jax.experimental.pallas import tpu as pltpu
from jax.sharding import PartitionSpec as P

LANES = 128
SECOND_ROWS = 27 * 64
FIRST_BLOCKS = 7
F32 = jnp.float32
BF16 = jnp.bfloat16


def pairs_on_line(count, kind):
    firsts = range(kind, count - 1, 2)
    swapped = [(i, i + 1) for i in firsts] + [(i + 1, i) for i in firsts]
    met = {i for i, j in swapped}
    return swapped + [(i, i) for i in range(count) if i not in met]


def pairs_of_lines(lines, count, kind):
    route = []
    for line in range(lines):
        for i, j in pairs_on_line(count, kind):
            route.append((line * count + i, (line ^ 1 if i == j else line) * count + j))
    return route


def add_up(*terms):
    terms = [term.astype(F32) for term in terms]
    while len(terms) > 1:
        terms = [terms[n] + terms[n + 1] for n in range(0, len(terms), 2)]
    return terms[0].astype(BF16)


def matmul(left, right):
    return lax.dot_general(left, right, (((1,), (0,)), ((), ())), preferred_element_type=F32)


def bring(
    flag_ref, vol_hbm, cot_hbm, first_hbm, second_hbm, vol_ref, cot_ref, first_ref, second_ref, dep_ref, arrived
):
    first_plane = flag_ref[0] == 0
    planes, width = vol_ref.shape[0], vol_ref.shape[2]
    inner = pl.ds(4, planes - 8)
    copies = [pltpu.make_async_copy(cot_hbm, cot_ref, arrived.at[0])]
    for n, part in enumerate((pl.ds(0, 4), pl.ds(planes - 4, 4), inner)):
        copies.append(pltpu.make_async_copy(vol_hbm.at[part], vol_ref.at[part], arrived.at[1 + n]))
    copies.append(pltpu.make_async_copy(first_hbm, first_ref, arrived.at[4]))
    copies.append(pltpu.make_async_copy(second_hbm, second_ref, arrived.at[5]))
    for copy in copies:
        copy.start()
    for copy in copies[:3]:
        copy.wait()
    dep_ref[16] = cot_ref[0]
    for q in range(4):
        for m in range(width // LANES):
            lanes = slice(m * LANES, (m + 1) * LANES)
            last, start = vol_ref[planes - 4 + q, :, lanes].astype(F32), vol_ref[q, :, lanes].astype(F32)
            block = jnp.where(first_plane, last, start)
            for g in range(4):
                dep_ref[4 * q + g, :, lanes] = block[4 * g : 4 * g + 4].astype(BF16)
    for copy in copies[3:]:
        copy.wait()


def pack_rows(flag_ref, vol_ref, cot_ref, row_b_ref, row_a_ref):
    row_even, row_inner = flag_ref[1] == 0, flag_ref[3] != 0
    planes, high, width = vol_ref.shape
    cots = cot_ref.shape[0]

    def run(even, inner):
        def plane(d, carry):
            for m in range(width // LANES):
                lanes = slice(m * LANES, (m + 1) * LANES)
                low, top = vol_ref[d, :4, lanes], vol_ref[d, high - 4 :, lanes]
                row_a_ref[d, :, lanes] = top if even else low
                if inner:
                    row_b_ref[d, :, lanes] = low if even else top
                else:
                    row_b_ref[d, :, lanes] = jnp.zeros_like(low)
            return carry

        lax.fori_loop(0, planes, plane, 0, unroll=4)

    for even in (True, False):
        for inner in (True, False):
            here = jnp.logical_and(row_even == even, row_inner == inner)
            pl.when(here)(functools.partial(run, even, inner))
    for g in range(cots // 4):
        tops = jnp.concatenate([cot_ref[4 * g + n].astype(F32)[:1] for n in range(4)], axis=0)
        row_a_ref[planes + g] = tops.astype(BF16)
        row_b_ref[planes + g] = jnp.where(row_inner, tops, 0.0).astype(BF16)


def pack_sides(flag_ref, vol_ref, cot_ref, col_a_ref, col_b_ref):
    col_even, col_inner = flag_ref[2] == 0, flag_ref[4] != 0
    planes, high, width = vol_ref.shape
    cots = cot_ref.shape[0]
    for g in range(cots // 4):
        side = jnp.concatenate([cot_ref[4 * g + n, :, :LANES].astype(F32) for n in range(4)], axis=0)
        col_a_ref[planes + g] = side.astype(BF16)
        col_b_ref[planes + g] = jnp.where(col_inner, side, 0.0).astype(BF16)

    def plane(d, carry):
        left = vol_ref[d, :, :LANES].astype(F32)
        right = vol_ref[d, :, width - LANES :].astype(F32)
        col_a_ref[d] = jnp.where(col_even, right, left).astype(BF16)
        col_b_ref[d] = jnp.where(col_inner, jnp.where(col_even, left, right), 0.0).astype(BF16)
        return carry

    lax.fori_loop(0, planes, plane, 0, unroll=4)


def pack_corners(flag_ref, row_b_ref, row_a_ref, dep_ref, edge_a_ref, edge_b_ref, col_a_ref, col_b_ref):
    row_even, col_even, col_inner = flag_ref[1] == 0, flag_ref[2] == 0, flag_ref[4] != 0
    width = dep_ref.shape[2]
    groups = row_a_ref.shape[0]
    planes = (groups * 16) // 17
    faces = (slice(0, LANES), slice(width - LANES, width))

    def store(n, left, right):
        col_a_ref[n] = jnp.where(col_even, right, left).astype(BF16)
        col_b_ref[n] = jnp.where(col_inner, jnp.where(col_even, left, right), 0.0).astype(BF16)

    def lower_upper(a_ref, b_ref, source, target):
        values = []
        for lanes in faces:
            a, b = a_ref[source, :, lanes].astype(F32), b_ref[source, :, lanes].astype(F32)
            values.append(jnp.concatenate([jnp.where(row_even, b, a), jnp.where(row_even, a, b)], axis=0))
        store(target, *values)

    def plane(d, carry):
        lower_upper(row_a_ref, row_b_ref, d, d)
        return carry

    lax.fori_loop(0, planes, plane, 0, unroll=4)
    for q in range(4):
        lower_upper(edge_a_ref, edge_b_ref, q, planes + q)
        for n in range(2):
            units = range(4 * q + 2 * n, 4 * q + 2 * n + 2)
            store(
                planes + 4 + 2 * q + n,
                *[jnp.concatenate([dep_ref[u, :, lanes].astype(F32) for u in units], axis=0) for lanes in faces],
            )
    lanes = faces[0]
    tops = [
        jnp.where(row_even, row_a_ref[g, :, lanes].astype(F32), row_b_ref[g, :, lanes].astype(F32))
        for g in range(planes, groups)
    ]
    corner = jnp.where(row_even, edge_a_ref[4, :, lanes].astype(F32), edge_b_ref[4, :, lanes].astype(F32))
    own = dep_ref[16, :, lanes].astype(F32)
    for n, values in enumerate((jnp.concatenate(tops, axis=0), jnp.concatenate([own, corner], axis=0))):
        col_a_ref[planes + 12 + n] = values.astype(BF16)
        col_b_ref[planes + 12 + n] = jnp.where(col_inner, values, 0.0).astype(BF16)


def bands(first_ref, second_ref, w1_ref, w2_ref, w2b_ref):
    out_chan = first_ref.shape[0]
    first = first_ref[...].astype(F32)
    blank = jnp.zeros((out_chan, LANES), F32)
    for tap in range(9):
        rows = slice(tap * LANES, (tap + 1) * LANES)
        taps = first[:, tap * 96 : (tap + 1) * 96]
        main_even = jnp.concatenate([taps[:, 32:], blank[:, :64]], axis=1)
        main_odd = jnp.concatenate([blank[:, :32], taps], axis=1)
        prev_even = jnp.concatenate([blank[:, :96], taps[:, :32]], axis=1)
        w1_ref[rows] = jnp.concatenate([main_even, main_odd, prev_even, blank], axis=0).T.astype(BF16)
        main = second_ref[tap * 192 + 64 : (tap + 1) * 192, :]
        prev = jnp.concatenate([jnp.zeros((64, LANES), BF16), second_ref[tap * 192 : tap * 192 + 64, :]], axis=0)
        both = jnp.concatenate([main, prev], axis=1)
        w2_ref[rows] = both
        w2b_ref[tap] = both.astype(F32).T.astype(BF16)


def split_rows(stage, tiles, index, blocks):
    for m in blocks:
        rows = [stage[m, pl.ds(4 + s, 8, stride=4), :] for s in range(-1, 4)]
        for b in range(3):
            tiles[b, index, m] = jnp.concatenate([rows[b], rows[b + 2]], axis=0).astype(BF16)


def clear_stage(stage):
    stage[:, :, 0:8, :] = jnp.zeros(stage.shape[:2] + (8, LANES), F32)
    stage[:, :, 24:40, :] = jnp.zeros(stage.shape[:2] + (16, LANES), F32)


def ahead(even, a, b):
    return jnp.where(even, a.astype(F32), b.astype(F32))


def behind(even, a, b):
    return jnp.where(even, b.astype(F32), a.astype(F32))


def own_blocks(
    flag_ref, vol_ref, dep_ref, row_a_ref, row_b_ref, edge_a_ref, edge_b_ref, w1_ref, tiles, parts, stage
):
    first_plane, row_even = flag_ref[0] == 0, flag_ref[1] == 0
    planes = vol_ref.shape[0]
    blocks = vol_ref.shape[2] // LANES
    clear_stage(stage)

    def run(even):
        def place(n, target, own, a, b, keep):
            def kept(values):
                return values if keep is None else jnp.where(keep, values, 0.0)

            for m in range(blocks):
                lanes = slice(m * LANES, (m + 1) * LANES)
                stage[n, m, 8:24, :] = kept(own(lanes).astype(F32))
                stage[n, m, 4:8, :] = kept((b if even else a)(lanes).astype(F32))
                stage[n, m, 24:28, :] = kept((a if even else b)(lanes).astype(F32))
            split_rows(stage.at[n], tiles, target, range(blocks))

        def place_own(group, carry):
            for n in range(4):
                d = 4 * group + n
                place(
                    n, d + 3, lambda lanes: vol_ref[d, :, lanes],
                    lambda lanes: row_a_ref[d, :, lanes], lambda lanes: row_b_ref[d, :, lanes], None,
                )
            return carry

        def place_halo(target, q, keep):
            place(
                target % 4, target,
                lambda lanes: jnp.concatenate([dep_ref[4 * q + g, :, lanes].astype(F32) for g in range(4)], axis=0),
                lambda lanes: edge_a_ref[q, :, lanes], lambda lanes: edge_b_ref[q, :, lanes], keep,
            )

        lax.fori_loop(0, planes // 4, place_own, 0, unroll=2)
        for q in range(3):
            place_halo(q, q + 1, jnp.logical_not(first_plane))
        for q in range(4):
            place_halo(planes + 3 + q, q, first_plane)

    for even in (True, False):
        pl.when(row_even == even)(functools.partial(run, even))
    tiles[:, planes + 7 :] = jnp.zeros((3, 2, blocks, 16, LANES), BF16)

    group = 5

    def product(step, carry):
        taps = []
        for a in range(3):
            for b in range(3):
                start = 2 * group * step + a
                found = [tiles[b, start + 2 * n].reshape(blocks * 16, LANES) for n in range(group)]
                taps.append(jnp.concatenate(found, axis=0))
        found = matmul(jnp.concatenate(taps, axis=1), w1_ref[...])
        parts[pl.ds(group * step, group)] = found.reshape(group, blocks, 16, 2 * LANES)
        return carry

    lax.fori_loop(0, parts.shape[0] // group, product, 0, unroll=True)


def body(
    flag_ref, place_ref, tiles, parts, dep_ref, row_a_ref, row_b_ref, edge_a_ref, edge_b_ref,
    side_a_ref, side_b_ref, col_a_ref, col_b_ref, cot_ref, w1_ref, w2_ref, w2b_ref, keep_ref, give_ref,
    out_ref, stage, rim_tiles, rim_parts, slopes, hid, pairs, ups, deltas, shifted,
):
    first_plane, row_even, col_even = flag_ref[0] == 0, flag_ref[1] == 0, flag_ref[2] == 0
    planes = tiles.shape[1] - 9
    blocks = tiles.shape[2]
    half_planes = planes // 4
    hidden_planes = planes // 2 + 3

    clear_stage(stage)

    def run(even):
        def place(n, target, source, side_a, side_b, keep):
            for m in range(2):
                first = even == (m == 1)
                corners = (col_a_ref if first else col_b_ref)[source].astype(F32)
                own = (side_a if first else side_b).astype(F32)
                if keep is not None:
                    corners, own = jnp.where(keep, corners, 0.0), jnp.where(keep, own, 0.0)
                stage[n, m, 4:8, :] = corners[:4]
                stage[n, m, 8:24, :] = own
                stage[n, m, 24:28, :] = corners[4:]
            split_rows(stage.at[n], rim_tiles, target, range(2))

        def place_own(group, carry):
            for n in range(4):
                d = 4 * group + n
                place(n, d + 3, d, side_a_ref[d], side_b_ref[d], None)
            return carry

        def place_halo(target, q, keep):
            start = planes + 4 + 2 * q
            side_a = jnp.concatenate([col_a_ref[start].astype(F32), col_a_ref[start + 1].astype(F32)], axis=0)
            side_b = jnp.concatenate([col_b_ref[start].astype(F32), col_b_ref[start + 1].astype(F32)], axis=0)
            place(target % 4, target, planes + q, side_a, side_b, keep)

        lax.fori_loop(0, planes // 4, place_own, 0, unroll=2)
        for q in range(3):
            place_halo(q, q + 1, jnp.logical_not(first_plane))
        for q in range(4):
            place_halo(planes + 3 + q, q, first_plane)

    for even in (True, False):
        pl.when(col_even == even)(functools.partial(run, even))

    taps = []
    for a in range(3):
        for b in range(3):
            rows = [rim_tiles[b, 2 * i + a].reshape(32, LANES) for i in range(hidden_planes)]
            taps.append(jnp.concatenate(rows, axis=0))
    found = matmul(jnp.concatenate(taps, axis=1), w1_ref[...])
    rim_parts[...] = found.reshape(hidden_planes, 2, 16, 2 * LANES)

    def conv_one(i):
        main, prev = parts[i, :, :, :LANES], parts[i, :, :, LANES:]
        rim, rim_prev = rim_parts[i, :, :, :LANES], rim_parts[i, 0:1, :, LANES:]
        blank = jnp.zeros((1, 16, LANES), F32)
        pre = jnp.concatenate([rim[:1], main, rim[1:]], axis=0) + jnp.concatenate([blank, rim_prev, prev], axis=0)
        square = pre * pre + 1.0
        inverse = lax.rsqrt(square)
        if 1 <= i <= planes // 2:
            own = slice(1, blocks + 1)
            slopes[i - 1] = 0.6 + 0.4 * (pre[own] * inverse[own])
        hidden = (0.6 * pre + 0.4 * (square * inverse - 1.0)).astype(BF16).astype(F32)
        odd = hidden[:, 8:, :]
        hid[0, i] = pltpu.roll(odd, 1, 1)
        hid[1, i] = hidden[:, :8, :]
        hid[2, i] = odd

    for i in range(hidden_planes):
        conv_one(i)

    wide = (blocks + 2) * 16

    def pair(i, carry):
        for b in range(3):
            pairs[b, i] = jnp.concatenate([hid[b, i], hid[b, i + half_planes]], axis=1).astype(BF16)
        return carry

    lax.fori_loop(0, half_planes + 3, pair, 0, unroll=True)

    ups[...] = jnp.zeros_like(ups)
    for k in range(blocks):
        lanes = slice(k * LANES, (k + 1) * LANES)
        ups[0:half_planes, k, 1:5, :] = cot_ref[:, :, lanes].astype(F32)
        ups[half_planes, k, 1:5, :] = jnp.where(first_plane, dep_ref[16, :, lanes].astype(F32), 0.0)
        for g in range(half_planes // 4):
            tops = ahead(row_even, row_a_ref[planes + g, :, lanes], row_b_ref[planes + g, :, lanes])
            for n in range(4):
                ups[4 * g + n, k, 5:6, :] = tops[n : n + 1]
        corner = ahead(row_even, edge_a_ref[4, :, lanes], edge_b_ref[4, :, lanes])[:1]
        ups[half_planes, k, 5:6, :] = jnp.where(first_plane, corner, 0.0)
    for g in range(half_planes // 4):
        side = ahead(col_even, side_a_ref[planes + g], side_b_ref[planes + g])
        for n in range(4):
            ups[4 * g + n, blocks, 1:5, :] = side[4 * n : 4 * n + 4]
    tops = ahead(col_even, col_a_ref[planes + 12], col_b_ref[planes + 12])
    for n in range(half_planes):
        ups[n, blocks, 5:6, :] = tops[n : n + 1]
    beyond = jnp.where(first_plane, ahead(col_even, col_a_ref[planes + 13], col_b_ref[planes + 13]), 0.0)
    ups[half_planes, blocks, 1:6, :] = beyond[:5]

    quarter = half_planes // 2

    taps = []
    for a in range(3):
        for b in range(3):
            rows = [pairs[b, 2 * t + a].reshape(wide, LANES) for t in range(quarter + 1)]
            taps.append(jnp.concatenate(rows, axis=0))
    found = matmul(jnp.concatenate(taps, axis=1), w2_ref[...]).reshape(quarter + 1, blocks + 2, 16, 2 * LANES)
    for t in range(quarter + 1):
        pre = found[t, 1:, :, :LANES] + found[t, :-1, :, LANES:]
        slope = 0.6 + 0.4 * (pre * lax.rsqrt(pre * pre + 1.0))
        upstream = jnp.concatenate([ups[t], ups[t + quarter]], axis=1)
        delta = (upstream * slope).astype(BF16).astype(F32)
        moved = jnp.concatenate([pltpu.roll(delta[:, :8], 7, 1), pltpu.roll(delta[:, 8:], 7, 1)], axis=1)
        deltas[t] = delta
        shifted[t] = moved.astype(BF16)

    sublane = lax.broadcasted_iota(jnp.int32, (1, 1, 16, 1), 2) % 8
    own_rows = jnp.logical_and(sublane >= 1, sublane <= 4)

    def with_next(values, needed):
        values = values.T
        edge = jnp.zeros((LANES, values.shape[1] // blocks), values.dtype)
        here = jnp.concatenate([edge, values], axis=1)
        after = jnp.concatenate([values, edge], axis=1)[:needed]
        return jnp.concatenate([here, after], axis=0)

    own_delta = [jnp.where(own_rows[0], deltas[t, 0:blocks], 0.0) for t in range(quarter)]
    left = with_next(jnp.stack(own_delta, axis=1).reshape(blocks * quarter * 16, LANES), LANES).astype(BF16)

    def second_taps(tap):
        a, b = tap // 3, tap % 3
        found = [pairs[b, 2 * t + a, 0 : blocks + 1] for t in range(quarter)]
        return jnp.stack(found, axis=1).reshape((blocks + 1) * quarter * 16, LANES)

    for tap in range(0, 9, 2):
        right = [second_taps(x) for x in range(tap, min(tap + 2, 9))]
        found = matmul(left, jnp.concatenate(right, axis=1))
        for n in range(len(right)):
            row = (tap + n) * 192
            lanes = slice(n * LANES, (n + 1) * LANES)
            out_ref[row : row + 64, :] = found[LANES:, lanes].T[64:]
            out_ref[row + 64 : row + 192, :] = found[:LANES, lanes].T

    def pack(values):
        both = jnp.concatenate([values[:, :-1], values[:, 1:]], axis=3)
        return both.reshape(quarter * blocks * 16, 2 * LANES)

    plain = deltas[...].astype(BF16)
    moved = shifted[...]
    here, after = pack(plain[:-1]), pack(plain[1:])
    here_up, after_up = pack(moved[:-1]), pack(moved[1:])

    def back(values, taps):
        weights = jnp.concatenate([w2b_ref[3 * a + b] for a, b in taps], axis=1)
        found = matmul(values, weights)
        found = [found[:, n * LANES : (n + 1) * LANES] for n in range(len(taps))]
        return [part.reshape(quarter, blocks, 16, LANES) for part in found]

    here_11, here_12, here_21, here_22 = back(here, ((1, 1), (1, 2), (2, 1), (2, 2)))
    up_10, up_20 = back(here_up, ((1, 0), (2, 0)))
    after_01, after_02 = back(after, ((0, 1), (0, 2)))
    (after_00,) = back(after_up, ((0, 0),))
    rows = [[here_11, up_10 + here_12], [after_01 + here_21, after_00 + after_02 + up_20 + here_22]]
    own_list = []
    for i in range(planes // 2):
        t, parity = i // 2, i % 2
        half = slice(0, 8) if t < quarter else slice(8, 16)
        back_one = jnp.concatenate([rows[parity][p][t % quarter, :, half, :] for p in (0, 1)], axis=1)
        delta = back_one * slopes[i]
        own_list.append(jnp.where(own_rows[0], delta, 0.0).astype(BF16))
    left_one = with_next(jnp.stack(own_list, axis=1).reshape(blocks * (planes // 2) * 16, LANES), 64)

    def first_taps(tap):
        a, b = tap // 3, tap % 3
        found = []
        for m in range(blocks + 1):
            for i in range(planes // 2):
                index = 2 * (i + 1) + a
                found.append(rim_tiles[b, index, 0] if m == 0 else tiles[b, index, m - 1])
        return jnp.concatenate(found, axis=0)

    grads = []
    for tap in range(0, 9, 2):
        right = [first_taps(x) for x in range(tap, min(tap + 2, 9))]
        found = matmul(left_one, jnp.concatenate(right, axis=1))
        for n in range(len(right)):
            main = found[:LANES, n * LANES : (n + 1) * LANES]
            prev = found[LANES:, n * LANES : (n + 1) * LANES]
            even = jnp.concatenate([prev[:, 96:], main[:64, :64]], axis=1)
            grads.append(even + main[64:, 32:])
    grads.append(jnp.zeros((64, FIRST_BLOCKS * LANES - 9 * 96), F32))
    first = jnp.concatenate(grads, axis=1)
    for n in range(FIRST_BLOCKS):
        row = SECOND_ROWS + 64 * n
        out_ref[row : row + 64, :] = first[:, n * LANES : (n + 1) * LANES]
    used = SECOND_ROWS + 64 * FIRST_BLOCKS
    if out_ref.shape[0] > used:
        out_ref[used:, :] = jnp.zeros((out_ref.shape[0] - used, LANES), F32)

    core, square = place_ref[0], place_ref[1]
    squares, size = keep_ref.shape[0], keep_ref.shape[1]
    for n in range(squares):
        for ref, half in ((keep_ref, core), (give_ref, 1 - core)):
            start = pl.multiple_of((half * squares + (square ^ n)) * size, 8)
            ref[n] = out_ref[pl.ds(start, size), :].astype(ref.dtype)


def unpack(place_ref, keep_ref, got_ref, g1_hbm, g2_hbm, sums, first, sent):
    core, square = place_ref[0], place_ref[1]
    squares, size = keep_ref.shape[0], keep_ref.shape[1]
    for n in range(squares):
        for ref, half in ((keep_ref, core), (got_ref, 1 - core)):
            start = pl.multiple_of((half * squares + (square ^ n)) * size, 8)
            sums[pl.ds(start, size), :] = ref[-n % squares].astype(F32)
    second = pltpu.make_async_copy(sums.at[pl.ds(0, SECOND_ROWS)], g2_hbm, sent.at[0])
    second.start()
    found = [sums[SECOND_ROWS + 64 * n : SECOND_ROWS + 64 * (n + 1), :] for n in range(FIRST_BLOCKS)]
    first[...] = jnp.concatenate(found, axis=1)[:, : first.shape[1]]
    copy = pltpu.make_async_copy(first, g1_hbm, sent.at[1])
    copy.start()
    copy.wait()
    second.wait()


def local_grads(flags, place, squares, volume, faces, corners, cotangent, weights):
    planes = volume.shape[0]
    blocks = volume.shape[2] // LANES
    hidden_planes = planes // 2 + 3
    out_planes = planes // 4
    unit = 2 * squares * 16
    rows = -(-(SECOND_ROWS + 64 * FIRST_BLOCKS) // unit) * unit
    whole = pl.BlockSpec(memory_space=pltpu.VMEM)
    smem = pl.BlockSpec(memory_space=pltpu.SMEM)
    dep, row_a, row_b, edge_a, edge_b = faces
    tiles, parts = pl.pallas_call(
        own_blocks,
        out_shape=[
            jax.ShapeDtypeStruct((3, planes + 9, blocks, 16, LANES), BF16),
            jax.ShapeDtypeStruct((hidden_planes + 1, blocks, 16, 2 * LANES), F32),
        ],
        in_specs=[smem] + [whole] * 7,
        out_specs=[whole] * 2,
        scratch_shapes=[pltpu.VMEM((4, blocks, 40, LANES), F32)],
        compiler_params=pltpu.CompilerParams(vmem_limit_bytes=16 * 1024 * 1024),
        cost_estimate=pl.CostEstimate(flops=2 * 10**9, bytes_accessed=10**7, transcendentals=0),
    )(flags, volume, *faces, weights[0])
    scratch = [
        pltpu.VMEM((rows, LANES), F32),
        pltpu.VMEM((4, 2, 40, LANES), F32),
        pltpu.VMEM((3, planes + 7, 2, 16, LANES), BF16),
        pltpu.VMEM((hidden_planes, 2, 16, 2 * LANES), F32),
        pltpu.VMEM((planes // 2, blocks, 16, LANES), F32),
        pltpu.VMEM((3, hidden_planes, blocks + 2, 8, LANES), F32),
        pltpu.VMEM((3, out_planes + 3, blocks + 2, 16, LANES), BF16),
        pltpu.VMEM((out_planes + 1, blocks + 1, 8, LANES), F32),
        pltpu.VMEM((out_planes // 2 + 1, blocks + 1, 16, LANES), F32),
        pltpu.VMEM((out_planes // 2 + 1, blocks + 1, 16, LANES), BF16),
    ]
    operands = (tiles, parts, *faces, *corners, cotangent, *weights)
    return pl.pallas_call(
        body,
        out_shape=[jax.ShapeDtypeStruct((squares, rows // (2 * squares), LANES), dtype) for dtype in (F32, BF16)],
        in_specs=[smem] * 2 + [whole] * len(operands),
        out_specs=[whole] * 2,
        scratch_shapes=scratch,
        compiler_params=pltpu.CompilerParams(vmem_limit_bytes=28 * 1024 * 1024),
        cost_estimate=pl.CostEstimate(flops=4 * 10**9, bytes_accessed=10**7, transcendentals=0),
    )(flags, place, *operands)


def shards(volume, first_weight, second_weight, cotangent):
    half = lax.axis_index("depth")
    row, col = lax.axis_index("row"), lax.axis_index("col")
    rows, cols = lax.axis_size("row"), lax.axis_size("col")
    inner = [jnp.logical_and(i > 0, i < n - 1).astype(jnp.int32) for i, n in ((row, rows), (col, cols))]
    flags = jnp.stack([half, row % 2, col % 2, *inner])
    whole = pl.BlockSpec(memory_space=pltpu.VMEM)
    smem = pl.BlockSpec(memory_space=pltpu.SMEM)
    small = pltpu.CompilerParams(vmem_limit_bytes=12 * 1024 * 1024)
    planes, high, width = volume.shape
    groups = planes + cotangent.shape[0] // 4
    in_hbm = pl.BlockSpec(memory_space=pltpu.HBM)

    def stay(argument):
        return pltpu.with_memory_space_constraint(argument, pltpu.HBM)

    arguments = (volume, cotangent, first_weight, second_weight.T)
    shapes = [argument.shape for argument in arguments] + [(17, 4, width)]
    volume, cotangent, first_taps, second_taps, dep = pl.pallas_call(
        bring,
        out_shape=[jax.ShapeDtypeStruct(shape, BF16) for shape in shapes],
        in_specs=[smem] + [in_hbm] * 4,
        out_specs=[whole] * len(shapes),
        scratch_shapes=[pltpu.SemaphoreType.DMA((6,))],
        compiler_params=small,
    )(flags, *[stay(argument) for argument in arguments])
    row_b, row_a = pl.pallas_call(
        pack_rows,
        out_shape=[jax.ShapeDtypeStruct((groups, 4, width), BF16)] * 2,
        in_specs=[smem] + [whole] * 2,
        out_specs=[whole] * 2,
        compiler_params=small,
    )(flags, volume, cotangent)

    def to_col(block, kind):
        return lax.ppermute(block, ("row", "col"), pairs_of_lines(rows, cols, kind))

    dep = lax.ppermute(dep, "depth", [(0, 1), (1, 0)])
    route = []
    for i, j in pairs_on_line(rows, 1):
        route += [((d * rows + i) * cols + c, (d * rows + j) * cols + (c ^ 1 if i == j else c)) for d in (0, 1) for c in range(cols)]
    row_b = lax.ppermute(row_b, ("depth", "row", "col"), route)
    row_a = lax.ppermute(row_a, "row", pairs_on_line(rows, 0))
    side_a, side_b = pl.pallas_call(
        pack_sides,
        out_shape=[jax.ShapeDtypeStruct((groups, high, LANES), BF16)] * 2,
        in_specs=[smem] + [whole] * 2,
        out_specs=[whole] * 2,
        compiler_params=small,
    )(flags, volume, cotangent)
    dep, side_a, side_b, first_taps = lax.optimization_barrier((dep, side_a, side_b, first_taps))
    row_a, side_b = lax.optimization_barrier((row_a, side_b))
    side_a, side_b = to_col(side_a, 0), to_col(side_b, 1)
    low, top = [jnp.concatenate([dep[n : n + 1] for n in (*range(k, 16, 4), 16)], axis=0) for k in (0, 3)]
    even, ends = row % 2 == 0, jnp.logical_or(row == 0, row == rows - 1)
    edge_a = jnp.where(even, top, low)
    edge_b = jnp.where(ends, 0, jnp.where(even, low, top))
    edge_a = lax.ppermute(edge_a, "row", pairs_on_line(rows, 0))
    edge_b = lax.ppermute(edge_b, ("depth", "row"), pairs_of_lines(2, rows, 1))
    weights = pl.pallas_call(
        bands,
        out_shape=[jax.ShapeDtypeStruct(shape, BF16) for shape in ((1152, 256), (1152, 256), (9, 256, 128))],
        in_specs=[whole] * 2,
        out_specs=[whole] * 3,
        compiler_params=small,
    )(first_taps, second_taps)
    row_b, weights = lax.optimization_barrier((row_b, weights))
    col_a, col_b = pl.pallas_call(
        pack_corners,
        out_shape=[jax.ShapeDtypeStruct((planes + 14, 8, LANES), BF16)] * 2,
        in_specs=[smem] + [whole] * 5,
        out_specs=[whole] * 2,
        compiler_params=small,
    )(flags, row_b, row_a, dep, edge_a, edge_b)
    col_a, col_b, volume = lax.optimization_barrier((col_a, col_b, volume))
    col_a, col_b = to_col(col_a, 0), to_col(col_b, 1)

    spot = lax.axis_index(("depth", "row"))
    squares = lax.axis_size(("depth", "row")) // 2
    where = jnp.stack([spot % 2, spot // 2])
    faces, corners = (dep, row_a, row_b, edge_a, edge_b), (side_a, side_b, col_a, col_b)
    keep, give = local_grads(flags, where, squares, volume, faces, corners, cotangent, weights)

    def to_square(block, n):
        route = [(2 * i + c, 2 * (i ^ n) + c) for i in range(squares) for c in (0, 1)]
        return lax.ppermute(block, ("depth", "row"), route)

    def to_core(block):
        return lax.ppermute(block, ("depth", "row"), [(i, i ^ 1) for i in range(2 * squares)])

    def along_col(block, n):
        return lax.ppermute(block, "col", [(i, i ^ n) for i in range(cols)])

    both = keep + to_core(give).astype(F32)
    near = both.astype(BF16)
    order = [1, *reversed(range(2, squares))]
    share = add_up(both[0], *[to_square(near[n], n) for n in order])
    share = add_up(share, *[along_col(share, n) for n in range(1, cols)])
    mine = jnp.stack([share] + [to_square(share, n) for n in reversed(range(1, squares))])
    other = to_core(mine)
    grads = [jax.ShapeDtypeStruct(shape, F32) for shape in (first_weight.shape, second_weight.shape[::-1])]
    first_grad, second_grad = pl.pallas_call(
        unpack,
        out_shape=grads,
        in_specs=[smem] + [whole] * 2,
        out_specs=[in_hbm] * 2,
        scratch_shapes=[
            pltpu.VMEM((mine.shape[0] * mine.shape[1] * 2, LANES), F32),
            pltpu.VMEM(first_weight.shape, F32),
            pltpu.SemaphoreType.DMA((2,)),
        ],
        compiler_params=small,
    )(where, mine, other)
    return first_grad, second_grad.T


def solution(mesh):
    placed = (P("depth", "row", "col"), P(), P(), P("depth", "row", "col"))
    return jax.shard_map(shards, mesh=mesh, in_specs=placed, out_specs=(P(), P()), check_vma=False)
```

```python
import functools

import jax
import jax.numpy as jnp
from jax import lax
from jax.experimental import pallas as pl
from jax.experimental.pallas import tpu as pltpu
from jax.sharding import PartitionSpec as P

LANES = 128
SECOND_ROWS = 27 * 64
FIRST_BLOCKS = 7
F32 = jnp.float32
BF16 = jnp.bfloat16


def pairs_on_line(count, kind):
    firsts = range(kind, count - 1, 2)
    swapped = [(i, i + 1) for i in firsts] + [(i + 1, i) for i in firsts]
    met = {i for i, j in swapped}
    return swapped + [(i, i) for i in range(count) if i not in met]


def pairs_of_lines(lines, count, kind):
    route = []
    for line in range(lines):
        for i, j in pairs_on_line(count, kind):
            route.append((line * count + i, (line ^ 1 if i == j else line) * count + j))
    return route


def add_up(*terms):
    terms = [term.astype(F32) for term in terms]
    while len(terms) > 1:
        terms = [terms[n] + terms[n + 1] for n in range(0, len(terms), 2)]
    return terms[0].astype(BF16)


def matmul(left, right):
    return lax.dot_general(left, right, (((1,), (0,)), ((), ())), preferred_element_type=F32)


def bring(
    flag_ref, vol_hbm, cot_hbm, first_hbm, second_hbm, vol_ref, cot_ref, first_ref, second_ref, dep_ref, arrived
):
    first_plane = flag_ref[0] == 0
    planes, width = vol_ref.shape[0], vol_ref.shape[2]
    inner = pl.ds(4, planes - 8)
    copies = [pltpu.make_async_copy(cot_hbm, cot_ref, arrived.at[0])]
    for n, part in enumerate((pl.ds(0, 4), pl.ds(planes - 4, 4), inner)):
        copies.append(pltpu.make_async_copy(vol_hbm.at[part], vol_ref.at[part], arrived.at[1 + n]))
    copies.append(pltpu.make_async_copy(first_hbm, first_ref, arrived.at[4]))
    copies.append(pltpu.make_async_copy(second_hbm, second_ref, arrived.at[5]))
    for copy in copies:
        copy.start()
    for copy in copies[:3]:
        copy.wait()
    dep_ref[16] = cot_ref[0]
    for q in range(4):
        for m in range(width // LANES):
            lanes = slice(m * LANES, (m + 1) * LANES)
            last, start = vol_ref[planes - 4 + q, :, lanes].astype(F32), vol_ref[q, :, lanes].astype(F32)
            block = jnp.where(first_plane, last, start)
            for g in range(4):
                dep_ref[4 * q + g, :, lanes] = block[4 * g : 4 * g + 4].astype(BF16)
    for copy in copies[3:]:
        copy.wait()


def pack_rows(flag_ref, vol_ref, cot_ref, row_b_ref, row_a_ref):
    row_even, row_inner = flag_ref[1] == 0, flag_ref[3] != 0
    planes, high, width = vol_ref.shape
    cots = cot_ref.shape[0]

    def run(even, inner):
        def plane(d, carry):
            for m in range(width // LANES):
                lanes = slice(m * LANES, (m + 1) * LANES)
                low, top = vol_ref[d, :4, lanes], vol_ref[d, high - 4 :, lanes]
                row_a_ref[d, :, lanes] = top if even else low
                if inner:
                    row_b_ref[d, :, lanes] = low if even else top
                else:
                    row_b_ref[d, :, lanes] = jnp.zeros_like(low)
            return carry

        lax.fori_loop(0, planes, plane, 0, unroll=4)

    for even in (True, False):
        for inner in (True, False):
            here = jnp.logical_and(row_even == even, row_inner == inner)
            pl.when(here)(functools.partial(run, even, inner))
    for g in range(cots // 4):
        tops = jnp.concatenate([cot_ref[4 * g + n].astype(F32)[:1] for n in range(4)], axis=0)
        row_a_ref[planes + g] = tops.astype(BF16)
        row_b_ref[planes + g] = jnp.where(row_inner, tops, 0.0).astype(BF16)


def pack_sides(flag_ref, vol_ref, cot_ref, col_a_ref, col_b_ref):
    col_even, col_inner = flag_ref[2] == 0, flag_ref[4] != 0
    planes, high, width = vol_ref.shape
    cots = cot_ref.shape[0]
    for g in range(cots // 4):
        side = jnp.concatenate([cot_ref[4 * g + n, :, :LANES].astype(F32) for n in range(4)], axis=0)
        col_a_ref[planes + g] = side.astype(BF16)
        col_b_ref[planes + g] = jnp.where(col_inner, side, 0.0).astype(BF16)

    def plane(d, carry):
        left = vol_ref[d, :, :LANES].astype(F32)
        right = vol_ref[d, :, width - LANES :].astype(F32)
        col_a_ref[d] = jnp.where(col_even, right, left).astype(BF16)
        col_b_ref[d] = jnp.where(col_inner, jnp.where(col_even, left, right), 0.0).astype(BF16)
        return carry

    lax.fori_loop(0, planes, plane, 0, unroll=4)


def pack_corners(flag_ref, row_b_ref, row_a_ref, dep_ref, edge_a_ref, edge_b_ref, col_a_ref, col_b_ref):
    row_even, col_even, col_inner = flag_ref[1] == 0, flag_ref[2] == 0, flag_ref[4] != 0
    width = dep_ref.shape[2]
    groups = row_a_ref.shape[0]
    planes = (groups * 16) // 17
    faces = (slice(0, LANES), slice(width - LANES, width))

    def store(n, left, right):
        col_a_ref[n] = jnp.where(col_even, right, left).astype(BF16)
        col_b_ref[n] = jnp.where(col_inner, jnp.where(col_even, left, right), 0.0).astype(BF16)

    def lower_upper(a_ref, b_ref, source, target):
        values = []
        for lanes in faces:
            a, b = a_ref[source, :, lanes].astype(F32), b_ref[source, :, lanes].astype(F32)
            values.append(jnp.concatenate([jnp.where(row_even, b, a), jnp.where(row_even, a, b)], axis=0))
        store(target, *values)

    def plane(d, carry):
        lower_upper(row_a_ref, row_b_ref, d, d)
        return carry

    lax.fori_loop(0, planes, plane, 0, unroll=4)
    for q in range(4):
        lower_upper(edge_a_ref, edge_b_ref, q, planes + q)
        for n in range(2):
            units = range(4 * q + 2 * n, 4 * q + 2 * n + 2)
            store(
                planes + 4 + 2 * q + n,
                *[jnp.concatenate([dep_ref[u, :, lanes].astype(F32) for u in units], axis=0) for lanes in faces],
            )
    lanes = faces[0]
    tops = [
        jnp.where(row_even, row_a_ref[g, :, lanes].astype(F32), row_b_ref[g, :, lanes].astype(F32))
        for g in range(planes, groups)
    ]
    corner = jnp.where(row_even, edge_a_ref[4, :, lanes].astype(F32), edge_b_ref[4, :, lanes].astype(F32))
    own = dep_ref[16, :, lanes].astype(F32)
    for n, values in enumerate((jnp.concatenate(tops, axis=0), jnp.concatenate([own, corner], axis=0))):
        col_a_ref[planes + 12 + n] = values.astype(BF16)
        col_b_ref[planes + 12 + n] = jnp.where(col_inner, values, 0.0).astype(BF16)


def bands(first_ref, second_ref, w1_ref, w2_ref, w2b_ref):
    out_chan = first_ref.shape[0]
    first = first_ref[...].astype(F32)
    blank = jnp.zeros((out_chan, LANES), F32)
    for tap in range(9):
        rows = slice(tap * LANES, (tap + 1) * LANES)
        taps = first[:, tap * 96 : (tap + 1) * 96]
        main_even = jnp.concatenate([taps[:, 32:], blank[:, :64]], axis=1)
        main_odd = jnp.concatenate([blank[:, :32], taps], axis=1)
        prev_even = jnp.concatenate([blank[:, :96], taps[:, :32]], axis=1)
        w1_ref[rows] = jnp.concatenate([main_even, main_odd, prev_even, blank], axis=0).T.astype(BF16)
        main = second_ref[tap * 192 + 64 : (tap + 1) * 192, :]
        prev = jnp.concatenate([jnp.zeros((64, LANES), BF16), second_ref[tap * 192 : tap * 192 + 64, :]], axis=0)
        both = jnp.concatenate([main, prev], axis=1)
        w2_ref[rows] = both
        w2b_ref[tap] = both.astype(F32).T.astype(BF16)


def split_rows(stage, tiles, index, blocks):
    for m in blocks:
        rows = [stage[m, pl.ds(4 + s, 8, stride=4), :] for s in range(-1, 4)]
        for b in range(3):
            tiles[b, index, m] = jnp.concatenate([rows[b], rows[b + 2]], axis=0).astype(BF16)


def clear_stage(stage):
    stage[:, :, 0:8, :] = jnp.zeros(stage.shape[:2] + (8, LANES), F32)
    stage[:, :, 24:40, :] = jnp.zeros(stage.shape[:2] + (16, LANES), F32)


def ahead(even, a, b):
    return jnp.where(even, a.astype(F32), b.astype(F32))


def behind(even, a, b):
    return jnp.where(even, b.astype(F32), a.astype(F32))


def first_values(pre):
    square = pre * pre + 1.0
    inverse = lax.rsqrt(square)
    hidden = (0.6 * pre + 0.4 * (square * inverse - 1.0)).astype(BF16).astype(F32)
    odd = hidden[:, 8:, :]
    return 0.6 + 0.4 * (pre * inverse), (pltpu.roll(odd, 1, 1), hidden[:, :8, :], odd)


def own_blocks(
    flag_ref, vol_ref, dep_ref, row_a_ref, row_b_ref, edge_a_ref, edge_b_ref, w1_ref,
    tiles, parts, hid, slopes, stage,
):
    first_plane, row_even = flag_ref[0] == 0, flag_ref[1] == 0
    planes = vol_ref.shape[0]
    blocks = vol_ref.shape[2] // LANES
    clear_stage(stage)

    def run(even):
        def place(n, target, own, a, b, keep):
            def kept(values):
                return values if keep is None else jnp.where(keep, values, 0.0)

            for m in range(blocks):
                lanes = slice(m * LANES, (m + 1) * LANES)
                stage[n, m, 8:24, :] = kept(own(lanes).astype(F32))
                stage[n, m, 4:8, :] = kept((b if even else a)(lanes).astype(F32))
                stage[n, m, 24:28, :] = kept((a if even else b)(lanes).astype(F32))
            split_rows(stage.at[n], tiles, target, range(blocks))

        def place_own(group, carry):
            for n in range(4):
                d = 4 * group + n
                place(
                    n, d + 3, lambda lanes: vol_ref[d, :, lanes],
                    lambda lanes: row_a_ref[d, :, lanes], lambda lanes: row_b_ref[d, :, lanes], None,
                )
            return carry

        def place_halo(target, q, keep):
            place(
                target % 4, target,
                lambda lanes: jnp.concatenate([dep_ref[4 * q + g, :, lanes].astype(F32) for g in range(4)], axis=0),
                lambda lanes: edge_a_ref[q, :, lanes], lambda lanes: edge_b_ref[q, :, lanes], keep,
            )

        lax.fori_loop(0, planes // 4, place_own, 0, unroll=2)
        for q in range(3):
            place_halo(q, q + 1, jnp.logical_not(first_plane))
        for q in range(4):
            place_halo(planes + 3 + q, q, first_plane)

    for even in (True, False):
        pl.when(row_even == even)(functools.partial(run, even))
    tiles[:, planes + 7 :] = jnp.zeros((3, 2, blocks, 16, LANES), BF16)

    group = 5

    def product(step, carry):
        taps = []
        for a in range(3):
            for b in range(3):
                start = 2 * group * step + a
                found = [tiles[b, start + 2 * n].reshape(blocks * 16, LANES) for n in range(group)]
                taps.append(jnp.concatenate(found, axis=0))
        found = matmul(jnp.concatenate(taps, axis=1), w1_ref[...])
        parts[pl.ds(group * step, group)] = found.reshape(group, blocks, 16, 2 * LANES)
        return carry

    lax.fori_loop(0, parts.shape[0] // group, product, 0, unroll=True)

    for i in range(planes // 2 + 3):
        slope, rows = first_values(parts[i, 1:, :, :LANES] + parts[i, :-1, :, LANES:])
        for b in range(3):
            hid[b, i] = rows[b]
        if 1 <= i <= planes // 2:
            slopes[i - 1] = slope


def body(
    flag_ref, place_ref, tiles, parts, inner_hid, inner_slopes, dep_ref, row_a_ref, row_b_ref, edge_a_ref, edge_b_ref,
    side_a_ref, side_b_ref, col_a_ref, col_b_ref, cot_ref, w1_ref, w2_ref, w2b_ref, keep_ref, give_ref,
    out_ref, stage, rim_tiles, rim_parts, slopes, hid, pairs, ups, deltas, shifted,
):
    first_plane, row_even, col_even = flag_ref[0] == 0, flag_ref[1] == 0, flag_ref[2] == 0
    planes = tiles.shape[1] - 9
    blocks = tiles.shape[2]
    half_planes = planes // 4
    hidden_planes = planes // 2 + 3

    clear_stage(stage)

    def run(even):
        def place(n, target, source, side_a, side_b, keep):
            for m in range(2):
                first = even == (m == 1)
                corners = (col_a_ref if first else col_b_ref)[source].astype(F32)
                own = (side_a if first else side_b).astype(F32)
                if keep is not None:
                    corners, own = jnp.where(keep, corners, 0.0), jnp.where(keep, own, 0.0)
                stage[n, m, 4:8, :] = corners[:4]
                stage[n, m, 8:24, :] = own
                stage[n, m, 24:28, :] = corners[4:]
            split_rows(stage.at[n], rim_tiles, target, range(2))

        def place_own(group, carry):
            for n in range(4):
                d = 4 * group + n
                place(n, d + 3, d, side_a_ref[d], side_b_ref[d], None)
            return carry

        def place_halo(target, q, keep):
            start = planes + 4 + 2 * q
            side_a = jnp.concatenate([col_a_ref[start].astype(F32), col_a_ref[start + 1].astype(F32)], axis=0)
            side_b = jnp.concatenate([col_b_ref[start].astype(F32), col_b_ref[start + 1].astype(F32)], axis=0)
            place(target % 4, target, planes + q, side_a, side_b, keep)

        lax.fori_loop(0, planes // 4, place_own, 0, unroll=2)
        for q in range(3):
            place_halo(q, q + 1, jnp.logical_not(first_plane))
        for q in range(4):
            place_halo(planes + 3 + q, q, first_plane)

    for even in (True, False):
        pl.when(col_even == even)(functools.partial(run, even))

    taps = []
    for a in range(3):
        for b in range(3):
            rows = [rim_tiles[b, 2 * i + a].reshape(32, LANES) for i in range(hidden_planes)]
            taps.append(jnp.concatenate(rows, axis=0))
    found = matmul(jnp.concatenate(taps, axis=1), w1_ref[...])
    rim_parts[...] = found.reshape(hidden_planes, 2, 16, 2 * LANES)

    for i in range(hidden_planes):
        rim, rim_prev = rim_parts[i, :, :, :LANES], rim_parts[i, 0:1, :, LANES:]
        first = parts[i, 0:1, :, :LANES] + rim_prev
        last = rim[1:] + parts[i, blocks - 1 :, :, LANES:]
        slope, rows = first_values(jnp.concatenate([rim[:1], first, last], axis=0))
        for b in range(3):
            hid[b, i] = rows[b]
        if 1 <= i <= planes // 2:
            slopes[i - 1] = slope[1:2]

    wide = (blocks + 2) * 16

    def pair(i, carry):
        for b in range(3):
            both = [
                jnp.concatenate([hid[b, n, 0:2], inner_hid[b, n], hid[b, n, 2:3]], axis=0) for n in (i, i + half_planes)
            ]
            pairs[b, i] = jnp.concatenate(both, axis=1).astype(BF16)
        return carry

    lax.fori_loop(0, half_planes + 3, pair, 0, unroll=True)

    ups[...] = jnp.zeros_like(ups)
    for k in range(blocks):
        lanes = slice(k * LANES, (k + 1) * LANES)
        ups[0:half_planes, k, 1:5, :] = cot_ref[:, :, lanes].astype(F32)
        ups[half_planes, k, 1:5, :] = jnp.where(first_plane, dep_ref[16, :, lanes].astype(F32), 0.0)
        for g in range(half_planes // 4):
            tops = ahead(row_even, row_a_ref[planes + g, :, lanes], row_b_ref[planes + g, :, lanes])
            for n in range(4):
                ups[4 * g + n, k, 5:6, :] = tops[n : n + 1]
        corner = ahead(row_even, edge_a_ref[4, :, lanes], edge_b_ref[4, :, lanes])[:1]
        ups[half_planes, k, 5:6, :] = jnp.where(first_plane, corner, 0.0)
    for g in range(half_planes // 4):
        side = ahead(col_even, side_a_ref[planes + g], side_b_ref[planes + g])
        for n in range(4):
            ups[4 * g + n, blocks, 1:5, :] = side[4 * n : 4 * n + 4]
    tops = ahead(col_even, col_a_ref[planes + 12], col_b_ref[planes + 12])
    for n in range(half_planes):
        ups[n, blocks, 5:6, :] = tops[n : n + 1]
    beyond = jnp.where(first_plane, ahead(col_even, col_a_ref[planes + 13], col_b_ref[planes + 13]), 0.0)
    ups[half_planes, blocks, 1:6, :] = beyond[:5]

    quarter = half_planes // 2

    taps = []
    for a in range(3):
        for b in range(3):
            rows = [pairs[b, 2 * t + a].reshape(wide, LANES) for t in range(quarter + 1)]
            taps.append(jnp.concatenate(rows, axis=0))
    found = matmul(jnp.concatenate(taps, axis=1), w2_ref[...]).reshape(quarter + 1, blocks + 2, 16, 2 * LANES)
    for t in range(quarter + 1):
        pre = found[t, 1:, :, :LANES] + found[t, :-1, :, LANES:]
        slope = 0.6 + 0.4 * (pre * lax.rsqrt(pre * pre + 1.0))
        upstream = jnp.concatenate([ups[t], ups[t + quarter]], axis=1)
        delta = (upstream * slope).astype(BF16).astype(F32)
        moved = jnp.concatenate([pltpu.roll(delta[:, :8], 7, 1), pltpu.roll(delta[:, 8:], 7, 1)], axis=1)
        deltas[t] = delta
        shifted[t] = moved.astype(BF16)

    sublane = lax.broadcasted_iota(jnp.int32, (1, 1, 16, 1), 2) % 8
    own_rows = jnp.logical_and(sublane >= 1, sublane <= 4)

    def with_next(values, needed):
        values = values.T
        edge = jnp.zeros((LANES, values.shape[1] // blocks), values.dtype)
        here = jnp.concatenate([edge, values], axis=1)
        after = jnp.concatenate([values, edge], axis=1)[:needed]
        return jnp.concatenate([here, after], axis=0)

    own_delta = [jnp.where(own_rows[0], deltas[t, 0:blocks], 0.0) for t in range(quarter)]
    left = with_next(jnp.stack(own_delta, axis=1).reshape(blocks * quarter * 16, LANES), LANES).astype(BF16)

    def second_taps(tap):
        a, b = tap // 3, tap % 3
        found = [pairs[b, 2 * t + a, 0 : blocks + 1] for t in range(quarter)]
        return jnp.stack(found, axis=1).reshape((blocks + 1) * quarter * 16, LANES)

    for tap in range(0, 9, 2):
        right = [second_taps(x) for x in range(tap, min(tap + 2, 9))]
        found = matmul(left, jnp.concatenate(right, axis=1))
        for n in range(len(right)):
            row = (tap + n) * 192
            lanes = slice(n * LANES, (n + 1) * LANES)
            out_ref[row : row + 64, :] = found[LANES:, lanes].T[64:]
            out_ref[row + 64 : row + 192, :] = found[:LANES, lanes].T

    def pack(values):
        both = jnp.concatenate([values[:, :-1], values[:, 1:]], axis=3)
        return both.reshape(quarter * blocks * 16, 2 * LANES)

    plain = deltas[...].astype(BF16)
    moved = shifted[...]
    here, after = pack(plain[:-1]), pack(plain[1:])
    here_up, after_up = pack(moved[:-1]), pack(moved[1:])

    def back(values, taps):
        weights = jnp.concatenate([w2b_ref[3 * a + b] for a, b in taps], axis=1)
        found = matmul(values, weights)
        found = [found[:, n * LANES : (n + 1) * LANES] for n in range(len(taps))]
        return [part.reshape(quarter, blocks, 16, LANES) for part in found]

    here_11, here_12, here_21, here_22 = back(here, ((1, 1), (1, 2), (2, 1), (2, 2)))
    up_10, up_20 = back(here_up, ((1, 0), (2, 0)))
    after_01, after_02 = back(after, ((0, 1), (0, 2)))
    (after_00,) = back(after_up, ((0, 0),))
    rows = [[here_11, up_10 + here_12], [after_01 + here_21, after_00 + after_02 + up_20 + here_22]]
    own_list = []
    for i in range(planes // 2):
        t, parity = i // 2, i % 2
        half = slice(0, 8) if t < quarter else slice(8, 16)
        back_one = jnp.concatenate([rows[parity][p][t % quarter, :, half, :] for p in (0, 1)], axis=1)
        delta = back_one * jnp.concatenate([slopes[i], inner_slopes[i]], axis=0)
        own_list.append(jnp.where(own_rows[0], delta, 0.0).astype(BF16))
    left_one = with_next(jnp.stack(own_list, axis=1).reshape(blocks * (planes // 2) * 16, LANES), 64)

    def first_taps(tap):
        a, b = tap // 3, tap % 3
        found = []
        for m in range(blocks + 1):
            for i in range(planes // 2):
                index = 2 * (i + 1) + a
                found.append(rim_tiles[b, index, 0] if m == 0 else tiles[b, index, m - 1])
        return jnp.concatenate(found, axis=0)

    grads = []
    for tap in range(0, 9, 2):
        right = [first_taps(x) for x in range(tap, min(tap + 2, 9))]
        found = matmul(left_one, jnp.concatenate(right, axis=1))
        for n in range(len(right)):
            main = found[:LANES, n * LANES : (n + 1) * LANES]
            prev = found[LANES:, n * LANES : (n + 1) * LANES]
            even = jnp.concatenate([prev[:, 96:], main[:64, :64]], axis=1)
            grads.append(even + main[64:, 32:])
    grads.append(jnp.zeros((64, FIRST_BLOCKS * LANES - 9 * 96), F32))
    first = jnp.concatenate(grads, axis=1)
    for n in range(FIRST_BLOCKS):
        row = SECOND_ROWS + 64 * n
        out_ref[row : row + 64, :] = first[:, n * LANES : (n + 1) * LANES]
    used = SECOND_ROWS + 64 * FIRST_BLOCKS
    if out_ref.shape[0] > used:
        out_ref[used:, :] = jnp.zeros((out_ref.shape[0] - used, LANES), F32)

    core, square = place_ref[0], place_ref[1]
    squares, size = keep_ref.shape[0], keep_ref.shape[1]
    for n in range(squares):
        for ref, half in ((keep_ref, core), (give_ref, 1 - core)):
            start = pl.multiple_of((half * squares + (square ^ n)) * size, 8)
            ref[n] = out_ref[pl.ds(start, size), :].astype(ref.dtype)


def unpack(place_ref, keep_ref, got_ref, g1_hbm, g2_hbm, sums, first, sent):
    core, square = place_ref[0], place_ref[1]
    squares, size = keep_ref.shape[0], keep_ref.shape[1]
    for n in range(squares):
        for ref, half in ((keep_ref, core), (got_ref, 1 - core)):
            start = pl.multiple_of((half * squares + (square ^ n)) * size, 8)
            sums[pl.ds(start, size), :] = ref[-n % squares].astype(F32)
    second = pltpu.make_async_copy(sums.at[pl.ds(0, SECOND_ROWS)], g2_hbm, sent.at[0])
    second.start()
    found = [sums[SECOND_ROWS + 64 * n : SECOND_ROWS + 64 * (n + 1), :] for n in range(FIRST_BLOCKS)]
    first[...] = jnp.concatenate(found, axis=1)[:, : first.shape[1]]
    copy = pltpu.make_async_copy(first, g1_hbm, sent.at[1])
    copy.start()
    copy.wait()
    second.wait()


def local_grads(flags, place, squares, volume, faces, corners, cotangent, weights):
    planes = volume.shape[0]
    blocks = volume.shape[2] // LANES
    hidden_planes = planes // 2 + 3
    out_planes = planes // 4
    unit = 2 * squares * 16
    rows = -(-(SECOND_ROWS + 64 * FIRST_BLOCKS) // unit) * unit
    whole = pl.BlockSpec(memory_space=pltpu.VMEM)
    smem = pl.BlockSpec(memory_space=pltpu.SMEM)
    dep, row_a, row_b, edge_a, edge_b = faces
    tiles, parts, inner_hid, inner_slopes = pl.pallas_call(
        own_blocks,
        out_shape=[
            jax.ShapeDtypeStruct((3, planes + 9, blocks, 16, LANES), BF16),
            jax.ShapeDtypeStruct((hidden_planes + 1, blocks, 16, 2 * LANES), F32),
            jax.ShapeDtypeStruct((3, hidden_planes, blocks - 1, 8, LANES), F32),
            jax.ShapeDtypeStruct((planes // 2, blocks - 1, 16, LANES), F32),
        ],
        in_specs=[smem] + [whole] * 7,
        out_specs=[whole] * 4,
        scratch_shapes=[pltpu.VMEM((4, blocks, 40, LANES), F32)],
        compiler_params=pltpu.CompilerParams(vmem_limit_bytes=16 * 1024 * 1024),
        cost_estimate=pl.CostEstimate(flops=2 * 10**9, bytes_accessed=10**7, transcendentals=0),
    )(flags, volume, *faces, weights[0])
    scratch = [
        pltpu.VMEM((rows, LANES), F32),
        pltpu.VMEM((4, 2, 40, LANES), F32),
        pltpu.VMEM((3, planes + 7, 2, 16, LANES), BF16),
        pltpu.VMEM((hidden_planes, 2, 16, 2 * LANES), F32),
        pltpu.VMEM((planes // 2, 1, 16, LANES), F32),
        pltpu.VMEM((3, hidden_planes, 3, 8, LANES), F32),
        pltpu.VMEM((3, out_planes + 3, blocks + 2, 16, LANES), BF16),
        pltpu.VMEM((out_planes + 1, blocks + 1, 8, LANES), F32),
        pltpu.VMEM((out_planes // 2 + 1, blocks + 1, 16, LANES), F32),
        pltpu.VMEM((out_planes // 2 + 1, blocks + 1, 16, LANES), BF16),
    ]
    operands = (tiles, parts, inner_hid, inner_slopes, *faces, *corners, cotangent, *weights)
    return pl.pallas_call(
        body,
        out_shape=[jax.ShapeDtypeStruct((squares, rows // (2 * squares), LANES), dtype) for dtype in (F32, BF16)],
        in_specs=[smem] * 2 + [whole] * len(operands),
        out_specs=[whole] * 2,
        scratch_shapes=scratch,
        compiler_params=pltpu.CompilerParams(vmem_limit_bytes=28 * 1024 * 1024),
        cost_estimate=pl.CostEstimate(flops=4 * 10**9, bytes_accessed=10**7, transcendentals=0),
    )(flags, place, *operands)


def shards(volume, first_weight, second_weight, cotangent):
    half = lax.axis_index("depth")
    row, col = lax.axis_index("row"), lax.axis_index("col")
    rows, cols = lax.axis_size("row"), lax.axis_size("col")
    inner = [jnp.logical_and(i > 0, i < n - 1).astype(jnp.int32) for i, n in ((row, rows), (col, cols))]
    flags = jnp.stack([half, row % 2, col % 2, *inner])
    whole = pl.BlockSpec(memory_space=pltpu.VMEM)
    smem = pl.BlockSpec(memory_space=pltpu.SMEM)
    small = pltpu.CompilerParams(vmem_limit_bytes=12 * 1024 * 1024)
    planes, high, width = volume.shape
    groups = planes + cotangent.shape[0] // 4
    in_hbm = pl.BlockSpec(memory_space=pltpu.HBM)

    def stay(argument):
        return pltpu.with_memory_space_constraint(argument, pltpu.HBM)

    arguments = (volume, cotangent, first_weight, second_weight.T)
    shapes = [argument.shape for argument in arguments] + [(17, 4, width)]
    volume, cotangent, first_taps, second_taps, dep = pl.pallas_call(
        bring,
        out_shape=[jax.ShapeDtypeStruct(shape, BF16) for shape in shapes],
        in_specs=[smem] + [in_hbm] * 4,
        out_specs=[whole] * len(shapes),
        scratch_shapes=[pltpu.SemaphoreType.DMA((6,))],
        compiler_params=small,
    )(flags, *[stay(argument) for argument in arguments])
    row_b, row_a = pl.pallas_call(
        pack_rows,
        out_shape=[jax.ShapeDtypeStruct((groups, 4, width), BF16)] * 2,
        in_specs=[smem] + [whole] * 2,
        out_specs=[whole] * 2,
        compiler_params=small,
    )(flags, volume, cotangent)

    def to_col(block, kind):
        return lax.ppermute(block, ("row", "col"), pairs_of_lines(rows, cols, kind))

    dep = lax.ppermute(dep, "depth", [(0, 1), (1, 0)])
    route = []
    for i, j in pairs_on_line(rows, 1):
        route += [((d * rows + i) * cols + c, (d * rows + j) * cols + (c ^ 1 if i == j else c)) for d in (0, 1) for c in range(cols)]
    row_b = lax.ppermute(row_b, ("depth", "row", "col"), route)
    row_a = lax.ppermute(row_a, "row", pairs_on_line(rows, 0))
    side_a, side_b = pl.pallas_call(
        pack_sides,
        out_shape=[jax.ShapeDtypeStruct((groups, high, LANES), BF16)] * 2,
        in_specs=[smem] + [whole] * 2,
        out_specs=[whole] * 2,
        compiler_params=small,
    )(flags, volume, cotangent)
    dep, side_a, side_b, first_taps = lax.optimization_barrier((dep, side_a, side_b, first_taps))
    row_a, side_b = lax.optimization_barrier((row_a, side_b))
    side_a, side_b = to_col(side_a, 0), to_col(side_b, 1)
    low, top = [jnp.concatenate([dep[n : n + 1] for n in (*range(k, 16, 4), 16)], axis=0) for k in (0, 3)]
    even, ends = row % 2 == 0, jnp.logical_or(row == 0, row == rows - 1)
    edge_a = jnp.where(even, top, low)
    edge_b = jnp.where(ends, 0, jnp.where(even, low, top))
    edge_a = lax.ppermute(edge_a, "row", pairs_on_line(rows, 0))
    edge_b = lax.ppermute(edge_b, ("depth", "row"), pairs_of_lines(2, rows, 1))
    weights = pl.pallas_call(
        bands,
        out_shape=[jax.ShapeDtypeStruct(shape, BF16) for shape in ((1152, 256), (1152, 256), (9, 256, 128))],
        in_specs=[whole] * 2,
        out_specs=[whole] * 3,
        compiler_params=small,
    )(first_taps, second_taps)
    row_b, weights = lax.optimization_barrier((row_b, weights))
    col_a, col_b = pl.pallas_call(
        pack_corners,
        out_shape=[jax.ShapeDtypeStruct((planes + 14, 8, LANES), BF16)] * 2,
        in_specs=[smem] + [whole] * 5,
        out_specs=[whole] * 2,
        compiler_params=small,
    )(flags, row_b, row_a, dep, edge_a, edge_b)
    col_a, col_b, volume = lax.optimization_barrier((col_a, col_b, volume))
    col_a, col_b = to_col(col_a, 0), to_col(col_b, 1)

    spot = lax.axis_index(("depth", "row"))
    squares = lax.axis_size(("depth", "row")) // 2
    where = jnp.stack([spot % 2, spot // 2])
    faces, corners = (dep, row_a, row_b, edge_a, edge_b), (side_a, side_b, col_a, col_b)
    keep, give = local_grads(flags, where, squares, volume, faces, corners, cotangent, weights)

    def to_square(block, n):
        route = [(2 * i + c, 2 * (i ^ n) + c) for i in range(squares) for c in (0, 1)]
        return lax.ppermute(block, ("depth", "row"), route)

    def to_core(block):
        return lax.ppermute(block, ("depth", "row"), [(i, i ^ 1) for i in range(2 * squares)])

    def along_col(block, n):
        return lax.ppermute(block, "col", [(i, i ^ n) for i in range(cols)])

    both = keep + to_core(give).astype(F32)
    near = both.astype(BF16)
    order = [1, *reversed(range(2, squares))]
    share = add_up(both[0], *[to_square(near[n], n) for n in order])
    share = add_up(share, *[along_col(share, n) for n in range(1, cols)])
    mine = jnp.stack([share] + [to_square(share, n) for n in reversed(range(1, squares))])
    other = to_core(mine)
    grads = [jax.ShapeDtypeStruct(shape, F32) for shape in (first_weight.shape, second_weight.shape[::-1])]
    first_grad, second_grad = pl.pallas_call(
        unpack,
        out_shape=grads,
        in_specs=[smem] + [whole] * 2,
        out_specs=[in_hbm] * 2,
        scratch_shapes=[
            pltpu.VMEM((mine.shape[0] * mine.shape[1] * 2, LANES), F32),
            pltpu.VMEM(first_weight.shape, F32),
            pltpu.SemaphoreType.DMA((2,)),
        ],
        compiler_params=small,
    )(where, mine, other)
    return first_grad, second_grad.T


def solution(mesh):
    placed = (P("depth", "row", "col"), P(), P(), P("depth", "row", "col"))
    return jax.shard_map(shards, mesh=mesh, in_specs=placed, out_specs=(P(), P()), check_vma=False)
```

```python
import functools

import jax
import jax.numpy as jnp
from jax import lax
from jax.experimental import pallas as pl
from jax.experimental.pallas import tpu as pltpu
from jax.sharding import PartitionSpec as P

LANES = 128
SECOND_ROWS = 27 * 64
FIRST_BLOCKS = 7
F32 = jnp.float32
BF16 = jnp.bfloat16


def pairs_on_line(count, kind):
    firsts = range(kind, count - 1, 2)
    swapped = [(i, i + 1) for i in firsts] + [(i + 1, i) for i in firsts]
    met = {i for i, j in swapped}
    return swapped + [(i, i) for i in range(count) if i not in met]


def pairs_of_lines(lines, count, kind):
    route = []
    for line in range(lines):
        for i, j in pairs_on_line(count, kind):
            route.append((line * count + i, (line ^ 1 if i == j else line) * count + j))
    return route


def add_up(*terms):
    terms = [term.astype(F32) for term in terms]
    while len(terms) > 1:
        terms = [terms[n] + terms[n + 1] for n in range(0, len(terms), 2)]
    return terms[0].astype(BF16)


def matmul(left, right):
    return lax.dot_general(left, right, (((1,), (0,)), ((), ())), preferred_element_type=F32)


def bring(
    flag_ref, vol_hbm, cot_hbm, first_hbm, second_hbm, vol_ref, cot_ref, first_ref, second_ref, dep_ref, arrived
):
    first_plane = flag_ref[0] == 0
    planes, width = vol_ref.shape[0], vol_ref.shape[2]
    inner = pl.ds(4, planes - 8)
    copies = [pltpu.make_async_copy(cot_hbm, cot_ref, arrived.at[0])]
    for n, part in enumerate((pl.ds(0, 4), pl.ds(planes - 4, 4), inner)):
        copies.append(pltpu.make_async_copy(vol_hbm.at[part], vol_ref.at[part], arrived.at[1 + n]))
    copies.append(pltpu.make_async_copy(first_hbm, first_ref, arrived.at[4]))
    copies.append(pltpu.make_async_copy(second_hbm, second_ref, arrived.at[5]))
    for copy in copies:
        copy.start()
    for copy in copies[:3]:
        copy.wait()
    dep_ref[16] = cot_ref[0]
    for q in range(4):
        for m in range(width // LANES):
            lanes = slice(m * LANES, (m + 1) * LANES)
            last, start = vol_ref[planes - 4 + q, :, lanes].astype(F32), vol_ref[q, :, lanes].astype(F32)
            block = jnp.where(first_plane, last, start)
            for g in range(4):
                dep_ref[4 * q + g, :, lanes] = block[4 * g : 4 * g + 4].astype(BF16)
    for copy in copies[3:]:
        copy.wait()


def pack_rows(flag_ref, vol_ref, cot_ref, row_b_ref, row_a_ref):
    row_even, row_inner = flag_ref[1] == 0, flag_ref[3] != 0
    planes, high, width = vol_ref.shape
    cots = cot_ref.shape[0]

    def run(even, inner):
        def plane(d, carry):
            for m in range(width // LANES):
                lanes = slice(m * LANES, (m + 1) * LANES)
                low, top = vol_ref[d, :4, lanes], vol_ref[d, high - 4 :, lanes]
                row_a_ref[d, :, lanes] = top if even else low
                if inner:
                    row_b_ref[d, :, lanes] = low if even else top
                else:
                    row_b_ref[d, :, lanes] = jnp.zeros_like(low)
            return carry

        lax.fori_loop(0, planes, plane, 0, unroll=4)

    for even in (True, False):
        for inner in (True, False):
            here = jnp.logical_and(row_even == even, row_inner == inner)
            pl.when(here)(functools.partial(run, even, inner))
    for g in range(cots // 4):
        tops = jnp.concatenate([cot_ref[4 * g + n].astype(F32)[:1] for n in range(4)], axis=0)
        row_a_ref[planes + g] = tops.astype(BF16)
        row_b_ref[planes + g] = jnp.where(row_inner, tops, 0.0).astype(BF16)


def pack_sides(flag_ref, vol_ref, cot_ref, col_a_ref, col_b_ref):
    col_even, col_inner = flag_ref[2] == 0, flag_ref[4] != 0
    planes, high, width = vol_ref.shape
    cots = cot_ref.shape[0]
    for g in range(cots // 4):
        side = jnp.concatenate([cot_ref[4 * g + n, :, :LANES].astype(F32) for n in range(4)], axis=0)
        col_a_ref[planes + g] = side.astype(BF16)
        col_b_ref[planes + g] = jnp.where(col_inner, side, 0.0).astype(BF16)

    def plane(d, carry):
        left = vol_ref[d, :, :LANES].astype(F32)
        right = vol_ref[d, :, width - LANES :].astype(F32)
        col_a_ref[d] = jnp.where(col_even, right, left).astype(BF16)
        col_b_ref[d] = jnp.where(col_inner, jnp.where(col_even, left, right), 0.0).astype(BF16)
        return carry

    lax.fori_loop(0, planes, plane, 0, unroll=4)


def pack_corners(flag_ref, row_b_ref, row_a_ref, dep_ref, edge_a_ref, edge_b_ref, col_a_ref, col_b_ref):
    col_inner = flag_ref[4] != 0

    def pick(even, a, b):
        return a if even else b

    def run(row_even, col_even):
        width = dep_ref.shape[2]
        groups = row_a_ref.shape[0]
        planes = (groups * 16) // 17
        faces = (slice(0, LANES), slice(width - LANES, width))

        def store(n, left, right):
            col_a_ref[n] = pick(col_even, right, left).astype(BF16)
            col_b_ref[n] = jnp.where(col_inner, pick(col_even, left, right), 0.0).astype(BF16)

        def lower_upper(a_ref, b_ref, source, target):
            values = []
            for lanes in faces:
                a, b = a_ref[source, :, lanes].astype(F32), b_ref[source, :, lanes].astype(F32)
                values.append(jnp.concatenate([pick(row_even, b, a), pick(row_even, a, b)], axis=0))
            store(target, *values)

        def plane(d, carry):
            lower_upper(row_a_ref, row_b_ref, d, d)
            return carry

        lax.fori_loop(0, planes, plane, 0, unroll=4)
        for q in range(4):
            lower_upper(edge_a_ref, edge_b_ref, q, planes + q)
            for n in range(2):
                units = range(4 * q + 2 * n, 4 * q + 2 * n + 2)
                store(
                    planes + 4 + 2 * q + n,
                    *[jnp.concatenate([dep_ref[u, :, lanes].astype(F32) for u in units], axis=0) for lanes in faces],
                )
        lanes = faces[0]
        tops = [
            pick(row_even, row_a_ref[g, :, lanes].astype(F32), row_b_ref[g, :, lanes].astype(F32))
            for g in range(planes, groups)
        ]
        corner = pick(row_even, edge_a_ref[4, :, lanes].astype(F32), edge_b_ref[4, :, lanes].astype(F32))
        own = dep_ref[16, :, lanes].astype(F32)
        for n, values in enumerate((jnp.concatenate(tops, axis=0), jnp.concatenate([own, corner], axis=0))):
            col_a_ref[planes + 12 + n] = values.astype(BF16)
            col_b_ref[planes + 12 + n] = jnp.where(col_inner, values, 0.0).astype(BF16)

    for rows in (True, False):
        for cols in (True, False):
            here = jnp.logical_and((flag_ref[1] == 0) == rows, (flag_ref[2] == 0) == cols)
            pl.when(here)(functools.partial(run, rows, cols))


def bands(first_ref, second_ref, w1_ref, w2_ref, w2b_ref):
    out_chan = first_ref.shape[0]
    first = first_ref[...].astype(F32)
    blank = jnp.zeros((out_chan, LANES), F32)
    for tap in range(9):
        rows = slice(tap * LANES, (tap + 1) * LANES)
        taps = first[:, tap * 96 : (tap + 1) * 96]
        main_even = jnp.concatenate([taps[:, 32:], blank[:, :64]], axis=1)
        main_odd = jnp.concatenate([blank[:, :32], taps], axis=1)
        prev_even = jnp.concatenate([blank[:, :96], taps[:, :32]], axis=1)
        w1_ref[rows] = jnp.concatenate([main_even, main_odd, prev_even, blank], axis=0).T.astype(BF16)
        main = second_ref[tap * 192 + 64 : (tap + 1) * 192, :]
        prev = jnp.concatenate([jnp.zeros((64, LANES), BF16), second_ref[tap * 192 : tap * 192 + 64, :]], axis=0)
        both = jnp.concatenate([main, prev], axis=1)
        w2_ref[rows] = both
        w2b_ref[tap] = both.astype(F32).T.astype(BF16)


def split_rows(stage, tiles, index, blocks):
    for m in blocks:
        rows = [stage[m, pl.ds(4 + s, 8, stride=4), :] for s in range(-1, 4)]
        for b in range(3):
            tiles[b, index, m] = jnp.concatenate([rows[b], rows[b + 2]], axis=0).astype(BF16)


def clear_stage(stage):
    stage[:, :, 0:8, :] = jnp.zeros(stage.shape[:2] + (8, LANES), F32)
    stage[:, :, 24:40, :] = jnp.zeros(stage.shape[:2] + (16, LANES), F32)


def ahead(even, a, b):
    return jnp.where(even, a.astype(F32), b.astype(F32))


def behind(even, a, b):
    return jnp.where(even, b.astype(F32), a.astype(F32))


def first_values(pre):
    square = pre * pre + 1.0
    inverse = lax.rsqrt(square)
    hidden = (0.6 * pre + 0.4 * (square * inverse - 1.0)).astype(BF16).astype(F32)
    odd = hidden[:, 8:, :]
    return 0.6 + 0.4 * (pre * inverse), (pltpu.roll(odd, 1, 1), hidden[:, :8, :], odd)


def own_blocks(
    flag_ref, vol_ref, dep_ref, row_a_ref, row_b_ref, edge_a_ref, edge_b_ref, w1_ref,
    tiles, parts, hid, slopes, stage,
):
    first_plane, row_even = flag_ref[0] == 0, flag_ref[1] == 0
    planes = vol_ref.shape[0]
    blocks = vol_ref.shape[2] // LANES
    clear_stage(stage)

    def run(even):
        def place(n, target, own, a, b, keep):
            def kept(values):
                return values if keep is None else jnp.where(keep, values, 0.0)

            for m in range(blocks):
                lanes = slice(m * LANES, (m + 1) * LANES)
                stage[n, m, 8:24, :] = kept(own(lanes).astype(F32))
                stage[n, m, 4:8, :] = kept((b if even else a)(lanes).astype(F32))
                stage[n, m, 24:28, :] = kept((a if even else b)(lanes).astype(F32))
            split_rows(stage.at[n], tiles, target, range(blocks))

        def place_own(group, carry):
            for n in range(4):
                d = 4 * group + n
                place(
                    n, d + 3, lambda lanes: vol_ref[d, :, lanes],
                    lambda lanes: row_a_ref[d, :, lanes], lambda lanes: row_b_ref[d, :, lanes], None,
                )
            return carry

        def place_halo(target, q, keep):
            place(
                target % 4, target,
                lambda lanes: jnp.concatenate([dep_ref[4 * q + g, :, lanes].astype(F32) for g in range(4)], axis=0),
                lambda lanes: edge_a_ref[q, :, lanes], lambda lanes: edge_b_ref[q, :, lanes], keep,
            )

        lax.fori_loop(0, planes // 4, place_own, 0, unroll=2)
        for q in range(3):
            place_halo(q, q + 1, jnp.logical_not(first_plane))
        for q in range(4):
            place_halo(planes + 3 + q, q, first_plane)

    for even in (True, False):
        pl.when(row_even == even)(functools.partial(run, even))
    tiles[:, planes + 7 :] = jnp.zeros((3, 2, blocks, 16, LANES), BF16)

    group = 5

    def product(step, carry):
        taps = []
        for a in range(3):
            for b in range(3):
                start = 2 * group * step + a
                found = [tiles[b, start + 2 * n].reshape(blocks * 16, LANES) for n in range(group)]
                taps.append(jnp.concatenate(found, axis=0))
        found = matmul(jnp.concatenate(taps, axis=1), w1_ref[...])
        parts[pl.ds(group * step, group)] = found.reshape(group, blocks, 16, 2 * LANES)
        return carry

    lax.fori_loop(0, parts.shape[0] // group, product, 0, unroll=True)

    for i in range(planes // 2 + 3):
        slope, rows = first_values(parts[i, 1:, :, :LANES] + parts[i, :-1, :, LANES:])
        for b in range(3):
            hid[b, i] = rows[b]
        if 1 <= i <= planes // 2:
            slopes[i - 1] = slope


def body(
    flag_ref, place_ref, tiles, parts, inner_hid, inner_slopes, dep_ref, row_a_ref, row_b_ref, edge_a_ref, edge_b_ref,
    side_a_ref, side_b_ref, col_a_ref, col_b_ref, cot_ref, w1_ref, w2_ref, w2b_ref, keep_ref, give_ref,
    out_ref, stage, rim_tiles, rim_parts, slopes, hid, pairs, ups, deltas, shifted,
):
    first_plane, row_even, col_even = flag_ref[0] == 0, flag_ref[1] == 0, flag_ref[2] == 0
    planes = tiles.shape[1] - 9
    blocks = tiles.shape[2]
    half_planes = planes // 4
    hidden_planes = planes // 2 + 3

    clear_stage(stage)

    def run(even):
        def place(n, target, source, side_a, side_b, keep):
            for m in range(2):
                first = even == (m == 1)
                corners = (col_a_ref if first else col_b_ref)[source].astype(F32)
                own = (side_a if first else side_b).astype(F32)
                if keep is not None:
                    corners, own = jnp.where(keep, corners, 0.0), jnp.where(keep, own, 0.0)
                stage[n, m, 4:8, :] = corners[:4]
                stage[n, m, 8:24, :] = own
                stage[n, m, 24:28, :] = corners[4:]
            split_rows(stage.at[n], rim_tiles, target, range(2))

        def place_own(group, carry):
            for n in range(4):
                d = 4 * group + n
                place(n, d + 3, d, side_a_ref[d], side_b_ref[d], None)
            return carry

        def place_halo(target, q, keep):
            start = planes + 4 + 2 * q
            side_a = jnp.concatenate([col_a_ref[start].astype(F32), col_a_ref[start + 1].astype(F32)], axis=0)
            side_b = jnp.concatenate([col_b_ref[start].astype(F32), col_b_ref[start + 1].astype(F32)], axis=0)
            place(target % 4, target, planes + q, side_a, side_b, keep)

        lax.fori_loop(0, planes // 4, place_own, 0, unroll=2)
        for q in range(3):
            place_halo(q, q + 1, jnp.logical_not(first_plane))
        for q in range(4):
            place_halo(planes + 3 + q, q, first_plane)

    for even in (True, False):
        pl.when(col_even == even)(functools.partial(run, even))

    taps = []
    for a in range(3):
        for b in range(3):
            rows = [rim_tiles[b, 2 * i + a].reshape(32, LANES) for i in range(hidden_planes)]
            taps.append(jnp.concatenate(rows, axis=0))
    found = matmul(jnp.concatenate(taps, axis=1), w1_ref[...])
    rim_parts[...] = found.reshape(hidden_planes, 2, 16, 2 * LANES)

    for i in range(hidden_planes):
        rim, rim_prev = rim_parts[i, :, :, :LANES], rim_parts[i, 0:1, :, LANES:]
        first = parts[i, 0:1, :, :LANES] + rim_prev
        last = rim[1:] + parts[i, blocks - 1 :, :, LANES:]
        slope, rows = first_values(jnp.concatenate([rim[:1], first, last], axis=0))
        for b in range(3):
            hid[b, i] = rows[b]
        if 1 <= i <= planes // 2:
            slopes[i - 1] = slope[1:2]

    wide = (blocks + 2) * 16

    def pair(i, carry):
        for b in range(3):
            both = [
                jnp.concatenate([hid[b, n, 0:2], inner_hid[b, n], hid[b, n, 2:3]], axis=0) for n in (i, i + half_planes)
            ]
            pairs[b, i] = jnp.concatenate(both, axis=1).astype(BF16)
        return carry

    lax.fori_loop(0, half_planes + 3, pair, 0, unroll=True)

    ups[...] = jnp.zeros_like(ups)
    for k in range(blocks):
        lanes = slice(k * LANES, (k + 1) * LANES)
        ups[0:half_planes, k, 1:5, :] = cot_ref[:, :, lanes].astype(F32)
        ups[half_planes, k, 1:5, :] = jnp.where(first_plane, dep_ref[16, :, lanes].astype(F32), 0.0)
        for g in range(half_planes // 4):
            tops = ahead(row_even, row_a_ref[planes + g, :, lanes], row_b_ref[planes + g, :, lanes])
            for n in range(4):
                ups[4 * g + n, k, 5:6, :] = tops[n : n + 1]
        corner = ahead(row_even, edge_a_ref[4, :, lanes], edge_b_ref[4, :, lanes])[:1]
        ups[half_planes, k, 5:6, :] = jnp.where(first_plane, corner, 0.0)
    for g in range(half_planes // 4):
        side = ahead(col_even, side_a_ref[planes + g], side_b_ref[planes + g])
        for n in range(4):
            ups[4 * g + n, blocks, 1:5, :] = side[4 * n : 4 * n + 4]
    tops = ahead(col_even, col_a_ref[planes + 12], col_b_ref[planes + 12])
    for n in range(half_planes):
        ups[n, blocks, 5:6, :] = tops[n : n + 1]
    beyond = jnp.where(first_plane, ahead(col_even, col_a_ref[planes + 13], col_b_ref[planes + 13]), 0.0)
    ups[half_planes, blocks, 1:6, :] = beyond[:5]

    quarter = half_planes // 2

    taps = []
    for a in range(3):
        for b in range(3):
            rows = [pairs[b, 2 * t + a].reshape(wide, LANES) for t in range(quarter + 1)]
            taps.append(jnp.concatenate(rows, axis=0))
    found = matmul(jnp.concatenate(taps, axis=1), w2_ref[...]).reshape(quarter + 1, blocks + 2, 16, 2 * LANES)
    for t in range(quarter + 1):
        pre = found[t, 1:, :, :LANES] + found[t, :-1, :, LANES:]
        slope = 0.6 + 0.4 * (pre * lax.rsqrt(pre * pre + 1.0))
        upstream = jnp.concatenate([ups[t], ups[t + quarter]], axis=1)
        delta = (upstream * slope).astype(BF16).astype(F32)
        moved = jnp.concatenate([pltpu.roll(delta[:, :8], 7, 1), pltpu.roll(delta[:, 8:], 7, 1)], axis=1)
        deltas[t] = delta
        shifted[t] = moved.astype(BF16)

    sublane = lax.broadcasted_iota(jnp.int32, (1, 1, 16, 1), 2) % 8
    own_rows = jnp.logical_and(sublane >= 1, sublane <= 4)

    def with_next(values, needed):
        values = values.T
        edge = jnp.zeros((LANES, values.shape[1] // blocks), values.dtype)
        here = jnp.concatenate([edge, values], axis=1)
        after = jnp.concatenate([values, edge], axis=1)[:needed]
        return jnp.concatenate([here, after], axis=0)

    own_delta = [jnp.where(own_rows[0], deltas[t, 0:blocks], 0.0) for t in range(quarter)]
    left = with_next(jnp.stack(own_delta, axis=1).reshape(blocks * quarter * 16, LANES), LANES).astype(BF16)

    def second_taps(tap):
        a, b = tap // 3, tap % 3
        found = [pairs[b, 2 * t + a, 0 : blocks + 1] for t in range(quarter)]
        return jnp.stack(found, axis=1).reshape((blocks + 1) * quarter * 16, LANES)

    for tap in range(0, 9, 2):
        right = [second_taps(x) for x in range(tap, min(tap + 2, 9))]
        found = matmul(left, jnp.concatenate(right, axis=1))
        for n in range(len(right)):
            row = (tap + n) * 192
            lanes = slice(n * LANES, (n + 1) * LANES)
            out_ref[row : row + 64, :] = found[LANES:, lanes].T[64:]
            out_ref[row + 64 : row + 192, :] = found[:LANES, lanes].T

    def pack(values):
        both = jnp.concatenate([values[:, :-1], values[:, 1:]], axis=3)
        return both.reshape(quarter * blocks * 16, 2 * LANES)

    plain = deltas[...].astype(BF16)
    moved = shifted[...]
    here, after = pack(plain[:-1]), pack(plain[1:])
    here_up, after_up = pack(moved[:-1]), pack(moved[1:])

    def back(values, taps):
        weights = jnp.concatenate([w2b_ref[3 * a + b] for a, b in taps], axis=1)
        found = matmul(values, weights)
        found = [found[:, n * LANES : (n + 1) * LANES] for n in range(len(taps))]
        return [part.reshape(quarter, blocks, 16, LANES) for part in found]

    here_11, here_12, here_21, here_22 = back(here, ((1, 1), (1, 2), (2, 1), (2, 2)))
    up_10, up_20 = back(here_up, ((1, 0), (2, 0)))
    after_01, after_02 = back(after, ((0, 1), (0, 2)))
    (after_00,) = back(after_up, ((0, 0),))
    rows = [[here_11, up_10 + here_12], [after_01 + here_21, after_00 + after_02 + up_20 + here_22]]
    own_list = []
    for i in range(planes // 2):
        t, parity = i // 2, i % 2
        half = slice(0, 8) if t < quarter else slice(8, 16)
        back_one = jnp.concatenate([rows[parity][p][t % quarter, :, half, :] for p in (0, 1)], axis=1)
        delta = back_one * jnp.concatenate([slopes[i], inner_slopes[i]], axis=0)
        own_list.append(jnp.where(own_rows[0], delta, 0.0).astype(BF16))
    left_one = with_next(jnp.stack(own_list, axis=1).reshape(blocks * (planes // 2) * 16, LANES), 64)

    def first_taps(tap):
        a, b = tap // 3, tap % 3
        found = []
        for m in range(blocks + 1):
            for i in range(planes // 2):
                index = 2 * (i + 1) + a
                found.append(rim_tiles[b, index, 0] if m == 0 else tiles[b, index, m - 1])
        return jnp.concatenate(found, axis=0)

    grads = []
    for tap in range(0, 9, 2):
        right = [first_taps(x) for x in range(tap, min(tap + 2, 9))]
        found = matmul(left_one, jnp.concatenate(right, axis=1))
        for n in range(len(right)):
            main = found[:LANES, n * LANES : (n + 1) * LANES]
            prev = found[LANES:, n * LANES : (n + 1) * LANES]
            even = jnp.concatenate([prev[:, 96:], main[:64, :64]], axis=1)
            grads.append(even + main[64:, 32:])
    grads.append(jnp.zeros((64, FIRST_BLOCKS * LANES - 9 * 96), F32))
    first = jnp.concatenate(grads, axis=1)
    for n in range(FIRST_BLOCKS):
        row = SECOND_ROWS + 64 * n
        out_ref[row : row + 64, :] = first[:, n * LANES : (n + 1) * LANES]
    used = SECOND_ROWS + 64 * FIRST_BLOCKS
    if out_ref.shape[0] > used:
        out_ref[used:, :] = jnp.zeros((out_ref.shape[0] - used, LANES), F32)

    core, square = place_ref[0], place_ref[1]
    squares, size = keep_ref.shape[0], keep_ref.shape[1]
    for n in range(squares):
        for ref, half in ((keep_ref, core), (give_ref, 1 - core)):
            start = pl.multiple_of((half * squares + (square ^ n)) * size, 8)
            ref[n] = out_ref[pl.ds(start, size), :].astype(ref.dtype)


def unpack(place_ref, keep_ref, got_ref, g1_hbm, g2_hbm, sums, first, sent):
    core, square = place_ref[0], place_ref[1]
    squares, size = keep_ref.shape[0], keep_ref.shape[1]
    for n in range(squares):
        for ref, half in ((keep_ref, core), (got_ref, 1 - core)):
            start = pl.multiple_of((half * squares + (square ^ n)) * size, 8)
            sums[pl.ds(start, size), :] = ref[-n % squares].astype(F32)
    second = pltpu.make_async_copy(sums.at[pl.ds(0, SECOND_ROWS)], g2_hbm, sent.at[0])
    second.start()
    found = [sums[SECOND_ROWS + 64 * n : SECOND_ROWS + 64 * (n + 1), :] for n in range(FIRST_BLOCKS)]
    first[...] = jnp.concatenate(found, axis=1)[:, : first.shape[1]]
    copy = pltpu.make_async_copy(first, g1_hbm, sent.at[1])
    copy.start()
    copy.wait()
    second.wait()


def local_grads(flags, place, squares, volume, faces, corners, cotangent, weights):
    planes = volume.shape[0]
    blocks = volume.shape[2] // LANES
    hidden_planes = planes // 2 + 3
    out_planes = planes // 4
    unit = 2 * squares * 16
    rows = -(-(SECOND_ROWS + 64 * FIRST_BLOCKS) // unit) * unit
    whole = pl.BlockSpec(memory_space=pltpu.VMEM)
    smem = pl.BlockSpec(memory_space=pltpu.SMEM)
    dep, row_a, row_b, edge_a, edge_b = faces
    tiles, parts, inner_hid, inner_slopes = pl.pallas_call(
        own_blocks,
        out_shape=[
            jax.ShapeDtypeStruct((3, planes + 9, blocks, 16, LANES), BF16),
            jax.ShapeDtypeStruct((hidden_planes + 1, blocks, 16, 2 * LANES), F32),
            jax.ShapeDtypeStruct((3, hidden_planes, blocks - 1, 8, LANES), F32),
            jax.ShapeDtypeStruct((planes // 2, blocks - 1, 16, LANES), F32),
        ],
        in_specs=[smem] + [whole] * 7,
        out_specs=[whole] * 4,
        scratch_shapes=[pltpu.VMEM((4, blocks, 40, LANES), F32)],
        compiler_params=pltpu.CompilerParams(vmem_limit_bytes=16 * 1024 * 1024),
        cost_estimate=pl.CostEstimate(flops=2 * 10**9, bytes_accessed=10**7, transcendentals=0),
    )(flags, volume, *faces, weights[0])
    scratch = [
        pltpu.VMEM((rows, LANES), F32),
        pltpu.VMEM((4, 2, 40, LANES), F32),
        pltpu.VMEM((3, planes + 7, 2, 16, LANES), BF16),
        pltpu.VMEM((hidden_planes, 2, 16, 2 * LANES), F32),
        pltpu.VMEM((planes // 2, 1, 16, LANES), F32),
        pltpu.VMEM((3, hidden_planes, 3, 8, LANES), F32),
        pltpu.VMEM((3, out_planes + 3, blocks + 2, 16, LANES), BF16),
        pltpu.VMEM((out_planes + 1, blocks + 1, 8, LANES), F32),
        pltpu.VMEM((out_planes // 2 + 1, blocks + 1, 16, LANES), F32),
        pltpu.VMEM((out_planes // 2 + 1, blocks + 1, 16, LANES), BF16),
    ]
    operands = (tiles, parts, inner_hid, inner_slopes, *faces, *corners, cotangent, *weights)
    return pl.pallas_call(
        body,
        out_shape=[jax.ShapeDtypeStruct((squares, rows // (2 * squares), LANES), dtype) for dtype in (F32, BF16)],
        in_specs=[smem] * 2 + [whole] * len(operands),
        out_specs=[whole] * 2,
        scratch_shapes=scratch,
        compiler_params=pltpu.CompilerParams(vmem_limit_bytes=28 * 1024 * 1024),
        cost_estimate=pl.CostEstimate(flops=4 * 10**9, bytes_accessed=10**7, transcendentals=0),
    )(flags, place, *operands)


def shards(volume, first_weight, second_weight, cotangent):
    half = lax.axis_index("depth")
    row, col = lax.axis_index("row"), lax.axis_index("col")
    rows, cols = lax.axis_size("row"), lax.axis_size("col")
    inner = [jnp.logical_and(i > 0, i < n - 1).astype(jnp.int32) for i, n in ((row, rows), (col, cols))]
    flags = jnp.stack([half, row % 2, col % 2, *inner])
    whole = pl.BlockSpec(memory_space=pltpu.VMEM)
    smem = pl.BlockSpec(memory_space=pltpu.SMEM)
    small = pltpu.CompilerParams(vmem_limit_bytes=12 * 1024 * 1024)
    planes, high, width = volume.shape
    groups = planes + cotangent.shape[0] // 4
    in_hbm = pl.BlockSpec(memory_space=pltpu.HBM)

    def stay(argument):
        return pltpu.with_memory_space_constraint(argument, pltpu.HBM)

    arguments = (volume, cotangent, first_weight, second_weight.T)
    shapes = [argument.shape for argument in arguments] + [(17, 4, width)]
    volume, cotangent, first_taps, second_taps, dep = pl.pallas_call(
        bring,
        out_shape=[jax.ShapeDtypeStruct(shape, BF16) for shape in shapes],
        in_specs=[smem] + [in_hbm] * 4,
        out_specs=[whole] * len(shapes),
        scratch_shapes=[pltpu.SemaphoreType.DMA((6,))],
        compiler_params=small,
    )(flags, *[stay(argument) for argument in arguments])
    row_b, row_a = pl.pallas_call(
        pack_rows,
        out_shape=[jax.ShapeDtypeStruct((groups, 4, width), BF16)] * 2,
        in_specs=[smem] + [whole] * 2,
        out_specs=[whole] * 2,
        compiler_params=small,
    )(flags, volume, cotangent)

    def to_col(block, kind):
        return lax.ppermute(block, ("row", "col"), pairs_of_lines(rows, cols, kind))

    dep = lax.ppermute(dep, "depth", [(0, 1), (1, 0)])
    route = []
    for i, j in pairs_on_line(rows, 1):
        route += [((d * rows + i) * cols + c, (d * rows + j) * cols + (c ^ 1 if i == j else c)) for d in (0, 1) for c in range(cols)]
    row_b = lax.ppermute(row_b, ("depth", "row", "col"), route)
    row_a = lax.ppermute(row_a, "row", pairs_on_line(rows, 0))
    side_a, side_b = pl.pallas_call(
        pack_sides,
        out_shape=[jax.ShapeDtypeStruct((groups, high, LANES), BF16)] * 2,
        in_specs=[smem] + [whole] * 2,
        out_specs=[whole] * 2,
        compiler_params=small,
    )(flags, volume, cotangent)
    dep, side_a, side_b, first_taps = lax.optimization_barrier((dep, side_a, side_b, first_taps))
    row_a, side_b = lax.optimization_barrier((row_a, side_b))
    side_a, side_b = to_col(side_a, 0), to_col(side_b, 1)
    low, top = [jnp.concatenate([dep[n : n + 1] for n in (*range(k, 16, 4), 16)], axis=0) for k in (0, 3)]
    even, ends = row % 2 == 0, jnp.logical_or(row == 0, row == rows - 1)
    edge_a = jnp.where(even, top, low)
    edge_b = jnp.where(ends, 0, jnp.where(even, low, top))
    edge_a = lax.ppermute(edge_a, "row", pairs_on_line(rows, 0))
    edge_b = lax.ppermute(edge_b, ("depth", "row"), pairs_of_lines(2, rows, 1))
    weights = pl.pallas_call(
        bands,
        out_shape=[jax.ShapeDtypeStruct(shape, BF16) for shape in ((1152, 256), (1152, 256), (9, 256, 128))],
        in_specs=[whole] * 2,
        out_specs=[whole] * 3,
        compiler_params=small,
    )(first_taps, second_taps)
    row_b, weights = lax.optimization_barrier((row_b, weights))
    col_a, col_b = pl.pallas_call(
        pack_corners,
        out_shape=[jax.ShapeDtypeStruct((planes + 14, 8, LANES), BF16)] * 2,
        in_specs=[smem] + [whole] * 5,
        out_specs=[whole] * 2,
        compiler_params=small,
    )(flags, row_b, row_a, dep, edge_a, edge_b)
    col_a, col_b, volume = lax.optimization_barrier((col_a, col_b, volume))
    col_a, col_b = to_col(col_a, 0), to_col(col_b, 1)

    spot = lax.axis_index(("depth", "row"))
    squares = lax.axis_size(("depth", "row")) // 2
    where = jnp.stack([spot % 2, spot // 2])
    faces, corners = (dep, row_a, row_b, edge_a, edge_b), (side_a, side_b, col_a, col_b)
    keep, give = local_grads(flags, where, squares, volume, faces, corners, cotangent, weights)

    def to_square(block, n):
        route = [(2 * i + c, 2 * (i ^ n) + c) for i in range(squares) for c in (0, 1)]
        return lax.ppermute(block, ("depth", "row"), route)

    def to_core(block):
        return lax.ppermute(block, ("depth", "row"), [(i, i ^ 1) for i in range(2 * squares)])

    def along_col(block, n):
        return lax.ppermute(block, "col", [(i, i ^ n) for i in range(cols)])

    both = keep + to_core(give).astype(F32)
    near = both.astype(BF16)
    order = [1, *reversed(range(2, squares))]
    share = add_up(both[0], *[to_square(near[n], n) for n in order])
    share = add_up(share, *[along_col(share, n) for n in range(1, cols)])
    mine = jnp.stack([share] + [to_square(share, n) for n in reversed(range(1, squares))])
    other = to_core(mine)
    grads = [jax.ShapeDtypeStruct(shape, F32) for shape in (first_weight.shape, second_weight.shape[::-1])]
    first_grad, second_grad = pl.pallas_call(
        unpack,
        out_shape=grads,
        in_specs=[smem] + [whole] * 2,
        out_specs=[in_hbm] * 2,
        scratch_shapes=[
            pltpu.VMEM((mine.shape[0] * mine.shape[1] * 2, LANES), F32),
            pltpu.VMEM(first_weight.shape, F32),
            pltpu.SemaphoreType.DMA((2,)),
        ],
        compiler_params=small,
    )(where, mine, other)
    return first_grad, second_grad.T


def solution(mesh):
    placed = (P("depth", "row", "col"), P(), P(), P("depth", "row", "col"))
    return jax.shard_map(shards, mesh=mesh, in_specs=placed, out_specs=(P(), P()), check_vma=False)
```
